32 devices in a mesh: dp: 16 (over z, y, x), tensor: 2 (over core).
Axes of the slice: x: 2, y: 2, z: 4, core: 2. Of those that a mesh axis runs over, the one named last changes fastest.
Arguments:
- tokens: bfloat16 [32768, 768], P('dp'), may hold values from -6 to 6
- cotangent: bfloat16 [32768, 768], P('dp'), may hold values from -6 to 6
- span_doc: int32 [256], replicated, may hold values from 0 to 191, as said below
- qkv_weight: float32 [768, 3, 768], P('dp', None, 'tensor'), may hold values from -0.21875 to 0.21875
- out_weight: float32 [768, 768], P('tensor', 'dp'), may hold values from -0.625 to 0.625
- ffn_in_weight: float32 [768, 3072], P('dp', 'tensor'), may hold values from -0.21875 to 0.21875
- ffn_out_weight: float32 [3072, 768], P('tensor', 'dp'), may hold values from -0.109375 to 0.109375
- norm_params: float32 [4, 768], P(None, 'dp'), may hold values from -1.2 to 2.5, as said below
- qkv_first: float32 [768, 3, 768], P('dp', None, 'tensor'), may hold values from -0.00061035156 to 0.00061035156
- qkv_second: float32 [768, 3, 768], P('dp', None, 'tensor'), may hold values from 7.061189e-11 to 1.1297903e-09
- out_first: float32 [768, 768], P('tensor', 'dp'), may hold values from -0.00061035156 to 0.00061035156
- out_second: float32 [768, 768], P('tensor', 'dp'), may hold values from 7.061189e-11 to 1.1297903e-09
- ffn_in_first: float32 [768, 3072], P('dp', 'tensor'), may hold values from -0.00061035156 to 0.00061035156
- ffn_in_second: float32 [768, 3072], P('dp', 'tensor'), may hold values from 7.061189e-11 to 1.1297903e-09
- ffn_out_first: float32 [3072, 768], P('tensor', 'dp'), may hold values from -0.00061035156 to 0.00061035156
- ffn_out_second: float32 [3072, 768], P('tensor', 'dp'), may hold values from 7.061189e-11 to 1.1297903e-09
- norm_first: float32 [4, 768], P(None, 'dp'), may hold values from -0.0024414062 to 0.0024414062
- norm_second: float32 [4, 768], P(None, 'dp'), may hold values from 1.1297903e-09 to 1.8076644e-08
Outputs:
- mixed: bfloat16 [32768, 768], P('dp')
- input_grad: float32 [32768, 768], P('dp')
- loss: float32 [], replicated
- clip_norm: float32 [], replicated
- qkv_first_new: float32 [768, 3, 768], P('dp', None, 'tensor')
- qkv_second_new: float32 [768, 3, 768], P('dp', None, 'tensor')
- qkv_weight_new: float32 [768, 3, 768], P('dp', None, 'tensor')
- out_first_new: float32 [768, 768], P('tensor', 'dp')
- out_second_new: float32 [768, 768], P('tensor', 'dp')
- out_weight_new: float32 [768, 768], P('tensor', 'dp')
- ffn_in_first_new: float32 [768, 3072], P('dp', 'tensor')
- ffn_in_second_new: float32 [768, 3072], P('dp', 'tensor')
- ffn_in_weight_new: float32 [768, 3072], P('dp', 'tensor')
- ffn_out_first_new: float32 [3072, 768], P('tensor', 'dp')
- ffn_out_second_new: float32 [3072, 768], P('tensor', 'dp')
- ffn_out_weight_new: float32 [3072, 768], P('tensor', 'dp')
- norm_first_new: float32 [4, 768], P(None, 'dp')
- norm_second_new: float32 [4, 768], P(None, 'dp')
- norm_params_new: float32 [4, 768], P(None, 'dp')
The draws below stay inside these ranges and needn't reach their ends.
Inputs may be any that keep to these rules, and one draw needn't show every extreme that they name: span_doc never falls along the spans and numbers the documents 0, 1, 2 and so on; each document holds one or two consecutive spans; exactly 64 documents hold two spans, document 0 among them. `norm_params`: rows 0 and 2 are gains, rows 1 and 3 shifts.
All inputs are finite; a program needn't handle non-finite values.
Results may differ from the reference program's by a relative error of at most 0.012.
Values may be sent and summed in bfloat16 or wider, within the bound.
No kernel may reach another device: no remote copies, remote signals or barrier semaphores. Data moves between devices by JAX's collectives and lax.ppermute only.
A program may use at most 192 MiB of HBM per device.

```python
import math
import jax
import jax.numpy as jnp
from jax import lax

D = 768
HEADS = 12
HEAD = 64
FF = 3072
SPAN = 128
SPANS_DEV = 16
STEP = 10
SPANS_ALL = 256
TOKENS = 32768
PARAMS = 7080960
N_DP = 16


def draw_span_doc(key, part):
    pair_count = SPANS_ALL // 4
    doc_count = SPANS_ALL - pair_count
    order = jax.random.permutation(jax.random.fold_in(key, 3), doc_count - 1).astype(jnp.int32)
    paired = jnp.concatenate([jnp.ones((1,), jnp.int32), (order < pair_count - 1).astype(jnp.int32)])
    lengths = (1 + paired).astype(jnp.int32)
    ends = jnp.cumsum(lengths).astype(jnp.int32)
    position = jnp.arange(SPANS_ALL, dtype=jnp.int32)
    return jnp.sum((ends[None, :] <= position[:, None]).astype(jnp.int32), axis=1).astype(jnp.int32)


def draw_norm_params(key, part):
    key_gain, key_shift = jax.random.split(jax.random.fold_in(key, 7))
    position = jnp.arange(D, dtype=jnp.float32) / (D - 1)
    rising = 0.6 * 3.0 ** position
    gains = rising[None, :] * jax.random.uniform(key_gain, (2, D), jnp.float32, 0.8, 1.25)
    shifts = jnp.clip(0.3 * jax.random.normal(key_shift, (2, D), jnp.float32), -1.2, 1.2)
    return jnp.stack([gains[0], shifts[0], gains[1], shifts[1]]).astype(jnp.float32)


def block_scale(own_key, dims, cuts, least, top_value):
    factor_of, own = 1.0, jax.random.fold_in(own_key, 6)
    for dim, blocks in cuts:
        heights = jnp.exp(jax.random.uniform(jax.random.fold_in(own, dim), (blocks,), jnp.float32, least / len(cuts), top_value / len(cuts)))
        factor_of = factor_of * jnp.repeat(heights, dims[dim] // blocks).reshape([-1 if axis == dim else 1 for axis in range(len(dims))])
    return factor_of


def gaussian(rng, shape, scale, reach, shards=(), kind=jnp.bfloat16):
    entries = jax.random.normal(rng, shape, jnp.float32) * scale
    if len(shards) > 0:
        entries = block_scale(rng, shape, shards, -0.22, 0.18) * entries
    return jnp.clip(entries, min=-reach, max=reach).astype(kind)


def setup_inputs(seed: int = 0) -> dict:
    splits = jax.random.split(jax.random.key(seed), 19)
    return {
        "tokens": gaussian(splits[0], (TOKENS, D), 1.0, 6.0, ((0, 16),)),
        "cotangent": gaussian(splits[1], (TOKENS, D), 1.0, 6.0, ((0, 16),)),
        "span_doc": draw_span_doc(jax.random.fold_in(splits[18], 71), 0),
        "qkv_weight": gaussian(splits[3], (D, 3, D), D ** -0.5, 0.21875, ((0, 16), (2, 2)), jnp.float32),
        "out_weight": gaussian(splits[4], (D, D), (D // 8) ** -0.5, 0.625, ((0, 2), (1, 16)), jnp.float32),
        "ffn_in_weight": gaussian(splits[5], (D, FF), D ** -0.5, 0.21875, ((0, 16), (1, 2)), jnp.float32),
        "ffn_out_weight": gaussian(splits[6], (FF, D), FF ** -0.5, 0.109375, ((0, 2), (1, 16)), jnp.float32),
        "norm_params": draw_norm_params(jax.random.fold_in(splits[18], 71), 0),
        "qkv_first": gaussian(splits[8], (D, 3, D), (0.11 / PARAMS ** 0.5), 0.00061035156, ((0, 16), (2, 2)), jnp.float32),
        "qkv_second": jnp.clip(jnp.exp(math.log(1.129790261344965e-09) - 2.7725887 * jax.random.uniform(splits[9], (D, 3, D), jnp.float32) ** block_scale(splits[9], (D, 3, D), ((0, 16), (2, 2)), -0.2, 0.2)), 7.061189133406032e-11, 1.129790261344965e-09),
        "out_first": gaussian(splits[10], (D, D), (0.11 / PARAMS ** 0.5), 0.00061035156, ((0, 2), (1, 16)), jnp.float32),
        "out_second": jnp.clip(jnp.exp(math.log(1.129790261344965e-09) - 2.7725887 * jax.random.uniform(splits[11], (D, D), jnp.float32) ** block_scale(splits[11], (D, D), ((0, 2), (1, 16)), -0.2, 0.2)), 7.061189133406032e-11, 1.129790261344965e-09),
        "ffn_in_first": gaussian(splits[12], (D, FF), (0.11 / PARAMS ** 0.5), 0.00061035156, ((0, 16), (1, 2)), jnp.float32),
        "ffn_in_second": jnp.clip(jnp.exp(math.log(1.129790261344965e-09) - 2.7725887 * jax.random.uniform(splits[13], (D, FF), jnp.float32) ** block_scale(splits[13], (D, FF), ((0, 16), (1, 2)), -0.2, 0.2)), 7.061189133406032e-11, 1.129790261344965e-09),
        "ffn_out_first": gaussian(splits[14], (FF, D), (0.11 / PARAMS ** 0.5), 0.00061035156, ((0, 2), (1, 16)), jnp.float32),
        "ffn_out_second": jnp.clip(jnp.exp(math.log(1.129790261344965e-09) - 2.7725887 * jax.random.uniform(splits[15], (FF, D), jnp.float32) ** block_scale(splits[15], (FF, D), ((0, 2), (1, 16)), -0.2, 0.2)), 7.061189133406032e-11, 1.129790261344965e-09),
        "norm_first": gaussian(splits[16], (4, D), (0.44 / PARAMS ** 0.5), 0.0024414062, ((1, 16),), jnp.float32),
        "norm_second": jnp.clip(jnp.exp(math.log(1.807664418151944e-08) - 2.7725887 * jax.random.uniform(splits[17], (4, D), jnp.float32) ** block_scale(splits[17], (4, D), ((1, 16),), -0.2, 0.2)), 1.129790261344965e-09, 1.807664418151944e-08),
    }


@jax.custom_vjp
def low(v):
    return lax.optimization_barrier(v.astype(jnp.bfloat16)).astype(jnp.float32)

@jax.custom_vjp
def low_back(v):
    return v

def low_keep(v):
    return (low(v), None)

def low_pass(kept, grad):
    return (grad,)

def back_keep(v):
    return (v, None)

def back_low(kept, grad):
    return (low(grad),)
low.defvjp(low_keep, low_pass)
low_back.defvjp(back_keep, back_low)
contrast_weight = 4.0

def matmul(left, right):
    return jnp.dot(left, right, precision=lax.Precision.HIGHEST, preferred_element_type=jnp.float32)

def einsum_high(form, left, right):
    return jnp.einsum(form, left, right, precision=lax.Precision.HIGHEST)

def layer_norm(hidden, norm_gain, norm_shift):
    center = hidden - lax.optimization_barrier(jnp.mean(hidden, axis=-1, keepdims=True))
    spread = lax.optimization_barrier(jnp.mean(center * center, axis=-1, keepdims=True))
    return center * lax.rsqrt(spread + 1e-06) * norm_gain + norm_shift

def contrast(cls_rows, span_doc):
    span_total = cls_rows.shape[0]
    logits = matmul(cls_rows, cls_rows.T) * cls_rows.shape[1] ** (-0.5)
    position = jnp.arange(span_total, dtype=jnp.int32)
    itself = position[:, None] == position[None, :]
    partner = jnp.logical_and(span_doc[:, None] == span_doc[None, :], jnp.logical_not(itself))
    masked = jnp.where(itself, -1000000000.0, logits)
    row_max = lax.optimization_barrier(jnp.max(masked, axis=1, keepdims=True))
    log_total = jnp.log(lax.optimization_barrier(jnp.sum(jnp.exp(masked - row_max), axis=1))) + row_max[:, 0]
    positive = lax.optimization_barrier(jnp.sum(jnp.where(partner, logits, 0.0), axis=1))
    flagged = jnp.where(jnp.any(partner, axis=1), 1.0, 0.0)
    return jnp.sum(flagged * (log_total - positive)) / jnp.sum(flagged)

def encode(span_group, weights):
    attn_in, attn_out, ffn_in, ffn_out, norm_rows = weights
    span_count = span_group.shape[0]
    row_count = span_count * SPAN
    flat_rows = span_group.reshape(row_count, D)
    packed = low(low_back(matmul(flat_rows, attn_in.reshape(D, 3 * D))))
    packed = packed.reshape(span_count, SPAN, 3, HEADS, HEAD)
    scores = low_back(einsum_high('nqhe,nkhe->nhqk', packed[:, :, 0], packed[:, :, 1]) * HEAD ** (-0.5))
    softmaxed = low(jax.nn.softmax(scores, axis=-1))
    context = low(low_back(einsum_high('nhqk,nkhe->nqhe', softmaxed, packed[:, :, 2])))
    attended = low_back(matmul(context.reshape(row_count, D), attn_out))
    normed = layer_norm(flat_rows + attended, norm_rows[0], norm_rows[1])
    hidden = low_back(matmul(low(normed), ffn_in))
    activated = low(jax.nn.gelu(hidden, approximate=False))
    resid_two = normed + low_back(matmul(activated, ffn_out))
    return layer_norm(resid_two, norm_rows[2], norm_rows[3]).reshape(span_count, SPAN, D)

def forward(inputs, attn_in, attn_out, ffn_in, ffn_out, norm_in, span_doc):
    weights = (low(attn_in), low(attn_out), low(ffn_in), low(ffn_out), low(norm_in))
    saved_encode = jax.checkpoint(encode)
    groups = inputs.reshape(N_DP, SPANS_DEV, SPAN, D)
    outputs = lax.map(lambda span_group: saved_encode(span_group, weights), groups)
    cls_rows = low(outputs[:, :, 0, :].reshape(SPANS_ALL, D))
    return (outputs.reshape(TOKENS, D), contrast(cls_rows, span_doc))

def adam_update(weight, gradient, moment_one, moment_two, step_rate, decay_rate):
    first_new = 0.9 * moment_one + 0.1 * gradient
    second_new = 0.999 * moment_two + 0.001 * gradient * gradient
    corr_first = first_new / (1.0 - 0.9 ** STEP)
    corr_second = second_new / (1.0 - 0.999 ** STEP)
    weight_new = weight - step_rate * (corr_first / (jnp.sqrt(corr_second) + 1e-08) + decay_rate * weight)
    return (first_new, second_new, weight_new)

def reference(tokens, cotangent, span_doc, qkv_weight, out_weight, ffn_in_weight, ffn_out_weight, norm_params, qkv_first, qkv_second, out_first, out_second, ffn_in_first, ffn_in_second, ffn_out_first, ffn_out_second, norm_first, norm_second):
    inputs = tokens.astype(jnp.float32)

    def objective(inputs_in, attn_in, attn_out, ffn_in, ffn_out, norm_in):
        return forward(inputs_in, attn_in, attn_out, ffn_in, ffn_out, norm_in, span_doc)
    (outputs, contrast_loss), pullback = jax.vjp(objective, inputs, qkv_weight, out_weight, ffn_in_weight, ffn_out_weight, norm_params)
    gradients = pullback((cotangent.astype(jnp.float32), jnp.asarray(contrast_weight * SPANS_ALL, dtype=jnp.float32)))
    square_sum = jnp.sum(gradients[1] * gradients[1]) + jnp.sum(gradients[2] * gradients[2])
    square_sum = square_sum + jnp.sum(gradients[3] * gradients[3]) + jnp.sum(gradients[4] * gradients[4])
    square_sum = square_sum + jnp.sum(gradients[5] * gradients[5])
    clip_norm = jnp.sqrt(square_sum)
    clip_scale = 1.0 / jnp.maximum(clip_norm, 1.0)
    qkv_new = adam_update(qkv_weight, gradients[1] * clip_scale, qkv_first, qkv_second, 0.02, 0.01)
    out_new = adam_update(out_weight, gradients[2] * clip_scale, out_first, out_second, 0.02, 0.01)
    up_new = adam_update(ffn_in_weight, gradients[3] * clip_scale, ffn_in_first, ffn_in_second, 0.02, 0.01)
    down_new = adam_update(ffn_out_weight, gradients[4] * clip_scale, ffn_out_first, ffn_out_second, 0.02, 0.01)
    norm_new = adam_update(norm_params, gradients[5] * clip_scale, norm_first, norm_second, 0.5, 0.0)
    return (outputs.astype(jnp.bfloat16), gradients[0], contrast_loss, clip_norm, qkv_new[0], qkv_new[1], qkv_new[2], out_new[0], out_new[1], out_new[2], up_new[0], up_new[1], up_new[2], down_new[0], down_new[1], down_new[2], norm_new[0], norm_new[1], norm_new[2])
```

```python
from functools import partial

import jax
import jax.numpy as jnp
from jax import lax
from jax.experimental import pallas as pl
from jax.experimental.pallas import tpu as pltpu
from jax.sharding import PartitionSpec as P

HEAD = 64
SPAN = 128
STEP = 10
D = 768
FF = 3072
NB = 16
RB = D // NB
HALF_QKV = 1152
HALF_OUT = 384
HALF_FF = 1536
ONE = HALF_QKV + HALF_OUT + 128
CONTRAST = 4.0
EPS = 1e-06
BF = jnp.bfloat16
F32 = jnp.float32
AXES = ("dp", "tensor")

NN = (((1,), (0,)), ((), ()))
NT = (((1,), (1,)), ((), ()))
TN = (((0,), (0,)), ((), ()))


def mm(left, right, dims=NN):
    return lax.dot_general(left, right, dims, preferred_element_type=F32)


def params(vmem=56):
    return pltpu.CompilerParams(vmem_limit_bytes=vmem * 2**20)


def cost(flops, bytes_accessed, trans=0):
    return pl.CostEstimate(flops=int(flops), bytes_accessed=int(bytes_accessed), transcendentals=int(trans))


HBM = pl.BlockSpec(memory_space=pl.ANY)


def bit_orders(n_dp):
    bits = n_dp.bit_length() - 1
    if bits == 4:
        return ((4, 8, 2, 1), (8, 4, 1, 2))
    up = tuple(1 << b for b in range(bits))[::-1]
    half = bits // 2
    return (up, up[: half - 1] + up[half - 1 :][::-1] if bits > 2 else up[::-1])


def pairs_of(n_dp, orders, step):
    out = []
    for d in range(n_dp):
        for c in range(2):
            out.append((d * 2 + c, (d ^ orders[c][step]) * 2 + c))
    return out


def rel_of(order):
    out = []
    for p in range(1 << len(order)):
        r = 0
        for k, b in enumerate(order):
            if (p >> k) & 1:
                r ^= b
        out.append(r)
    return out


def core_swap(block):
    return lax.ppermute(block, "tensor", [(0, 1), (1, 0)])


def gather_group(shard, n_dp):
    orders = bit_orders(n_dp)
    steps = len(orders[0])
    held = shard[None]
    for k in range(steps):
        came = lax.ppermute(held, AXES, pairs_of(n_dp, orders, k))
        if k == steps - 1:
            return held, came
        held = jnp.concatenate([held, came], axis=0)


def scatter_group(own, other, n_dp):
    orders = bit_orders(n_dp)
    steps = len(orders[0])
    size = n_dp // 2
    keep = own[:size].astype(F32) + other[:size].astype(F32)
    send = (own[size:].astype(F32) + other[size:].astype(F32)).astype(BF)
    keep = keep.astype(BF)
    for k in reversed(range(steps)):
        came = lax.ppermute(send, AXES, pairs_of(n_dp, orders, k))
        if k == 0:
            return keep[0].astype(F32) + came[0].astype(F32)
        size //= 2
        total = keep.astype(F32) + came.astype(F32)
        keep = total[:size].astype(BF)
        send = total[size:].astype(BF)


def load_pieces(refs, tab, dest, sems):
    copies = []
    core = tab[0]
    for n, ref in enumerate(refs):
        half = core if n < 2 else 1 - core
        for p in range(NB // 2):
            q = (n % 2) * (NB // 2) + p
            place = tab[2 + (n // 2) * NB + q]
            copies.append(pltpu.make_async_copy(ref.at[p], dest.at[half, place], sems.at[n * (NB // 2) + p]))
    for c in copies:
        c.start()
    for c in copies:
        c.wait()


def weight(scratch, half, first, last):
    return scratch[half, :, :, first:last].reshape(D, last - first)


def norm_fwd(hidden):
    center = hidden - jnp.mean(hidden, axis=-1, keepdims=True)
    spread = jnp.mean(center * center, axis=-1, keepdims=True)
    rstd = lax.rsqrt(spread + EPS)
    return center * rstd, rstd


def norm_bwd(grad, xh, rstd, gain):
    e = grad * gain
    m1 = jnp.mean(e, axis=-1, keepdims=True)
    m2 = jnp.mean(e * xh, axis=-1, keepdims=True)
    return rstd * (e - m1 - xh * m2)


def head_masks(rows, scale):
    lane = lax.broadcasted_iota(jnp.int32, (rows, 128), 1)
    return (
        jnp.where(lane < HEAD, scale, 0.0).astype(BF),
        jnp.where(lane < HEAD, 0.0, scale).astype(BF),
    )


def stack_heads(pair, masks):
    return jnp.concatenate([pair * masks[0], pair * masks[1]], axis=0)


def merge_heads(both):
    lane = lax.broadcasted_iota(jnp.int32, (SPAN, 128), 1)
    return jnp.where(lane < HEAD, both[:SPAN], both[SPAN:])


def attn_fwd_kernel(
    tab, tok_ref, w0, w1, w2, w3, qkv_ref, ctx_ref, lse_ref, xh_ref, rstd_ref, tokt_ref, p_ref, w, sems
):
    @pl.when(pl.program_id(0) == 0)
    def _():
        load_pieces((w0, w1, w2, w3), tab, w, sems)
        cols = weight(w, 0, HALF_QKV + HALF_OUT, ONE).astype(F32)
        p_ref[...] = cols.T[:8]

    x = tok_ref[...]
    tokt_ref[...] = x.T
    masks = head_masks(SPAN, HEAD ** (-0.5))
    attn = x.astype(F32)
    for h in range(2):
        qkv = mm(x, weight(w, h, 0, HALF_QKV)).astype(BF)
        qkv_ref[h] = qkv
        rows = []
        for s in range(2):
            own = qkv[s * SPAN : (s + 1) * SPAN]
            parts = []
            for j in range(3):
                q = stack_heads(own[:, j * 128 : (j + 1) * 128], masks)
                k = own[:, HALF_OUT + j * 128 : HALF_OUT + (j + 1) * 128]
                v = own[:, 2 * HALF_OUT + j * 128 : 2 * HALF_OUT + (j + 1) * 128]
                st = mm(k, q, NT)
                top = jnp.max(st, axis=0, keepdims=True)
                ex = jnp.exp(st - top)
                total = jnp.sum(ex, axis=0, keepdims=True)
                pt = (ex * (1.0 / total)).astype(BF)
                lse_ref[s, h * 3 + j : h * 3 + j + 1, :] = top + jnp.log(total)
                parts.append(merge_heads(mm(pt, v, TN)).astype(BF))
            rows.append(jnp.concatenate(parts, axis=1))
        ctx = jnp.concatenate(rows, axis=0)
        ctx_ref[h] = ctx
        attn = attn + mm(ctx, weight(w, h, HALF_QKV, HALF_QKV + HALF_OUT), NT)
    xh, rstd = norm_fwd(attn)
    rstd = jnp.broadcast_to(rstd, (2 * SPAN, 128))
    for s in range(2):
        for q in range(4):
            r = s * SPAN + q * 32
            xh_ref[q, s] = xh[r : r + 32]
            rstd_ref[q, s] = rstd[r : r + 32]


def attn_fwd(tab, tokens, pieces, rows):
    spans = rows // SPAN
    steps = spans // 2
    out = [
        jax.ShapeDtypeStruct((2, rows, HALF_QKV), BF),
        jax.ShapeDtypeStruct((2, rows, HALF_OUT), BF),
        jax.ShapeDtypeStruct((spans, 8, 2 * SPAN), F32),
        jax.ShapeDtypeStruct((4, spans, 32, D), F32),
        jax.ShapeDtypeStruct((4, spans, 32, 128), F32),
        jax.ShapeDtypeStruct((D, rows), BF),
        jax.ShapeDtypeStruct((8, D), F32),
    ]
    return pl.pallas_call(
        attn_fwd_kernel,
        out_shape=out,
        grid_spec=pltpu.PrefetchScalarGridSpec(
            num_scalar_prefetch=1,
            grid=(steps,),
            in_specs=[pl.BlockSpec((2 * SPAN, D), lambda i, tab: (tab[0] * steps + i, 0))] + [HBM] * 4,
            out_specs=[
                pl.BlockSpec((2, 2 * SPAN, HALF_QKV), lambda i, tab: (0, i, 0)),
                pl.BlockSpec((2, 2 * SPAN, HALF_OUT), lambda i, tab: (0, i, 0)),
                pl.BlockSpec((2, 8, 2 * SPAN), lambda i, tab: (i, 0, 0)),
                pl.BlockSpec((4, 2, 32, D), lambda i, tab: (0, i, 0, 0)),
                pl.BlockSpec((4, 2, 32, 128), lambda i, tab: (0, i, 0, 0)),
                pl.BlockSpec((D, 2 * SPAN), lambda i, tab: (0, i)),
                pl.BlockSpec((8, D), lambda i, tab: (0, 0)),
            ],
            scratch_shapes=[pltpu.VMEM((2, NB, RB, ONE), BF), pltpu.SemaphoreType.DMA((2 * NB,))],
        ),
        compiler_params=params(),
        cost_estimate=cost(rows * 8.2e6, rows * 20000 + 5e6, rows * 1600),
        name="attn_fwd",
    )(tab, tokens, *pieces)


def gelu_pair(u):
    a = jnp.abs(u)
    t = 1.0 / (1.0 + (0.3275911 * 0.5**0.5) * a)
    e = jnp.exp(-0.5 * u * u)
    poly = 1.061405429 * t - 1.453152027
    poly = poly * t + 1.421413741
    poly = poly * t - 0.284496736
    poly = poly * t + 0.254829592
    tail = (0.5 * poly * t) * e
    phi = jnp.where(u >= 0.0, 1.0 - tail, tail)
    return u * phi, phi + (0.3989422804014327 * u) * e


TILE = 512


def ffn_up_kernel(tab, xh_ref, p_ref, w0, w1, w2, w3, g_ref, gp_ref, yt_ref, w, sems):
    @pl.when(pl.program_id(0) == 0)
    def _():
        load_pieces((w0, w1, w2, w3), tab, w, sems)

    y = xh_ref[...] * p_ref[0:1, :] + p_ref[1:2, :]
    yb = y.astype(BF)
    yt_ref[...] = yb.T
    for h in range(2):
        for t in range(HALF_FF // TILE):
            u = mm(yb, weight(w, h, t * TILE, (t + 1) * TILE))
            g, gp = gelu_pair(u)
            g_ref[h, :, t * TILE : (t + 1) * TILE] = g.astype(BF)
            gp_ref[h, :, t * TILE : (t + 1) * TILE] = gp.astype(BF)


def ffn_up(tab, xh, prow, pieces, rows):
    steps = 4
    blk = rows // steps
    return pl.pallas_call(
        ffn_up_kernel,
        out_shape=[
            jax.ShapeDtypeStruct((2, rows, HALF_FF), BF),
            jax.ShapeDtypeStruct((2, rows, HALF_FF), BF),
            jax.ShapeDtypeStruct((D, rows), BF),
        ],
        grid_spec=pltpu.PrefetchScalarGridSpec(
            num_scalar_prefetch=1,
            grid=(steps,),
            in_specs=[
                pl.BlockSpec((blk, D), lambda i, tab: (i, 0)),
                pl.BlockSpec((8, D), lambda i, tab: (0, 0)),
            ]
            + [HBM] * 4,
            out_specs=[
                pl.BlockSpec((2, blk, HALF_FF), lambda i, tab: (0, i, 0)),
                pl.BlockSpec((2, blk, HALF_FF), lambda i, tab: (0, i, 0)),
                pl.BlockSpec((D, blk), lambda i, tab: (0, i)),
            ],
            scratch_shapes=[pltpu.VMEM((2, NB, RB, HALF_FF), BF), pltpu.SemaphoreType.DMA((2 * NB,))],
        ),
        compiler_params=params(),
        cost_estimate=cost(rows * 4.8e6, rows * 18000 + 5e6, rows * 6000),
        name="ffn_up",
    )(tab, xh, prow, *pieces)


def ffn_down_kernel(tab, xh1_ref, p_ref, g_ref, w0, w1, w2, w3, mixed_ref, cls_ref, xh_ref, rstd_ref, w, sems):
    @pl.when(pl.program_id(0) == 0)
    def _():
        load_pieces((w0, w1, w2, w3), tab, w, sems)

    total = xh1_ref[...] * p_ref[0:1, :] + p_ref[1:2, :]
    for h in range(2):
        total = total + mm(g_ref[h], weight(w, h, 0, HALF_FF), NT)
    xh, rstd = norm_fwd(total)
    xh_ref[...] = xh
    rstd_ref[...] = jnp.broadcast_to(rstd, rstd_ref.shape)
    out = xh * p_ref[2:3, :] + p_ref[3:4, :]
    mixed_ref[...] = out.astype(BF).reshape(mixed_ref.shape)

    @pl.when(pl.program_id(0) == 0)
    def _():
        cls_ref[...] = out.reshape(mixed_ref.shape)[:, 0, :]


def ffn_down(tab, xh1, prow, g, pieces, rows):
    steps = 4
    blk = rows // steps
    spans = rows // SPAN
    return pl.pallas_call(
        ffn_down_kernel,
        out_shape=[
            jax.ShapeDtypeStruct((spans, SPAN, D), BF),
            jax.ShapeDtypeStruct((spans, D), F32),
            jax.ShapeDtypeStruct((rows, D), F32),
            jax.ShapeDtypeStruct((rows, 128), F32),
        ],
        grid_spec=pltpu.PrefetchScalarGridSpec(
            num_scalar_prefetch=1,
            grid=(steps,),
            in_specs=[
                pl.BlockSpec((blk, D), lambda i, tab: (i, 0)),
                pl.BlockSpec((8, D), lambda i, tab: (0, 0)),
                pl.BlockSpec((2, blk, HALF_FF), lambda i, tab: (0, i, 0)),
            ]
            + [HBM] * 4,
            out_specs=[
                pl.BlockSpec((spans, 32, D), lambda i, tab: (0, i, 0)),
                pl.BlockSpec((spans, D), lambda i, tab: (0, 0)),
                pl.BlockSpec((blk, D), lambda i, tab: (i, 0)),
                pl.BlockSpec((blk, 128), lambda i, tab: (i, 0)),
            ],
            scratch_shapes=[pltpu.VMEM((2, NB, RB, HALF_FF), BF), pltpu.SemaphoreType.DMA((2 * NB,))],
        ),
        compiler_params=params(),
        cost_estimate=cost(rows * 4.8e6, rows * 16000 + 5e6, rows),
        name="ffn_down",
    )(tab, xh1, prow, g, *pieces)


def contrast_kernel(where, doc_row, doc_col, cls_ref, loss_ref, grad_ref, rows, own_doc):
    spans = doc_row.shape[1]
    blocks, per = cls_ref.shape[0], cls_ref.shape[1]
    me = where[0]
    for n in range(blocks):
        rows[where[1 + n]] = cls_ref[n].astype(F32)
    a = rows[...].reshape(spans, D).astype(BF)
    own = rows[me].astype(BF)
    scale = D ** (-0.5)
    col = lax.broadcasted_iota(jnp.int32, (spans, spans), 1)
    row = lax.broadcasted_iota(jnp.int32, (spans, spans), 0)
    logits = mm(a, a, NT) * scale
    partner = (doc_col[...] == doc_row[...]) & (row != col)
    masked = jnp.where(row == col, -1000000000.0, logits)
    top = jnp.max(masked, axis=0, keepdims=True)
    lse = jnp.log(jnp.sum(jnp.exp(masked - top), axis=0, keepdims=True)) + top
    positive = jnp.sum(jnp.where(partner, logits, 0.0), axis=0, keepdims=True)
    flagged = jnp.max(jnp.where(partner, 1.0, 0.0), axis=0, keepdims=True)
    count = jnp.sum(flagged, axis=1, keepdims=True)
    loss = jnp.sum(flagged * (lse - positive), axis=1, keepdims=True) / count
    loss_ref[...] = jnp.broadcast_to(loss, loss_ref.shape)

    weight_row = flagged * (CONTRAST * spans) / count
    own_doc[...] = doc_col[...].reshape(blocks, per, 1)
    docs = own_doc[me]
    col = lax.broadcasted_iota(jnp.int32, (per, spans), 1)
    row = lax.broadcasted_iota(jnp.int32, (per, spans), 0) + me * per
    logits = mm(own, a, NT) * scale
    same = jnp.where((docs == doc_row[...]) & (row != col), 1.0, 0.0)
    masked = jnp.where(row == col, -1000000000.0, logits)
    top = jnp.max(masked, axis=1, keepdims=True)
    ex = jnp.exp(masked - top)
    soft = ex / jnp.sum(ex, axis=1, keepdims=True)
    own_weight = jnp.max(same, axis=1, keepdims=True) * (CONTRAST * spans) / count
    sym = own_weight * (soft - same) + weight_row * (jnp.exp(masked - lse) - same)
    high = sym.astype(BF)
    low = (sym - high.astype(F32)).astype(BF)
    grad_ref[...] = (mm(high, a) + mm(low, a)) * scale


def contrast(where, span_doc, cls_all):
    blocks, per, _ = cls_all.shape
    spans = blocks * per
    vm = pl.BlockSpec(memory_space=pltpu.VMEM)
    return pl.pallas_call(
        contrast_kernel,
        out_shape=[jax.ShapeDtypeStruct((1, 128), F32), jax.ShapeDtypeStruct((per, D), F32)],
        in_specs=[pl.BlockSpec(memory_space=pltpu.SMEM), vm, vm, vm],
        out_specs=[vm, vm],
        scratch_shapes=[pltpu.VMEM((blocks, per, D), F32), pltpu.VMEM((blocks, per, 1), jnp.int32)],
        compiler_params=params(),
        name="contrast",
    )(where, span_doc.reshape(1, spans), span_doc.reshape(spans, 1), cls_all)


def norm_two_kernel(tab, cot_ref, cls_ref, xh_ref, rstd_ref, p_ref, dh_ref, dft_ref, sums_ref):
    i = pl.program_id(0)
    spans = cls_ref.shape[0]
    grad = cot_ref[...].astype(F32)
    first = lax.broadcasted_iota(jnp.int32, grad.shape, 1) == 0
    extra = jnp.where(jnp.logical_and(first, i == 0), cls_ref[...].reshape(spans, 1, D), 0.0)
    grad = (grad + extra).reshape(spans * 32, D)
    xh = xh_ref[...]
    dh = norm_bwd(grad, xh, rstd_ref[:, 0:1], p_ref[2:3, :])
    dh_ref[...] = dh
    dft_ref[...] = dh.astype(BF).T

    @pl.when(i == 0)
    def _():
        sums_ref[...] = jnp.zeros_like(sums_ref)

    sums_ref[0:1, :] += jnp.sum(grad * xh, axis=0, keepdims=True)
    sums_ref[1:2, :] += jnp.sum(grad, axis=0, keepdims=True)


def norm_two(tab, cotangent, grad_cls, xh, rstd, prow, rows):
    spans = rows // SPAN
    blk = rows // 4
    return pl.pallas_call(
        norm_two_kernel,
        out_shape=[
            jax.ShapeDtypeStruct((rows, D), F32),
            jax.ShapeDtypeStruct((D, rows), BF),
            jax.ShapeDtypeStruct((8, D), F32),
        ],
        grid_spec=pltpu.PrefetchScalarGridSpec(
            num_scalar_prefetch=1,
            grid=(4,),
            in_specs=[
                pl.BlockSpec((spans, 32, D), lambda i, tab: (tab[0], i, 0)),
                pl.BlockSpec((spans, D), lambda i, tab: (0, 0)),
                pl.BlockSpec((blk, D), lambda i, tab: (i, 0)),
                pl.BlockSpec((blk, 128), lambda i, tab: (i, 0)),
                pl.BlockSpec((8, D), lambda i, tab: (0, 0)),
            ],
            out_specs=[
                pl.BlockSpec((blk, D), lambda i, tab: (i, 0)),
                pl.BlockSpec((D, blk), lambda i, tab: (0, i)),
                pl.BlockSpec((8, D), lambda i, tab: (0, 0)),
            ],
        ),
        compiler_params=params(),
        cost_estimate=cost(rows * D * 20, rows * 12000, rows),
        name="norm_two",
    )(tab, cotangent.reshape(-1, SPAN, D), grad_cls, xh, rstd, prow)


def ffn_back_kernel(
    tab, dh_ref, gp_ref, xh1_ref, rstd1_ref, p_ref, u0, u1, u2, u3, d0, d1, d2, d3,
    du_ref, dh1_ref, sums_ref, wu, wd, sem_u, sem_d,
):
    i = pl.program_id(0)

    @pl.when(i == 0)
    def _():
        load_pieces((d0, d1, d2, d3), tab, wd, sem_d)
        load_pieces((u0, u1, u2, u3), tab, wu, sem_u)
        sums_ref[...] = jnp.zeros_like(sums_ref)

    dh = dh_ref[...]
    df = dh.astype(BF)
    grad = dh
    for h in range(2):
        for t in range(HALF_FF // TILE):
            lo, hi = t * TILE, (t + 1) * TILE
            dg = mm(df, weight(wd, h, lo, hi))
            du = (dg * gp_ref[h, :, lo:hi].astype(F32)).astype(BF)
            du_ref[h, :, lo:hi] = du
        grad = grad + mm(du_ref[h], weight(wu, h, 0, HALF_FF), NT)
    xh = xh1_ref[...]
    dh1_ref[...] = norm_bwd(grad, xh, rstd1_ref[:, 0:1], p_ref[0:1, :])
    sums_ref[0:1, :] += jnp.sum(grad * xh, axis=0, keepdims=True)
    sums_ref[1:2, :] += jnp.sum(grad, axis=0, keepdims=True)


def ffn_back(tab, dh2, gp, xh1, rstd1, prow, up, down, rows):
    steps = 4
    blk = rows // steps
    return pl.pallas_call(
        ffn_back_kernel,
        out_shape=[
            jax.ShapeDtypeStruct((2, rows, HALF_FF), BF),
            jax.ShapeDtypeStruct((rows, D), F32),
            jax.ShapeDtypeStruct((8, D), F32),
        ],
        grid_spec=pltpu.PrefetchScalarGridSpec(
            num_scalar_prefetch=1,
            grid=(steps,),
            in_specs=[
                pl.BlockSpec((blk, D), lambda i, tab: (i, 0)),
                pl.BlockSpec((2, blk, HALF_FF), lambda i, tab: (0, i, 0)),
                pl.BlockSpec((blk, D), lambda i, tab: (i, 0)),
                pl.BlockSpec((blk, 128), lambda i, tab: (i, 0)),
                pl.BlockSpec((8, D), lambda i, tab: (0, 0)),
            ]
            + [HBM] * 8,
            out_specs=[
                pl.BlockSpec((2, blk, HALF_FF), lambda i, tab: (0, i, 0)),
                pl.BlockSpec((blk, D), lambda i, tab: (i, 0)),
                pl.BlockSpec((8, D), lambda i, tab: (0, 0)),
            ],
            scratch_shapes=[
                pltpu.VMEM((2, NB, RB, HALF_FF), BF),
                pltpu.VMEM((2, NB, RB, HALF_FF), BF),
                pltpu.SemaphoreType.DMA((2 * NB,)),
                pltpu.SemaphoreType.DMA((2 * NB,)),
            ],
        ),
        compiler_params=params(),
        cost_estimate=cost(rows * 9.5e6, rows * 24000 + 1e7, rows),
        name="ffn_back",
    )(tab, dh2, gp, xh1, rstd1, prow, *up, *down)


def store_blocks(out_ref, grad, tab, first):
    for j in range(NB):
        out_ref[tab[first + j]] = grad[j * RB : (j + 1) * RB].astype(BF)


def weight_grad_kernel(tab, xt_ref, y_ref, out_ref):
    store_blocks(out_ref, mm(xt_ref[...], y_ref[...]), tab, 1)


def weight_grad(tab, xt, y, name):
    rows = xt.shape[1]
    width = y.shape[2]
    tile = 512
    return pl.pallas_call(
        weight_grad_kernel,
        out_shape=jax.ShapeDtypeStruct((NB, RB, width), BF),
        grid_spec=pltpu.PrefetchScalarGridSpec(
            num_scalar_prefetch=1,
            grid=(width // tile,),
            in_specs=[
                pl.BlockSpec((D, rows), lambda t, tab: (0, 0)),
                pl.BlockSpec((None, rows, tile), lambda t, tab: (tab[0], 0, t)),
            ],
            out_specs=pl.BlockSpec((NB, RB, tile), lambda t, tab: (0, 0, t)),
        ),
        compiler_params=params(),
        cost_estimate=cost(2 * rows * D * width, rows * (D + width) * 2 + D * width * 2),
        name=name,
    )(tab, xt, y)


def attn_back_kernel(
    tab, dh1_ref, qkv_ref, lse_ref, w0, w1, w2, w3, dqkv_ref, dat_ref, dh1n_ref, w, sems
):
    @pl.when(pl.program_id(0) == 0)
    def _():
        load_pieces((w0, w1, w2, w3), tab, w, sems)

    dh1 = jnp.concatenate([dh1_ref[q, s] for s in range(2) for q in range(4)], axis=0)
    dh1n_ref[...] = dh1
    da = dh1.astype(BF)
    dat_ref[...] = da.T
    masks = head_masks(SPAN, HEAD ** (-0.5))
    plain = head_masks(SPAN, 1.0)
    for h in range(2):
        dctx = mm(da, weight(w, h, HALF_QKV, HALF_QKV + HALF_OUT)).astype(BF)
        for s in range(2):
            lo, hi = s * SPAN, (s + 1) * SPAN
            for j in range(3):
                a, b = j * 128, (j + 1) * 128
                q = stack_heads(qkv_ref[h, lo:hi, a:b], masks)
                k = qkv_ref[h, lo:hi, HALF_OUT + a : HALF_OUT + b]
                v = qkv_ref[h, lo:hi, 2 * HALF_OUT + a : 2 * HALF_OUT + b]
                dc = stack_heads(dctx[lo:hi, a:b], plain)
                st = mm(k, q, NT)
                pt = jnp.exp(st - lse_ref[s, h * 3 + j : h * 3 + j + 1, :])
                dpt = mm(v, dc, NT)
                dst = pt * (dpt - jnp.sum(pt * dpt, axis=0, keepdims=True))
                dst = dst.astype(BF)
                dv = mm(pt.astype(BF), dc)
                dk = mm(dst, q)
                dq = merge_heads(mm(dst, k, TN)) * HEAD ** (-0.5)
                dqkv_ref[h, lo:hi, a:b] = dq.astype(BF)
                dqkv_ref[h, lo:hi, HALF_OUT + a : HALF_OUT + b] = dk.astype(BF)
                dqkv_ref[h, lo:hi, 2 * HALF_OUT + a : 2 * HALF_OUT + b] = dv.astype(BF)


def attn_back(tab, dh1, qkv, lse, pieces, rows):
    spans = rows // SPAN
    steps = spans // 2
    return pl.pallas_call(
        attn_back_kernel,
        out_shape=[
            jax.ShapeDtypeStruct((2, rows, HALF_QKV), BF),
            jax.ShapeDtypeStruct((D, rows), BF),
            jax.ShapeDtypeStruct((rows, D), F32),
        ],
        grid_spec=pltpu.PrefetchScalarGridSpec(
            num_scalar_prefetch=1,
            grid=(steps,),
            in_specs=[
                pl.BlockSpec((4, 2, 32, D), lambda i, tab: (0, i, 0, 0)),
                pl.BlockSpec((2, 2 * SPAN, HALF_QKV), lambda i, tab: (0, i, 0)),
                pl.BlockSpec((2, 8, 2 * SPAN), lambda i, tab: (i, 0, 0)),
            ]
            + [HBM] * 4,
            out_specs=[
                pl.BlockSpec((2, 2 * SPAN, HALF_QKV), lambda i, tab: (0, i, 0)),
                pl.BlockSpec((D, 2 * SPAN), lambda i, tab: (0, i)),
                pl.BlockSpec((2 * SPAN, D), lambda i, tab: (i, 0)),
            ],
            scratch_shapes=[pltpu.VMEM((2, NB, RB, ONE), BF), pltpu.SemaphoreType.DMA((2 * NB,))],
        ),
        compiler_params=params(),
        cost_estimate=cost(rows * 12e6, rows * 20000 + 5e6, rows * 1600),
        name="attn_back",
    )(tab, dh1.reshape(4, spans, 32, D), qkv, lse, *pieces)


def last_grad_kernel(tab, tokt_ref, dqkv_ref, dat_ref, ctx_ref, one_ref, two_ref, out_ref):
    t = pl.program_id(0)
    grad = mm(tokt_ref[...], dqkv_ref[...])
    for part in range(3):

        @pl.when(t == part)
        def _():
            for j in range(NB):
                out_ref[tab[1 + j], :, part * HALF_OUT : (part + 1) * HALF_OUT] = grad[
                    j * RB : (j + 1) * RB
                ].astype(BF)

    @pl.when(t == 2)
    def _():
        proj = mm(dat_ref[...], ctx_ref[...])
        norm = jnp.concatenate([one_ref[0:2, :], two_ref[0:2, :], jnp.zeros((124, D), F32)], axis=0).T
        for j in range(NB):
            out_ref[tab[1 + j], :, HALF_QKV : HALF_QKV + HALF_OUT] = proj[j * RB : (j + 1) * RB].astype(BF)
            out_ref[tab[1 + j], :, HALF_QKV + HALF_OUT : ONE] = norm[j * RB : (j + 1) * RB].astype(BF)


def last_grad(tab, tokt, dqkv, dat, ctx, one, two, name):
    rows = tokt.shape[1]
    return pl.pallas_call(
        last_grad_kernel,
        out_shape=jax.ShapeDtypeStruct((NB, RB, ONE), BF),
        grid_spec=pltpu.PrefetchScalarGridSpec(
            num_scalar_prefetch=1,
            grid=(3,),
            in_specs=[
                pl.BlockSpec((D, rows), lambda t, tab: (0, 0)),
                pl.BlockSpec((None, rows, HALF_OUT), lambda t, tab: (tab[0], 0, t)),
                pl.BlockSpec((D, rows), lambda t, tab: (0, 0)),
                pl.BlockSpec((None, rows, HALF_OUT), lambda t, tab: (tab[0], 0, 0)),
                pl.BlockSpec((8, D), lambda t, tab: (0, 0)),
                pl.BlockSpec((8, D), lambda t, tab: (0, 0)),
            ],
            out_specs=pl.BlockSpec((NB, RB, ONE), lambda t, tab: (0, 0, 0)),
        ),
        compiler_params=params(),
        cost_estimate=cost(2 * rows * D * ONE, rows * (D + ONE) * 4 + D * ONE * 2),
        name=name,
    )(tab, tokt, dqkv, dat, ctx, one, two)


def input_grad_kernel(tab, dh1_ref, dqkv_ref, w0, w1, w2, w3, out_ref, w, sems):
    @pl.when(pl.program_id(0) == 0)
    def _():
        load_pieces((w0, w1, w2, w3), tab, w, sems)

    total = dh1_ref[...]
    for h in range(2):
        total = total + mm(dqkv_ref[h], weight(w, h, 0, HALF_QKV), NT)
    out_ref[...] = total


def input_grads(tab, dh1, dqkv, pieces, rows):
    blk = 2 * SPAN
    return pl.pallas_call(
        input_grad_kernel,
        out_shape=jax.ShapeDtypeStruct((rows, D), F32),
        grid_spec=pltpu.PrefetchScalarGridSpec(
            num_scalar_prefetch=1,
            grid=(rows // blk,),
            in_specs=[
                pl.BlockSpec((blk, D), lambda i, tab: (i, 0)),
                pl.BlockSpec((2, blk, HALF_QKV), lambda i, tab: (0, i, 0)),
            ]
            + [HBM] * 4,
            out_specs=pl.BlockSpec((blk, D), lambda i, tab: (i, 0)),
            scratch_shapes=[pltpu.VMEM((2, NB, RB, ONE), BF), pltpu.SemaphoreType.DMA((2 * NB,))],
        ),
        compiler_params=params(),
        cost_estimate=cost(rows * 3.6e6, rows * 12000 + 5e6),
        name="input_grads",
    )(tab, dh1, dqkv, *pieces)


def adam_update(weight, gradient, moment_one, moment_two, step_rate, decay_rate):
    first_new = 0.9 * moment_one + 0.1 * gradient
    second_new = 0.999 * moment_two + 0.001 * gradient * gradient
    corr_first = first_new / (1.0 - 0.9**STEP)
    corr_second = second_new / (1.0 - 0.999**STEP)
    weight_new = weight - step_rate * (
        corr_first / (jnp.sqrt(corr_second) + 1e-08) + decay_rate * weight
    )
    return (first_new, second_new, weight_new)


def both_halves(own, core):
    other = core_swap(own)
    low = jnp.where(core == 0, own, other)
    high = jnp.where(core == 0, other, own)
    return jnp.concatenate([low, high], axis=0)


def body(
    tokens,
    cotangent,
    span_doc,
    qkv_weight,
    out_weight,
    ffn_in_weight,
    ffn_out_weight,
    norm_params,
    qkv_first,
    qkv_second,
    out_first,
    out_second,
    ffn_in_first,
    ffn_in_second,
    ffn_out_first,
    ffn_out_second,
    norm_first,
    norm_second,
):
    n_dp = lax.axis_size("dp")
    dp = lax.axis_index("dp")
    core = lax.axis_index("tensor")
    shard = D // n_dp
    rows = tokens.shape[0] // 2
    spans = rows // SPAN
    direct = n_dp == NB

    orders = bit_orders(n_dp)
    rel = jnp.array([rel_of(orders[0]), rel_of(orders[1])], jnp.int32)
    own_place = dp ^ rel[core]
    other_place = dp ^ rel[1 - core]
    if direct:
        head = jnp.stack([core, dp]).astype(jnp.int32)
        tab = jnp.concatenate([head, own_place, other_place]).astype(jnp.int32)
        back_own = jnp.argsort(own_place).astype(jnp.int32)
        back_other = jnp.argsort(other_place).astype(jnp.int32)
    else:
        plain = jnp.arange(NB, dtype=jnp.int32)
        head = jnp.stack([core, dp]).astype(jnp.int32)
        tab = jnp.concatenate([head, plain, plain]).astype(jnp.int32)
        back_own = back_other = plain
    tab_own = jnp.concatenate([core[None], back_own]).astype(jnp.int32)
    tab_other = jnp.concatenate([1 - core[None], back_other]).astype(jnp.int32)

    def gather(group):
        low, high = gather_group(group, n_dp)
        if direct:
            return low, high, core_swap(low), core_swap(high)
        full = jnp.concatenate([low, high], axis=0)
        full = full[jnp.argsort(own_place)].reshape(NB, RB, -1)
        other = core_swap(full)
        return full[: NB // 2], full[NB // 2 :], other[: NB // 2], other[NB // 2 :]

    def scatter(own, other):
        if not direct:
            own = own.reshape(n_dp, shard, -1)[own_place]
            other = other.reshape(n_dp, shard, -1)[other_place]
        return scatter_group(own, core_swap(other), n_dp)

    norm_cols = jnp.pad(norm_params.astype(BF).T, ((0, 0), (0, 124)))
    qkv_low = jnp.concatenate([qkv_weight[:, n].astype(BF) for n in range(3)], axis=1)
    group_one = jnp.concatenate([qkv_low, out_weight.T.astype(BF), norm_cols], axis=1)
    one = gather(group_one)
    up = gather(ffn_in_weight.astype(BF))
    down = gather(ffn_out_weight.T.astype(BF))

    qkv, ctx, lse, xh1, rstd1, tokt, prow = attn_fwd(tab, tokens, one, rows)
    xh1 = xh1.reshape(rows, D)
    rstd1 = rstd1.reshape(rows, 128)
    act, act_grad, yt = ffn_up(tab, xh1, prow, up, rows)
    mixed_own, cls_own, xh2, rstd2 = ffn_down(tab, xh1, prow, act, down, rows)

    held = cls_own.astype(BF)[None]
    order = ("tensor",) + tuple(1 << b for b in range(n_dp.bit_length() - 1))
    for step in order:
        if step == "tensor":
            came = core_swap(held)
        else:
            came = lax.ppermute(held, "dp", [(d, d ^ step) for d in range(n_dp)])
        held = jnp.concatenate([held, came], axis=0)
    me = dp * 2 + core
    where = jnp.concatenate([me[None], me ^ jnp.arange(2 * n_dp, dtype=jnp.int32)]).astype(jnp.int32)
    loss, grad_cls = contrast(where, span_doc, held)

    dh2, dft, two_sums = norm_two(tab, cotangent, grad_cls, xh2, rstd2, prow, rows)
    down_other = weight_grad(tab_other, dft, act, "down_other")
    down_own = weight_grad(tab_own, dft, act, "down_own")
    shard_down = scatter(down_own, down_other)
    du, dh1, one_sums = ffn_back(tab, dh2, act_grad, xh1, rstd1, prow, up, down, rows)
    up_other = weight_grad(tab_other, yt, du, "up_other")
    up_own = weight_grad(tab_own, yt, du, "up_own")
    shard_up = scatter(up_own, up_other)
    dqkv, dat, dh1 = attn_back(tab, dh1, qkv, lse, one, rows)
    last_other = last_grad(tab_other, tokt, dqkv, dat, ctx, one_sums, two_sums, "last_other")
    last_own = last_grad(tab_own, tokt, dqkv, dat, ctx, one_sums, two_sums, "last_own")
    shard_last = scatter(last_own, last_other)
    grad_in = input_grads(tab, dh1, dqkv, one, rows)

    mixed = both_halves(mixed_own.reshape(rows, D), core)
    input_grad = both_halves(grad_in, core)

    shard_qkv = shard_last[:, :HALF_QKV]
    shard_out = shard_last[:, HALF_QKV : HALF_QKV + HALF_OUT]
    shard_norm = shard_last[:, HALF_QKV + HALF_OUT : HALF_QKV + HALF_OUT + 4]
    shard_norm = (0.5 * (shard_norm + core_swap(shard_norm))).T
    squares = jnp.sum(shard_qkv * shard_qkv) + jnp.sum(shard_out * shard_out)
    squares = squares + jnp.sum(shard_up * shard_up) + jnp.sum(shard_down * shard_down)
    squares = squares + 0.5 * jnp.sum(shard_norm * shard_norm)
    squares = squares.reshape(1, 1)
    for step in order:
        if step == "tensor":
            squares = squares + core_swap(squares)
        else:
            squares = squares + lax.ppermute(squares, "dp", [(d, d ^ step) for d in range(n_dp)])
    clip_norm = jnp.sqrt(squares[0, 0])
    clip_scale = 1.0 / jnp.maximum(clip_norm, 1.0)
    grad_qkv = shard_qkv.reshape(shard, 3, HALF_OUT)
    qkv_new = adam_update(qkv_weight, grad_qkv * clip_scale, qkv_first, qkv_second, 0.02, 0.01)
    out_new = adam_update(out_weight, shard_out.T * clip_scale, out_first, out_second, 0.02, 0.01)
    up_new = adam_update(ffn_in_weight, shard_up * clip_scale, ffn_in_first, ffn_in_second, 0.02, 0.01)
    down_new = adam_update(
        ffn_out_weight, shard_down.T * clip_scale, ffn_out_first, ffn_out_second, 0.02, 0.01
    )
    norm_new = adam_update(norm_params, shard_norm * clip_scale, norm_first, norm_second, 0.5, 0.0)
    return (
        mixed,
        input_grad,
        loss[0, 0],
        clip_norm,
        *qkv_new,
        *out_new,
        *up_new,
        *down_new,
        *norm_new,
    )


def solution(mesh):
    rows = P("dp", None)
    qkv = P("dp", None, "tensor")
    turned = P("tensor", "dp")
    up = P("dp", "tensor")
    norm = P(None, "dp")
    weights = (qkv, turned, up, turned, norm)
    moments = tuple(spec for spec in weights for _ in range(2))
    updated = tuple(spec for spec in weights for _ in range(3))
    return jax.shard_map(
        body,
        mesh=mesh,
        in_specs=(rows, rows, P()) + weights + moments,
        out_specs=(rows, rows, P(), P()) + updated,
        check_vma=False,
    )
```

```python
from functools import partial

import jax
import jax.numpy as jnp
from jax import lax
from jax.experimental import pallas as pl
from jax.experimental.pallas import tpu as pltpu
from jax.sharding import PartitionSpec as P

HEAD = 64
SPAN = 128
STEP = 10
D = 768
FF = 3072
NB = 16
RB = D // NB
HALF_QKV = 1152
HALF_OUT = 384
HALF_FF = 1536
ONE = HALF_QKV + HALF_OUT + 128
CONTRAST = 4.0
EPS = 1e-06
BF = jnp.bfloat16
F32 = jnp.float32
AXES = ("dp", "tensor")
SHRINK = 100

NN = (((1,), (0,)), ((), ()))
NT = (((1,), (1,)), ((), ()))
TN = (((0,), (0,)), ((), ()))


def mm(left, right, dims=NN):
    return lax.dot_general(left, right, dims, preferred_element_type=F32)


def params(vmem=56):
    return pltpu.CompilerParams(vmem_limit_bytes=vmem * 2**20)


def cost(flops, bytes_accessed, trans=0):
    flops, bytes_accessed, trans = (n // SHRINK + 1 for n in (flops, bytes_accessed, trans))
    return pl.CostEstimate(flops=int(flops), bytes_accessed=int(bytes_accessed), transcendentals=int(trans))


HBM = pl.BlockSpec(memory_space=pl.ANY)


def bit_orders(n_dp):
    bits = n_dp.bit_length() - 1
    if bits == 4:
        return ((4, 8, 2, 1), (8, 4, 1, 2)), ((1, 4, 8, 2), (2, 8, 4, 1))
    up = tuple(1 << b for b in range(bits))[::-1]
    both = (up, up[: bits // 2] + up[bits // 2 :][::-1])
    return both, both


def pairs_of(n_dp, orders, step):
    out = []
    for d in range(n_dp):
        for c in range(2):
            out.append((d * 2 + c, (d ^ orders[c][step]) * 2 + c))
    return out


def rel_of(order):
    out = []
    for p in range(1 << len(order)):
        r = 0
        for k, b in enumerate(order):
            if (p >> k) & 1:
                r ^= b
        out.append(r)
    return out


def core_swap(block):
    return lax.ppermute(block, "tensor", [(0, 1), (1, 0)])


VM = pl.BlockSpec(memory_space=pltpu.VMEM)
SM = pl.BlockSpec(memory_space=pltpu.SMEM)
BLK = 256


def call(kernel, out, in_specs, *args, vmem=16, flops=0, moved=0, trans=0, scratch=(), name=None):
    return pl.pallas_call(
        kernel,
        out_shape=[jax.ShapeDtypeStruct(s, t) for s, t in out],
        in_specs=in_specs,
        out_specs=[VM] * len(out),
        scratch_shapes=list(scratch),
        compiler_params=params(vmem),
        cost_estimate=cost(flops, moved, trans),
        name=name,
    )(*args)


def pack_kernel(qkv, out, up, down, norm, one_ref, two_ref, three_ref, wide, a0, a1, a2, a3, sems):
    rows = up.shape[0]
    wide[...] = jnp.zeros_like(wide)
    copies = [
        pltpu.make_async_copy(src, dst, sems.at[n])
        for n, (src, dst) in enumerate(
            ((qkv, a0), (out, a1), (down, a3), (up, a2))
        )
    ]
    for c in copies:
        c.start()
    copies[0].wait()
    for part in range(3):
        one_ref[0, :, part * HALF_OUT : (part + 1) * HALF_OUT] = a0[part].astype(BF)
    copies[1].wait()
    one_ref[0, :, HALF_QKV : HALF_QKV + HALF_OUT] = a1[...].astype(BF)
    wide[0:4, 0:rows] = norm[...]
    one_ref[0, :, HALF_QKV + HALF_OUT :] = wide[...].T[0:rows].astype(BF)
    copies[2].wait()
    three_ref[0] = a3[...].astype(BF)
    copies[3].wait()
    two_ref[0] = a2[...].astype(BF)


def pack(*shards):
    rows = shards[2].shape[0]
    return call(
        pack_kernel,
        [((1, rows, ONE), BF), ((1, rows, HALF_FF), BF), ((1, rows, HALF_FF), BF)],
        [pl.BlockSpec(memory_space=pltpu.HBM)] * 4 + [VM], *shards,
        vmem=8, moved=rows * 28000,
        scratch=[pltpu.VMEM((128, 128), F32)]
        + [pltpu.VMEM(w.shape, F32) for w in shards[:4]]
        + [pltpu.SemaphoreType.DMA((4,))],
        name="pack",
    )


def assemble_kernel(tab, low, high, out_ref, sems):
    copies = []
    for n, ref in enumerate((low, high)):
        for p in range(NB // 2):
            q = n * (NB // 2) + p
            copies.append(pltpu.make_async_copy(ref.at[p], out_ref.at[tab[q]], sems.at[q]))
    for c in copies:
        c.start()
    for c in copies:
        c.wait()


def assemble(tab, low, high, name):
    width = low.shape[-1]
    return call(
        assemble_kernel,
        [((NB, RB, width), BF)],
        [SM] + [HBM] * 2,
        tab,
        low,
        high,
        vmem=8,
        moved=4 * D * width,
        scratch=[pltpu.SemaphoreType.DMA((NB,))],
        name=name,
    )[0]


def weight(w_ref, first, last):
    return w_ref[:, :, first:last].reshape(D, last - first)


def norm_fwd(hidden):
    center = hidden - jnp.mean(hidden, axis=-1, keepdims=True)
    spread = jnp.mean(center * center, axis=-1, keepdims=True)
    rstd = lax.rsqrt(spread + EPS)
    return center * rstd, rstd


def norm_bwd(grad, xh, rstd, gain):
    e = grad * gain
    m1 = jnp.mean(e, axis=-1, keepdims=True)
    m2 = jnp.mean(e * xh, axis=-1, keepdims=True)
    return rstd * (e - m1 - xh * m2)


def store_turned(ref, tab, value, col, width):
    turned = value.T
    for j in range(NB):
        block = turned[j * RB : (j + 1) * RB]
        for n in range(2):
            ref[n, tab[n * NB + j], :, pl.ds(col, width)] = block


def head_masks(rows, scale):
    lane = lax.broadcasted_iota(jnp.int32, (rows, 128), 1)
    return (
        jnp.where(lane < HEAD, scale, 0.0).astype(BF),
        jnp.where(lane < HEAD, 0.0, scale).astype(BF),
    )


def stack_heads(pair, masks):
    return jnp.concatenate([pair * masks[0], pair * masks[1]], axis=0)


def merge_heads(both):
    lane = lax.broadcasted_iota(jnp.int32, (SPAN, 128), 1)
    return jnp.where(lane < HEAD, both[:SPAN], both[SPAN:])


def turn_kernel(pos, x_ref, out_ref):
    rows = x_ref.shape[0]
    for i in range(rows // BLK):
        store_turned(out_ref, pos, x_ref[i * BLK : (i + 1) * BLK, :], i * BLK, BLK)


def turn(pos, x):
    rows = x.shape[0]
    return call(
        turn_kernel, [((2, NB, RB, rows), BF)], [SM, VM], pos, x, moved=rows * D * 6, name="turn"
    )[0]


def attn_rows(i, x, w_ref, masks, qkv_ref, ctx_ref, lse_ref):
    r0 = pl.multiple_of(i * BLK, BLK)
    qkv = mm(x, weight(w_ref, 0, HALF_QKV)).astype(BF)
    qkv_ref[pl.ds(r0, BLK), :] = qkv
    rows = []
    for s in range(2):
        own = qkv[s * SPAN : (s + 1) * SPAN]
        parts = []
        for j in range(3):
            q = stack_heads(own[:, j * 128 : (j + 1) * 128], masks)
            k = own[:, HALF_OUT + j * 128 : HALF_OUT + (j + 1) * 128]
            v = own[:, 2 * HALF_OUT + j * 128 : 2 * HALF_OUT + (j + 1) * 128]
            st = mm(k, q, NT)
            top = jnp.max(st, axis=0, keepdims=True)
            ex = jnp.exp(st - top)
            total = jnp.sum(ex, axis=0, keepdims=True)
            pt = (ex * (1.0 / total)).astype(BF)
            lse_ref[i * 2 + s, j : j + 1, :] = top + jnp.log(total)
            parts.append(merge_heads(mm(pt, v, TN)).astype(BF))
        rows.append(jnp.concatenate(parts, axis=1))
    ctx = jnp.concatenate(rows, axis=0)
    ctx_ref[pl.ds(r0, BLK), :] = ctx
    return ctx


def attn_one_kernel(x_ref, w_ref, qkv_ref, ctx_ref, lse_ref):
    masks = head_masks(SPAN, HEAD ** (-0.5))

    def step(i, carry):
        x = x_ref[pl.ds(pl.multiple_of(i * BLK, BLK), BLK), :]
        attn_rows(i, x, w_ref, masks, qkv_ref, ctx_ref, lse_ref)
        return carry

    lax.fori_loop(0, x_ref.shape[0] // BLK, step, 0)


def attn_two_kernel(x_ref, w_ref, wo_ref, ctxo_ref, qkv_ref, ctx_ref, lse_ref, xh_ref, rstd_ref, p_ref):
    cols = weight(w_ref, HALF_QKV + HALF_OUT, ONE).astype(F32)
    p_ref[...] = cols.T[:8]
    masks = head_masks(SPAN, HEAD ** (-0.5))

    def step(i, carry):
        rs = pl.ds(pl.multiple_of(i * BLK, BLK), BLK)
        x = x_ref[rs, :]
        ctx = attn_rows(i, x, w_ref, masks, qkv_ref, ctx_ref, lse_ref)
        attn = x.astype(F32) + mm(ctxo_ref[rs, :], weight(wo_ref, HALF_QKV, HALF_QKV + HALF_OUT), NT)
        attn = attn + mm(ctx, weight(w_ref, HALF_QKV, HALF_QKV + HALF_OUT), NT)
        xh, rstd = norm_fwd(attn)
        rstd = jnp.broadcast_to(rstd, (BLK, 128))
        for s in range(2):
            for q in range(4):
                r = s * SPAN + q * 32
                xh_ref[q, i * 2 + s] = xh[r : r + 32]
                rstd_ref[q, i * 2 + s] = rstd[r : r + 32]
        return carry

    lax.fori_loop(0, x_ref.shape[0] // BLK, step, 0)


def attn_shapes(rows):
    return [((rows, HALF_QKV), BF), ((rows, HALF_OUT), BF), ((rows // SPAN, 8, 2 * SPAN), F32)]


def attn_one(x, w):
    rows = x.shape[0]
    return call(
        attn_one_kernel, attn_shapes(rows), [VM, VM], x, w,
        vmem=16, flops=rows * 4e6, moved=rows * 8000 + 2e6, trans=rows * 800, name="attn_one",
    )


def attn_two(x, w, w_own, ctx_own):
    rows = x.shape[0]
    spans = rows // SPAN
    out = attn_shapes(rows) + [
        ((4, spans, 32, D), F32),
        ((4, spans, 32, 128), F32),
        ((8, D), F32),
    ]
    return call(
        attn_two_kernel, out, [VM] * 4, x, w, w_own, ctx_own,
        vmem=16, flops=rows * 5e6, moved=rows * 12000 + 4e6, trans=rows * 800, name="attn_two",
    )


def gelu_pair(u):
    a = jnp.abs(u)
    d = 1.0 + (0.3275911 * 0.5**0.5) * a
    t = pl.reciprocal(d, approx=True)
    t = t * (2.0 - d * t)
    e = jnp.exp(-0.5 * u * u)
    poly = 0.5307027145 * t - 0.7265760135
    poly = poly * t + 0.7107068705
    poly = poly * t - 0.142248368
    poly = poly * t + 0.127414796
    tail = (poly * t) * e
    phi = jnp.where(u >= 0.0, 1.0 - tail, tail)
    return u * phi, phi + (0.3989422804014327 * u) * e


TILE = 512


def ffn_up_kernel(pos, xh_ref, p_ref, w_ref, g_ref, gp_ref, *yt_ref):
    def step(i, carry):
        rs = pl.ds(pl.multiple_of(i * BLK, BLK), BLK)
        y = xh_ref[rs, :] * p_ref[0:1, :] + p_ref[1:2, :]
        yb = y.astype(BF)
        if yt_ref:
            store_turned(yt_ref[0], pos, yb, pl.multiple_of(i * BLK, BLK), BLK)
        for t in range(HALF_FF // TILE):
            u = mm(yb, weight(w_ref, t * TILE, (t + 1) * TILE))
            g, gp = gelu_pair(u)
            g_ref[rs, t * TILE : (t + 1) * TILE] = g.astype(BF)
            gp_ref[rs, t * TILE : (t + 1) * TILE] = gp.astype(BF)
        return carry

    lax.fori_loop(0, xh_ref.shape[0] // BLK, step, 0)


def ffn_up(pos, xh, prow, w, turned, name):
    rows = xh.shape[0]
    out = [((rows, HALF_FF), BF), ((rows, HALF_FF), BF)]
    if turned:
        out.append(((2, NB, RB, rows), BF))
    return call(
        ffn_up_kernel, out, [SM, VM, VM, VM], pos, xh, prow, w,
        vmem=16, flops=rows * 2.4e6, moved=rows * 9000 + 2e6, trans=rows * 6000, name=name,
    )


def down_block(r0, xh1_ref, p_ref, acts, downs):
    rs = pl.ds(r0, BLK)
    total = xh1_ref[rs, :] * p_ref[0:1, :] + p_ref[1:2, :]
    for g_ref, w_ref in zip(acts, downs):
        total = total + mm(g_ref[rs, :], weight(w_ref, 0, HALF_FF), NT)
    return norm_fwd(total)


def first_kernel(xh1_ref, p_ref, g0, g1, d0, d1, mixed_ref, cls_ref, xh_ref, rstd_ref):
    xh, rstd = down_block(0, xh1_ref, p_ref, (g0, g1), (d0, d1))
    xh_ref[...] = xh
    rstd_ref[...] = jnp.broadcast_to(rstd, rstd_ref.shape)
    out = (xh * p_ref[2:3, :] + p_ref[3:4, :]).reshape(mixed_ref.shape)
    mixed_ref[...] = out.astype(BF)
    cls_ref[...] = out[:, 0, :]


def first_rows(xh1, prow, acts, downs):
    spans = BLK // 32
    return call(
        first_kernel,
        [((spans, 32, D), BF), ((spans, D), F32), ((BLK, D), F32), ((BLK, 128), F32)],
        [VM] * 6, xh1, prow, *acts, *downs,
        vmem=8, flops=BLK * 4.8e6, moved=BLK * 16000 + 5e6, name="first_rows",
    )


def back_block(r0, grad, xh2, rstd2, gps, xh1_ref, rstd1_ref, p_ref, ups, downs, dus):
    rs = pl.ds(r0, BLK)
    sum_g2 = jnp.sum(grad * xh2, axis=0, keepdims=True)
    sum_b2 = jnp.sum(grad, axis=0, keepdims=True)
    dh = norm_bwd(grad, xh2, rstd2, p_ref[2:3, :])
    df = dh.astype(BF)
    total = dh
    for gp_ref, up_ref, down_ref, du_ref in zip(gps, ups, downs, dus):
        for t in range(HALF_FF // TILE):
            lo, hi = t * TILE, (t + 1) * TILE
            dg = mm(df, weight(down_ref, lo, hi))
            du_ref[:, lo:hi] = (dg * gp_ref[rs, lo:hi].astype(F32)).astype(BF)
        total = total + mm(du_ref[...], weight(up_ref, 0, HALF_FF), NT)
    xh1 = xh1_ref[rs, :]
    sum_g1 = jnp.sum(total * xh1, axis=0, keepdims=True)
    sum_b1 = jnp.sum(total, axis=0, keepdims=True)
    dh1 = norm_bwd(total, xh1, rstd1_ref[rs, 0:1], p_ref[0:1, :])
    return df, dh1, (sum_g1, sum_b1, sum_g2, sum_b2)


def back_shapes():
    return [
        ((2, NB, RB, BLK), BF),
        ((BLK, HALF_FF), BF),
        ((BLK, HALF_FF), BF),
        ((BLK // 32, 32, D), F32),
        ((8, D), F32),
    ]


def rest_kernel(
    at, pos, xh1_ref, rstd1_ref, p_ref, g0, g1, gp0, gp1, cot_ref, u0, u1, d0, d1,
    dft_ref, du0_ref, du1_ref, dh1_ref, sums_ref, mixed_ref,
):
    r0, c0 = at * BLK, at * 32
    xh, rstd = down_block(r0, xh1_ref, p_ref, (g0, g1), (d0, d1))
    out = xh * p_ref[2:3, :] + p_ref[3:4, :]
    mixed_ref[...] = out.reshape(mixed_ref.shape).astype(BF)
    grad = cot_ref[:, c0 : c0 + 32, :].astype(F32).reshape(BLK, D)
    df, dh1, sums = back_block(
        r0, grad, xh, rstd, (gp0, gp1), xh1_ref, rstd1_ref, p_ref, (u0, u1), (d0, d1), (du0_ref, du1_ref)
    )
    store_turned(dft_ref, pos, df, 0, BLK)
    dh1_ref[...] = dh1.reshape(dh1_ref.shape)
    for n in range(4):
        sums_ref[n : n + 1, :] = sums[n]


def rest_rows(at, pos, xh1, rstd1, prow, acts, gps, cot, ups, downs):
    return call(
        partial(rest_kernel, at),
        back_shapes() + [((BLK // 32, 32, D), BF)],
        [SM] + [VM] * 12, pos, xh1, rstd1, prow, *acts, *gps, cot, *ups, *downs,
        vmem=16, flops=BLK * 14.5e6, moved=BLK * 40000 + 1e7, name=f"rest_rows_{at}",
    )


def class_kernel(
    pos, cls_ref, cot_ref, xh2_ref, rstd2_ref, xh1_ref, rstd1_ref, p_ref, gp0, gp1, u0, u1, d0, d1,
    dft_ref, du0_ref, du1_ref, dh1_ref, sums_ref,
):
    spans = cls_ref.shape[0]
    grad = cot_ref[:, 0:32, :].astype(F32)
    first = lax.broadcasted_iota(jnp.int32, grad.shape, 1) == 0
    grad = grad + jnp.where(first, cls_ref[...].reshape(spans, 1, D), 0.0)
    grad = grad.reshape(BLK, D)
    df, dh1, sums = back_block(
        0, grad, xh2_ref[...], rstd2_ref[:, 0:1], (gp0, gp1), xh1_ref, rstd1_ref, p_ref,
        (u0, u1), (d0, d1), (du0_ref, du1_ref),
    )
    store_turned(dft_ref, pos, df, 0, BLK)
    dh1_ref[...] = dh1.reshape(dh1_ref.shape)
    for n in range(4):
        sums_ref[n : n + 1, :] = sums[n]


def class_rows(pos, grad_cls, cot, xh2, rstd2, xh1, rstd1, prow, gps, ups, downs):
    return call(
        class_kernel,
        back_shapes(),
        [SM] + [VM] * 13, pos, grad_cls, cot, xh2, rstd2, xh1, rstd1, prow, *gps, *ups, *downs,
        vmem=16, flops=BLK * 9.7e6, moved=BLK * 30000 + 1e7, name="class_rows",
    )


def contrast_kernel(where, doc_ref, cls_ref, loss_ref, grad_ref, rows, own_doc):
    spans = doc_ref.shape[1]
    doc_row = doc_ref[...].astype(F32)
    doc_col = jnp.broadcast_to(doc_row, (128, spans)).T[:, 0:1]
    blocks, per = cls_ref.shape[0], cls_ref.shape[1]
    me = where[0]
    for n in range(blocks):
        rows[where[1 + n]] = cls_ref[n].astype(F32)
    a = rows[...].reshape(spans, D).astype(BF)
    own = rows[me].astype(BF)
    scale = D ** (-0.5)
    col = lax.broadcasted_iota(jnp.int32, (spans, spans), 1)
    row = lax.broadcasted_iota(jnp.int32, (spans, spans), 0)
    logits = mm(a, a, NT) * scale
    partner = (doc_col == doc_row) & (row != col)
    masked = jnp.where(row == col, -1000000000.0, logits)
    top = jnp.max(masked, axis=0, keepdims=True)
    lse = jnp.log(jnp.sum(jnp.exp(masked - top), axis=0, keepdims=True)) + top
    positive = jnp.sum(jnp.where(partner, logits, 0.0), axis=0, keepdims=True)
    flagged = jnp.max(jnp.where(partner, 1.0, 0.0), axis=0, keepdims=True)
    count = jnp.sum(flagged, axis=1, keepdims=True)
    loss = jnp.sum(flagged * (lse - positive), axis=1, keepdims=True) / count
    loss_ref[...] = jnp.broadcast_to(loss, loss_ref.shape)

    weight_row = flagged * (CONTRAST * spans) / count
    own_doc[...] = doc_col.reshape(blocks, per, 1)
    docs = own_doc[me]
    col = lax.broadcasted_iota(jnp.int32, (per, spans), 1)
    row = lax.broadcasted_iota(jnp.int32, (per, spans), 0) + me * per
    logits = mm(own, a, NT) * scale
    same = jnp.where((docs == doc_row) & (row != col), 1.0, 0.0)
    masked = jnp.where(row == col, -1000000000.0, logits)
    top = jnp.max(masked, axis=1, keepdims=True)
    ex = jnp.exp(masked - top)
    soft = ex / jnp.sum(ex, axis=1, keepdims=True)
    own_weight = jnp.max(same, axis=1, keepdims=True) * (CONTRAST * spans) / count
    sym = own_weight * (soft - same) + weight_row * (jnp.exp(masked - lse) - same)
    high = sym.astype(BF)
    low = (sym - high.astype(F32)).astype(BF)
    grad_ref[...] = (mm(high, a) + mm(low, a)) * scale


def contrast(where, doc_row, cls_all):
    blocks, per, _ = cls_all.shape
    spans = blocks * per
    return call(
        contrast_kernel,
        [((1, 128), F32), ((per, D), F32)],
        [SM, VM, VM],
        where, doc_row, cls_all,
        vmem=8 if spans <= 256 else 40, flops=2 * spans * spans * D, moved=spans * D * 2,
        scratch=[pltpu.VMEM((blocks, per, D), F32), pltpu.VMEM((blocks, per, 1), F32)],
        name="contrast",
    )


def turned_of(refs, n):
    return jnp.concatenate([ref[n].reshape(D, ref.shape[3]) for ref in refs], axis=1)


def grad_other_kernel(count, *refs):
    xts, ys, out_ref = refs[:count], refs[count:-1], refs[-1]
    xt = turned_of(xts, 1)
    for t in range(HALF_FF // TILE):
        lo, hi = t * TILE, (t + 1) * TILE
        grad = mm(xt, jnp.concatenate([y[:, lo:hi] for y in ys], axis=0))
        out_ref[:, :, lo:hi] = grad.astype(BF).reshape(NB, RB, TILE)


def grad_other(xts, ys, name):
    rows = sum(y.shape[0] for y in ys)
    return call(
        partial(grad_other_kernel, len(xts)),
        [((NB, RB, HALF_FF), BF)],
        [VM] * (len(xts) + len(ys)), *xts, *ys,
        vmem=12, flops=2 * rows * D * HALF_FF, moved=rows * 8000 + 2.4e6, name=name,
    )[0]


def grad_own_kernel(count, came_ref, *refs):
    xts, ys, keep_ref, send_ref = refs[:count], refs[count:-2], refs[-2], refs[-1]
    nh = NB // 2
    xt = turned_of(xts, 0)
    for t in range(HALF_FF // TILE):
        lo, hi = t * TILE, (t + 1) * TILE
        grad = mm(xt, jnp.concatenate([y[:, lo:hi] for y in ys], axis=0))
        grad = (grad.reshape(NB, RB, TILE) + came_ref[:, :, lo:hi].astype(F32)).astype(BF)
        keep_ref[:, :, lo:hi] = grad[:nh]
        send_ref[:, :, lo:hi] = grad[nh:]


def grad_own(xts, ys, came, name):
    rows = sum(y.shape[0] for y in ys)
    return call(
        partial(grad_own_kernel, len(xts)),
        [((NB // 2, RB, HALF_FF), BF)] * 2,
        [VM] * (1 + len(xts) + len(ys)), came, *xts, *ys,
        vmem=12, flops=2 * rows * D * HALF_FF, moved=rows * 8000 + 4.8e6, name=name,
    )


def natural(refs, i):
    return jnp.concatenate([ref[i * 2 + s] for s in range(2) for ref in refs], axis=0)


def attn_back_kernel(pos, r0_ref, r1_ref, r2_ref, r3_ref, qkv_ref, lse_ref, w_ref, dqkv_ref, *dat_ref):
    masks = head_masks(SPAN, HEAD ** (-0.5))
    plain = head_masks(SPAN, 1.0)
    spans = r0_ref.shape[0]

    def step(i, carry):
        r0 = pl.multiple_of(i * BLK, BLK)
        da = natural((r0_ref, r1_ref, r2_ref, r3_ref), i).astype(BF)
        if dat_ref:
            store_turned(dat_ref[0], pos, da, r0, BLK)
        dctx = mm(da, weight(w_ref, HALF_QKV, HALF_QKV + HALF_OUT)).astype(BF)
        for s in range(2):
            rs = pl.ds(pl.multiple_of(r0 + s * SPAN, SPAN), SPAN)
            for j in range(3):
                a, b = j * 128, (j + 1) * 128
                q = stack_heads(qkv_ref[rs, a:b], masks)
                k = qkv_ref[rs, HALF_OUT + a : HALF_OUT + b]
                v = qkv_ref[rs, 2 * HALF_OUT + a : 2 * HALF_OUT + b]
                dc = stack_heads(dctx[s * SPAN : (s + 1) * SPAN, a:b], plain)
                st = mm(k, q, NT)
                pt = jnp.exp(st - lse_ref[i * 2 + s, j : j + 1, :])
                dpt = mm(v, dc, NT)
                dst = pt * (dpt - jnp.sum(pt * dpt, axis=0, keepdims=True))
                dst = dst.astype(BF)
                dv = mm(pt.astype(BF), dc)
                dk = mm(dst, q)
                dq = merge_heads(mm(dst, k, TN)) * HEAD ** (-0.5)
                dqkv_ref[rs, a:b] = dq.astype(BF)
                dqkv_ref[rs, HALF_OUT + a : HALF_OUT + b] = dk.astype(BF)
                dqkv_ref[rs, 2 * HALF_OUT + a : 2 * HALF_OUT + b] = dv.astype(BF)
        return carry

    lax.fori_loop(0, spans // 2, step, 0)


def attn_back(pos, dh1, qkv, lse, w, turned, name):
    rows = qkv.shape[0]
    out = [((rows, HALF_QKV), BF)]
    if turned:
        out.append(((2, NB, RB, rows), BF))
    return call(
        attn_back_kernel, out,
        [SM] + [VM] * 7, pos, *dh1, qkv, lse, w,
        vmem=16, flops=rows * 6e6, moved=rows * 10000 + 3e6, trans=rows * 800, name=name,
    )


def last_value(order, xt_ref, dqkv_ref, dat_ref, ctx_ref, t):
    rows = xt_ref.shape[3]
    if t < 3:
        return mm(xt_ref[order].reshape(D, rows), dqkv_ref[:, t * HALF_OUT : (t + 1) * HALF_OUT])
    return mm(dat_ref[order].reshape(D, rows), ctx_ref[...])


def norm_columns(sums):
    total = sums[0][0:4, :]
    for ref in sums[1:]:
        total = total + ref[0:4, :]
    return jnp.concatenate([total, jnp.zeros((124, D), F32)], axis=0).T


def last_other_kernel(pos, xt_ref, dqkv_ref, dat_ref, ctx_ref, s0, s1, s2, s3, out_ref):
    for t in range(4):
        grad = last_value(1, xt_ref, dqkv_ref, dat_ref, ctx_ref, t)
        lo = t * HALF_OUT
        out_ref[:, :, lo : lo + HALF_OUT] = grad.astype(BF).reshape(NB, RB, HALF_OUT)
    norm = norm_columns((s0, s1, s2, s3)).astype(BF)
    for j in range(NB):
        out_ref[pos[NB + j], :, HALF_QKV + HALF_OUT :] = norm[j * RB : (j + 1) * RB]


def last_other(pos, xt, dqkv, dat, ctx, sums):
    rows = xt.shape[3]
    return call(
        last_other_kernel,
        [((NB, RB, ONE), BF)],
        [SM] + [VM] * 8, pos, xt, dqkv, dat, ctx, *sums,
        vmem=12, flops=2 * rows * D * HALF_FF, moved=rows * 8000 + 2.4e6, name="last_other",
    )[0]


def last_own_kernel(
    pos, xt_ref, dqkv_ref, dat_ref, ctx_ref, s0, s1, s2, s3, came_ref, keep_ref, send_ref, cols
):
    nh = NB // 2
    norm = norm_columns((s0, s1, s2, s3))
    for j in range(NB):
        cols[pos[j]] = norm[j * RB : (j + 1) * RB]
    for t in range(5):
        lo = t * HALF_OUT
        hi = min(lo + HALF_OUT, ONE)
        if t < 4:
            grad = last_value(0, xt_ref, dqkv_ref, dat_ref, ctx_ref, t).reshape(NB, RB, HALF_OUT)
        else:
            grad = cols[...]
        grad = (grad + came_ref[:, :, lo:hi].astype(F32)).astype(BF)
        keep_ref[:, :, lo:hi] = grad[:nh]
        send_ref[:, :, lo:hi] = grad[nh:]


def last_own(pos, xt, dqkv, dat, ctx, sums, came):
    rows = xt.shape[3]
    return call(
        last_own_kernel,
        [((NB // 2, RB, ONE), BF)] * 2,
        [SM] + [VM] * 9, pos, xt, dqkv, dat, ctx, *sums, came,
        vmem=12, flops=2 * rows * D * HALF_FF, moved=rows * 8000 + 4.8e6,
        scratch=[pltpu.VMEM((NB, RB, 128), F32)], name="last_own",
    )


def input_grad_kernel(r0_ref, r1_ref, r2_ref, r3_ref, own_ref, other_ref, w0_ref, w1_ref, out_ref):
    spans = r0_ref.shape[0]

    def step(i, carry):
        rs = pl.ds(pl.multiple_of(i * BLK, BLK), BLK)
        total = natural((r0_ref, r1_ref, r2_ref, r3_ref), i)
        total = total + mm(own_ref[rs, :], weight(w0_ref, 0, HALF_QKV), NT)
        total = total + mm(other_ref[rs, :], weight(w1_ref, 0, HALF_QKV), NT)
        out_ref[rs, :] = total
        return carry

    lax.fori_loop(0, spans // 2, step, 0)


def input_grads(dh1, own, other, w_own, w_other):
    rows = own.shape[0]
    return call(
        input_grad_kernel,
        [((rows, D), F32)],
        [VM] * 8, *dh1, own, other, w_own, w_other,
        vmem=12, flops=rows * 3.6e6, moved=rows * 12000 + 5e6, name="input_grads",
    )[0]


def place_kernel(half, *refs):
    own, other, g_own, g_other = refs[0:4], refs[4:8], refs[8], refs[9]
    mixed_ref, grad_ref, sems = refs[10:]
    spans = g_own.shape[0]
    copies = []
    for n, (pieces, g) in enumerate(((own, g_own), (other, g_other))):
        at = pl.ds(half[n] * spans, spans)
        for q in range(4):
            to = mixed_ref.at[at, 32 * q : 32 * q + 32, :]
            copies.append(pltpu.make_async_copy(pieces[q], to, sems.at[5 * n + q]))
        copies.append(pltpu.make_async_copy(g, grad_ref.at[at], sems.at[5 * n + 4]))
    for c in copies:
        c.start()
    for c in copies:
        c.wait()


def place(half, own, other, g_own, g_other):
    spans = own[0].shape[0]
    g_own, g_other = (g.reshape(spans, SPAN, D) for g in (g_own, g_other))
    return pl.pallas_call(
        place_kernel,
        out_shape=[
            jax.ShapeDtypeStruct((2 * spans, SPAN, D), BF),
            jax.ShapeDtypeStruct((2 * spans, SPAN, D), F32),
        ],
        in_specs=[SM] + [VM] * 10,
        out_specs=[HBM] * 2,
        scratch_shapes=[pltpu.SemaphoreType.DMA((10,))],
        compiler_params=params(16),
        cost_estimate=cost(0, spans * SPAN * D * 24),
        name="place",
    )(half, *own, *other, g_own, g_other)


def squares_kernel(k0, c0, k1, c1, k2, c2, g0, g1, g2, sq_ref):
    main = HALF_QKV + HALF_OUT
    total = jnp.zeros((1, 1), F32)
    for keep, came, out in ((k0, c0, g0), (k1, c1, g1), (k2, c2, g2)):
        grad = keep[0].astype(F32) + came[0].astype(F32)
        out[...] = grad
        sq = jnp.sum(grad[:, :main] * grad[:, :main], axis=1, keepdims=True)
        if grad.shape[1] > main:
            cols = grad[:, main:]
            sq = sq + 0.5 * jnp.sum(cols * cols, axis=1, keepdims=True)
        total = total + jnp.sum(sq, axis=0, keepdims=True)
    sq_ref[...] = jnp.broadcast_to(total, sq_ref.shape)


def squares_of(pairs):
    shard = pairs[0][0].shape[1]
    out = [((shard, k.shape[2]), F32) for k, _ in pairs] + [((8, 128), F32)]
    flat = [a for pair in pairs for a in pair]
    return call(squares_kernel, out, [VM] * 6, *flat, vmem=8, moved=shard * 40000, name="squares")


def adam_parts(weight, gradient, moment_one, moment_two, step_rate, decay_rate):
    first_new = 0.9 * moment_one + 0.1 * gradient
    second_new = 0.999 * moment_two + 0.001 * gradient * gradient
    corr_first = first_new * (1.0 / (1.0 - 0.9**STEP))
    corr_second = second_new * (1.0 / (1.0 - 0.999**STEP))
    weight_new = weight - step_rate * (
        corr_first / (jnp.sqrt(corr_second) + 1e-08) + decay_rate * weight
    )
    return first_new, second_new, weight_new


def adam_kernel(sq_ref, last_ref, up_ref, down_ref, cols_ref, *refs):
    ins, outs, wide = refs[:15], refs[15:-1], refs[-1]
    norm = jnp.sqrt(sq_ref[0:1, 0:1])
    outs[15][...] = jnp.broadcast_to(norm, outs[15].shape)
    scale = 1.0 / jnp.maximum(norm, 1.0)

    def update(n, at, grad, rate, decay):
        new = adam_parts(ins[n][at], grad * scale, ins[5 + 2 * n][at], ins[6 + 2 * n][at], rate, decay)
        for m in range(3):
            outs[3 * n + m][at] = new[m]

    for part in range(3):
        update(0, part, last_ref[:, part * HALF_OUT : (part + 1) * HALF_OUT], 0.02, 0.01)
    update(1, Ellipsis, last_ref[:, HALF_QKV : HALF_QKV + HALF_OUT], 0.02, 0.01)
    update(2, Ellipsis, up_ref[...], 0.02, 0.01)
    update(3, Ellipsis, down_ref[...], 0.02, 0.01)
    shard = last_ref.shape[0]
    wide[...] = jnp.zeros_like(wide)
    wide[0:shard, :] = 0.5 * (last_ref[:, HALF_QKV + HALF_OUT :] + cols_ref[...])
    update(4, Ellipsis, wide[...].T[0:4, 0:shard], 0.5, 0.0)


def adam(squares, last, up, down, cols, weights, moments):
    shapes = [w.shape for w in weights]
    out = [(s, F32) for s in shapes for _ in range(3)] + [((8, 128), F32)]
    args = (squares, last, up, down, cols, *weights, *moments)
    return call(
        adam_kernel, out, [VM] * len(args), *args, vmem=16, moved=7 * 4 * last.shape[0] * 4608,
        scratch=[pltpu.VMEM((128, 128), F32)], name="adam",
    )


def after(value, *others):
    return lax.optimization_barrier((value, others))[0]


def body(
    tokens,
    cotangent,
    span_doc,
    qkv_weight,
    out_weight,
    ffn_in_weight,
    ffn_out_weight,
    norm_params,
    qkv_first,
    qkv_second,
    out_first,
    out_second,
    ffn_in_first,
    ffn_in_second,
    ffn_out_first,
    ffn_out_second,
    norm_first,
    norm_second,
):
    n_dp = lax.axis_size("dp")
    dp = lax.axis_index("dp")
    core = lax.axis_index("tensor")
    shard = D // n_dp
    rows = tokens.shape[0] // 2
    spans = rows // SPAN
    direct = n_dp == NB
    early, late = bit_orders(n_dp)
    steps = len(early[0])
    last = steps - 1

    def tables(orders):
        rel = [rel_of(order) for order in orders]
        place = jnp.array(rel, jnp.int32)
        own, other = dp ^ place[core], dp ^ place[1 - core]
        if direct:
            back = jnp.array([[r.index(j) for j in range(NB)] for r in rel], jnp.int32)
            at = jnp.arange(NB, dtype=jnp.int32) ^ dp
            pos = jnp.concatenate([back[core][at], back[1 - core][at]]).astype(jnp.int32)
            return own.astype(jnp.int32), other.astype(jnp.int32), pos
        plain = jnp.arange(NB, dtype=jnp.int32)
        return own.astype(jnp.int32), other.astype(jnp.int32), jnp.concatenate([plain, plain])

    own_early, other_early, pos_early = tables(early)
    own_late, other_late, pos_late = tables(late)
    half = jnp.stack([core, 1 - core]).astype(jnp.int32)

    me = dp * 2 + core
    rel = [(r << 1) | c for c in range(2) for r in rel_of([1 << k for k in reversed(range(steps))])]
    where = jnp.concatenate([me[None], me ^ jnp.array(rel, jnp.int32)]).astype(jnp.int32)
    tables = (own_early, other_early, pos_early, own_late, other_late, pos_late, half, where)
    x = lax.dynamic_slice_in_dim(tokens, core * rows, rows, 0)
    cot = lax.dynamic_slice_in_dim(cotangent, core * rows, rows, 0).reshape(spans, SPAN, D)

    def send_on(block, orders, k):
        return lax.ppermute(block, AXES, pairs_of(n_dp, orders, k))

    def join(held, came):
        return jnp.concatenate([held, came], axis=0)

    def settle(place, low, high, name):
        if direct:
            return assemble(place, low, high, name)
        full = join(low, high)[jnp.argsort(place)].reshape(NB, RB, -1)
        plain = jnp.arange(NB, dtype=jnp.int32)
        return assemble(plain, full[: NB // 2], full[NB // 2 :], name)

    def halves(place, keep, send):
        if direct:
            return keep, send
        full = join(keep, send).reshape(n_dp, shard, -1)[place]
        return full[: n_dp // 2], full[n_dp // 2 :]

    def add(keep, came):
        total = keep.astype(F32) + came.astype(F32)
        size = total.shape[0] // 2
        return total[:size].astype(BF), total[size:].astype(BF)

    turned = ((1, 0, 2), (1, 0), (0, 1), (1, 0), (0, 1))
    weights = (qkv_weight, out_weight, ffn_in_weight, ffn_out_weight, norm_params)
    weights = tuple(w.transpose(t) for w, t in zip(weights, turned))
    one, up, down = pack(*weights)
    one_came = send_on(one, early, 0)
    up_came = send_on(up, late, 0)
    one, tables, x, cot = after((join(one, one_came), tables, x, cot), up_came)
    own_early, other_early, pos_early, own_late, other_late, pos_late, half, where = tables
    for k in range(1, last):
        one_came = send_on(one, early, k)
        if k == 1:
            tokt = turn(pos_early, x)
            one_came = after(one_came, tokt)
        else:
            up = after(join(up, up_came), one)
            up_came = send_on(up, late, k - 1)
        one = join(one, one_came)
        if k > 1:
            one = after(one, up_came)
    one_came = send_on(one, early, last)
    for k in range(max(last - 1, 1), last):
        up = join(up, up_came)
        up_came = send_on(up, late, k)
    down_came = send_on(after(down, one), early, 0)
    one, one_came = after((one, one_came), up_came, down_came)
    one_other = (core_swap(one), core_swap(one_came))
    up = after(join(up, up_came), one_came)
    up_came = send_on(up, late, last)
    down = after(join(down, down_came), one_came)
    down_came = send_on(down, early, 1)

    w1 = settle(own_early, one, one_came, "one_own")
    qkv0, ctx0, lse0 = attn_one(x, w1)
    ctx0 = after(ctx0, down_came)
    for k in range(2, last):
        down = join(down, after(down_came, ctx0))
        down_came = send_on(down, early, k)
    w1 = (w1, settle(other_early, *one_other, "one_other"))
    qkv1, ctx1, lse1, xh1, rstd1, prow = attn_two(x, w1[1], w1[0], ctx0)
    xh1 = xh1.reshape(rows, D)
    rstd1 = rstd1.reshape(rows, 128)
    up_came, down_came = after((up_came, down_came), xh1)
    up_other = (core_swap(up), core_swap(up_came))
    down = join(down, down_came)
    down_came = send_on(down, early, last)
    wu = settle(own_late, up, up_came, "up_own")
    act0, gp0, yt = ffn_up(pos_early, after(xh1, down), prow, wu, True, "ffn_up_own")
    up_other = (up_other[0], after(up_other[1], act0))
    wu = (wu, settle(other_late, *up_other, "up_other"))
    down_came = after(down_came, act0)
    down_other = (core_swap(down), core_swap(down_came))
    act1, gp1 = ffn_up(pos_late, xh1, prow, wu[1], False, "ffn_up_other")
    acts, gps = (act0, act1), (gp0, gp1)
    wd = (settle(own_early, down, down_came, "down_own"), settle(other_early, *down_other, "down_other"))
    mixed0, cls_own, xh2, rstd2 = first_rows(xh1, prow, acts, wd)

    held = cls_own.astype(BF)[None]
    back = []
    for k in reversed(range(steps)):
        came = lax.ppermute(held, "dp", [(d, d ^ (1 << k)) for d in range(n_dp)])
        if len(back) < 3:
            at = len(back) + 1
            back.append(rest_rows(at, pos_late, after(xh1, held), rstd1, prow, acts, gps, cot, wu, wd))
            came = after(came, back[-1][4])
        held = join(held, came)
    held = join(held, core_swap(held))
    loss, grad_cls = contrast(where, span_doc.reshape(1, -1), held)
    back.insert(0, (*class_rows(pos_late, grad_cls, cot, xh2, rstd2, xh1, rstd1, prow, gps, wu, wd), mixed0))
    dft, du0, du1, dh1, sums, mixed_own = zip(*back)

    d_other = grad_other(dft, (act1,), "grad_down_other")
    d_came = core_swap(d_other)
    u_other = grad_other((after(yt, d_other),), du1, "grad_up_other")
    u_came = core_swap(u_other)
    d_keep, d_send = halves(
        own_late, *grad_own((after(dft[0], u_other),) + dft[1:], (act0,), d_came, "grad_down_own")
    )
    d_came = send_on(d_send, late, last)
    u_keep, u_send = halves(own_early, *grad_own((after(yt, d_keep),), du0, u_came, "grad_up_own"))
    dh1 = (after(dh1[0], u_keep),) + dh1[1:]
    dqkv1, dat = attn_back(pos_early, dh1, qkv1, lse1, w1[1], True, "attn_back_other")
    l_other = last_other(pos_early, tokt, dqkv1, dat, ctx1, sums)

    d_came, l_other = after((d_came, l_other))
    d_keep, d_send = add(d_keep, d_came)
    u_came = send_on(after(u_send, l_other), early, last)
    d_came = send_on(d_send, late, last - 1)
    l_came = core_swap(l_other)
    (dqkv0,) = attn_back(
        pos_early, (after(dh1[0], l_other),) + dh1[1:], qkv0, lse0, w1[0], False, "attn_back_own"
    )
    grad_in = input_grads((after(dh1[0], dqkv0),) + dh1[1:], dqkv0, dqkv1, w1[0], w1[1])
    l_keep, l_send = halves(
        own_early, *last_own(pos_early, tokt, after(dqkv0, grad_in), dat, ctx0, sums, l_came)
    )

    u_came, d_came, l_send = after((u_came, d_came, l_send))
    u_keep, u_send = add(u_keep, u_came)
    d_keep, d_send = add(d_keep, d_came)
    l_came = send_on(l_send, early, last)
    u_came = send_on(u_send, early, last - 1)
    d_came = send_on(d_send, late, last - 2)
    for k in reversed(range(last)):
        l_came, u_came, d_came = after((l_came, u_came, d_came))
        l_keep, l_send = add(l_keep, l_came)
        l_came = send_on(l_send, early, k)
        if k > 0:
            u_keep, u_send = add(u_keep, u_came)
            u_came = send_on(u_send, early, k - 1)
        if k > 1:
            d_keep, d_send = add(d_keep, d_came)
            d_came = send_on(d_send, late, k - 2)
        if k == last - 1:
            grad_came = core_swap(after(grad_in, l_send))
            mixed_other = tuple(core_swap(m) for m in after(mixed_own, l_send))
            l_came = after(l_came, grad_came, mixed_other)
        if k == last - 2:
            mixed, input_grad = place(half, mixed_own, mixed_other, after(grad_in, l_send), grad_came)
            l_came = after(l_came, input_grad)

    last_grad, down_grad, up_grad, squares = squares_of(((l_keep, l_came), (d_keep, d_came), (u_keep, u_came)))
    cols = core_swap(last_grad[:, HALF_QKV + HALF_OUT :])
    squares = squares + core_swap(squares)
    for k in reversed(range(steps)):
        squares = squares + lax.ppermute(squares, "dp", [(d, d ^ (1 << k)) for d in range(n_dp)])
    moments = (
        qkv_first, qkv_second, out_first, out_second, ffn_in_first, ffn_in_second,
        ffn_out_first, ffn_out_second, norm_first, norm_second,
    )
    new = adam(
        squares, last_grad, up_grad, down_grad, cols,
        weights,
        [m.transpose(turned[n // 2]) for n, m in enumerate(moments)],
    )
    updated = [value.transpose(turned[n // 3]) for n, value in enumerate(new[:15])]
    return (
        mixed.reshape(2 * rows, D),
        input_grad.reshape(2 * rows, D),
        loss[0, 0],
        new[15][0, 0],
        *updated,
    )


def solution(mesh):
    rows = P("dp", None)
    qkv = P("dp", None, "tensor")
    turned = P("tensor", "dp")
    up = P("dp", "tensor")
    norm = P(None, "dp")
    weights = (qkv, turned, up, turned, norm)
    moments = tuple(spec for spec in weights for _ in range(2))
    updated = tuple(spec for spec in weights for _ in range(3))
    return jax.shard_map(
        body,
        mesh=mesh,
        in_specs=(rows, rows, P()) + weights + moments,
        out_specs=(rows, rows, P(), P()) + updated,
        check_vma=False,
    )
```

```python
from functools import partial

import jax
import jax.numpy as jnp
import numpy as np
from jax import lax
from jax.experimental import pallas as pl
from jax.experimental.pallas import tpu as pltpu
from jax.sharding import PartitionSpec as P

HEAD = 64
SPAN = 128
STEP = 10
D = 768
FF = 3072
NB = 16
RB = D // NB
HALF_QKV = 1152
HALF_OUT = 384
HALF_FF = 1536
ONE = HALF_QKV + HALF_OUT + 128
CONTRAST = 4.0
EPS = 1e-06
BF = jnp.bfloat16
F32 = jnp.float32
AXES = ("dp", "tensor")
SHRINK = 100

NN = (((1,), (0,)), ((), ()))
NT = (((1,), (1,)), ((), ()))
TN = (((0,), (0,)), ((), ()))


def mm(left, right, dims=NN):
    return lax.dot_general(left, right, dims, preferred_element_type=F32)


def params(vmem=56):
    return pltpu.CompilerParams(vmem_limit_bytes=vmem * 2**20)


def cost(flops, bytes_accessed, trans=0):
    flops, bytes_accessed, trans = (n // SHRINK + 1 for n in (flops, bytes_accessed, trans))
    return pl.CostEstimate(flops=int(flops), bytes_accessed=int(bytes_accessed), transcendentals=int(trans))


HBM = pl.BlockSpec(memory_space=pl.ANY)


def bit_orders(n_dp):
    bits = n_dp.bit_length() - 1
    if bits == 4:
        return ((4, 8, 2, 1), (8, 4, 1, 2)), ((1, 4, 8, 2), (2, 8, 4, 1))
    up = tuple(1 << b for b in range(bits))[::-1]
    both = (up, up[: bits // 2] + up[bits // 2 :][::-1])
    return both, both


def pairs_of(n_dp, orders, step):
    out = []
    for d in range(n_dp):
        for c in range(2):
            out.append((d * 2 + c, (d ^ orders[c][step]) * 2 + c))
    return out


def rel_of(order):
    out = []
    for p in range(1 << len(order)):
        r = 0
        for k, b in enumerate(order):
            if (p >> k) & 1:
                r ^= b
        out.append(r)
    return out


AT_EARLY, AT_LATE, POS_EARLY, POS_LATE, HALF_AT, CLASS_AT = 0, NB, 2 * NB, 4 * NB, 6 * NB, 6 * NB + 2


class At:
    def __init__(self, ref, first):
        self.ref, self.first = ref, first

    def __getitem__(self, n):
        return self.ref[self.first + n]


def device_tables(n_dp):
    kinds = [[rel_of(order) for order in orders] for orders in bit_orders(n_dp)]
    classes = rel_of([1 << k for k in reversed(range(n_dp.bit_length() - 1))])
    plain = list(range(NB))
    table = []
    for d in range(n_dp):
        for c in range(2):
            direct = n_dp == NB
            row = []
            for rel in kinds:
                row += [d ^ r for r in rel[c]] if direct else plain
            for rel in kinds:
                for half in (c, 1 - c):
                    row += [rel[half].index(d ^ j) for j in range(NB)] if direct else plain
            me = d * 2 + c
            row += [c, 1 - c, me] + [me ^ (r << 1 | b) for b in range(2) for r in classes]
            table.append(row)
    return np.array(table, np.int32)


def core_swap(block):
    return lax.ppermute(block, "tensor", [(0, 1), (1, 0)])


VM = pl.BlockSpec(memory_space=pltpu.VMEM)
SM = pl.BlockSpec(memory_space=pltpu.SMEM)
BLK = 256


def call(kernel, out, in_specs, *args, vmem=16, flops=0, moved=0, trans=0, scratch=(), name=None):
    return pl.pallas_call(
        kernel,
        out_shape=[jax.ShapeDtypeStruct(s, t) for s, t in out],
        in_specs=in_specs,
        out_specs=[VM] * len(out),
        scratch_shapes=list(scratch),
        compiler_params=params(vmem),
        cost_estimate=cost(flops, moved, trans),
        name=name,
    )(*args)


def pack_kernel(qkv, out, up, down, norm, one_ref, two_ref, three_ref, wide, a0, a1, a2, a3, sems):
    rows = up.shape[0]
    wide[...] = jnp.zeros_like(wide)
    copies = [
        pltpu.make_async_copy(src, dst, sems.at[n])
        for n, (src, dst) in enumerate(
            ((qkv, a0), (out, a1), (down, a3), (up, a2))
        )
    ]
    for c in copies:
        c.start()
    copies[0].wait()
    for part in range(3):
        one_ref[0, :, part * HALF_OUT : (part + 1) * HALF_OUT] = a0[part].astype(BF)
    copies[1].wait()
    one_ref[0, :, HALF_QKV : HALF_QKV + HALF_OUT] = a1[...].astype(BF)
    wide[0:4, 0:rows] = norm[...]
    one_ref[0, :, HALF_QKV + HALF_OUT :] = wide[...].T[0:rows].astype(BF)
    copies[2].wait()
    three_ref[0] = a3[...].astype(BF)
    copies[3].wait()
    two_ref[0] = a2[...].astype(BF)


def pack(*shards):
    rows = shards[2].shape[0]
    return call(
        pack_kernel,
        [((1, rows, ONE), BF), ((1, rows, HALF_FF), BF), ((1, rows, HALF_FF), BF)],
        [pl.BlockSpec(memory_space=pltpu.HBM)] * 4 + [VM], *shards,
        vmem=60, moved=rows * 28000,
        scratch=[pltpu.VMEM((128, 128), F32)]
        + [pltpu.VMEM(w.shape, F32) for w in shards[:4]]
        + [pltpu.SemaphoreType.DMA((4,))],
        name="pack",
    )


def assemble_kernel(first, tab, low, high, out_ref, sems):
    copies = []
    for n, ref in enumerate((low, high)):
        for p in range(NB // 2):
            q = n * (NB // 2) + p
            copies.append(pltpu.make_async_copy(ref.at[p], out_ref.at[tab[first + q]], sems.at[q]))
    for c in copies:
        c.start()
    for c in copies:
        c.wait()


def assemble(first, tab, low, high, name):
    width = low.shape[-1]
    return call(
        partial(assemble_kernel, first),
        [((NB, RB, width), BF)],
        [SM] + [HBM] * 2,
        tab,
        low,
        high,
        vmem=8,
        moved=4 * D * width,
        scratch=[pltpu.SemaphoreType.DMA((NB,))],
        name=name,
    )[0]


def weight(w_ref, first, last):
    return w_ref[:, :, first:last].reshape(D, last - first)


def norm_fwd(hidden):
    center = hidden - jnp.mean(hidden, axis=-1, keepdims=True)
    spread = jnp.mean(center * center, axis=-1, keepdims=True)
    rstd = lax.rsqrt(spread + EPS)
    return center * rstd, rstd


def norm_bwd(grad, xh, rstd, gain):
    e = grad * gain
    m1 = jnp.mean(e, axis=-1, keepdims=True)
    m2 = jnp.mean(e * xh, axis=-1, keepdims=True)
    return rstd * (e - m1 - xh * m2)


def store_turned(ref, tab, value, col, width):
    turned = value.T
    for j in range(NB):
        block = turned[j * RB : (j + 1) * RB]
        for n in range(2):
            ref[n, tab[n * NB + j], :, pl.ds(col, width)] = block


def head_masks(rows, scale):
    lane = lax.broadcasted_iota(jnp.int32, (rows, 128), 1)
    return (
        jnp.where(lane < HEAD, scale, 0.0).astype(BF),
        jnp.where(lane < HEAD, 0.0, scale).astype(BF),
    )


def stack_heads(pair, masks):
    return jnp.concatenate([pair * masks[0], pair * masks[1]], axis=0)


def merge_heads(both):
    lane = lax.broadcasted_iota(jnp.int32, (SPAN, 128), 1)
    return jnp.where(lane < HEAD, both[:SPAN], both[SPAN:])


def turn_kernel(pos, x_ref, out_ref):
    rows = x_ref.shape[0]
    for i in range(rows // BLK):
        store_turned(out_ref, At(pos, POS_EARLY), x_ref[i * BLK : (i + 1) * BLK, :], i * BLK, BLK)


def turn(pos, x):
    rows = x.shape[0]
    return call(
        turn_kernel, [((2, NB, RB, rows), BF)], [SM, VM], pos, x, moved=rows * D * 6, name="turn"
    )[0]


def attn_rows(i, x, w_ref, masks, qkv_ref, ctx_ref, lse_ref):
    r0 = pl.multiple_of(i * BLK, BLK)
    qkv = mm(x, weight(w_ref, 0, HALF_QKV)).astype(BF)
    qkv_ref[pl.ds(r0, BLK), :] = qkv
    rows = []
    for s in range(2):
        own = qkv[s * SPAN : (s + 1) * SPAN]
        parts = []
        for j in range(3):
            q = stack_heads(own[:, j * 128 : (j + 1) * 128], masks)
            k = own[:, HALF_OUT + j * 128 : HALF_OUT + (j + 1) * 128]
            v = own[:, 2 * HALF_OUT + j * 128 : 2 * HALF_OUT + (j + 1) * 128]
            st = mm(k, q, NT)
            top = jnp.max(st, axis=0, keepdims=True)
            ex = jnp.exp(st - top)
            total = jnp.sum(ex, axis=0, keepdims=True)
            pt = (ex * (1.0 / total)).astype(BF)
            lse_ref[i * 2 + s, j : j + 1, :] = top + jnp.log(total)
            parts.append(merge_heads(mm(pt, v, TN)).astype(BF))
        rows.append(jnp.concatenate(parts, axis=1))
    ctx = jnp.concatenate(rows, axis=0)
    ctx_ref[pl.ds(r0, BLK), :] = ctx
    return ctx


def attn_one_kernel(x_ref, w_ref, qkv_ref, ctx_ref, lse_ref):
    masks = head_masks(SPAN, HEAD ** (-0.5))

    def step(i, carry):
        x = x_ref[pl.ds(pl.multiple_of(i * BLK, BLK), BLK), :]
        attn_rows(i, x, w_ref, masks, qkv_ref, ctx_ref, lse_ref)
        return carry

    lax.fori_loop(0, x_ref.shape[0] // BLK, step, 0, unroll=2)


def attn_two_kernel(x_ref, w_ref, wo_ref, ctxo_ref, qkv_ref, ctx_ref, lse_ref, xh_ref, rstd_ref, p_ref):
    cols = weight(w_ref, HALF_QKV + HALF_OUT, ONE).astype(F32)
    p_ref[...] = cols.T[:8]
    masks = head_masks(SPAN, HEAD ** (-0.5))

    def step(i, carry):
        rs = pl.ds(pl.multiple_of(i * BLK, BLK), BLK)
        x = x_ref[rs, :]
        ctx = attn_rows(i, x, w_ref, masks, qkv_ref, ctx_ref, lse_ref)
        attn = x.astype(F32) + mm(ctxo_ref[rs, :], weight(wo_ref, HALF_QKV, HALF_QKV + HALF_OUT), NT)
        attn = attn + mm(ctx, weight(w_ref, HALF_QKV, HALF_QKV + HALF_OUT), NT)
        xh, rstd = norm_fwd(attn)
        rstd = jnp.broadcast_to(rstd, (BLK, 128))
        for s in range(2):
            for q in range(4):
                r = s * SPAN + q * 32
                xh_ref[q, i * 2 + s] = xh[r : r + 32]
                rstd_ref[q, i * 2 + s] = rstd[r : r + 32]
        return carry

    lax.fori_loop(0, x_ref.shape[0] // BLK, step, 0, unroll=2)


def attn_shapes(rows):
    return [((rows, HALF_QKV), BF), ((rows, HALF_OUT), BF), ((rows // SPAN, 8, 2 * SPAN), F32)]


def attn_one(x, w):
    rows = x.shape[0]
    return call(
        attn_one_kernel, attn_shapes(rows), [VM, VM], x, w,
        vmem=16, flops=rows * 4e6, moved=rows * 8000 + 2e6, trans=rows * 800, name="attn_one",
    )


def attn_two(x, w, w_own, ctx_own):
    rows = x.shape[0]
    spans = rows // SPAN
    out = attn_shapes(rows) + [
        ((4, spans, 32, D), F32),
        ((4, spans, 32, 128), F32),
        ((8, D), F32),
    ]
    return call(
        attn_two_kernel, out, [VM] * 4, x, w, w_own, ctx_own,
        vmem=16, flops=rows * 5e6, moved=rows * 12000 + 4e6, trans=rows * 800, name="attn_two",
    )


def gelu_pair(u):
    a = jnp.abs(u)
    d = 1.0 + (0.3275911 * 0.5**0.5) * a
    t = pl.reciprocal(d, approx=True)
    t = t * (2.0 - d * t)
    e = jnp.exp(-0.5 * u * u)
    poly = 0.5307027145 * t - 0.7265760135
    poly = poly * t + 0.7107068705
    poly = poly * t - 0.142248368
    poly = poly * t + 0.127414796
    tail = (poly * t) * e
    phi = jnp.where(u >= 0.0, 1.0 - tail, tail)
    return u * phi, phi + (0.3989422804014327 * u) * e


TILE = 512


def ffn_up_kernel(pos, xh_ref, p_ref, w_ref, g_ref, gp_ref, *yt_ref):
    def step(i, carry):
        rs = pl.ds(pl.multiple_of(i * BLK, BLK), BLK)
        y = xh_ref[rs, :] * p_ref[0:1, :] + p_ref[1:2, :]
        yb = y.astype(BF)
        if yt_ref:
            store_turned(yt_ref[0], At(pos, POS_EARLY), yb, pl.multiple_of(i * BLK, BLK), BLK)
        for t in range(HALF_FF // TILE):
            u = mm(yb, weight(w_ref, t * TILE, (t + 1) * TILE))
            g, gp = gelu_pair(u)
            g_ref[rs, t * TILE : (t + 1) * TILE] = g.astype(BF)
            gp_ref[rs, t * TILE : (t + 1) * TILE] = gp.astype(BF)
        return carry

    lax.fori_loop(0, xh_ref.shape[0] // BLK, step, 0, unroll=2)


def ffn_up(pos, xh, prow, w, turned, name):
    rows = xh.shape[0]
    out = [((rows, HALF_FF), BF), ((rows, HALF_FF), BF)]
    if turned:
        out.append(((2, NB, RB, rows), BF))
    return call(
        ffn_up_kernel, out, [SM, VM, VM, VM], pos, xh, prow, w,
        vmem=16, flops=rows * 2.4e6, moved=rows * 9000 + 2e6, trans=rows * 6000, name=name,
    )


def down_block(r0, xh1_ref, p_ref, acts, downs):
    rs = pl.ds(r0, BLK)
    total = xh1_ref[rs, :] * p_ref[0:1, :] + p_ref[1:2, :]
    for g_ref, w_ref in zip(acts, downs):
        total = total + mm(g_ref[rs, :], weight(w_ref, 0, HALF_FF), NT)
    return norm_fwd(total)


def first_kernel(xh1_ref, p_ref, g0, g1, d0, d1, mixed_ref, cls_ref, xh_ref, rstd_ref):
    xh, rstd = down_block(0, xh1_ref, p_ref, (g0, g1), (d0, d1))
    xh_ref[...] = xh
    rstd_ref[...] = jnp.broadcast_to(rstd, rstd_ref.shape)
    out = (xh * p_ref[2:3, :] + p_ref[3:4, :]).reshape(mixed_ref.shape)
    mixed_ref[...] = out.astype(BF)
    cls_ref[...] = out[:, 0, :]


def first_rows(xh1, prow, acts, downs):
    spans = BLK // 32
    return call(
        first_kernel,
        [((spans, 32, D), BF), ((spans, D), F32), ((BLK, D), F32), ((BLK, 128), F32)],
        [VM] * 6, xh1, prow, *acts, *downs,
        vmem=8, flops=BLK * 4.8e6, moved=BLK * 16000 + 5e6, name="first_rows",
    )


def back_block(r0, grad, xh2, rstd2, gps, xh1_ref, rstd1_ref, p_ref, ups, downs, dus):
    rs = pl.ds(r0, BLK)
    sum_g2 = jnp.sum(grad * xh2, axis=0, keepdims=True)
    sum_b2 = jnp.sum(grad, axis=0, keepdims=True)
    dh = norm_bwd(grad, xh2, rstd2, p_ref[2:3, :])
    df = dh.astype(BF)
    total = dh
    for gp_ref, up_ref, down_ref, du_ref in zip(gps, ups, downs, dus):
        for t in range(HALF_FF // TILE):
            lo, hi = t * TILE, (t + 1) * TILE
            dg = mm(df, weight(down_ref, lo, hi))
            du_ref[:, lo:hi] = (dg * gp_ref[rs, lo:hi].astype(F32)).astype(BF)
        total = total + mm(du_ref[...], weight(up_ref, 0, HALF_FF), NT)
    xh1 = xh1_ref[rs, :]
    sum_g1 = jnp.sum(total * xh1, axis=0, keepdims=True)
    sum_b1 = jnp.sum(total, axis=0, keepdims=True)
    dh1 = norm_bwd(total, xh1, rstd1_ref[rs, 0:1], p_ref[0:1, :])
    return df, dh1, (sum_g1, sum_b1, sum_g2, sum_b2)


def back_shapes():
    return [
        ((2, NB, RB, BLK), BF),
        ((BLK, HALF_FF), BF),
        ((BLK, HALF_FF), BF),
        ((BLK // 32, 32, D), F32),
        ((8, D), F32),
    ]


def rest_kernel(
    at, pos, xh1_ref, rstd1_ref, p_ref, g0, g1, gp0, gp1, cot_ref, u0, u1, d0, d1,
    dft_ref, du0_ref, du1_ref, dh1_ref, sums_ref, mixed_ref,
):
    r0, c0 = at * BLK, at * 32
    xh, rstd = down_block(r0, xh1_ref, p_ref, (g0, g1), (d0, d1))
    out = xh * p_ref[2:3, :] + p_ref[3:4, :]
    mixed_ref[...] = out.reshape(mixed_ref.shape).astype(BF)
    grad = cot_ref[:, c0 : c0 + 32, :].astype(F32).reshape(BLK, D)
    df, dh1, sums = back_block(
        r0, grad, xh, rstd, (gp0, gp1), xh1_ref, rstd1_ref, p_ref, (u0, u1), (d0, d1), (du0_ref, du1_ref)
    )
    store_turned(dft_ref, At(pos, POS_LATE), df, 0, BLK)
    dh1_ref[...] = dh1.reshape(dh1_ref.shape)
    for n in range(4):
        sums_ref[n : n + 1, :] = sums[n]


def rest_rows(at, pos, xh1, rstd1, prow, acts, gps, cot, ups, downs):
    return call(
        partial(rest_kernel, at),
        back_shapes() + [((BLK // 32, 32, D), BF)],
        [SM] + [VM] * 12, pos, xh1, rstd1, prow, *acts, *gps, cot, *ups, *downs,
        vmem=16, flops=BLK * 14.5e6, moved=BLK * 40000 + 1e7, name=f"rest_rows_{at}",
    )


def class_kernel(
    pos, cls_ref, cot_ref, xh2_ref, rstd2_ref, xh1_ref, rstd1_ref, p_ref, gp0, gp1, u0, u1, d0, d1,
    dft_ref, du0_ref, du1_ref, dh1_ref, sums_ref,
):
    spans = cls_ref.shape[0]
    grad = cot_ref[:, 0:32, :].astype(F32)
    first = lax.broadcasted_iota(jnp.int32, grad.shape, 1) == 0
    grad = grad + jnp.where(first, cls_ref[...].reshape(spans, 1, D), 0.0)
    grad = grad.reshape(BLK, D)
    df, dh1, sums = back_block(
        0, grad, xh2_ref[...], rstd2_ref[:, 0:1], (gp0, gp1), xh1_ref, rstd1_ref, p_ref,
        (u0, u1), (d0, d1), (du0_ref, du1_ref),
    )
    store_turned(dft_ref, At(pos, POS_LATE), df, 0, BLK)
    dh1_ref[...] = dh1.reshape(dh1_ref.shape)
    for n in range(4):
        sums_ref[n : n + 1, :] = sums[n]


def class_rows(pos, grad_cls, cot, xh2, rstd2, xh1, rstd1, prow, gps, ups, downs):
    return call(
        class_kernel,
        back_shapes(),
        [SM] + [VM] * 13, pos, grad_cls, cot, xh2, rstd2, xh1, rstd1, prow, *gps, *ups, *downs,
        vmem=16, flops=BLK * 9.7e6, moved=BLK * 30000 + 1e7, name="class_rows",
    )


def contrast_kernel(where, doc_ref, cls_ref, loss_ref, grad_ref, rows, own_doc):
    spans = doc_ref.shape[1]
    doc_row = doc_ref[...].astype(F32)
    doc_col = jnp.broadcast_to(doc_row, (128, spans)).T[:, 0:1]
    blocks, per = cls_ref.shape[0], cls_ref.shape[1]
    where = At(where, CLASS_AT)
    me = where[0]
    for n in range(blocks):
        rows[where[1 + n]] = cls_ref[n].astype(F32)
    a = rows[...].reshape(spans, D).astype(BF)
    own = rows[me].astype(BF)
    scale = D ** (-0.5)
    col = lax.broadcasted_iota(jnp.int32, (spans, spans), 1)
    row = lax.broadcasted_iota(jnp.int32, (spans, spans), 0)
    logits = mm(a, a, NT) * scale
    partner = (doc_col == doc_row) & (row != col)
    masked = jnp.where(row == col, -1000000000.0, logits)
    top = jnp.max(masked, axis=0, keepdims=True)
    lse = jnp.log(jnp.sum(jnp.exp(masked - top), axis=0, keepdims=True)) + top
    positive = jnp.sum(jnp.where(partner, logits, 0.0), axis=0, keepdims=True)
    flagged = jnp.max(jnp.where(partner, 1.0, 0.0), axis=0, keepdims=True)
    count = jnp.sum(flagged, axis=1, keepdims=True)
    loss = jnp.sum(flagged * (lse - positive), axis=1, keepdims=True) / count
    loss_ref[...] = jnp.broadcast_to(loss, loss_ref.shape)

    weight_row = flagged * (CONTRAST * spans) / count
    own_doc[...] = doc_col.reshape(blocks, per, 1)
    docs = own_doc[me]
    col = lax.broadcasted_iota(jnp.int32, (per, spans), 1)
    row = lax.broadcasted_iota(jnp.int32, (per, spans), 0) + me * per
    logits = mm(own, a, NT) * scale
    same = jnp.where((docs == doc_row) & (row != col), 1.0, 0.0)
    masked = jnp.where(row == col, -1000000000.0, logits)
    top = jnp.max(masked, axis=1, keepdims=True)
    ex = jnp.exp(masked - top)
    soft = ex / jnp.sum(ex, axis=1, keepdims=True)
    own_weight = jnp.max(same, axis=1, keepdims=True) * (CONTRAST * spans) / count
    sym = own_weight * (soft - same) + weight_row * (jnp.exp(masked - lse) - same)
    high = sym.astype(BF)
    low = (sym - high.astype(F32)).astype(BF)
    grad_ref[...] = (mm(high, a) + mm(low, a)) * scale


def contrast(where, doc_row, cls_all):
    blocks, per, _ = cls_all.shape
    spans = blocks * per
    return call(
        contrast_kernel,
        [((1, 128), F32), ((per, D), F32)],
        [SM, VM, VM],
        where, doc_row, cls_all,
        vmem=8 if spans <= 256 else 40, flops=2 * spans * spans * D, moved=spans * D * 2,
        scratch=[pltpu.VMEM((blocks, per, D), F32), pltpu.VMEM((blocks, per, 1), F32)],
        name="contrast",
    )


def turned_of(refs, n):
    return jnp.concatenate([ref[n].reshape(D, ref.shape[3]) for ref in refs], axis=1)


def grad_other_kernel(count, *refs):
    xts, ys, out_ref = refs[:count], refs[count:-1], refs[-1]
    xt = turned_of(xts, 1)
    for t in range(HALF_FF // TILE):
        lo, hi = t * TILE, (t + 1) * TILE
        grad = mm(xt, jnp.concatenate([y[:, lo:hi] for y in ys], axis=0))
        out_ref[:, :, lo:hi] = grad.astype(BF).reshape(NB, RB, TILE)


def grad_other(xts, ys, name):
    rows = sum(y.shape[0] for y in ys)
    return call(
        partial(grad_other_kernel, len(xts)),
        [((NB, RB, HALF_FF), BF)],
        [VM] * (len(xts) + len(ys)), *xts, *ys,
        vmem=12, flops=2 * rows * D * HALF_FF, moved=rows * 8000 + 2.4e6, name=name,
    )[0]


def grad_own_kernel(count, came_ref, *refs):
    xts, ys, keep_ref, send_ref = refs[:count], refs[count:-2], refs[-2], refs[-1]
    nh = NB // 2
    xt = turned_of(xts, 0)
    for t in range(HALF_FF // TILE):
        lo, hi = t * TILE, (t + 1) * TILE
        grad = mm(xt, jnp.concatenate([y[:, lo:hi] for y in ys], axis=0))
        grad = (grad.reshape(NB, RB, TILE) + came_ref[:, :, lo:hi].astype(F32)).astype(BF)
        keep_ref[:, :, lo:hi] = grad[:nh]
        send_ref[:, :, lo:hi] = grad[nh:]


def grad_own(xts, ys, came, name):
    rows = sum(y.shape[0] for y in ys)
    return call(
        partial(grad_own_kernel, len(xts)),
        [((NB // 2, RB, HALF_FF), BF)] * 2,
        [VM] * (1 + len(xts) + len(ys)), came, *xts, *ys,
        vmem=12, flops=2 * rows * D * HALF_FF, moved=rows * 8000 + 4.8e6, name=name,
    )


def natural(refs, i):
    return jnp.concatenate([ref[i * 2 + s] for s in range(2) for ref in refs], axis=0)


def attn_back_kernel(pos, r0_ref, r1_ref, r2_ref, r3_ref, qkv_ref, lse_ref, w_ref, dqkv_ref, *dat_ref):
    masks = head_masks(SPAN, HEAD ** (-0.5))
    plain = head_masks(SPAN, 1.0)
    spans = r0_ref.shape[0]

    def step(i, carry):
        r0 = pl.multiple_of(i * BLK, BLK)
        da = natural((r0_ref, r1_ref, r2_ref, r3_ref), i).astype(BF)
        if dat_ref:
            store_turned(dat_ref[0], At(pos, POS_EARLY), da, r0, BLK)
        dctx = mm(da, weight(w_ref, HALF_QKV, HALF_QKV + HALF_OUT)).astype(BF)
        for s in range(2):
            rs = pl.ds(pl.multiple_of(r0 + s * SPAN, SPAN), SPAN)
            for j in range(3):
                a, b = j * 128, (j + 1) * 128
                q = stack_heads(qkv_ref[rs, a:b], masks)
                k = qkv_ref[rs, HALF_OUT + a : HALF_OUT + b]
                v = qkv_ref[rs, 2 * HALF_OUT + a : 2 * HALF_OUT + b]
                dc = stack_heads(dctx[s * SPAN : (s + 1) * SPAN, a:b], plain)
                st = mm(k, q, NT)
                pt = jnp.exp(st - lse_ref[i * 2 + s, j : j + 1, :])
                dpt = mm(v, dc, NT)
                dst = pt * (dpt - jnp.sum(pt * dpt, axis=0, keepdims=True))
                dst = dst.astype(BF)
                dv = mm(pt.astype(BF), dc)
                dk = mm(dst, q)
                dq = merge_heads(mm(dst, k, TN)) * HEAD ** (-0.5)
                dqkv_ref[rs, a:b] = dq.astype(BF)
                dqkv_ref[rs, HALF_OUT + a : HALF_OUT + b] = dk.astype(BF)
                dqkv_ref[rs, 2 * HALF_OUT + a : 2 * HALF_OUT + b] = dv.astype(BF)
        return carry

    lax.fori_loop(0, spans // 2, step, 0, unroll=2)


def attn_back(pos, dh1, qkv, lse, w, turned, name):
    rows = qkv.shape[0]
    out = [((rows, HALF_QKV), BF)]
    if turned:
        out.append(((2, NB, RB, rows), BF))
    return call(
        attn_back_kernel, out,
        [SM] + [VM] * 7, pos, *dh1, qkv, lse, w,
        vmem=16, flops=rows * 6e6, moved=rows * 10000 + 3e6, trans=rows * 800, name=name,
    )


def last_value(order, xt_ref, dqkv_ref, dat_ref, ctx_ref, t):
    rows = xt_ref.shape[3]
    if t < 3:
        return mm(xt_ref[order].reshape(D, rows), dqkv_ref[:, t * HALF_OUT : (t + 1) * HALF_OUT])
    return mm(dat_ref[order].reshape(D, rows), ctx_ref[...])


def norm_columns(sums):
    total = sums[0][0:4, :]
    for ref in sums[1:]:
        total = total + ref[0:4, :]
    return jnp.concatenate([total, jnp.zeros((124, D), F32)], axis=0).T


def last_other_kernel(pos, xt_ref, dqkv_ref, dat_ref, ctx_ref, s0, s1, s2, s3, out_ref):
    for t in range(4):
        grad = last_value(1, xt_ref, dqkv_ref, dat_ref, ctx_ref, t)
        lo = t * HALF_OUT
        out_ref[:, :, lo : lo + HALF_OUT] = grad.astype(BF).reshape(NB, RB, HALF_OUT)
    norm = norm_columns((s0, s1, s2, s3)).astype(BF)
    for j in range(NB):
        out_ref[pos[POS_EARLY + NB + j], :, HALF_QKV + HALF_OUT :] = norm[j * RB : (j + 1) * RB]


def last_other(pos, xt, dqkv, dat, ctx, sums):
    rows = xt.shape[3]
    return call(
        last_other_kernel,
        [((NB, RB, ONE), BF)],
        [SM] + [VM] * 8, pos, xt, dqkv, dat, ctx, *sums,
        vmem=12, flops=2 * rows * D * HALF_FF, moved=rows * 8000 + 2.4e6, name="last_other",
    )[0]


def last_own_kernel(
    pos, xt_ref, dqkv_ref, dat_ref, ctx_ref, s0, s1, s2, s3, came_ref, keep_ref, send_ref, cols
):
    nh = NB // 2
    norm = norm_columns((s0, s1, s2, s3))
    for j in range(NB):
        cols[pos[POS_EARLY + j]] = norm[j * RB : (j + 1) * RB]
    for t in range(5):
        lo = t * HALF_OUT
        hi = min(lo + HALF_OUT, ONE)
        if t < 4:
            grad = last_value(0, xt_ref, dqkv_ref, dat_ref, ctx_ref, t).reshape(NB, RB, HALF_OUT)
        else:
            grad = cols[...]
        grad = (grad + came_ref[:, :, lo:hi].astype(F32)).astype(BF)
        keep_ref[:, :, lo:hi] = grad[:nh]
        send_ref[:, :, lo:hi] = grad[nh:]


def last_own(pos, xt, dqkv, dat, ctx, sums, came):
    rows = xt.shape[3]
    return call(
        last_own_kernel,
        [((NB // 2, RB, ONE), BF)] * 2,
        [SM] + [VM] * 9, pos, xt, dqkv, dat, ctx, *sums, came,
        vmem=12, flops=2 * rows * D * HALF_FF, moved=rows * 8000 + 4.8e6,
        scratch=[pltpu.VMEM((NB, RB, 128), F32)], name="last_own",
    )


def input_grad_kernel(r0_ref, r1_ref, r2_ref, r3_ref, own_ref, other_ref, w0_ref, w1_ref, out_ref):
    spans = r0_ref.shape[0]

    def step(i, carry):
        rs = pl.ds(pl.multiple_of(i * BLK, BLK), BLK)
        total = natural((r0_ref, r1_ref, r2_ref, r3_ref), i)
        total = total + mm(own_ref[rs, :], weight(w0_ref, 0, HALF_QKV), NT)
        total = total + mm(other_ref[rs, :], weight(w1_ref, 0, HALF_QKV), NT)
        out_ref[rs, :] = total
        return carry

    lax.fori_loop(0, spans // 2, step, 0, unroll=2)


def input_grads(dh1, own, other, w_own, w_other):
    rows = own.shape[0]
    return call(
        input_grad_kernel,
        [((rows, D), F32)],
        [VM] * 8, *dh1, own, other, w_own, w_other,
        vmem=12, flops=rows * 3.6e6, moved=rows * 12000 + 5e6, name="input_grads",
    )[0]


def place_kernel(half, *refs):
    own, other, g_own, g_other = refs[0:4], refs[4:8], refs[8], refs[9]
    mixed_ref, grad_ref, sems = refs[10:]
    spans = g_own.shape[0]
    copies = []
    for n, (pieces, g) in enumerate(((own, g_own), (other, g_other))):
        at = pl.ds(half[HALF_AT + n] * spans, spans)
        for q in range(4):
            to = mixed_ref.at[at, 32 * q : 32 * q + 32, :]
            copies.append(pltpu.make_async_copy(pieces[q], to, sems.at[5 * n + q]))
        copies.append(pltpu.make_async_copy(g, grad_ref.at[at], sems.at[5 * n + 4]))
    for c in copies:
        c.start()
    for c in copies:
        c.wait()


def place(half, own, other, g_own, g_other):
    spans = own[0].shape[0]
    g_own, g_other = (g.reshape(spans, SPAN, D) for g in (g_own, g_other))
    return pl.pallas_call(
        place_kernel,
        out_shape=[
            jax.ShapeDtypeStruct((2 * spans, SPAN, D), BF),
            jax.ShapeDtypeStruct((2 * spans, SPAN, D), F32),
        ],
        in_specs=[SM] + [VM] * 10,
        out_specs=[HBM] * 2,
        scratch_shapes=[pltpu.SemaphoreType.DMA((10,))],
        compiler_params=params(16),
        cost_estimate=cost(0, spans * SPAN * D * 24),
        name="place",
    )(half, *own, *other, g_own, g_other)


def squares_kernel(k0, c0, k1, c1, k2, c2, g0, g1, g2, sq_ref):
    main = HALF_QKV + HALF_OUT
    total = jnp.zeros((1, 1), F32)
    for keep, came, out in ((k0, c0, g0), (k1, c1, g1), (k2, c2, g2)):
        grad = keep[0].astype(F32) + came[0].astype(F32)
        out[...] = grad
        sq = jnp.sum(grad[:, :main] * grad[:, :main], axis=1, keepdims=True)
        if grad.shape[1] > main:
            cols = grad[:, main:]
            sq = sq + 0.5 * jnp.sum(cols * cols, axis=1, keepdims=True)
        total = total + jnp.sum(sq, axis=0, keepdims=True)
    sq_ref[...] = jnp.broadcast_to(total, sq_ref.shape)


def squares_of(pairs):
    shard = pairs[0][0].shape[1]
    out = [((shard, k.shape[2]), F32) for k, _ in pairs] + [((8, 128), F32)]
    flat = [a for pair in pairs for a in pair]
    return call(squares_kernel, out, [VM] * 6, *flat, vmem=8, moved=shard * 40000, name="squares")


def adam_parts(weight, gradient, moment_one, moment_two, step_rate, decay_rate):
    first_new = 0.9 * moment_one + 0.1 * gradient
    second_new = 0.999 * moment_two + 0.001 * gradient * gradient
    corr_first = first_new * (1.0 / (1.0 - 0.9**STEP))
    corr_second = second_new * (1.0 / (1.0 - 0.999**STEP))
    weight_new = weight - step_rate * (
        corr_first / (jnp.sqrt(corr_second) + 1e-08) + decay_rate * weight
    )
    return first_new, second_new, weight_new


def adam_kernel(sq_ref, last_ref, up_ref, down_ref, cols_ref, *refs):
    ins, outs, wide = refs[:15], refs[15:-1], refs[-1]
    norm = jnp.sqrt(sq_ref[0:1, 0:1])
    outs[15][...] = jnp.broadcast_to(norm, outs[15].shape)
    scale = 1.0 / jnp.maximum(norm, 1.0)

    def update(n, at, grad, rate, decay):
        new = adam_parts(ins[n][at], grad * scale, ins[5 + 2 * n][at], ins[6 + 2 * n][at], rate, decay)
        for m in range(3):
            outs[3 * n + m][at] = new[m]

    for part in range(3):
        update(0, part, last_ref[:, part * HALF_OUT : (part + 1) * HALF_OUT], 0.02, 0.01)
    update(1, Ellipsis, last_ref[:, HALF_QKV : HALF_QKV + HALF_OUT], 0.02, 0.01)
    update(2, Ellipsis, up_ref[...], 0.02, 0.01)
    update(3, Ellipsis, down_ref[...], 0.02, 0.01)
    shard = last_ref.shape[0]
    wide[...] = jnp.zeros_like(wide)
    wide[0:shard, :] = 0.5 * (last_ref[:, HALF_QKV + HALF_OUT :] + cols_ref[...])
    update(4, Ellipsis, wide[...].T[0:4, 0:shard], 0.5, 0.0)


def adam(squares, last, up, down, cols, weights, moments):
    shapes = [w.shape for w in weights]
    out = [(s, F32) for s in shapes for _ in range(3)] + [((8, 128), F32)]
    args = (squares, last, up, down, cols, *weights, *moments)
    return call(
        adam_kernel, out, [VM] * len(args), *args, vmem=16, moved=7 * 4 * last.shape[0] * 4608,
        scratch=[pltpu.VMEM((128, 128), F32)], name="adam",
    )


def after(value, *others):
    return lax.optimization_barrier((value, others))[0]


def body(
    tokens,
    cotangent,
    span_doc,
    qkv_weight,
    out_weight,
    ffn_in_weight,
    ffn_out_weight,
    norm_params,
    qkv_first,
    qkv_second,
    out_first,
    out_second,
    ffn_in_first,
    ffn_in_second,
    ffn_out_first,
    ffn_out_second,
    norm_first,
    norm_second,
):
    n_dp = lax.axis_size("dp")
    dp = lax.axis_index("dp")
    core = lax.axis_index("tensor")
    shard = D // n_dp
    rows = tokens.shape[0] // 2
    spans = rows // SPAN
    direct = n_dp == NB
    early, late = bit_orders(n_dp)
    steps = len(early[0])
    last = steps - 1

    tab = lax.dynamic_index_in_dim(device_tables(n_dp), dp * 2 + core, 0, keepdims=False)
    x = lax.dynamic_slice_in_dim(tokens, core * rows, rows, 0)
    cot = lax.dynamic_slice_in_dim(cotangent, core * rows, rows, 0).reshape(spans, SPAN, D)

    def places(orders):
        return dp ^ jnp.array([rel_of(order) for order in orders], jnp.int32)[core]

    def send_on(block, orders, k):
        return lax.ppermute(block, AXES, pairs_of(n_dp, orders, k))

    def join(held, came):
        return jnp.concatenate([held, came], axis=0)

    def settle(orders, low, high, name):
        if direct:
            return assemble(AT_EARLY if orders is early else AT_LATE, tab, low, high, name)
        full = join(low, high)[jnp.argsort(places(orders))].reshape(NB, RB, -1)
        return assemble(0, tab, full[: NB // 2], full[NB // 2 :], name)

    def halves(orders, keep, send):
        if direct:
            return keep, send
        full = join(keep, send).reshape(n_dp, shard, -1)[places(orders)]
        return full[: n_dp // 2], full[n_dp // 2 :]

    def add(keep, came):
        total = keep.astype(F32) + came.astype(F32)
        size = total.shape[0] // 2
        return total[:size].astype(BF), total[size:].astype(BF)

    turned = ((1, 0, 2), (1, 0), (0, 1), (1, 0), (0, 1))
    weights = (qkv_weight, out_weight, ffn_in_weight, ffn_out_weight, norm_params)
    weights = tuple(w.transpose(t) for w, t in zip(weights, turned))
    one, up, down = pack(*weights)
    one_came = send_on(one, early, 0)
    up_came = send_on(up, late, 0)
    one, tab, x, cot = after((join(one, one_came), tab, x, cot), up_came)
    for k in range(1, last):
        one_came = send_on(one, early, k)
        if k == 1:
            tokt = turn(tab, x)
            one_came = after(one_came, tokt)
        else:
            up = after(join(up, up_came), one)
            up_came = send_on(up, late, k - 1)
        one = join(one, one_came)
        if k > 1:
            one = after(one, up_came)
    one_came = send_on(one, early, last)
    for k in range(max(last - 1, 1), last):
        up = join(up, up_came)
        up_came = send_on(up, late, k)
    down_came = send_on(after(down, one), early, 0)
    one, one_came = after((one, one_came), up_came, down_came)
    up = after(join(up, up_came), one_came)
    up_came = send_on(up, late, last)
    down = after(join(down, down_came), one_came)
    down_came = send_on(down, early, 1)

    w1 = settle(early, one, one_came, "one_own")
    w1 = (w1, core_swap(w1))
    qkv0, ctx0, lse0 = attn_one(x, w1[0])
    ctx0 = after(ctx0, down_came)
    for k in range(2, last):
        down = join(down, after(down_came, ctx0))
        down_came = send_on(down, early, k)
    qkv1, ctx1, lse1, xh1, rstd1, prow = attn_two(x, w1[1], w1[0], ctx0)
    xh1 = xh1.reshape(rows, D)
    rstd1 = rstd1.reshape(rows, 128)
    up_came, down_came = after((up_came, down_came), xh1)
    wu = settle(late, up, up_came, "up_own")
    wu = (wu, core_swap(wu))
    down = join(down, down_came)
    down_came = send_on(down, early, last)
    act0, gp0, yt = ffn_up(tab, after(xh1, down), prow, wu[0], True, "ffn_up_own")
    wd = settle(early, down, after(down_came, act0), "down_own")
    wd = (wd, core_swap(wd))
    act1, gp1 = ffn_up(tab, after(xh1, wd[0]), prow, wu[1], False, "ffn_up_other")
    acts, gps = (act0, act1), (gp0, gp1)
    mixed0, cls_own, xh2, rstd2 = first_rows(xh1, prow, acts, wd)

    held = cls_own.astype(BF)[None]
    back = []
    for k in reversed(range(steps)):
        came = lax.ppermute(held, "dp", [(d, d ^ (1 << k)) for d in range(n_dp)])
        if len(back) < 3:
            at = len(back) + 1
            back.append(rest_rows(at, tab, after(xh1, held), rstd1, prow, acts, gps, cot, wu, wd))
            came = after(came, back[-1][4])
        held = join(held, came)
    held = join(held, core_swap(held))
    loss, grad_cls = contrast(tab, span_doc.reshape(1, -1), held)
    back.insert(0, (*class_rows(tab, grad_cls, cot, xh2, rstd2, xh1, rstd1, prow, gps, wu, wd), mixed0))
    dft, du0, du1, dh1, sums, mixed_own = zip(*back)

    d_other = grad_other(dft, (act1,), "grad_down_other")
    d_came = core_swap(d_other)
    u_other = grad_other((after(yt, d_other),), du1, "grad_up_other")
    u_came = core_swap(u_other)
    d_keep, d_send = halves(
        late, *grad_own((after(dft[0], u_other),) + dft[1:], (act0,), d_came, "grad_down_own")
    )
    d_came = send_on(d_send, late, last)
    u_keep, u_send = halves(early, *grad_own((after(yt, d_keep),), du0, u_came, "grad_up_own"))
    dh1 = (after(dh1[0], u_keep),) + dh1[1:]
    dqkv1, dat = attn_back(tab, dh1, qkv1, lse1, w1[1], True, "attn_back_other")
    l_other = last_other(tab, tokt, dqkv1, dat, ctx1, sums)

    d_came, l_other = after((d_came, l_other))
    d_keep, d_send = add(d_keep, d_came)
    u_came = send_on(after(u_send, l_other), early, last)
    d_came = send_on(d_send, late, last - 1)
    l_came = core_swap(l_other)
    (dqkv0,) = attn_back(
        tab, (after(dh1[0], l_other),) + dh1[1:], qkv0, lse0, w1[0], False, "attn_back_own"
    )
    l_keep, l_send = halves(early, *last_own(tab, tokt, dqkv0, dat, ctx0, sums, l_came))
    l_came = send_on(l_send, early, last)
    grad_in = input_grads((after(dh1[0], l_send),) + dh1[1:], dqkv0, dqkv1, w1[0], w1[1])
    u_came, d_came = after((u_came, d_came), l_send)
    u_keep, u_send = add(u_keep, u_came)
    d_keep, d_send = add(d_keep, d_came)
    u_came = send_on(u_send, early, last - 1)
    d_came = send_on(d_send, late, last - 2)
    for k in reversed(range(last)):
        l_came, u_came, d_came = after((l_came, u_came, d_came))
        l_keep, l_send = add(l_keep, l_came)
        l_came = send_on(l_send, early, k)
        if k > 0:
            u_keep, u_send = add(u_keep, u_came)
            u_came = send_on(u_send, early, k - 1)
        if k > 1:
            d_keep, d_send = add(d_keep, d_came)
            d_came = send_on(d_send, late, k - 2)
        if k == last - 1:
            grad_came = core_swap(after(grad_in, l_send))
            mixed_other = tuple(core_swap(m) for m in after(mixed_own, l_send))
            l_came = after(l_came, grad_came, mixed_other)
        if k == last - 2:
            mixed, input_grad = place(tab, mixed_own, mixed_other, after(grad_in, l_send), grad_came)
            l_came = after(l_came, input_grad)

    last_grad, down_grad, up_grad, squares = squares_of(((l_keep, l_came), (d_keep, d_came), (u_keep, u_came)))
    cols = core_swap(last_grad[:, HALF_QKV + HALF_OUT :])
    squares = squares + core_swap(squares)
    for k in reversed(range(steps)):
        squares = squares + lax.ppermute(squares, "dp", [(d, d ^ (1 << k)) for d in range(n_dp)])
    moments = (
        qkv_first, qkv_second, out_first, out_second, ffn_in_first, ffn_in_second,
        ffn_out_first, ffn_out_second, norm_first, norm_second,
    )
    new = adam(
        squares, last_grad, up_grad, down_grad, cols,
        weights,
        [m.transpose(turned[n // 2]) for n, m in enumerate(moments)],
    )
    updated = [value.transpose(turned[n // 3]) for n, value in enumerate(new[:15])]
    return (
        mixed.reshape(2 * rows, D),
        input_grad.reshape(2 * rows, D),
        loss[0, 0],
        new[15][0, 0],
        *updated,
    )


def solution(mesh):
    rows = P("dp", None)
    qkv = P("dp", None, "tensor")
    turned = P("tensor", "dp")
    up = P("dp", "tensor")
    norm = P(None, "dp")
    weights = (qkv, turned, up, turned, norm)
    moments = tuple(spec for spec in weights for _ in range(2))
    updated = tuple(spec for spec in weights for _ in range(3))
    return jax.shard_map(
        body,
        mesh=mesh,
        in_specs=(rows, rows, P()) + weights + moments,
        out_specs=(rows, rows, P(), P()) + updated,
        check_vma=False,
    )
```

```python
from functools import partial

import jax
import jax.numpy as jnp
import numpy as np
from jax import lax
from jax.experimental import pallas as pl
from jax.experimental.pallas import tpu as pltpu
from jax.sharding import PartitionSpec as P

HEAD = 64
SPAN = 128
STEP = 10
D = 768
FF = 3072
NB = 16
RB = D // NB
HALF_QKV = 1152
HALF_OUT = 384
HALF_FF = 1536
ONE = HALF_QKV + HALF_OUT + 128
CONTRAST = 4.0
EPS = 1e-06
BF = jnp.bfloat16
F32 = jnp.float32
AXES = ("dp", "tensor")
SHRINK = 100

NN = (((1,), (0,)), ((), ()))
NT = (((1,), (1,)), ((), ()))
TN = (((0,), (0,)), ((), ()))


def mm(left, right, dims=NN):
    return lax.dot_general(left, right, dims, preferred_element_type=F32)


def params(vmem=56):
    vmem = vmem if vmem > 24 else min(vmem, 8)
    return pltpu.CompilerParams(vmem_limit_bytes=vmem * 2**20)


def cost(flops, bytes_accessed, trans=0):
    flops, bytes_accessed, trans = (n // SHRINK + 1 for n in (flops, bytes_accessed, trans))
    return pl.CostEstimate(flops=int(flops), bytes_accessed=int(bytes_accessed), transcendentals=int(trans))


HBM = pl.BlockSpec(memory_space=pl.ANY)


def bit_orders(n_dp):
    bits = n_dp.bit_length() - 1
    if bits == 4:
        return ((4, 8, 2, 1), (8, 4, 1, 2)), ((1, 4, 8, 2), (2, 8, 4, 1))
    up = tuple(1 << b for b in range(bits))[::-1]
    both = (up, up[: bits // 2] + up[bits // 2 :][::-1])
    return both, both


def pairs_of(n_dp, orders, step):
    out = []
    for d in range(n_dp):
        for c in range(2):
            out.append((d * 2 + c, (d ^ orders[c][step]) * 2 + c))
    return out


def rel_of(order):
    out = []
    for p in range(1 << len(order)):
        r = 0
        for k, b in enumerate(order):
            if (p >> k) & 1:
                r ^= b
        out.append(r)
    return out


AT_EARLY, AT_LATE, AT_OTHER, POS_EARLY, POS_LATE = 0, NB, 2 * NB, 3 * NB, 5 * NB
HALF_AT, CLASS_AT = 7 * NB, 7 * NB + 2


class At:
    def __init__(self, ref, first):
        self.ref, self.first = ref, first

    def __getitem__(self, n):
        return self.ref[self.first + n]


def device_tables(n_dp):
    kinds = [[rel_of(order) for order in orders] for orders in bit_orders(n_dp)]
    classes = rel_of([1 << k for k in reversed(range(n_dp.bit_length() - 1))])
    plain = list(range(NB))
    table = []
    for d in range(n_dp):
        for c in range(2):
            direct = n_dp == NB
            row = []
            for rel in kinds:
                row += [d ^ r for r in rel[c]] if direct else plain
            row += [d ^ r for r in kinds[0][1 - c]] if direct else plain
            for rel in kinds:
                for half in (c, 1 - c):
                    row += [rel[half].index(d ^ j) for j in range(NB)] if direct else plain
            me = d * 2 + c
            row += [c, 1 - c, me] + [me ^ (r << 1 | b) for b in range(2) for r in classes]
            table.append(row)
    return np.array(table, np.int32)


def core_swap(block):
    return lax.ppermute(block, "tensor", [(0, 1), (1, 0)])


VM = pl.BlockSpec(memory_space=pltpu.VMEM)
SM = pl.BlockSpec(memory_space=pltpu.SMEM)
BLK = 256


def call(kernel, out, in_specs, *args, vmem=16, flops=0, moved=0, trans=0, scratch=(), name=None):
    return pl.pallas_call(
        kernel,
        out_shape=[jax.ShapeDtypeStruct(s, t) for s, t in out],
        in_specs=in_specs,
        out_specs=[VM] * len(out),
        scratch_shapes=list(scratch),
        compiler_params=params(vmem),
        cost_estimate=cost(flops, moved, trans),
        name=name,
    )(*args)


def pack_kernel(qkv, out, up, down, norm, one_ref, two_ref, three_ref, wide, a0, a1, a2, a3, sems):
    rows = up.shape[0]
    wide[...] = jnp.zeros_like(wide)
    copies = [
        pltpu.make_async_copy(src, dst, sems.at[n])
        for n, (src, dst) in enumerate(
            ((qkv, a0), (out, a1), (down, a3), (up, a2))
        )
    ]
    for c in copies:
        c.start()
    copies[0].wait()
    for part in range(3):
        one_ref[0, :, part * HALF_OUT : (part + 1) * HALF_OUT] = a0[part].astype(BF)
    copies[1].wait()
    one_ref[0, :, HALF_QKV : HALF_QKV + HALF_OUT] = a1[...].astype(BF)
    wide[0:4, 0:rows] = norm[...]
    one_ref[0, :, HALF_QKV + HALF_OUT :] = wide[...].T[0:rows].astype(BF)
    copies[2].wait()
    three_ref[0] = a3[...].astype(BF)
    copies[3].wait()
    two_ref[0] = a2[...].astype(BF)


def pack(*shards):
    rows = shards[2].shape[0]
    return call(
        pack_kernel,
        [((1, rows, ONE), BF), ((1, rows, HALF_FF), BF), ((1, rows, HALF_FF), BF)],
        [pl.BlockSpec(memory_space=pltpu.HBM)] * 4 + [VM], *shards,
        vmem=60, moved=rows * 28000,
        scratch=[pltpu.VMEM((128, 128), F32)]
        + [pltpu.VMEM(w.shape, F32) for w in shards[:4]]
        + [pltpu.SemaphoreType.DMA((4,))],
        name="pack",
    )


def assemble_kernel(first, tab, low, high, out_ref, sems):
    copies = []
    for n, ref in enumerate((low, high)):
        for p in range(NB // 2):
            q = n * (NB // 2) + p
            copies.append(pltpu.make_async_copy(ref.at[p], out_ref.at[tab[first + q]], sems.at[q]))
    for c in copies:
        c.start()
    for c in copies:
        c.wait()


def assemble(first, tab, low, high, name):
    width = low.shape[-1]
    return call(
        partial(assemble_kernel, first),
        [((NB, RB, width), BF)],
        [SM] + [HBM] * 2,
        tab,
        low,
        high,
        vmem=8,
        moved=4 * D * width,
        scratch=[pltpu.SemaphoreType.DMA((NB,))],
        name=name,
    )[0]


def weight(w_ref, first, last):
    return w_ref[:, :, first:last].reshape(D, last - first)


def norm_fwd(hidden):
    center = hidden - jnp.mean(hidden, axis=-1, keepdims=True)
    spread = jnp.mean(center * center, axis=-1, keepdims=True)
    rstd = lax.rsqrt(spread + EPS)
    return center * rstd, rstd


def norm_bwd(grad, xh, rstd, gain):
    e = grad * gain
    m1 = jnp.mean(e, axis=-1, keepdims=True)
    m2 = jnp.mean(e * xh, axis=-1, keepdims=True)
    return rstd * (e - m1 - xh * m2)


def store_turned(ref, tab, value, col, width):
    turned = value.T
    for j in range(NB):
        block = turned[j * RB : (j + 1) * RB]
        for n in range(2):
            ref[n, tab[n * NB + j], :, pl.ds(col, width)] = block


def head_masks(rows, scale):
    lane = lax.broadcasted_iota(jnp.int32, (rows, 128), 1)
    return (
        jnp.where(lane < HEAD, scale, 0.0).astype(BF),
        jnp.where(lane < HEAD, 0.0, scale).astype(BF),
    )


def stack_heads(pair, masks):
    return jnp.concatenate([pair * masks[0], pair * masks[1]], axis=0)


def merge_heads(both):
    lane = lax.broadcasted_iota(jnp.int32, (SPAN, 128), 1)
    return jnp.where(lane < HEAD, both[:SPAN], both[SPAN:])


def turn_kernel(pos, x_ref, out_ref):
    rows = x_ref.shape[0]
    for i in range(rows // BLK):
        store_turned(out_ref, At(pos, POS_EARLY), x_ref[i * BLK : (i + 1) * BLK, :], i * BLK, BLK)


def turn(pos, x):
    rows = x.shape[0]
    return call(
        turn_kernel, [((2, NB, RB, rows), BF)], [SM, VM], pos, x, moved=rows * D * 6, name="turn"
    )[0]


def attn_rows(i, x, w_ref, masks, qkv_ref, ctx_ref, lse_ref):
    r0 = pl.multiple_of(i * BLK, BLK)
    qkv = mm(x, weight(w_ref, 0, HALF_QKV)).astype(BF)
    qkv_ref[pl.ds(r0, BLK), :] = qkv
    rows = []
    for s in range(2):
        own = qkv[s * SPAN : (s + 1) * SPAN]
        parts = []
        for j in range(3):
            q = stack_heads(own[:, j * 128 : (j + 1) * 128], masks)
            k = own[:, HALF_OUT + j * 128 : HALF_OUT + (j + 1) * 128]
            v = own[:, 2 * HALF_OUT + j * 128 : 2 * HALF_OUT + (j + 1) * 128]
            st = mm(k, q, NT)
            top = jnp.max(st, axis=0, keepdims=True)
            ex = jnp.exp(st - top)
            total = jnp.sum(ex, axis=0, keepdims=True)
            pt = (ex * (1.0 / total)).astype(BF)
            lse_ref[i * 2 + s, j : j + 1, :] = top + jnp.log(total)
            parts.append(merge_heads(mm(pt, v, TN)).astype(BF))
        rows.append(jnp.concatenate(parts, axis=1))
    ctx = jnp.concatenate(rows, axis=0)
    ctx_ref[pl.ds(r0, BLK), :] = ctx
    return ctx


def attn_one_kernel(first, tab, low, high, x_ref, qkv_ref, ctx_ref, lse_ref, w_ref, sems):
    assemble_kernel(first, tab, low, high, w_ref, sems)
    masks = head_masks(SPAN, HEAD ** (-0.5))

    def step(i, carry):
        x = x_ref[pl.ds(pl.multiple_of(i * BLK, BLK), BLK), :]
        attn_rows(i, x, w_ref, masks, qkv_ref, ctx_ref, lse_ref)
        return carry

    lax.fori_loop(0, x_ref.shape[0] // BLK, step, 0, unroll=2)


def attn_two_kernel(
    first, tab, low, high, x_ref, wo_ref, ctxo_ref,
    qkv_ref, ctx_ref, lse_ref, xh_ref, rstd_ref, p_ref, w_ref, sems,
):
    assemble_kernel(first, tab, low, high, w_ref, sems)
    cols = weight(w_ref, HALF_QKV + HALF_OUT, ONE).astype(F32)
    p_ref[...] = cols.T[:8]
    masks = head_masks(SPAN, HEAD ** (-0.5))

    def step(i, carry):
        rs = pl.ds(pl.multiple_of(i * BLK, BLK), BLK)
        x = x_ref[rs, :]
        ctx = attn_rows(i, x, w_ref, masks, qkv_ref, ctx_ref, lse_ref)
        attn = x.astype(F32) + mm(ctxo_ref[rs, :], weight(wo_ref, HALF_QKV, HALF_QKV + HALF_OUT), NT)
        attn = attn + mm(ctx, weight(w_ref, HALF_QKV, HALF_QKV + HALF_OUT), NT)
        xh, rstd = norm_fwd(attn)
        rstd = jnp.broadcast_to(rstd, (BLK, 128))
        for s in range(2):
            for q in range(4):
                r = s * SPAN + q * 32
                xh_ref[q, i * 2 + s] = xh[r : r + 32]
                rstd_ref[q, i * 2 + s] = rstd[r : r + 32]
        return carry

    lax.fori_loop(0, x_ref.shape[0] // BLK, step, 0, unroll=2)


def attn_shapes(rows):
    return [((rows, HALF_QKV), BF), ((rows, HALF_OUT), BF), ((rows // SPAN, 8, 2 * SPAN), F32)]


def attn_one(first, tab, low, high, x):
    rows = x.shape[0]
    return call(
        partial(attn_one_kernel, first), attn_shapes(rows) + [((NB, RB, ONE), BF)],
        [SM, HBM, HBM, VM], tab, low, high, x,
        scratch=[pltpu.SemaphoreType.DMA((NB,))], vmem=16, flops=rows * 4e6, moved=rows * 8000 + 2e6, trans=rows * 800, name="attn_one",
    )


def attn_two(first, tab, low, high, x, w_own, ctx_own):
    rows = x.shape[0]
    spans = rows // SPAN
    out = attn_shapes(rows) + [
        ((4, spans, 32, D), F32),
        ((4, spans, 32, 128), F32),
        ((8, D), F32),
        ((NB, RB, ONE), BF),
    ]
    return call(
        partial(attn_two_kernel, first), out, [SM, HBM, HBM, VM, VM, VM], tab, low, high, x, w_own, ctx_own,
        scratch=[pltpu.SemaphoreType.DMA((NB,))],
        vmem=16, flops=rows * 5e6, moved=rows * 12000 + 4e6, trans=rows * 800, name="attn_two",
    )


def gelu_pair(u):
    a = jnp.abs(u)
    d = 1.0 + (0.3275911 * 0.5**0.5) * a
    t = pl.reciprocal(d, approx=True)
    t = t * (2.0 - d * t)
    e = jnp.exp(-0.5 * u * u)
    poly = 0.5307027145 * t - 0.7265760135
    poly = poly * t + 0.7107068705
    poly = poly * t - 0.142248368
    poly = poly * t + 0.127414796
    tail = (poly * t) * e
    phi = jnp.where(u >= 0.0, 1.0 - tail, tail)
    return u * phi, phi + (0.3989422804014327 * u) * e


TILE = 512


def ffn_up_kernel(pos, xh_ref, p_ref, w_ref, g_ref, gp_ref, *yt_ref):
    def step(i, carry):
        rs = pl.ds(pl.multiple_of(i * BLK, BLK), BLK)
        y = xh_ref[rs, :] * p_ref[0:1, :] + p_ref[1:2, :]
        yb = y.astype(BF)
        if yt_ref:
            store_turned(yt_ref[0], At(pos, POS_EARLY), yb, pl.multiple_of(i * BLK, BLK), BLK)
        for t in range(HALF_FF // TILE):
            u = mm(yb, weight(w_ref, t * TILE, (t + 1) * TILE))
            g, gp = gelu_pair(u)
            g_ref[rs, t * TILE : (t + 1) * TILE] = g.astype(BF)
            gp_ref[rs, t * TILE : (t + 1) * TILE] = gp.astype(BF)
        return carry

    lax.fori_loop(0, xh_ref.shape[0] // BLK, step, 0, unroll=2)


def ffn_up(pos, xh, prow, w, turned, name):
    rows = xh.shape[0]
    out = [((rows, HALF_FF), BF), ((rows, HALF_FF), BF)]
    if turned:
        out.append(((2, NB, RB, rows), BF))
    return call(
        ffn_up_kernel, out, [SM, VM, VM, VM], pos, xh, prow, w,
        vmem=16, flops=rows * 2.4e6, moved=rows * 9000 + 2e6, trans=rows * 6000, name=name,
    )


def down_block(r0, xh1_ref, p_ref, acts, downs):
    rs = pl.ds(r0, BLK)
    total = xh1_ref[rs, :] * p_ref[0:1, :] + p_ref[1:2, :]
    for g_ref, w_ref in zip(acts, downs):
        total = total + mm(g_ref[rs, :], weight(w_ref, 0, HALF_FF), NT)
    return norm_fwd(total)


def first_kernel(xh1_ref, p_ref, g0, g1, d0, d1, mixed_ref, cls_ref, xh_ref, rstd_ref):
    xh, rstd = down_block(0, xh1_ref, p_ref, (g0, g1), (d0, d1))
    xh_ref[...] = xh
    rstd_ref[...] = jnp.broadcast_to(rstd, rstd_ref.shape)
    out = (xh * p_ref[2:3, :] + p_ref[3:4, :]).reshape(mixed_ref.shape)
    mixed_ref[...] = out.astype(BF)
    cls_ref[...] = out[:, 0, :]


def first_rows(xh1, prow, acts, downs):
    spans = BLK // 32
    return call(
        first_kernel,
        [((spans, 32, D), BF), ((spans, D), F32), ((BLK, D), F32), ((BLK, 128), F32)],
        [VM] * 6, xh1, prow, *acts, *downs,
        vmem=8, flops=BLK * 4.8e6, moved=BLK * 16000 + 5e6, name="first_rows",
    )


def back_block(r0, grad, xh2, rstd2, gps, xh1_ref, rstd1_ref, p_ref, ups, downs, dus):
    rs = pl.ds(r0, BLK)
    sum_g2 = jnp.sum(grad * xh2, axis=0, keepdims=True)
    sum_b2 = jnp.sum(grad, axis=0, keepdims=True)
    dh = norm_bwd(grad, xh2, rstd2, p_ref[2:3, :])
    df = dh.astype(BF)
    total = dh
    for gp_ref, up_ref, down_ref, du_ref in zip(gps, ups, downs, dus):
        for t in range(HALF_FF // TILE):
            lo, hi = t * TILE, (t + 1) * TILE
            dg = mm(df, weight(down_ref, lo, hi))
            du_ref[:, lo:hi] = (dg * gp_ref[rs, lo:hi].astype(F32)).astype(BF)
        total = total + mm(du_ref[...], weight(up_ref, 0, HALF_FF), NT)
    xh1 = xh1_ref[rs, :]
    sum_g1 = jnp.sum(total * xh1, axis=0, keepdims=True)
    sum_b1 = jnp.sum(total, axis=0, keepdims=True)
    dh1 = norm_bwd(total, xh1, rstd1_ref[rs, 0:1], p_ref[0:1, :])
    return df, dh1, (sum_g1, sum_b1, sum_g2, sum_b2)


def back_shapes():
    return [
        ((2, NB, RB, BLK), BF),
        ((BLK, HALF_FF), BF),
        ((BLK, HALF_FF), BF),
        ((BLK // 32, 32, D), F32),
        ((8, D), F32),
    ]


def rest_kernel(
    at, pos, xh1_ref, rstd1_ref, p_ref, g0, g1, gp0, gp1, cot_ref, u0, u1, d0, d1,
    dft_ref, du0_ref, du1_ref, dh1_ref, sums_ref, mixed_ref,
):
    r0, c0 = at * BLK, at * 32
    xh, rstd = down_block(r0, xh1_ref, p_ref, (g0, g1), (d0, d1))
    out = xh * p_ref[2:3, :] + p_ref[3:4, :]
    mixed_ref[...] = out.reshape(mixed_ref.shape).astype(BF)
    grad = cot_ref[:, c0 : c0 + 32, :].astype(F32).reshape(BLK, D)
    df, dh1, sums = back_block(
        r0, grad, xh, rstd, (gp0, gp1), xh1_ref, rstd1_ref, p_ref, (u0, u1), (d0, d1), (du0_ref, du1_ref)
    )
    store_turned(dft_ref, At(pos, POS_LATE), df, 0, BLK)
    dh1_ref[...] = dh1.reshape(dh1_ref.shape)
    for n in range(4):
        sums_ref[n : n + 1, :] = sums[n]


def rest_rows(at, pos, xh1, rstd1, prow, acts, gps, cot, ups, downs):
    return call(
        partial(rest_kernel, at),
        back_shapes() + [((BLK // 32, 32, D), BF)],
        [SM] + [VM] * 12, pos, xh1, rstd1, prow, *acts, *gps, cot, *ups, *downs,
        vmem=16, flops=BLK * 14.5e6, moved=BLK * 40000 + 1e7, name=f"rest_rows_{at}",
    )


def class_kernel(
    pos, cls_ref, cot_ref, xh2_ref, rstd2_ref, xh1_ref, rstd1_ref, p_ref, gp0, gp1, u0, u1, d0, d1,
    dft_ref, du0_ref, du1_ref, dh1_ref, sums_ref,
):
    spans = cls_ref.shape[0]
    grad = cot_ref[:, 0:32, :].astype(F32)
    first = lax.broadcasted_iota(jnp.int32, grad.shape, 1) == 0
    grad = grad + jnp.where(first, cls_ref[...].reshape(spans, 1, D), 0.0)
    grad = grad.reshape(BLK, D)
    df, dh1, sums = back_block(
        0, grad, xh2_ref[...], rstd2_ref[:, 0:1], (gp0, gp1), xh1_ref, rstd1_ref, p_ref,
        (u0, u1), (d0, d1), (du0_ref, du1_ref),
    )
    store_turned(dft_ref, At(pos, POS_LATE), df, 0, BLK)
    dh1_ref[...] = dh1.reshape(dh1_ref.shape)
    for n in range(4):
        sums_ref[n : n + 1, :] = sums[n]


def class_rows(pos, grad_cls, cot, xh2, rstd2, xh1, rstd1, prow, gps, ups, downs):
    return call(
        class_kernel,
        back_shapes(),
        [SM] + [VM] * 13, pos, grad_cls, cot, xh2, rstd2, xh1, rstd1, prow, *gps, *ups, *downs,
        vmem=16, flops=BLK * 9.7e6, moved=BLK * 30000 + 1e7, name="class_rows",
    )


def contrast_kernel(where, doc_ref, cls_ref, loss_ref, grad_ref, rows, own_doc):
    spans = doc_ref.shape[1]
    doc_row = doc_ref[...].astype(F32)
    doc_col = jnp.broadcast_to(doc_row, (128, spans)).T[:, 0:1]
    blocks, per = cls_ref.shape[0], cls_ref.shape[1]
    where = At(where, CLASS_AT)
    me = where[0]
    for n in range(blocks):
        rows[where[1 + n]] = cls_ref[n].astype(F32)
    a = rows[...].reshape(spans, D).astype(BF)
    own = rows[me].astype(BF)
    scale = D ** (-0.5)
    col = lax.broadcasted_iota(jnp.int32, (spans, spans), 1)
    row = lax.broadcasted_iota(jnp.int32, (spans, spans), 0)
    logits = mm(a, a, NT) * scale
    partner = (doc_col == doc_row) & (row != col)
    masked = jnp.where(row == col, -1000000000.0, logits)
    top = jnp.max(masked, axis=0, keepdims=True)
    lse = jnp.log(jnp.sum(jnp.exp(masked - top), axis=0, keepdims=True)) + top
    positive = jnp.sum(jnp.where(partner, logits, 0.0), axis=0, keepdims=True)
    flagged = jnp.max(jnp.where(partner, 1.0, 0.0), axis=0, keepdims=True)
    count = jnp.sum(flagged, axis=1, keepdims=True)
    loss = jnp.sum(flagged * (lse - positive), axis=1, keepdims=True) / count
    loss_ref[...] = jnp.broadcast_to(loss, loss_ref.shape)

    weight_row = flagged * (CONTRAST * spans) / count
    own_doc[...] = doc_col.reshape(blocks, per, 1)
    docs = own_doc[me]
    col = lax.broadcasted_iota(jnp.int32, (per, spans), 1)
    row = lax.broadcasted_iota(jnp.int32, (per, spans), 0) + me * per
    logits = mm(own, a, NT) * scale
    same = jnp.where((docs == doc_row) & (row != col), 1.0, 0.0)
    masked = jnp.where(row == col, -1000000000.0, logits)
    top = jnp.max(masked, axis=1, keepdims=True)
    ex = jnp.exp(masked - top)
    soft = ex / jnp.sum(ex, axis=1, keepdims=True)
    own_weight = jnp.max(same, axis=1, keepdims=True) * (CONTRAST * spans) / count
    sym = own_weight * (soft - same) + weight_row * (jnp.exp(masked - lse) - same)
    high = sym.astype(BF)
    low = (sym - high.astype(F32)).astype(BF)
    grad_ref[...] = (mm(high, a) + mm(low, a)) * scale


def contrast(where, doc_row, cls_all):
    blocks, per, _ = cls_all.shape
    spans = blocks * per
    return call(
        contrast_kernel,
        [((1, 128), F32), ((per, D), F32)],
        [SM, VM, VM],
        where, doc_row, cls_all,
        vmem=8 if spans <= 256 else 40, flops=2 * spans * spans * D, moved=spans * D * 2,
        scratch=[pltpu.VMEM((blocks, per, D), F32), pltpu.VMEM((blocks, per, 1), F32)],
        name="contrast",
    )


def turned_of(refs, n):
    return jnp.concatenate([ref[n].reshape(D, ref.shape[3]) for ref in refs], axis=1)


def grad_other_kernel(count, *refs):
    xts, ys, out_ref = refs[:count], refs[count:-1], refs[-1]
    xt = turned_of(xts, 1)
    for t in range(HALF_FF // TILE):
        lo, hi = t * TILE, (t + 1) * TILE
        grad = mm(xt, jnp.concatenate([y[:, lo:hi] for y in ys], axis=0))
        out_ref[:, :, lo:hi] = grad.astype(BF).reshape(NB, RB, TILE)


def grad_other(xts, ys, name):
    rows = sum(y.shape[0] for y in ys)
    return call(
        partial(grad_other_kernel, len(xts)),
        [((NB, RB, HALF_FF), BF)],
        [VM] * (len(xts) + len(ys)), *xts, *ys,
        vmem=12, flops=2 * rows * D * HALF_FF, moved=rows * 8000 + 2.4e6, name=name,
    )[0]


def grad_own_kernel(count, came_ref, *refs):
    xts, ys, keep_ref, send_ref = refs[:count], refs[count:-2], refs[-2], refs[-1]
    nh = NB // 2
    xt = turned_of(xts, 0)
    for t in range(HALF_FF // TILE):
        lo, hi = t * TILE, (t + 1) * TILE
        grad = mm(xt, jnp.concatenate([y[:, lo:hi] for y in ys], axis=0))
        grad = (grad.reshape(NB, RB, TILE) + came_ref[:, :, lo:hi].astype(F32)).astype(BF)
        keep_ref[:, :, lo:hi] = grad[:nh]
        send_ref[:, :, lo:hi] = grad[nh:]


def grad_own(xts, ys, came, name):
    rows = sum(y.shape[0] for y in ys)
    return call(
        partial(grad_own_kernel, len(xts)),
        [((NB // 2, RB, HALF_FF), BF)] * 2,
        [VM] * (1 + len(xts) + len(ys)), came, *xts, *ys,
        vmem=12, flops=2 * rows * D * HALF_FF, moved=rows * 8000 + 4.8e6, name=name,
    )


def natural(refs, i):
    return jnp.concatenate([ref[i * 2 + s] for s in range(2) for ref in refs], axis=0)


def attn_back_kernel(pos, r0_ref, r1_ref, r2_ref, r3_ref, qkv_ref, lse_ref, w_ref, dqkv_ref, *dat_ref):
    masks = head_masks(SPAN, HEAD ** (-0.5))
    plain = head_masks(SPAN, 1.0)
    spans = r0_ref.shape[0]

    def step(i, carry):
        r0 = pl.multiple_of(i * BLK, BLK)
        da = natural((r0_ref, r1_ref, r2_ref, r3_ref), i).astype(BF)
        if dat_ref:
            store_turned(dat_ref[0], At(pos, POS_EARLY), da, r0, BLK)
        dctx = mm(da, weight(w_ref, HALF_QKV, HALF_QKV + HALF_OUT)).astype(BF)
        for s in range(2):
            rs = pl.ds(pl.multiple_of(r0 + s * SPAN, SPAN), SPAN)
            for j in range(3):
                a, b = j * 128, (j + 1) * 128
                q = stack_heads(qkv_ref[rs, a:b], masks)
                k = qkv_ref[rs, HALF_OUT + a : HALF_OUT + b]
                v = qkv_ref[rs, 2 * HALF_OUT + a : 2 * HALF_OUT + b]
                dc = stack_heads(dctx[s * SPAN : (s + 1) * SPAN, a:b], plain)
                st = mm(k, q, NT)
                pt = jnp.exp(st - lse_ref[i * 2 + s, j : j + 1, :])
                dpt = mm(v, dc, NT)
                dst = pt * (dpt - jnp.sum(pt * dpt, axis=0, keepdims=True))
                dst = dst.astype(BF)
                dv = mm(pt.astype(BF), dc)
                dk = mm(dst, q)
                dq = merge_heads(mm(dst, k, TN)) * HEAD ** (-0.5)
                dqkv_ref[rs, a:b] = dq.astype(BF)
                dqkv_ref[rs, HALF_OUT + a : HALF_OUT + b] = dk.astype(BF)
                dqkv_ref[rs, 2 * HALF_OUT + a : 2 * HALF_OUT + b] = dv.astype(BF)
        return carry

    lax.fori_loop(0, spans // 2, step, 0, unroll=2)


def attn_back(pos, dh1, qkv, lse, w, turned, name):
    rows = qkv.shape[0]
    out = [((rows, HALF_QKV), BF)]
    if turned:
        out.append(((2, NB, RB, rows), BF))
    return call(
        attn_back_kernel, out,
        [SM] + [VM] * 7, pos, *dh1, qkv, lse, w,
        vmem=16, flops=rows * 6e6, moved=rows * 10000 + 3e6, trans=rows * 800, name=name,
    )


def last_value(order, xt_ref, dqkv_ref, dat_ref, ctx_ref, t):
    rows = xt_ref.shape[3]
    if t < 3:
        return mm(xt_ref[order].reshape(D, rows), dqkv_ref[:, t * HALF_OUT : (t + 1) * HALF_OUT])
    return mm(dat_ref[order].reshape(D, rows), ctx_ref[...])


def norm_columns(sums):
    total = sums[0][0:4, :]
    for ref in sums[1:]:
        total = total + ref[0:4, :]
    return jnp.concatenate([total, jnp.zeros((124, D), F32)], axis=0).T


def last_other_kernel(pos, xt_ref, dqkv_ref, dat_ref, ctx_ref, s0, s1, s2, s3, out_ref):
    for t in range(4):
        grad = last_value(1, xt_ref, dqkv_ref, dat_ref, ctx_ref, t)
        lo = t * HALF_OUT
        out_ref[:, :, lo : lo + HALF_OUT] = grad.astype(BF).reshape(NB, RB, HALF_OUT)
    norm = norm_columns((s0, s1, s2, s3)).astype(BF)
    for j in range(NB):
        out_ref[pos[POS_EARLY + NB + j], :, HALF_QKV + HALF_OUT :] = norm[j * RB : (j + 1) * RB]


def last_other(pos, xt, dqkv, dat, ctx, sums):
    rows = xt.shape[3]
    return call(
        last_other_kernel,
        [((NB, RB, ONE), BF)],
        [SM] + [VM] * 8, pos, xt, dqkv, dat, ctx, *sums,
        vmem=12, flops=2 * rows * D * HALF_FF, moved=rows * 8000 + 2.4e6, name="last_other",
    )[0]


def last_own_kernel(
    pos, xt_ref, dqkv_ref, dat_ref, ctx_ref, s0, s1, s2, s3, came_ref, keep_ref, send_ref, cols
):
    nh = NB // 2
    norm = norm_columns((s0, s1, s2, s3))
    for j in range(NB):
        cols[pos[POS_EARLY + j]] = norm[j * RB : (j + 1) * RB]
    for t in range(5):
        lo = t * HALF_OUT
        hi = min(lo + HALF_OUT, ONE)
        if t < 4:
            grad = last_value(0, xt_ref, dqkv_ref, dat_ref, ctx_ref, t).reshape(NB, RB, HALF_OUT)
        else:
            grad = cols[...]
        grad = (grad + came_ref[:, :, lo:hi].astype(F32)).astype(BF)
        keep_ref[:, :, lo:hi] = grad[:nh]
        send_ref[:, :, lo:hi] = grad[nh:]


def last_own(pos, xt, dqkv, dat, ctx, sums, came):
    rows = xt.shape[3]
    return call(
        last_own_kernel,
        [((NB // 2, RB, ONE), BF)] * 2,
        [SM] + [VM] * 9, pos, xt, dqkv, dat, ctx, *sums, came,
        vmem=12, flops=2 * rows * D * HALF_FF, moved=rows * 8000 + 4.8e6,
        scratch=[pltpu.VMEM((NB, RB, 128), F32)], name="last_own",
    )


def input_grad_kernel(r0_ref, r1_ref, r2_ref, r3_ref, own_ref, other_ref, w0_ref, w1_ref, out_ref):
    spans = r0_ref.shape[0]

    def step(i, carry):
        rs = pl.ds(pl.multiple_of(i * BLK, BLK), BLK)
        total = natural((r0_ref, r1_ref, r2_ref, r3_ref), i)
        total = total + mm(own_ref[rs, :], weight(w0_ref, 0, HALF_QKV), NT)
        total = total + mm(other_ref[rs, :], weight(w1_ref, 0, HALF_QKV), NT)
        out_ref[rs, :] = total
        return carry

    lax.fori_loop(0, spans // 2, step, 0, unroll=2)


def input_grads(dh1, own, other, w_own, w_other):
    rows = own.shape[0]
    return call(
        input_grad_kernel,
        [((rows, D), F32)],
        [VM] * 8, *dh1, own, other, w_own, w_other,
        vmem=12, flops=rows * 3.6e6, moved=rows * 12000 + 5e6, name="input_grads",
    )[0]


def place_kernel(half, *refs):
    own, other, g_own, g_other = refs[0:4], refs[4:8], refs[8], refs[9]
    mixed_ref, grad_ref, sems = refs[10:]
    spans = g_own.shape[0]
    copies = []
    for n, (pieces, g) in enumerate(((own, g_own), (other, g_other))):
        at = pl.ds(half[HALF_AT + n] * spans, spans)
        for q in range(4):
            to = mixed_ref.at[at, 32 * q : 32 * q + 32, :]
            copies.append(pltpu.make_async_copy(pieces[q], to, sems.at[5 * n + q]))
        copies.append(pltpu.make_async_copy(g, grad_ref.at[at], sems.at[5 * n + 4]))
    for c in copies:
        c.start()
    for c in copies:
        c.wait()


def place(half, own, other, g_own, g_other):
    spans = own[0].shape[0]
    g_own, g_other = (g.reshape(spans, SPAN, D) for g in (g_own, g_other))
    return pl.pallas_call(
        place_kernel,
        out_shape=[
            jax.ShapeDtypeStruct((2 * spans, SPAN, D), BF),
            jax.ShapeDtypeStruct((2 * spans, SPAN, D), F32),
        ],
        in_specs=[SM] + [VM] * 10,
        out_specs=[HBM] * 2,
        scratch_shapes=[pltpu.SemaphoreType.DMA((10,))],
        compiler_params=params(16),
        cost_estimate=cost(0, spans * SPAN * D * 24),
        name="place",
    )(half, *own, *other, g_own, g_other)


def squares_kernel(k0, c0, k1, c1, k2, c2, g0, g1, g2, sq_ref):
    main = HALF_QKV + HALF_OUT
    total = jnp.zeros((1, 1), F32)
    for keep, came, out in ((k0, c0, g0), (k1, c1, g1), (k2, c2, g2)):
        grad = keep[0].astype(F32) + came[0].astype(F32)
        out[...] = grad
        sq = jnp.sum(grad[:, :main] * grad[:, :main], axis=1, keepdims=True)
        if grad.shape[1] > main:
            cols = grad[:, main:]
            sq = sq + 0.5 * jnp.sum(cols * cols, axis=1, keepdims=True)
        total = total + jnp.sum(sq, axis=0, keepdims=True)
    sq_ref[...] = jnp.broadcast_to(total, sq_ref.shape)


def squares_of(pairs):
    shard = pairs[0][0].shape[1]
    out = [((shard, k.shape[2]), F32) for k, _ in pairs] + [((8, 128), F32)]
    flat = [a for pair in pairs for a in pair]
    return call(squares_kernel, out, [VM] * 6, *flat, vmem=8, moved=shard * 40000, name="squares")


def adam_parts(weight, gradient, moment_one, moment_two, step_rate, decay_rate):
    first_new = 0.9 * moment_one + 0.1 * gradient
    second_new = 0.999 * moment_two + 0.001 * gradient * gradient
    corr_first = first_new * (1.0 / (1.0 - 0.9**STEP))
    corr_second = second_new * (1.0 / (1.0 - 0.999**STEP))
    weight_new = weight - step_rate * (
        corr_first / (jnp.sqrt(corr_second) + 1e-08) + decay_rate * weight
    )
    return first_new, second_new, weight_new


def adam_kernel(sq_ref, last_ref, up_ref, down_ref, cols_ref, *refs):
    ins, outs, wide = refs[:15], refs[15:-1], refs[-1]
    norm = jnp.sqrt(sq_ref[0:1, 0:1])
    outs[15][...] = jnp.broadcast_to(norm, outs[15].shape)
    scale = 1.0 / jnp.maximum(norm, 1.0)

    def update(n, at, grad, rate, decay):
        new = adam_parts(ins[n][at], grad * scale, ins[5 + 2 * n][at], ins[6 + 2 * n][at], rate, decay)
        for m in range(3):
            outs[3 * n + m][at] = new[m]

    for part in range(3):
        update(0, part, last_ref[:, part * HALF_OUT : (part + 1) * HALF_OUT], 0.02, 0.01)
    update(1, Ellipsis, last_ref[:, HALF_QKV : HALF_QKV + HALF_OUT], 0.02, 0.01)
    update(2, Ellipsis, up_ref[...], 0.02, 0.01)
    update(3, Ellipsis, down_ref[...], 0.02, 0.01)
    shard = last_ref.shape[0]
    wide[...] = jnp.zeros_like(wide)
    wide[0:shard, :] = 0.5 * (last_ref[:, HALF_QKV + HALF_OUT :] + cols_ref[...])
    update(4, Ellipsis, wide[...].T[0:4, 0:shard], 0.5, 0.0)


def adam(squares, last, up, down, cols, weights, moments):
    shapes = [w.shape for w in weights]
    out = [(s, F32) for s in shapes for _ in range(3)] + [((8, 128), F32)]
    args = (squares, last, up, down, cols, *weights, *moments)
    return call(
        adam_kernel, out, [VM] * len(args), *args, vmem=16, moved=7 * 4 * last.shape[0] * 4608,
        scratch=[pltpu.VMEM((128, 128), F32)], name="adam",
    )


def after(value, *others):
    return lax.optimization_barrier((value, others))[0]


def body(
    tokens,
    cotangent,
    span_doc,
    qkv_weight,
    out_weight,
    ffn_in_weight,
    ffn_out_weight,
    norm_params,
    qkv_first,
    qkv_second,
    out_first,
    out_second,
    ffn_in_first,
    ffn_in_second,
    ffn_out_first,
    ffn_out_second,
    norm_first,
    norm_second,
):
    n_dp = lax.axis_size("dp")
    dp = lax.axis_index("dp")
    core = lax.axis_index("tensor")
    shard = D // n_dp
    rows = tokens.shape[0] // 2
    spans = rows // SPAN
    direct = n_dp == NB
    early, late = bit_orders(n_dp)
    steps = len(early[0])
    last = steps - 1

    tab = lax.dynamic_index_in_dim(device_tables(n_dp), dp * 2 + core, 0, keepdims=False)
    x = lax.dynamic_slice_in_dim(tokens, core * rows, rows, 0)
    cot = lax.dynamic_slice_in_dim(cotangent, core * rows, rows, 0).reshape(spans, SPAN, D)

    def places(orders, other=0):
        return dp ^ jnp.array([rel_of(order) for order in orders], jnp.int32)[core ^ other]

    def send_on(block, orders, k):
        return lax.ppermute(block, AXES, pairs_of(n_dp, orders, k))

    def join(held, came):
        return jnp.concatenate([held, came], axis=0)

    def pieces(at, low, high):
        if direct:
            return at, tab, low, high
        which = {AT_EARLY: places(early), AT_LATE: places(late), AT_OTHER: places(early, 1)}[at]
        full = join(low, high)[jnp.argsort(which)].reshape(NB, RB, -1)
        return at, tab, full[: NB // 2], full[NB // 2 :]

    def halves(orders, keep, send):
        if direct:
            return keep, send
        full = join(keep, send).reshape(n_dp, shard, -1)[places(orders)]
        return full[: n_dp // 2], full[n_dp // 2 :]

    def add(keep, came):
        total = keep.astype(F32) + came.astype(F32)
        size = total.shape[0] // 2
        return total[:size].astype(BF), total[size:].astype(BF)

    turned = ((1, 0, 2), (1, 0), (0, 1), (1, 0), (0, 1))
    weights = (qkv_weight, out_weight, ffn_in_weight, ffn_out_weight, norm_params)
    weights = tuple(w.transpose(t) for w, t in zip(weights, turned))
    one, up, down = pack(*weights)
    one_came = send_on(one, early, 0)
    up_came = send_on(up, late, 0)
    one, tab, x, cot = after((join(one, one_came), tab, x, cot), up_came)
    for k in range(1, last):
        one_came = send_on(one, early, k)
        if k == 1:
            tokt = turn(tab, x)
            one_came = after(one_came, tokt)
        else:
            up = after(join(up, up_came), one)
            up_came = send_on(up, late, k - 1)
        one = join(one, one_came)
        if k > 1:
            one = after(one, up_came)
    one_came = send_on(one, early, last)
    for k in range(max(last - 1, 1), last):
        up = join(up, up_came)
        up_came = send_on(up, late, k)
    down_came = send_on(after(down, one), early, 0)
    one, one_came = after((one, one_came), up_came, down_came)
    up = after(join(up, up_came), one_came)
    up_came = send_on(up, late, last)
    down = after(join(down, down_came), one_came)
    down_came = send_on(down, early, 1)

    one_other = (core_swap(one), core_swap(one_came))
    qkv0, ctx0, lse0, w10 = attn_one(*pieces(AT_EARLY, one, one_came), x)
    ctx0 = after(ctx0, down_came)
    for k in range(2, last):
        down = join(down, after(down_came, ctx0))
        down_came = send_on(down, early, k)
    qkv1, ctx1, lse1, xh1, rstd1, prow, w11 = attn_two(*pieces(AT_OTHER, *one_other), x, w10, ctx0)
    w1 = (w10, w11)
    xh1 = xh1.reshape(rows, D)
    rstd1 = rstd1.reshape(rows, 128)
    up_came, down_came = after((up_came, down_came), xh1)
    wu = assemble(*pieces(AT_LATE, up, up_came), "up_own")
    wu = (wu, core_swap(wu))
    down = join(down, down_came)
    down_came = send_on(down, early, last)
    act0, gp0, yt = ffn_up(tab, after(xh1, down), prow, wu[0], True, "ffn_up_own")
    wd = assemble(*pieces(AT_EARLY, down, after(down_came, act0)), "down_own")
    wd = (wd, core_swap(wd))
    act1, gp1 = ffn_up(tab, after(xh1, wd[0]), prow, wu[1], False, "ffn_up_other")
    acts, gps = (act0, act1), (gp0, gp1)
    mixed0, cls_own, xh2, rstd2 = first_rows(xh1, prow, acts, wd)

    held = cls_own.astype(BF)[None]
    back = []
    for k in reversed(range(steps)):
        came = lax.ppermute(held, "dp", [(d, d ^ (1 << k)) for d in range(n_dp)])
        if len(back) < 3:
            at = len(back) + 1
            back.append(rest_rows(at, tab, after(xh1, held), rstd1, prow, acts, gps, cot, wu, wd))
            came = after(came, back[-1][4])
        held = join(held, came)
    held = join(held, core_swap(held))
    loss, grad_cls = contrast(tab, span_doc.reshape(1, -1), held)
    back.insert(0, (*class_rows(tab, grad_cls, cot, xh2, rstd2, xh1, rstd1, prow, gps, wu, wd), mixed0))
    dft, du0, du1, dh1, sums, mixed_own = zip(*back)

    d_other = grad_other(dft, (act1,), "grad_down_other")
    d_came = core_swap(d_other)
    u_other = grad_other((after(yt, d_other),), du1, "grad_up_other")
    u_came = core_swap(u_other)
    d_keep, d_send = halves(
        late, *grad_own((after(dft[0], u_other),) + dft[1:], (act0,), d_came, "grad_down_own")
    )
    d_came = send_on(d_send, late, last)
    u_keep, u_send = halves(early, *grad_own((after(yt, d_keep),), du0, u_came, "grad_up_own"))
    dh1 = (after(dh1[0], u_keep),) + dh1[1:]
    dqkv1, dat = attn_back(tab, dh1, qkv1, lse1, w1[1], True, "attn_back_other")
    l_other = last_other(tab, tokt, dqkv1, dat, ctx1, sums)

    d_came, l_other = after((d_came, l_other))
    d_keep, d_send = add(d_keep, d_came)
    u_came = send_on(after(u_send, l_other), early, last)
    d_came = send_on(d_send, late, last - 1)
    l_came = core_swap(l_other)
    (dqkv0,) = attn_back(
        tab, (after(dh1[0], l_other),) + dh1[1:], qkv0, lse0, w1[0], False, "attn_back_own"
    )
    l_keep, l_send = halves(early, *last_own(tab, tokt, dqkv0, dat, ctx0, sums, l_came))
    l_came = send_on(l_send, early, last)
    grad_in = input_grads((after(dh1[0], l_send),) + dh1[1:], dqkv0, dqkv1, w1[0], w1[1])
    u_came, d_came = after((u_came, d_came), l_send)
    u_keep, u_send = add(u_keep, u_came)
    d_keep, d_send = add(d_keep, d_came)
    u_came = send_on(u_send, early, last - 1)
    d_came = send_on(d_send, late, last - 2)
    for k in reversed(range(last)):
        l_came, u_came, d_came = after((l_came, u_came, d_came))
        l_keep, l_send = add(l_keep, l_came)
        l_came = send_on(l_send, early, k)
        if k > 0:
            u_keep, u_send = add(u_keep, u_came)
            u_came = send_on(u_send, early, k - 1)
        if k > 1:
            d_keep, d_send = add(d_keep, d_came)
            d_came = send_on(d_send, late, k - 2)
        if k == last - 1:
            grad_came = core_swap(after(grad_in, l_send))
            mixed_other = tuple(core_swap(m) for m in after(mixed_own, l_send))
            l_came = after(l_came, grad_came, mixed_other)
        if k == last - 2:
            mixed, input_grad = place(tab, mixed_own, mixed_other, after(grad_in, l_send), grad_came)
            l_came = after(l_came, input_grad)

    last_grad, down_grad, up_grad, squares = squares_of(((l_keep, l_came), (d_keep, d_came), (u_keep, u_came)))
    cols = core_swap(last_grad[:, HALF_QKV + HALF_OUT :])
    squares = squares + core_swap(squares)
    bits = [1 << k for k in reversed(range(steps))]
    for one_bit, two_bit in zip(bits[::2], bits[1::2]):
        near, far, both = (
            lax.ppermute(squares, "dp", [(d, d ^ b) for d in range(n_dp)])
            for b in (one_bit, two_bit, one_bit ^ two_bit)
        )
        squares = (squares + near) + (far + both)
    moments = (
        qkv_first, qkv_second, out_first, out_second, ffn_in_first, ffn_in_second,
        ffn_out_first, ffn_out_second, norm_first, norm_second,
    )
    new = adam(
        squares, last_grad, up_grad, down_grad, cols,
        weights,
        [m.transpose(turned[n // 2]) for n, m in enumerate(moments)],
    )
    updated = [value.transpose(turned[n // 3]) for n, value in enumerate(new[:15])]
    return (
        mixed.reshape(2 * rows, D),
        input_grad.reshape(2 * rows, D),
        loss[0, 0],
        new[15][0, 0],
        *updated,
    )


def solution(mesh):
    rows = P("dp", None)
    qkv = P("dp", None, "tensor")
    turned = P("tensor", "dp")
    up = P("dp", "tensor")
    norm = P(None, "dp")
    weights = (qkv, turned, up, turned, norm)
    moments = tuple(spec for spec in weights for _ in range(2))
    updated = tuple(spec for spec in weights for _ in range(3))
    return jax.shard_map(
        body,
        mesh=mesh,
        in_specs=(rows, rows, P()) + weights + moments,
        out_specs=(rows, rows, P(), P()) + updated,
        check_vma=False,
    )
```

```python
from functools import partial

import jax
import jax.numpy as jnp
import numpy as np
from jax import lax
from jax.experimental import pallas as pl
from jax.experimental.pallas import tpu as pltpu
from jax.sharding import PartitionSpec as P

HEAD = 64
SPAN = 128
STEP = 10
D = 768
FF = 3072
NB = 16
RB = D // NB
HALF_QKV = 1152
HALF_OUT = 384
HALF_FF = 1536
ONE = HALF_QKV + HALF_OUT + 128
CONTRAST = 4.0
EPS = 1e-06
BF = jnp.bfloat16
F32 = jnp.float32
AXES = ("dp", "tensor")
SHRINK = 100

NN = (((1,), (0,)), ((), ()))
NT = (((1,), (1,)), ((), ()))
TN = (((0,), (0,)), ((), ()))


def mm(left, right, dims=NN):
    return lax.dot_general(left, right, dims, preferred_element_type=F32)


def params(vmem=56):
    vmem = vmem if vmem > 24 else min(vmem, 8)
    return pltpu.CompilerParams(vmem_limit_bytes=vmem * 2**20)


def cost(flops, bytes_accessed, trans=0):
    flops, bytes_accessed, trans = (n // SHRINK + 1 for n in (flops, bytes_accessed, trans))
    return pl.CostEstimate(flops=int(flops), bytes_accessed=int(bytes_accessed), transcendentals=int(trans))


HBM = pl.BlockSpec(memory_space=pl.ANY)


def bit_orders(n_dp):
    bits = n_dp.bit_length() - 1
    if bits == 4:
        return ((4, 8, 2, 1), (8, 4, 1, 2)), ((1, 4, 8, 2), (2, 8, 4, 1))
    up = tuple(1 << b for b in range(bits))[::-1]
    both = (up, up[: bits // 2] + up[bits // 2 :][::-1])
    return both, both


def pairs_of(n_dp, orders, step):
    out = []
    for d in range(n_dp):
        for c in range(2):
            out.append((d * 2 + c, (d ^ orders[c][step]) * 2 + c))
    return out


def rel_of(order):
    out = []
    for p in range(1 << len(order)):
        r = 0
        for k, b in enumerate(order):
            if (p >> k) & 1:
                r ^= b
        out.append(r)
    return out


AT_EARLY, AT_LATE, AT_OTHER, POS_EARLY, POS_LATE = 0, NB, 2 * NB, 3 * NB, 5 * NB
HALF_AT, CLASS_AT = 7 * NB, 7 * NB + 2


class At:
    def __init__(self, ref, first):
        self.ref, self.first = ref, first

    def __getitem__(self, n):
        return self.ref[self.first + n]


def device_tables(n_dp):
    kinds = [[rel_of(order) for order in orders] for orders in bit_orders(n_dp)]
    classes = rel_of([1 << k for k in reversed(range(n_dp.bit_length() - 1))])
    plain = list(range(NB))
    table = []
    for d in range(n_dp):
        for c in range(2):
            direct = n_dp == NB
            row = []
            for rel in kinds:
                row += [d ^ r for r in rel[c]] if direct else plain
            row += [d ^ r for r in kinds[0][1 - c]] if direct else plain
            for rel in kinds:
                for half in (c, 1 - c):
                    row += [rel[half].index(d ^ j) for j in range(NB)] if direct else plain
            me = d * 2 + c
            row += [c, 1 - c, me] + [me ^ (r << 1 | b) for b in range(2) for r in classes]
            table.append(row)
    return np.array(table, np.int32)


def core_swap(block):
    return lax.ppermute(block, "tensor", [(0, 1), (1, 0)])


VM = pl.BlockSpec(memory_space=pltpu.VMEM)
SM = pl.BlockSpec(memory_space=pltpu.SMEM)
BLK = 256


def call(kernel, out, in_specs, *args, vmem=16, flops=0, moved=0, trans=0, scratch=(), name=None):
    return pl.pallas_call(
        kernel,
        out_shape=[jax.ShapeDtypeStruct(s, t) for s, t in out],
        in_specs=in_specs,
        out_specs=[VM] * len(out),
        scratch_shapes=list(scratch),
        compiler_params=params(vmem),
        cost_estimate=cost(flops, moved, trans),
        name=name,
    )(*args)


def pack_kernel(qkv, out, up, down, norm, one_ref, two_ref, three_ref, wide, a0, a1, a2, a3, sems):
    rows = up.shape[0]
    wide[...] = jnp.zeros_like(wide)
    copies = [
        pltpu.make_async_copy(src, dst, sems.at[n])
        for n, (src, dst) in enumerate(
            ((qkv, a0), (out, a1), (down, a3), (up, a2))
        )
    ]
    for c in copies:
        c.start()
    copies[0].wait()
    for part in range(3):
        one_ref[0, :, part * HALF_OUT : (part + 1) * HALF_OUT] = a0[part].astype(BF)
    copies[1].wait()
    one_ref[0, :, HALF_QKV : HALF_QKV + HALF_OUT] = a1[...].astype(BF)
    wide[0:4, 0:rows] = norm[...]
    one_ref[0, :, HALF_QKV + HALF_OUT :] = wide[...].T[0:rows].astype(BF)
    copies[2].wait()
    three_ref[0] = a3[...].astype(BF)
    copies[3].wait()
    two_ref[0] = a2[...].astype(BF)


def pack(*shards):
    rows = shards[2].shape[0]
    return call(
        pack_kernel,
        [((1, rows, ONE), BF), ((1, rows, HALF_FF), BF), ((1, rows, HALF_FF), BF)],
        [pl.BlockSpec(memory_space=pltpu.HBM)] * 4 + [VM], *shards,
        vmem=60, moved=rows * 28000,
        scratch=[pltpu.VMEM((128, 128), F32)]
        + [pltpu.VMEM(w.shape, F32) for w in shards[:4]]
        + [pltpu.SemaphoreType.DMA((4,))],
        name="pack",
    )


def assemble_kernel(first, tab, low, high, out_ref):
    for n, ref in enumerate((low, high)):
        for p in range(NB // 2):
            out_ref[tab[first + n * (NB // 2) + p]] = ref[p]


def assemble(first, tab, low, high, name):
    width = low.shape[-1]
    return call(
        partial(assemble_kernel, first),
        [((NB, RB, width), BF)],
        [SM, VM, VM], tab, low, high,
        moved=4 * D * width, name=name,
    )[0]


def weight(w_ref, first, last):
    return w_ref[:, :, first:last].reshape(D, last - first)


def norm_fwd(hidden):
    center = hidden - jnp.mean(hidden, axis=-1, keepdims=True)
    spread = jnp.mean(center * center, axis=-1, keepdims=True)
    rstd = lax.rsqrt(spread + EPS)
    return center * rstd, rstd


def norm_bwd(grad, xh, rstd, gain):
    e = grad * gain
    m1 = jnp.mean(e, axis=-1, keepdims=True)
    m2 = jnp.mean(e * xh, axis=-1, keepdims=True)
    return rstd * (e - m1 - xh * m2)


def store_turned(ref, tab, value, col, width):
    turned = value.T
    for j in range(NB):
        block = turned[j * RB : (j + 1) * RB]
        for n in range(2):
            ref[n, tab[n * NB + j], :, pl.ds(col, width)] = block


def head_masks(rows, scale):
    lane = lax.broadcasted_iota(jnp.int32, (rows, 128), 1)
    return (
        jnp.where(lane < HEAD, scale, 0.0).astype(BF),
        jnp.where(lane < HEAD, 0.0, scale).astype(BF),
    )


def stack_heads(pair, masks):
    return jnp.concatenate([pair * masks[0], pair * masks[1]], axis=0)


def merge_heads(both):
    lane = lax.broadcasted_iota(jnp.int32, (SPAN, 128), 1)
    return jnp.where(lane < HEAD, both[:SPAN], both[SPAN:])


def turn_kernel(pos, x_ref, out_ref):
    rows = x_ref.shape[0]
    for i in range(rows // BLK):
        store_turned(out_ref, At(pos, POS_EARLY), x_ref[i * BLK : (i + 1) * BLK, :], i * BLK, BLK)


def turn(pos, x):
    rows = x.shape[0]
    return call(
        turn_kernel, [((2, NB, RB, rows), BF)], [SM, VM], pos, x, moved=rows * D * 6, name="turn"
    )[0]


def attn_rows(i, x, w_ref, masks, qkv_ref, ctx_ref, lse_ref):
    r0 = pl.multiple_of(i * BLK, BLK)
    qkv = mm(x, weight(w_ref, 0, HALF_QKV)).astype(BF)
    qkv_ref[pl.ds(r0, BLK), :] = qkv
    rows = []
    for s in range(2):
        own = qkv[s * SPAN : (s + 1) * SPAN]
        parts = []
        for j in range(3):
            q = stack_heads(own[:, j * 128 : (j + 1) * 128], masks)
            k = own[:, HALF_OUT + j * 128 : HALF_OUT + (j + 1) * 128]
            v = own[:, 2 * HALF_OUT + j * 128 : 2 * HALF_OUT + (j + 1) * 128]
            st = mm(k, q, NT)
            top = jnp.max(st, axis=0, keepdims=True)
            ex = jnp.exp(st - top)
            total = jnp.sum(ex, axis=0, keepdims=True)
            pt = (ex * (1.0 / total)).astype(BF)
            lse_ref[i * 2 + s, j : j + 1, :] = top + jnp.log(total)
            parts.append(merge_heads(mm(pt, v, TN)).astype(BF))
        rows.append(jnp.concatenate(parts, axis=1))
    ctx = jnp.concatenate(rows, axis=0)
    ctx_ref[pl.ds(r0, BLK), :] = ctx
    return ctx


def attn_one_kernel(first, tab, low, high, x_ref, qkv_ref, ctx_ref, lse_ref, w_ref):
    assemble_kernel(first, tab, low, high, w_ref)
    masks = head_masks(SPAN, HEAD ** (-0.5))

    def step(i, carry):
        x = x_ref[pl.ds(pl.multiple_of(i * BLK, BLK), BLK), :]
        attn_rows(i, x, w_ref, masks, qkv_ref, ctx_ref, lse_ref)
        return carry

    lax.fori_loop(0, x_ref.shape[0] // BLK, step, 0, unroll=2)


def attn_two_kernel(
    first, tab, low, high, x_ref, wo_ref, ctxo_ref,
    qkv_ref, ctx_ref, lse_ref, xh_ref, rstd_ref, p_ref, w_ref,
):
    assemble_kernel(first, tab, low, high, w_ref)
    cols = weight(w_ref, HALF_QKV + HALF_OUT, ONE).astype(F32)
    p_ref[...] = cols.T[:8]
    masks = head_masks(SPAN, HEAD ** (-0.5))

    def step(i, carry):
        rs = pl.ds(pl.multiple_of(i * BLK, BLK), BLK)
        x = x_ref[rs, :]
        ctx = attn_rows(i, x, w_ref, masks, qkv_ref, ctx_ref, lse_ref)
        attn = x.astype(F32) + mm(ctxo_ref[rs, :], weight(wo_ref, HALF_QKV, HALF_QKV + HALF_OUT), NT)
        attn = attn + mm(ctx, weight(w_ref, HALF_QKV, HALF_QKV + HALF_OUT), NT)
        xh, rstd = norm_fwd(attn)
        rstd = jnp.broadcast_to(rstd, (BLK, 128))
        for s in range(2):
            for q in range(4):
                r = s * SPAN + q * 32
                xh_ref[q, i * 2 + s] = xh[r : r + 32]
                rstd_ref[q, i * 2 + s] = rstd[r : r + 32]
        return carry

    lax.fori_loop(0, x_ref.shape[0] // BLK, step, 0, unroll=2)


def attn_shapes(rows):
    return [((rows, HALF_QKV), BF), ((rows, HALF_OUT), BF), ((rows // SPAN, 8, 2 * SPAN), F32)]


def attn_one(first, tab, low, high, x):
    rows = x.shape[0]
    return call(
        partial(attn_one_kernel, first), attn_shapes(rows) + [((NB, RB, ONE), BF)],
        [SM, VM, VM, VM], tab, low, high, x,
        vmem=16, flops=rows * 4e6, moved=rows * 8000 + 2e6, trans=rows * 800, name="attn_one",
    )


def attn_two(first, tab, low, high, x, w_own, ctx_own):
    rows = x.shape[0]
    spans = rows // SPAN
    out = attn_shapes(rows) + [
        ((4, spans, 32, D), F32),
        ((4, spans, 32, 128), F32),
        ((8, D), F32),
        ((NB, RB, ONE), BF),
    ]
    return call(
        partial(attn_two_kernel, first), out, [SM] + [VM] * 5, tab, low, high, x, w_own, ctx_own,
        vmem=16, flops=rows * 5e6, moved=rows * 12000 + 4e6, trans=rows * 800, name="attn_two",
    )


def gelu_pair(u):
    a = jnp.abs(u)
    d = 1.0 + (0.3275911 * 0.5**0.5) * a
    t = pl.reciprocal(d, approx=True)
    t = t * (2.0 - d * t)
    e = jnp.exp(-0.5 * u * u)
    poly = 0.5307027145 * t - 0.7265760135
    poly = poly * t + 0.7107068705
    poly = poly * t - 0.142248368
    poly = poly * t + 0.127414796
    tail = (poly * t) * e
    phi = jnp.where(u >= 0.0, 1.0 - tail, tail)
    return u * phi, phi + (0.3989422804014327 * u) * e


TILE = 512


def ffn_up_kernel(pos, xh_ref, p_ref, w_ref, g_ref, gp_ref, *yt_ref):
    def step(i, carry):
        rs = pl.ds(pl.multiple_of(i * BLK, BLK), BLK)
        y = xh_ref[rs, :] * p_ref[0:1, :] + p_ref[1:2, :]
        yb = y.astype(BF)
        if yt_ref:
            store_turned(yt_ref[0], At(pos, POS_EARLY), yb, pl.multiple_of(i * BLK, BLK), BLK)
        for t in range(HALF_FF // TILE):
            u = mm(yb, weight(w_ref, t * TILE, (t + 1) * TILE))
            g, gp = gelu_pair(u)
            g_ref[rs, t * TILE : (t + 1) * TILE] = g.astype(BF)
            gp_ref[rs, t * TILE : (t + 1) * TILE] = gp.astype(BF)
        return carry

    lax.fori_loop(0, xh_ref.shape[0] // BLK, step, 0, unroll=2)


def ffn_up(pos, xh, prow, w, turned, name):
    rows = xh.shape[0]
    out = [((rows, HALF_FF), BF), ((rows, HALF_FF), BF)]
    if turned:
        out.append(((2, NB, RB, rows), BF))
    return call(
        ffn_up_kernel, out, [SM, VM, VM, VM], pos, xh, prow, w,
        vmem=16, flops=rows * 2.4e6, moved=rows * 9000 + 2e6, trans=rows * 6000, name=name,
    )


def down_block(r0, xh1_ref, p_ref, acts, downs):
    rs = pl.ds(r0, BLK)
    total = xh1_ref[rs, :] * p_ref[0:1, :] + p_ref[1:2, :]
    for g_ref, w_ref in zip(acts, downs):
        total = total + mm(g_ref[rs, :], weight(w_ref, 0, HALF_FF), NT)
    return norm_fwd(total)


def first_kernel(xh1_ref, p_ref, g0, g1, d0, d1, mixed_ref, cls_ref, xh_ref, rstd_ref):
    xh, rstd = down_block(0, xh1_ref, p_ref, (g0, g1), (d0, d1))
    xh_ref[...] = xh
    rstd_ref[...] = jnp.broadcast_to(rstd, rstd_ref.shape)
    out = (xh * p_ref[2:3, :] + p_ref[3:4, :]).reshape(mixed_ref.shape)
    mixed_ref[...] = out.astype(BF)
    cls_ref[...] = out[:, 0, :]


def first_rows(xh1, prow, acts, downs):
    spans = BLK // 32
    return call(
        first_kernel,
        [((spans, 32, D), BF), ((spans, D), F32), ((BLK, D), F32), ((BLK, 128), F32)],
        [VM] * 6, xh1, prow, *acts, *downs,
        vmem=8, flops=BLK * 4.8e6, moved=BLK * 16000 + 5e6, name="first_rows",
    )


def back_block(r0, grad, xh2, rstd2, gps, xh1_ref, rstd1_ref, p_ref, ups, downs, dus):
    rs = pl.ds(r0, BLK)
    sum_g2 = jnp.sum(grad * xh2, axis=0, keepdims=True)
    sum_b2 = jnp.sum(grad, axis=0, keepdims=True)
    dh = norm_bwd(grad, xh2, rstd2, p_ref[2:3, :])
    df = dh.astype(BF)
    total = dh
    for gp_ref, up_ref, down_ref, du_ref in zip(gps, ups, downs, dus):
        for t in range(HALF_FF // TILE):
            lo, hi = t * TILE, (t + 1) * TILE
            dg = mm(df, weight(down_ref, lo, hi))
            du_ref[:, lo:hi] = (dg * gp_ref[rs, lo:hi].astype(F32)).astype(BF)
        total = total + mm(du_ref[...], weight(up_ref, 0, HALF_FF), NT)
    xh1 = xh1_ref[rs, :]
    sum_g1 = jnp.sum(total * xh1, axis=0, keepdims=True)
    sum_b1 = jnp.sum(total, axis=0, keepdims=True)
    dh1 = norm_bwd(total, xh1, rstd1_ref[rs, 0:1], p_ref[0:1, :])
    return df, dh1, (sum_g1, sum_b1, sum_g2, sum_b2)


def back_shapes():
    return [
        ((2, NB, RB, BLK), BF),
        ((BLK, HALF_FF), BF),
        ((BLK, HALF_FF), BF),
        ((BLK // 32, 32, D), F32),
        ((8, D), F32),
    ]


def rest_kernel(
    at, pos, xh1_ref, rstd1_ref, p_ref, g0, g1, gp0, gp1, cot_ref, u0, u1, d0, d1,
    dft_ref, du0_ref, du1_ref, dh1_ref, sums_ref, mixed_ref,
):
    r0, c0 = at * BLK, at * 32
    xh, rstd = down_block(r0, xh1_ref, p_ref, (g0, g1), (d0, d1))
    out = xh * p_ref[2:3, :] + p_ref[3:4, :]
    mixed_ref[...] = out.reshape(mixed_ref.shape).astype(BF)
    grad = cot_ref[:, c0 : c0 + 32, :].astype(F32).reshape(BLK, D)
    df, dh1, sums = back_block(
        r0, grad, xh, rstd, (gp0, gp1), xh1_ref, rstd1_ref, p_ref, (u0, u1), (d0, d1), (du0_ref, du1_ref)
    )
    store_turned(dft_ref, At(pos, POS_LATE), df, 0, BLK)
    dh1_ref[...] = dh1.reshape(dh1_ref.shape)
    for n in range(4):
        sums_ref[n : n + 1, :] = sums[n]


def rest_rows(at, pos, xh1, rstd1, prow, acts, gps, cot, ups, downs):
    return call(
        partial(rest_kernel, at),
        back_shapes() + [((BLK // 32, 32, D), BF)],
        [SM] + [VM] * 12, pos, xh1, rstd1, prow, *acts, *gps, cot, *ups, *downs,
        vmem=16, flops=BLK * 14.5e6, moved=BLK * 40000 + 1e7, name=f"rest_rows_{at}",
    )


def class_kernel(
    pos, cls_ref, cot_ref, xh2_ref, rstd2_ref, xh1_ref, rstd1_ref, p_ref, gp0, gp1, u0, u1, d0, d1,
    dft_ref, du0_ref, du1_ref, dh1_ref, sums_ref,
):
    spans = cls_ref.shape[0]
    grad = cot_ref[:, 0:32, :].astype(F32)
    first = lax.broadcasted_iota(jnp.int32, grad.shape, 1) == 0
    grad = grad + jnp.where(first, cls_ref[...].reshape(spans, 1, D), 0.0)
    grad = grad.reshape(BLK, D)
    df, dh1, sums = back_block(
        0, grad, xh2_ref[...], rstd2_ref[:, 0:1], (gp0, gp1), xh1_ref, rstd1_ref, p_ref,
        (u0, u1), (d0, d1), (du0_ref, du1_ref),
    )
    store_turned(dft_ref, At(pos, POS_LATE), df, 0, BLK)
    dh1_ref[...] = dh1.reshape(dh1_ref.shape)
    for n in range(4):
        sums_ref[n : n + 1, :] = sums[n]


def class_rows(pos, grad_cls, cot, xh2, rstd2, xh1, rstd1, prow, gps, ups, downs):
    return call(
        class_kernel,
        back_shapes(),
        [SM] + [VM] * 13, pos, grad_cls, cot, xh2, rstd2, xh1, rstd1, prow, *gps, *ups, *downs,
        vmem=16, flops=BLK * 9.7e6, moved=BLK * 30000 + 1e7, name="class_rows",
    )


def contrast_kernel(where, doc_ref, cls_ref, loss_ref, grad_ref, rows, own_doc):
    spans = doc_ref.shape[1]
    doc_row = doc_ref[...].astype(F32)
    doc_col = jnp.broadcast_to(doc_row, (128, spans)).T[:, 0:1]
    blocks, per = cls_ref.shape[0], cls_ref.shape[1]
    where = At(where, CLASS_AT)
    me = where[0]
    for n in range(blocks):
        rows[where[1 + n]] = cls_ref[n].astype(F32)
    a = rows[...].reshape(spans, D).astype(BF)
    own = rows[me].astype(BF)
    scale = D ** (-0.5)
    col = lax.broadcasted_iota(jnp.int32, (spans, spans), 1)
    row = lax.broadcasted_iota(jnp.int32, (spans, spans), 0)
    logits = mm(a, a, NT) * scale
    partner = (doc_col == doc_row) & (row != col)
    masked = jnp.where(row == col, -1000000000.0, logits)
    top = jnp.max(masked, axis=0, keepdims=True)
    lse = jnp.log(jnp.sum(jnp.exp(masked - top), axis=0, keepdims=True)) + top
    positive = jnp.sum(jnp.where(partner, logits, 0.0), axis=0, keepdims=True)
    flagged = jnp.max(jnp.where(partner, 1.0, 0.0), axis=0, keepdims=True)
    count = jnp.sum(flagged, axis=1, keepdims=True)
    loss = jnp.sum(flagged * (lse - positive), axis=1, keepdims=True) / count
    loss_ref[...] = jnp.broadcast_to(loss, loss_ref.shape)

    weight_row = flagged * (CONTRAST * spans) / count
    own_doc[...] = doc_col.reshape(blocks, per, 1)
    docs = own_doc[me]
    col = lax.broadcasted_iota(jnp.int32, (per, spans), 1)
    row = lax.broadcasted_iota(jnp.int32, (per, spans), 0) + me * per
    logits = mm(own, a, NT) * scale
    same = jnp.where((docs == doc_row) & (row != col), 1.0, 0.0)
    masked = jnp.where(row == col, -1000000000.0, logits)
    top = jnp.max(masked, axis=1, keepdims=True)
    ex = jnp.exp(masked - top)
    soft = ex / jnp.sum(ex, axis=1, keepdims=True)
    own_weight = jnp.max(same, axis=1, keepdims=True) * (CONTRAST * spans) / count
    sym = own_weight * (soft - same) + weight_row * (jnp.exp(masked - lse) - same)
    high = sym.astype(BF)
    low = (sym - high.astype(F32)).astype(BF)
    grad_ref[...] = (mm(high, a) + mm(low, a)) * scale


def contrast(where, doc_row, cls_all):
    blocks, per, _ = cls_all.shape
    spans = blocks * per
    return call(
        contrast_kernel,
        [((1, 128), F32), ((per, D), F32)],
        [SM, VM, VM],
        where, doc_row, cls_all,
        vmem=8 if spans <= 256 else 40, flops=2 * spans * spans * D, moved=spans * D * 2,
        scratch=[pltpu.VMEM((blocks, per, D), F32), pltpu.VMEM((blocks, per, 1), F32)],
        name="contrast",
    )


def turned_of(refs, n):
    return jnp.concatenate([ref[n].reshape(D, ref.shape[3]) for ref in refs], axis=1)


def grad_other_kernel(count, *refs):
    xts, ys, out_ref = refs[:count], refs[count:-1], refs[-1]
    xt = turned_of(xts, 1)
    for t in range(HALF_FF // TILE):
        lo, hi = t * TILE, (t + 1) * TILE
        grad = mm(xt, jnp.concatenate([y[:, lo:hi] for y in ys], axis=0))
        out_ref[:, :, lo:hi] = grad.astype(BF).reshape(NB, RB, TILE)


def grad_other(xts, ys, name):
    rows = sum(y.shape[0] for y in ys)
    return call(
        partial(grad_other_kernel, len(xts)),
        [((NB, RB, HALF_FF), BF)],
        [VM] * (len(xts) + len(ys)), *xts, *ys,
        vmem=12, flops=2 * rows * D * HALF_FF, moved=rows * 8000 + 2.4e6, name=name,
    )[0]


def grad_own_kernel(count, came_ref, *refs):
    xts, ys, keep_ref, send_ref = refs[:count], refs[count:-2], refs[-2], refs[-1]
    nh = NB // 2
    xt = turned_of(xts, 0)
    for t in range(HALF_FF // TILE):
        lo, hi = t * TILE, (t + 1) * TILE
        grad = mm(xt, jnp.concatenate([y[:, lo:hi] for y in ys], axis=0))
        grad = (grad.reshape(NB, RB, TILE) + came_ref[:, :, lo:hi].astype(F32)).astype(BF)
        keep_ref[:, :, lo:hi] = grad[:nh]
        send_ref[:, :, lo:hi] = grad[nh:]


def grad_own(xts, ys, came, name):
    rows = sum(y.shape[0] for y in ys)
    return call(
        partial(grad_own_kernel, len(xts)),
        [((NB // 2, RB, HALF_FF), BF)] * 2,
        [VM] * (1 + len(xts) + len(ys)), came, *xts, *ys,
        vmem=12, flops=2 * rows * D * HALF_FF, moved=rows * 8000 + 4.8e6, name=name,
    )


def natural(refs, i):
    return jnp.concatenate([ref[i * 2 + s] for s in range(2) for ref in refs], axis=0)


def attn_back_kernel(pos, r0_ref, r1_ref, r2_ref, r3_ref, qkv_ref, lse_ref, w_ref, dqkv_ref, *dat_ref):
    masks = head_masks(SPAN, HEAD ** (-0.5))
    plain = head_masks(SPAN, 1.0)
    spans = r0_ref.shape[0]

    def step(i, carry):
        r0 = pl.multiple_of(i * BLK, BLK)
        da = natural((r0_ref, r1_ref, r2_ref, r3_ref), i).astype(BF)
        if dat_ref:
            store_turned(dat_ref[0], At(pos, POS_EARLY), da, r0, BLK)
        dctx = mm(da, weight(w_ref, HALF_QKV, HALF_QKV + HALF_OUT)).astype(BF)
        for s in range(2):
            rs = pl.ds(pl.multiple_of(r0 + s * SPAN, SPAN), SPAN)
            for j in range(3):
                a, b = j * 128, (j + 1) * 128
                q = stack_heads(qkv_ref[rs, a:b], masks)
                k = qkv_ref[rs, HALF_OUT + a : HALF_OUT + b]
                v = qkv_ref[rs, 2 * HALF_OUT + a : 2 * HALF_OUT + b]
                dc = stack_heads(dctx[s * SPAN : (s + 1) * SPAN, a:b], plain)
                st = mm(k, q, NT)
                pt = jnp.exp(st - lse_ref[i * 2 + s, j : j + 1, :])
                dpt = mm(v, dc, NT)
                dst = pt * (dpt - jnp.sum(pt * dpt, axis=0, keepdims=True))
                dst = dst.astype(BF)
                dv = mm(pt.astype(BF), dc)
                dk = mm(dst, q)
                dq = merge_heads(mm(dst, k, TN)) * HEAD ** (-0.5)
                dqkv_ref[rs, a:b] = dq.astype(BF)
                dqkv_ref[rs, HALF_OUT + a : HALF_OUT + b] = dk.astype(BF)
                dqkv_ref[rs, 2 * HALF_OUT + a : 2 * HALF_OUT + b] = dv.astype(BF)
        return carry

    lax.fori_loop(0, spans // 2, step, 0, unroll=2)


def attn_back(pos, dh1, qkv, lse, w, turned, name):
    rows = qkv.shape[0]
    out = [((rows, HALF_QKV), BF)]
    if turned:
        out.append(((2, NB, RB, rows), BF))
    return call(
        attn_back_kernel, out,
        [SM] + [VM] * 7, pos, *dh1, qkv, lse, w,
        vmem=16, flops=rows * 6e6, moved=rows * 10000 + 3e6, trans=rows * 800, name=name,
    )


def last_value(order, xt_ref, dqkv_ref, dat_ref, ctx_ref, t):
    rows = xt_ref.shape[3]
    if t < 3:
        return mm(xt_ref[order].reshape(D, rows), dqkv_ref[:, t * HALF_OUT : (t + 1) * HALF_OUT])
    return mm(dat_ref[order].reshape(D, rows), ctx_ref[...])


def norm_columns(sums):
    total = sums[0][0:4, :]
    for ref in sums[1:]:
        total = total + ref[0:4, :]
    return jnp.concatenate([total, jnp.zeros((124, D), F32)], axis=0).T


def last_other_kernel(pos, xt_ref, dqkv_ref, dat_ref, ctx_ref, s0, s1, s2, s3, out_ref):
    for t in range(4):
        grad = last_value(1, xt_ref, dqkv_ref, dat_ref, ctx_ref, t)
        lo = t * HALF_OUT
        out_ref[:, :, lo : lo + HALF_OUT] = grad.astype(BF).reshape(NB, RB, HALF_OUT)
    norm = norm_columns((s0, s1, s2, s3)).astype(BF)
    for j in range(NB):
        out_ref[pos[POS_EARLY + NB + j], :, HALF_QKV + HALF_OUT :] = norm[j * RB : (j + 1) * RB]


def last_other(pos, xt, dqkv, dat, ctx, sums):
    rows = xt.shape[3]
    return call(
        last_other_kernel,
        [((NB, RB, ONE), BF)],
        [SM] + [VM] * 8, pos, xt, dqkv, dat, ctx, *sums,
        vmem=12, flops=2 * rows * D * HALF_FF, moved=rows * 8000 + 2.4e6, name="last_other",
    )[0]


def last_own_kernel(
    pos, xt_ref, dqkv_ref, dat_ref, ctx_ref, s0, s1, s2, s3, came_ref, keep_ref, send_ref, cols
):
    nh = NB // 2
    norm = norm_columns((s0, s1, s2, s3))
    for j in range(NB):
        cols[pos[POS_EARLY + j]] = norm[j * RB : (j + 1) * RB]
    for t in range(5):
        lo = t * HALF_OUT
        hi = min(lo + HALF_OUT, ONE)
        if t < 4:
            grad = last_value(0, xt_ref, dqkv_ref, dat_ref, ctx_ref, t).reshape(NB, RB, HALF_OUT)
        else:
            grad = cols[...]
        grad = (grad + came_ref[:, :, lo:hi].astype(F32)).astype(BF)
        keep_ref[:, :, lo:hi] = grad[:nh]
        send_ref[:, :, lo:hi] = grad[nh:]


def last_own(pos, xt, dqkv, dat, ctx, sums, came):
    rows = xt.shape[3]
    return call(
        last_own_kernel,
        [((NB // 2, RB, ONE), BF)] * 2,
        [SM] + [VM] * 9, pos, xt, dqkv, dat, ctx, *sums, came,
        vmem=12, flops=2 * rows * D * HALF_FF, moved=rows * 8000 + 4.8e6,
        scratch=[pltpu.VMEM((NB, RB, 128), F32)], name="last_own",
    )


def input_grad_kernel(r0_ref, r1_ref, r2_ref, r3_ref, own_ref, other_ref, w0_ref, w1_ref, out_ref):
    spans = r0_ref.shape[0]

    def step(i, carry):
        rs = pl.ds(pl.multiple_of(i * BLK, BLK), BLK)
        total = natural((r0_ref, r1_ref, r2_ref, r3_ref), i)
        total = total + mm(own_ref[rs, :], weight(w0_ref, 0, HALF_QKV), NT)
        total = total + mm(other_ref[rs, :], weight(w1_ref, 0, HALF_QKV), NT)
        out_ref[rs, :] = total
        return carry

    lax.fori_loop(0, spans // 2, step, 0, unroll=2)


def input_grads(dh1, own, other, w_own, w_other):
    rows = own.shape[0]
    return call(
        input_grad_kernel,
        [((rows, D), F32)],
        [VM] * 8, *dh1, own, other, w_own, w_other,
        vmem=12, flops=rows * 3.6e6, moved=rows * 12000 + 5e6, name="input_grads",
    )[0]


def place_kernel(half, *refs):
    own, other, g_own, g_other = refs[0:4], refs[4:8], refs[8], refs[9]
    mixed_ref, grad_ref, sems = refs[10:]
    spans = g_own.shape[0]
    copies = []
    for n, (pieces, g) in enumerate(((own, g_own), (other, g_other))):
        at = pl.ds(half[HALF_AT + n] * spans, spans)
        for q in range(4):
            to = mixed_ref.at[at, 32 * q : 32 * q + 32, :]
            copies.append(pltpu.make_async_copy(pieces[q], to, sems.at[5 * n + q]))
        copies.append(pltpu.make_async_copy(g, grad_ref.at[at], sems.at[5 * n + 4]))
    for c in copies:
        c.start()
    for c in copies:
        c.wait()


def place(half, own, other, g_own, g_other):
    spans = own[0].shape[0]
    g_own, g_other = (g.reshape(spans, SPAN, D) for g in (g_own, g_other))
    return pl.pallas_call(
        place_kernel,
        out_shape=[
            jax.ShapeDtypeStruct((2 * spans, SPAN, D), BF),
            jax.ShapeDtypeStruct((2 * spans, SPAN, D), F32),
        ],
        in_specs=[SM] + [VM] * 10,
        out_specs=[HBM] * 2,
        scratch_shapes=[pltpu.SemaphoreType.DMA((10,))],
        compiler_params=params(16),
        cost_estimate=cost(0, spans * SPAN * D * 24),
        name="place",
    )(half, *own, *other, g_own, g_other)


def squares_kernel(k0, c0, k1, c1, k2, c2, g0, g1, g2, sq_ref):
    main = HALF_QKV + HALF_OUT
    total = jnp.zeros((1, 1), F32)
    for keep, came, out in ((k0, c0, g0), (k1, c1, g1), (k2, c2, g2)):
        grad = keep[0].astype(F32) + came[0].astype(F32)
        out[...] = grad
        sq = jnp.sum(grad[:, :main] * grad[:, :main], axis=1, keepdims=True)
        if grad.shape[1] > main:
            cols = grad[:, main:]
            sq = sq + 0.5 * jnp.sum(cols * cols, axis=1, keepdims=True)
        total = total + jnp.sum(sq, axis=0, keepdims=True)
    sq_ref[...] = jnp.broadcast_to(total, sq_ref.shape)


def squares_of(pairs):
    shard = pairs[0][0].shape[1]
    out = [((shard, k.shape[2]), F32) for k, _ in pairs] + [((8, 128), F32)]
    flat = [a for pair in pairs for a in pair]
    return call(squares_kernel, out, [VM] * 6, *flat, vmem=8, moved=shard * 40000, name="squares")


def adam_parts(weight, gradient, moment_one, moment_two, step_rate, decay_rate):
    first_new = 0.9 * moment_one + 0.1 * gradient
    second_new = 0.999 * moment_two + 0.001 * gradient * gradient
    corr_first = first_new * (1.0 / (1.0 - 0.9**STEP))
    corr_second = second_new * (1.0 / (1.0 - 0.999**STEP))
    weight_new = weight - step_rate * (
        corr_first / (jnp.sqrt(corr_second) + 1e-08) + decay_rate * weight
    )
    return first_new, second_new, weight_new


def adam_kernel(sq_ref, last_ref, up_ref, down_ref, cols_ref, *refs):
    ins, outs, wide = refs[:15], refs[15:-1], refs[-1]
    norm = jnp.sqrt(sq_ref[0:1, 0:1])
    outs[15][...] = jnp.broadcast_to(norm, outs[15].shape)
    scale = 1.0 / jnp.maximum(norm, 1.0)

    def update(n, at, grad, rate, decay):
        new = adam_parts(ins[n][at], grad * scale, ins[5 + 2 * n][at], ins[6 + 2 * n][at], rate, decay)
        for m in range(3):
            outs[3 * n + m][at] = new[m]

    for part in range(3):
        update(0, part, last_ref[:, part * HALF_OUT : (part + 1) * HALF_OUT], 0.02, 0.01)
    update(1, Ellipsis, last_ref[:, HALF_QKV : HALF_QKV + HALF_OUT], 0.02, 0.01)
    update(2, Ellipsis, up_ref[...], 0.02, 0.01)
    update(3, Ellipsis, down_ref[...], 0.02, 0.01)
    shard = last_ref.shape[0]
    wide[...] = jnp.zeros_like(wide)
    wide[0:shard, :] = 0.5 * (last_ref[:, HALF_QKV + HALF_OUT :] + cols_ref[...])
    update(4, Ellipsis, wide[...].T[0:4, 0:shard], 0.5, 0.0)


def adam(squares, last, up, down, cols, weights, moments):
    shapes = [w.shape for w in weights]
    out = [(s, F32) for s in shapes for _ in range(3)] + [((8, 128), F32)]
    args = (squares, last, up, down, cols, *weights, *moments)
    return call(
        adam_kernel, out, [VM] * len(args), *args, vmem=16, moved=7 * 4 * last.shape[0] * 4608,
        scratch=[pltpu.VMEM((128, 128), F32)], name="adam",
    )


def after(value, *others):
    return lax.optimization_barrier((value, others))[0]


def body(
    tokens,
    cotangent,
    span_doc,
    qkv_weight,
    out_weight,
    ffn_in_weight,
    ffn_out_weight,
    norm_params,
    qkv_first,
    qkv_second,
    out_first,
    out_second,
    ffn_in_first,
    ffn_in_second,
    ffn_out_first,
    ffn_out_second,
    norm_first,
    norm_second,
):
    n_dp = lax.axis_size("dp")
    dp = lax.axis_index("dp")
    core = lax.axis_index("tensor")
    shard = D // n_dp
    rows = tokens.shape[0] // 2
    spans = rows // SPAN
    direct = n_dp == NB
    early, late = bit_orders(n_dp)
    steps = len(early[0])
    last = steps - 1

    tab = lax.dynamic_index_in_dim(device_tables(n_dp), dp * 2 + core, 0, keepdims=False)
    x = lax.dynamic_slice_in_dim(tokens, core * rows, rows, 0)
    cot = lax.dynamic_slice_in_dim(cotangent, core * rows, rows, 0).reshape(spans, SPAN, D)

    def places(orders, other=0):
        return dp ^ jnp.array([rel_of(order) for order in orders], jnp.int32)[core ^ other]

    def send_on(block, orders, k):
        return lax.ppermute(block, AXES, pairs_of(n_dp, orders, k))

    def join(held, came):
        return jnp.concatenate([held, came], axis=0)

    def pieces(at, low, high):
        if direct:
            return at, tab, low, high
        which = {AT_EARLY: places(early), AT_LATE: places(late), AT_OTHER: places(early, 1)}[at]
        full = join(low, high)[jnp.argsort(which)].reshape(NB, RB, -1)
        return at, tab, full[: NB // 2], full[NB // 2 :]

    def halves(orders, keep, send):
        if direct:
            return keep, send
        full = join(keep, send).reshape(n_dp, shard, -1)[places(orders)]
        return full[: n_dp // 2], full[n_dp // 2 :]

    def add(keep, came):
        total = keep.astype(F32) + came.astype(F32)
        size = total.shape[0] // 2
        return total[:size].astype(BF), total[size:].astype(BF)

    turned = ((1, 0, 2), (1, 0), (0, 1), (1, 0), (0, 1))
    weights = (qkv_weight, out_weight, ffn_in_weight, ffn_out_weight, norm_params)
    weights = tuple(w.transpose(t) for w, t in zip(weights, turned))
    one, up, down = pack(*weights)
    one_came = send_on(one, early, 0)
    up_came = send_on(up, late, 0)
    one, tab, x, cot = after((join(one, one_came), tab, x, cot), up_came)
    for k in range(1, last):
        one_came = send_on(one, early, k)
        if k == 1:
            tokt = turn(tab, x)
            one_came = after(one_came, tokt)
        else:
            up = after(join(up, up_came), one)
            up_came = send_on(up, late, k - 1)
        one = join(one, one_came)
        if k > 1:
            one = after(one, up_came)
    one_came = send_on(one, early, last)
    for k in range(max(last - 1, 1), last):
        up = join(up, up_came)
        up_came = send_on(up, late, k)
    down_came = send_on(after(down, one), early, 0)
    one, one_came = after((one, one_came), up_came, down_came)
    up = after(join(up, up_came), one_came)
    up_came = send_on(up, late, last)
    down = after(join(down, down_came), one_came)
    down_came = send_on(down, early, 1)

    one_other = (core_swap(one), core_swap(one_came))
    qkv0, ctx0, lse0, w10 = attn_one(*pieces(AT_EARLY, one, one_came), x)
    ctx0 = after(ctx0, down_came)
    for k in range(2, last):
        down = join(down, after(down_came, ctx0))
        down_came = send_on(down, early, k)
    qkv1, ctx1, lse1, xh1, rstd1, prow, w11 = attn_two(*pieces(AT_OTHER, *one_other), x, w10, ctx0)
    w1 = (w10, w11)
    xh1 = xh1.reshape(rows, D)
    rstd1 = rstd1.reshape(rows, 128)
    up_came, down_came = after((up_came, down_came), xh1)
    wu = assemble(*pieces(AT_LATE, up, up_came), "up_own")
    wu = (wu, core_swap(wu))
    down = join(down, down_came)
    down_came = send_on(down, early, last)
    act0, gp0, yt = ffn_up(tab, after(xh1, down), prow, wu[0], True, "ffn_up_own")
    wd = assemble(*pieces(AT_EARLY, down, after(down_came, act0)), "down_own")
    wd = (wd, core_swap(wd))
    act1, gp1 = ffn_up(tab, after(xh1, wd[0]), prow, wu[1], False, "ffn_up_other")
    acts, gps = (act0, act1), (gp0, gp1)
    mixed0, cls_own, xh2, rstd2 = first_rows(xh1, prow, acts, wd)

    held = cls_own.astype(BF)[None]
    back = []
    for k in reversed(range(steps)):
        came = lax.ppermute(held, "dp", [(d, d ^ (1 << k)) for d in range(n_dp)])
        if len(back) < 3:
            at = len(back) + 1
            back.append(rest_rows(at, tab, after(xh1, held), rstd1, prow, acts, gps, cot, wu, wd))
            came = after(came, back[-1][4])
        held = join(held, came)
    held = join(held, core_swap(held))
    loss, grad_cls = contrast(tab, span_doc.reshape(1, -1), held)
    back.insert(0, (*class_rows(tab, grad_cls, cot, xh2, rstd2, xh1, rstd1, prow, gps, wu, wd), mixed0))
    dft, du0, du1, dh1, sums, mixed_own = zip(*back)

    d_other = grad_other(dft, (act1,), "grad_down_other")
    d_came = core_swap(d_other)
    u_other = grad_other((after(yt, d_other),), du1, "grad_up_other")
    u_came = core_swap(u_other)
    d_keep, d_send = halves(
        late, *grad_own((after(dft[0], u_other),) + dft[1:], (act0,), d_came, "grad_down_own")
    )
    d_came = send_on(d_send, late, last)
    u_keep, u_send = halves(early, *grad_own((after(yt, d_keep),), du0, u_came, "grad_up_own"))
    dh1 = (after(dh1[0], u_keep),) + dh1[1:]
    dqkv1, dat = attn_back(tab, dh1, qkv1, lse1, w1[1], True, "attn_back_other")
    l_other = last_other(tab, tokt, dqkv1, dat, ctx1, sums)

    d_came, l_other = after((d_came, l_other))
    d_keep, d_send = add(d_keep, d_came)
    u_came = send_on(after(u_send, l_other), early, last)
    d_came = send_on(d_send, late, last - 1)
    l_came = core_swap(l_other)
    (dqkv0,) = attn_back(
        tab, (after(dh1[0], l_other),) + dh1[1:], qkv0, lse0, w1[0], False, "attn_back_own"
    )
    l_keep, l_send = halves(early, *last_own(tab, tokt, dqkv0, dat, ctx0, sums, l_came))
    l_came = send_on(l_send, early, last)
    grad_in = input_grads((after(dh1[0], l_send),) + dh1[1:], dqkv0, dqkv1, w1[0], w1[1])
    u_came, d_came = after((u_came, d_came), l_send)
    u_keep, u_send = add(u_keep, u_came)
    d_keep, d_send = add(d_keep, d_came)
    u_came = send_on(u_send, early, last - 1)
    d_came = send_on(d_send, late, last - 2)
    for k in reversed(range(last)):
        l_came, u_came, d_came = after((l_came, u_came, d_came))
        l_keep, l_send = add(l_keep, l_came)
        l_came = send_on(l_send, early, k)
        if k > 0:
            u_keep, u_send = add(u_keep, u_came)
            u_came = send_on(u_send, early, k - 1)
        if k > 1:
            d_keep, d_send = add(d_keep, d_came)
            d_came = send_on(d_send, late, k - 2)
        if k == last - 1:
            grad_came = core_swap(after(grad_in, l_send))
            mixed_other = tuple(core_swap(m) for m in after(mixed_own, l_send))
            l_came = after(l_came, grad_came, mixed_other)
        if k == last - 2:
            mixed, input_grad = place(tab, mixed_own, mixed_other, after(grad_in, l_send), grad_came)
            l_came = after(l_came, input_grad)

    last_grad, down_grad, up_grad, squares = squares_of(((l_keep, l_came), (d_keep, d_came), (u_keep, u_came)))
    cols = core_swap(last_grad[:, HALF_QKV + HALF_OUT :])
    squares = squares + core_swap(squares)
    bits = [1 << k for k in reversed(range(steps))]
    for one_bit, two_bit in zip(bits[::2], bits[1::2]):
        near, far, both = (
            lax.ppermute(squares, "dp", [(d, d ^ b) for d in range(n_dp)])
            for b in (one_bit, two_bit, one_bit ^ two_bit)
        )
        squares = (squares + near) + (far + both)
    moments = (
        qkv_first, qkv_second, out_first, out_second, ffn_in_first, ffn_in_second,
        ffn_out_first, ffn_out_second, norm_first, norm_second,
    )
    new = adam(
        squares, last_grad, up_grad, down_grad, cols,
        weights,
        [m.transpose(turned[n // 2]) for n, m in enumerate(moments)],
    )
    updated = [value.transpose(turned[n // 3]) for n, value in enumerate(new[:15])]
    return (
        mixed.reshape(2 * rows, D),
        input_grad.reshape(2 * rows, D),
        loss[0, 0],
        new[15][0, 0],
        *updated,
    )


def solution(mesh):
    rows = P("dp", None)
    qkv = P("dp", None, "tensor")
    turned = P("tensor", "dp")
    up = P("dp", "tensor")
    norm = P(None, "dp")
    weights = (qkv, turned, up, turned, norm)
    moments = tuple(spec for spec in weights for _ in range(2))
    updated = tuple(spec for spec in weights for _ in range(3))
    return jax.shard_map(
        body,
        mesh=mesh,
        in_specs=(rows, rows, P()) + weights + moments,
        out_specs=(rows, rows, P(), P()) + updated,
        check_vma=False,
    )
```

```python
from functools import partial

import jax
import jax.numpy as jnp
import numpy as np
from jax import lax
from jax.experimental import pallas as pl
from jax.experimental.pallas import tpu as pltpu
from jax.sharding import PartitionSpec as P

HEAD = 64
SPAN = 128
STEP = 10
D = 768
FF = 3072
NB = 16
RB = D // NB
HALF_QKV = 1152
HALF_OUT = 384
HALF_FF = 1536
ONE = HALF_QKV + HALF_OUT + 128
CONTRAST = 4.0
EPS = 1e-06
BF = jnp.bfloat16
F32 = jnp.float32
AXES = ("dp", "tensor")
SHRINK = 100

NN = (((1,), (0,)), ((), ()))
NT = (((1,), (1,)), ((), ()))
TN = (((0,), (0,)), ((), ()))


def mm(left, right, dims=NN):
    return lax.dot_general(left, right, dims, preferred_element_type=F32)


def params(vmem=56):
    vmem = vmem if vmem > 24 else min(vmem, 8)
    return pltpu.CompilerParams(vmem_limit_bytes=vmem * 2**20)


def cost(flops, bytes_accessed, trans=0):
    flops, bytes_accessed, trans = (n // SHRINK + 1 for n in (flops, bytes_accessed, trans))
    return pl.CostEstimate(flops=int(flops), bytes_accessed=int(bytes_accessed), transcendentals=int(trans))


HBM = pl.BlockSpec(memory_space=pl.ANY)


def bit_orders(n_dp):
    bits = n_dp.bit_length() - 1
    if bits == 4:
        return ((4, 8, 2, 1), (8, 4, 1, 2)), ((1, 4, 8, 2), (2, 8, 4, 1))
    up = tuple(1 << b for b in range(bits))[::-1]
    both = (up, up[: bits // 2] + up[bits // 2 :][::-1])
    return both, both


def pairs_of(n_dp, orders, step):
    out = []
    for d in range(n_dp):
        for c in range(2):
            out.append((d * 2 + c, (d ^ orders[c][step]) * 2 + c))
    return out


def rel_of(order):
    out = []
    for p in range(1 << len(order)):
        r = 0
        for k, b in enumerate(order):
            if (p >> k) & 1:
                r ^= b
        out.append(r)
    return out


AT_EARLY, AT_LATE, AT_OTHER, POS_EARLY, POS_LATE = 0, NB, 2 * NB, 3 * NB, 5 * NB
HALF_AT, CLASS_AT = 7 * NB, 7 * NB + 2


class At:
    def __init__(self, ref, first):
        self.ref, self.first = ref, first

    def __getitem__(self, n):
        return self.ref[self.first + n]


def device_tables(n_dp):
    kinds = [[rel_of(order) for order in orders] for orders in bit_orders(n_dp)]
    classes = rel_of([1 << k for k in reversed(range(n_dp.bit_length() - 1))])
    plain = list(range(NB))
    table = []
    for d in range(n_dp):
        for c in range(2):
            direct = n_dp == NB
            row = []
            for rel in kinds:
                row += [d ^ r for r in rel[c]] if direct else plain
            row += [d ^ r for r in kinds[0][1 - c]] if direct else plain
            for rel in kinds:
                for half in (c, 1 - c):
                    row += [rel[half].index(d ^ j) for j in range(NB)] if direct else plain
            me = d * 2 + c
            row += [c, 1 - c, me] + [me ^ (r << 1 | b) for b in range(2) for r in classes]
            table.append(row)
    return np.array(table, np.int32)


def core_swap(block):
    return lax.ppermute(block, "tensor", [(0, 1), (1, 0)])


VM = pl.BlockSpec(memory_space=pltpu.VMEM)
SM = pl.BlockSpec(memory_space=pltpu.SMEM)
BLK = 256


def call(kernel, out, in_specs, *args, vmem=16, flops=0, moved=0, trans=0, scratch=(), name=None):
    return pl.pallas_call(
        kernel,
        out_shape=[jax.ShapeDtypeStruct(s, t) for s, t in out],
        in_specs=in_specs,
        out_specs=[VM] * len(out),
        scratch_shapes=list(scratch),
        compiler_params=params(vmem),
        cost_estimate=cost(flops, moved, trans),
        name=name,
    )(*args)


def pack_kernel(qkv, out, up, down, norm, one_ref, two_ref, three_ref, wide, a0, a1, a2, a3, sems):
    rows = up.shape[0]
    wide[...] = jnp.zeros_like(wide)
    copies = [
        pltpu.make_async_copy(src, dst, sems.at[n])
        for n, (src, dst) in enumerate(
            ((qkv, a0), (out, a1), (down, a3), (up, a2))
        )
    ]
    for c in copies:
        c.start()
    copies[0].wait()
    for part in range(3):
        one_ref[0, :, part * HALF_OUT : (part + 1) * HALF_OUT] = a0[part].astype(BF)
    copies[1].wait()
    one_ref[0, :, HALF_QKV : HALF_QKV + HALF_OUT] = a1[...].astype(BF)
    wide[0:4, 0:rows] = norm[...]
    one_ref[0, :, HALF_QKV + HALF_OUT :] = wide[...].T[0:rows].astype(BF)
    copies[2].wait()
    three_ref[0] = a3[...].astype(BF)
    copies[3].wait()
    two_ref[0] = a2[...].astype(BF)


def pack(*shards):
    rows = shards[2].shape[0]
    return call(
        pack_kernel,
        [((1, rows, ONE), BF), ((1, rows, HALF_FF), BF), ((1, rows, HALF_FF), BF)],
        [pl.BlockSpec(memory_space=pltpu.HBM)] * 4 + [VM], *shards,
        vmem=60, moved=rows * 28000,
        scratch=[pltpu.VMEM((128, 128), F32)]
        + [pltpu.VMEM(w.shape, F32) for w in shards[:4]]
        + [pltpu.SemaphoreType.DMA((4,))],
        name="pack",
    )


def assemble_kernel(first, tab, low, high, out_ref):
    for n, ref in enumerate((low, high)):
        for p in range(NB // 2):
            out_ref[tab[first + n * (NB // 2) + p]] = ref[p]


def assemble(first, tab, low, high, name):
    width = low.shape[-1]
    return call(
        partial(assemble_kernel, first),
        [((NB, RB, width), BF)],
        [SM, VM, VM], tab, low, high,
        moved=4 * D * width, name=name,
    )[0]


def weight(w_ref, first, last):
    return w_ref[:, :, first:last].reshape(D, last - first)


def norm_fwd(hidden):
    center = hidden - jnp.mean(hidden, axis=-1, keepdims=True)
    spread = jnp.mean(center * center, axis=-1, keepdims=True)
    rstd = lax.rsqrt(spread + EPS)
    return center * rstd, rstd


def norm_bwd(grad, xh, rstd, gain):
    e = grad * gain
    m1 = jnp.mean(e, axis=-1, keepdims=True)
    m2 = jnp.mean(e * xh, axis=-1, keepdims=True)
    return rstd * (e - m1 - xh * m2)


def store_turned(ref, tab, value, col, width):
    turned = value.T
    for j in range(NB):
        block = turned[j * RB : (j + 1) * RB]
        for n in range(2):
            ref[n, tab[n * NB + j], :, pl.ds(col, width)] = block


def head_masks(rows, scale):
    lane = lax.broadcasted_iota(jnp.int32, (rows, 128), 1)
    return (
        jnp.where(lane < HEAD, scale, 0.0).astype(BF),
        jnp.where(lane < HEAD, 0.0, scale).astype(BF),
    )


def stack_heads(pair, masks):
    return jnp.concatenate([pair * masks[0], pair * masks[1]], axis=0)


def merge_heads(both):
    lane = lax.broadcasted_iota(jnp.int32, (SPAN, 128), 1)
    return jnp.where(lane < HEAD, both[:SPAN], both[SPAN:])


def turn_kernel(pos, x_ref, out_ref):
    rows = x_ref.shape[0]
    for i in range(rows // BLK):
        store_turned(out_ref, At(pos, POS_EARLY), x_ref[i * BLK : (i + 1) * BLK, :], i * BLK, BLK)


def turn(pos, x):
    rows = x.shape[0]
    return call(
        turn_kernel, [((2, NB, RB, rows), BF)], [SM, VM], pos, x, moved=rows * D * 6, name="turn"
    )[0]


def attn_rows(i, x, w_ref, masks, qkv_ref, ctx_ref, lse_ref):
    r0 = pl.multiple_of(i * BLK, BLK)
    qkv = mm(x, weight(w_ref, 0, HALF_QKV)).astype(BF)
    qkv_ref[pl.ds(r0, BLK), :] = qkv
    pairs = [(s, j) for s in range(2) for j in range(3)]

    def part(n, s, j):
        return qkv[s * SPAN : (s + 1) * SPAN, n * HALF_OUT + j * 128 : n * HALF_OUT + (j + 1) * 128]

    sts = [mm(part(1, s, j), stack_heads(part(0, s, j), masks), NT) for s, j in pairs]
    tops = [jnp.max(st, axis=0, keepdims=True) for st in sts]
    exs = [jnp.exp(st - top) for st, top in zip(sts, tops)]
    totals = [jnp.sum(ex, axis=0, keepdims=True) for ex in exs]
    pts = [(ex * (1.0 / total)).astype(BF) for ex, total in zip(exs, totals)]
    parts = [merge_heads(mm(pt, part(2, s, j), TN)).astype(BF) for pt, (s, j) in zip(pts, pairs)]
    for (s, j), top, total in zip(pairs, tops, totals):
        lse_ref[i * 2 + s, j : j + 1, :] = top + jnp.log(total)
    ctx = jnp.concatenate([jnp.concatenate(parts[s * 3 : s * 3 + 3], axis=1) for s in range(2)], axis=0)
    ctx_ref[pl.ds(r0, BLK), :] = ctx
    return ctx


def attn_one_kernel(first, tab, low, high, x_ref, qkv_ref, ctx_ref, lse_ref, w_ref):
    assemble_kernel(first, tab, low, high, w_ref)
    masks = head_masks(SPAN, HEAD ** (-0.5))

    def step(i, carry):
        x = x_ref[pl.ds(pl.multiple_of(i * BLK, BLK), BLK), :]
        attn_rows(i, x, w_ref, masks, qkv_ref, ctx_ref, lse_ref)
        return carry

    lax.fori_loop(0, x_ref.shape[0] // BLK, step, 0, unroll=2)


def attn_two_kernel(
    first, tab, low, high, x_ref, wo_ref, ctxo_ref,
    qkv_ref, ctx_ref, lse_ref, xh_ref, rstd_ref, p_ref, w_ref,
):
    assemble_kernel(first, tab, low, high, w_ref)
    cols = weight(w_ref, HALF_QKV + HALF_OUT, ONE).astype(F32)
    p_ref[...] = cols.T[:8]
    masks = head_masks(SPAN, HEAD ** (-0.5))

    def step(i, carry):
        rs = pl.ds(pl.multiple_of(i * BLK, BLK), BLK)
        x = x_ref[rs, :]
        ctx = attn_rows(i, x, w_ref, masks, qkv_ref, ctx_ref, lse_ref)
        attn = x.astype(F32) + mm(ctxo_ref[rs, :], weight(wo_ref, HALF_QKV, HALF_QKV + HALF_OUT), NT)
        attn = attn + mm(ctx, weight(w_ref, HALF_QKV, HALF_QKV + HALF_OUT), NT)
        xh, rstd = norm_fwd(attn)
        rstd = jnp.broadcast_to(rstd, (BLK, 128))
        for s in range(2):
            for q in range(4):
                r = s * SPAN + q * 32
                xh_ref[q, i * 2 + s] = xh[r : r + 32]
                rstd_ref[q, i * 2 + s] = rstd[r : r + 32]
        return carry

    lax.fori_loop(0, x_ref.shape[0] // BLK, step, 0, unroll=2)


def attn_shapes(rows):
    return [((rows, HALF_QKV), BF), ((rows, HALF_OUT), BF), ((rows // SPAN, 8, 2 * SPAN), F32)]


def attn_one(first, tab, low, high, x):
    rows = x.shape[0]
    return call(
        partial(attn_one_kernel, first), attn_shapes(rows) + [((NB, RB, ONE), BF)],
        [SM, VM, VM, VM], tab, low, high, x,
        vmem=16, flops=rows * 4e6, moved=rows * 8000 + 2e6, trans=rows * 800, name="attn_one",
    )


def attn_two(first, tab, low, high, x, w_own, ctx_own):
    rows = x.shape[0]
    spans = rows // SPAN
    out = attn_shapes(rows) + [
        ((4, spans, 32, D), F32),
        ((4, spans, 32, 128), F32),
        ((8, D), F32),
        ((NB, RB, ONE), BF),
    ]
    return call(
        partial(attn_two_kernel, first), out, [SM] + [VM] * 5, tab, low, high, x, w_own, ctx_own,
        vmem=16, flops=rows * 5e6, moved=rows * 12000 + 4e6, trans=rows * 800, name="attn_two",
    )


def gelu_pair(u):
    a = jnp.abs(u)
    d = 1.0 + (0.3275911 * 0.5**0.5) * a
    t = pl.reciprocal(d, approx=True)
    t = t * (2.0 - d * t)
    e = jnp.exp(-0.5 * u * u)
    poly = 0.5307027145 * t - 0.7265760135
    poly = poly * t + 0.7107068705
    poly = poly * t - 0.142248368
    poly = poly * t + 0.127414796
    tail = (poly * t) * e
    phi = jnp.where(u >= 0.0, 1.0 - tail, tail)
    return u * phi, phi + (0.3989422804014327 * u) * e


TILE = 512


def ffn_up_kernel(pos, xh_ref, p_ref, w_ref, g_ref, gp_ref, *yt_ref):
    def step(i, carry):
        rs = pl.ds(pl.multiple_of(i * BLK, BLK), BLK)
        y = xh_ref[rs, :] * p_ref[0:1, :] + p_ref[1:2, :]
        yb = y.astype(BF)
        if yt_ref:
            store_turned(yt_ref[0], At(pos, POS_EARLY), yb, pl.multiple_of(i * BLK, BLK), BLK)
        for t in range(HALF_FF // TILE):
            u = mm(yb, weight(w_ref, t * TILE, (t + 1) * TILE))
            g, gp = gelu_pair(u)
            g_ref[rs, t * TILE : (t + 1) * TILE] = g.astype(BF)
            gp_ref[rs, t * TILE : (t + 1) * TILE] = gp.astype(BF)
        return carry

    lax.fori_loop(0, xh_ref.shape[0] // BLK, step, 0, unroll=2)


def ffn_up(pos, xh, prow, w, turned, name):
    rows = xh.shape[0]
    out = [((rows, HALF_FF), BF), ((rows, HALF_FF), BF)]
    if turned:
        out.append(((2, NB, RB, rows), BF))
    return call(
        ffn_up_kernel, out, [SM, VM, VM, VM], pos, xh, prow, w,
        vmem=16, flops=rows * 2.4e6, moved=rows * 9000 + 2e6, trans=rows * 6000, name=name,
    )


def down_block(r0, xh1_ref, p_ref, acts, downs):
    rs = pl.ds(r0, BLK)
    total = xh1_ref[rs, :] * p_ref[0:1, :] + p_ref[1:2, :]
    for g_ref, w_ref in zip(acts, downs):
        total = total + mm(g_ref[rs, :], weight(w_ref, 0, HALF_FF), NT)
    return norm_fwd(total)


def first_kernel(xh1_ref, p_ref, g0, g1, d0, d1, mixed_ref, cls_ref, xh_ref, rstd_ref):
    xh, rstd = down_block(0, xh1_ref, p_ref, (g0, g1), (d0, d1))
    xh_ref[...] = xh
    rstd_ref[...] = jnp.broadcast_to(rstd, rstd_ref.shape)
    out = (xh * p_ref[2:3, :] + p_ref[3:4, :]).reshape(mixed_ref.shape)
    mixed_ref[...] = out.astype(BF)
    cls_ref[...] = out[:, 0, :]


def first_rows(xh1, prow, acts, downs):
    spans = BLK // 32
    return call(
        first_kernel,
        [((spans, 32, D), BF), ((spans, D), F32), ((BLK, D), F32), ((BLK, 128), F32)],
        [VM] * 6, xh1, prow, *acts, *downs,
        vmem=8, flops=BLK * 4.8e6, moved=BLK * 16000 + 5e6, name="first_rows",
    )


def back_block(r0, grad, xh2, rstd2, gps, xh1_ref, rstd1_ref, p_ref, ups, downs, dus):
    rs = pl.ds(r0, BLK)
    sum_g2 = jnp.sum(grad * xh2, axis=0, keepdims=True)
    sum_b2 = jnp.sum(grad, axis=0, keepdims=True)
    dh = norm_bwd(grad, xh2, rstd2, p_ref[2:3, :])
    df = dh.astype(BF)
    total = dh
    for gp_ref, up_ref, down_ref, du_ref in zip(gps, ups, downs, dus):
        for t in range(HALF_FF // TILE):
            lo, hi = t * TILE, (t + 1) * TILE
            dg = mm(df, weight(down_ref, lo, hi))
            du_ref[:, lo:hi] = (dg * gp_ref[rs, lo:hi].astype(F32)).astype(BF)
        total = total + mm(du_ref[...], weight(up_ref, 0, HALF_FF), NT)
    xh1 = xh1_ref[rs, :]
    sum_g1 = jnp.sum(total * xh1, axis=0, keepdims=True)
    sum_b1 = jnp.sum(total, axis=0, keepdims=True)
    dh1 = norm_bwd(total, xh1, rstd1_ref[rs, 0:1], p_ref[0:1, :])
    return df, dh1, (sum_g1, sum_b1, sum_g2, sum_b2)


def back_shapes():
    return [
        ((2, NB, RB, BLK), BF),
        ((BLK, HALF_FF), BF),
        ((BLK, HALF_FF), BF),
        ((BLK // 32, 32, D), F32),
        ((8, D), F32),
    ]


def rest_kernel(
    at, pos, xh1_ref, rstd1_ref, p_ref, g0, g1, gp0, gp1, cot_ref, u0, u1, d0, d1,
    dft_ref, du0_ref, du1_ref, dh1_ref, sums_ref, mixed_ref,
):
    r0, c0 = at * BLK, at * 32
    xh, rstd = down_block(r0, xh1_ref, p_ref, (g0, g1), (d0, d1))
    out = xh * p_ref[2:3, :] + p_ref[3:4, :]
    mixed_ref[...] = out.reshape(mixed_ref.shape).astype(BF)
    grad = cot_ref[:, c0 : c0 + 32, :].astype(F32).reshape(BLK, D)
    df, dh1, sums = back_block(
        r0, grad, xh, rstd, (gp0, gp1), xh1_ref, rstd1_ref, p_ref, (u0, u1), (d0, d1), (du0_ref, du1_ref)
    )
    store_turned(dft_ref, At(pos, POS_LATE), df, 0, BLK)
    dh1_ref[...] = dh1.reshape(dh1_ref.shape)
    for n in range(4):
        sums_ref[n : n + 1, :] = sums[n]


def rest_rows(at, pos, xh1, rstd1, prow, acts, gps, cot, ups, downs):
    return call(
        partial(rest_kernel, at),
        back_shapes() + [((BLK // 32, 32, D), BF)],
        [SM] + [VM] * 12, pos, xh1, rstd1, prow, *acts, *gps, cot, *ups, *downs,
        vmem=16, flops=BLK * 14.5e6, moved=BLK * 40000 + 1e7, name=f"rest_rows_{at}",
    )


def class_kernel(
    pos, cls_ref, cot_ref, xh2_ref, rstd2_ref, xh1_ref, rstd1_ref, p_ref, gp0, gp1, u0, u1, d0, d1,
    dft_ref, du0_ref, du1_ref, dh1_ref, sums_ref,
):
    spans = cls_ref.shape[0]
    grad = cot_ref[:, 0:32, :].astype(F32)
    first = lax.broadcasted_iota(jnp.int32, grad.shape, 1) == 0
    grad = grad + jnp.where(first, cls_ref[...].reshape(spans, 1, D), 0.0)
    grad = grad.reshape(BLK, D)
    df, dh1, sums = back_block(
        0, grad, xh2_ref[...], rstd2_ref[:, 0:1], (gp0, gp1), xh1_ref, rstd1_ref, p_ref,
        (u0, u1), (d0, d1), (du0_ref, du1_ref),
    )
    store_turned(dft_ref, At(pos, POS_LATE), df, 0, BLK)
    dh1_ref[...] = dh1.reshape(dh1_ref.shape)
    for n in range(4):
        sums_ref[n : n + 1, :] = sums[n]


def class_rows(pos, grad_cls, cot, xh2, rstd2, xh1, rstd1, prow, gps, ups, downs):
    return call(
        class_kernel,
        back_shapes(),
        [SM] + [VM] * 13, pos, grad_cls, cot, xh2, rstd2, xh1, rstd1, prow, *gps, *ups, *downs,
        vmem=16, flops=BLK * 9.7e6, moved=BLK * 30000 + 1e7, name="class_rows",
    )


def contrast_kernel(where, doc_ref, cls_ref, loss_ref, grad_ref, rows, own_doc):
    spans = doc_ref.shape[1]
    doc_row = doc_ref[...].astype(F32)
    doc_col = jnp.broadcast_to(doc_row, (128, spans)).T[:, 0:1]
    blocks, per = cls_ref.shape[0], cls_ref.shape[1]
    where = At(where, CLASS_AT)
    me = where[0]
    for n in range(blocks):
        rows[where[1 + n]] = cls_ref[n].astype(F32)
    a = rows[...].reshape(spans, D).astype(BF)
    own = rows[me].astype(BF)
    scale = D ** (-0.5)
    col = lax.broadcasted_iota(jnp.int32, (spans, spans), 1)
    row = lax.broadcasted_iota(jnp.int32, (spans, spans), 0)
    logits = mm(a, a, NT) * scale
    partner = (doc_col == doc_row) & (row != col)
    masked = jnp.where(row == col, -1000000000.0, logits)
    top = jnp.max(masked, axis=0, keepdims=True)
    lse = jnp.log(jnp.sum(jnp.exp(masked - top), axis=0, keepdims=True)) + top
    positive = jnp.sum(jnp.where(partner, logits, 0.0), axis=0, keepdims=True)
    flagged = jnp.max(jnp.where(partner, 1.0, 0.0), axis=0, keepdims=True)
    count = jnp.sum(flagged, axis=1, keepdims=True)
    loss = jnp.sum(flagged * (lse - positive), axis=1, keepdims=True) / count
    loss_ref[...] = jnp.broadcast_to(loss, loss_ref.shape)

    weight_row = flagged * (CONTRAST * spans) / count
    own_doc[...] = doc_col.reshape(blocks, per, 1)
    docs = own_doc[me]
    col = lax.broadcasted_iota(jnp.int32, (per, spans), 1)
    row = lax.broadcasted_iota(jnp.int32, (per, spans), 0) + me * per
    logits = mm(own, a, NT) * scale
    same = jnp.where((docs == doc_row) & (row != col), 1.0, 0.0)
    masked = jnp.where(row == col, -1000000000.0, logits)
    top = jnp.max(masked, axis=1, keepdims=True)
    ex = jnp.exp(masked - top)
    soft = ex / jnp.sum(ex, axis=1, keepdims=True)
    own_weight = jnp.max(same, axis=1, keepdims=True) * (CONTRAST * spans) / count
    sym = own_weight * (soft - same) + weight_row * (jnp.exp(masked - lse) - same)
    high = sym.astype(BF)
    low = (sym - high.astype(F32)).astype(BF)
    grad_ref[...] = (mm(high, a) + mm(low, a)) * scale


def contrast(where, doc_row, cls_all):
    blocks, per, _ = cls_all.shape
    spans = blocks * per
    return call(
        contrast_kernel,
        [((1, 128), F32), ((per, D), F32)],
        [SM, VM, VM],
        where, doc_row, cls_all,
        vmem=8 if spans <= 256 else 40, flops=2 * spans * spans * D, moved=spans * D * 2,
        scratch=[pltpu.VMEM((blocks, per, D), F32), pltpu.VMEM((blocks, per, 1), F32)],
        name="contrast",
    )


def turned_of(refs, n):
    return jnp.concatenate([ref[n].reshape(D, ref.shape[3]) for ref in refs], axis=1)


def grad_other_kernel(count, *refs):
    xts, ys, out_ref = refs[:count], refs[count:-1], refs[-1]
    xt = turned_of(xts, 1)
    for t in range(HALF_FF // TILE):
        lo, hi = t * TILE, (t + 1) * TILE
        grad = mm(xt, jnp.concatenate([y[:, lo:hi] for y in ys], axis=0))
        out_ref[:, :, lo:hi] = grad.astype(BF).reshape(NB, RB, TILE)


def grad_other(xts, ys, name):
    rows = sum(y.shape[0] for y in ys)
    return call(
        partial(grad_other_kernel, len(xts)),
        [((NB, RB, HALF_FF), BF)],
        [VM] * (len(xts) + len(ys)), *xts, *ys,
        vmem=12, flops=2 * rows * D * HALF_FF, moved=rows * 8000 + 2.4e6, name=name,
    )[0]


def grad_own_kernel(count, came_ref, *refs):
    xts, ys, keep_ref, send_ref = refs[:count], refs[count:-2], refs[-2], refs[-1]
    nh = NB // 2
    xt = turned_of(xts, 0)
    for t in range(HALF_FF // TILE):
        lo, hi = t * TILE, (t + 1) * TILE
        grad = mm(xt, jnp.concatenate([y[:, lo:hi] for y in ys], axis=0))
        grad = (grad.reshape(NB, RB, TILE) + came_ref[:, :, lo:hi].astype(F32)).astype(BF)
        keep_ref[:, :, lo:hi] = grad[:nh]
        send_ref[:, :, lo:hi] = grad[nh:]


def grad_own(xts, ys, came, name):
    rows = sum(y.shape[0] for y in ys)
    return call(
        partial(grad_own_kernel, len(xts)),
        [((NB // 2, RB, HALF_FF), BF)] * 2,
        [VM] * (1 + len(xts) + len(ys)), came, *xts, *ys,
        vmem=12, flops=2 * rows * D * HALF_FF, moved=rows * 8000 + 4.8e6, name=name,
    )


def natural(refs, i):
    return jnp.concatenate([ref[i * 2 + s] for s in range(2) for ref in refs], axis=0)


def attn_back_kernel(pos, r0_ref, r1_ref, r2_ref, r3_ref, qkv_ref, lse_ref, w_ref, dqkv_ref, *dat_ref):
    masks = head_masks(SPAN, HEAD ** (-0.5))
    plain = head_masks(SPAN, 1.0)
    spans = r0_ref.shape[0]

    def step(i, carry):
        r0 = pl.multiple_of(i * BLK, BLK)
        da = natural((r0_ref, r1_ref, r2_ref, r3_ref), i).astype(BF)
        if dat_ref:
            store_turned(dat_ref[0], At(pos, POS_EARLY), da, r0, BLK)
        dctx = mm(da, weight(w_ref, HALF_QKV, HALF_QKV + HALF_OUT)).astype(BF)
        pairs = [(s, j) for s in range(2) for j in range(3)]

        def part(ref, n, s, j):
            rs = pl.ds(pl.multiple_of(r0 + s * SPAN, SPAN), SPAN)
            return ref.at[rs, n * HALF_OUT + j * 128 : n * HALF_OUT + (j + 1) * 128]

        qs = [stack_heads(part(qkv_ref, 0, s, j)[...], masks) for s, j in pairs]
        ks = [part(qkv_ref, 1, s, j)[...] for s, j in pairs]
        sts = [mm(k, q, NT) for k, q in zip(ks, qs)]
        dcs = [stack_heads(dctx[s * SPAN : (s + 1) * SPAN, j * 128 : (j + 1) * 128], plain) for s, j in pairs]
        dpts = [mm(part(qkv_ref, 2, s, j)[...], dc, NT) for (s, j), dc in zip(pairs, dcs)]
        pts = [jnp.exp(st - lse_ref[i * 2 + s, j : j + 1, :]) for (s, j), st in zip(pairs, sts)]
        dvs = [mm(pt.astype(BF), dc) for pt, dc in zip(pts, dcs)]
        dsts = [
            (pt * (dpt - jnp.sum(pt * dpt, axis=0, keepdims=True))).astype(BF) for pt, dpt in zip(pts, dpts)
        ]
        dks = [mm(dst, q) for dst, q in zip(dsts, qs)]
        dqs = [merge_heads(mm(dst, k, TN)) * HEAD ** (-0.5) for dst, k in zip(dsts, ks)]
        for n, grads in enumerate((dqs, dks, dvs)):
            for (s, j), grad in zip(pairs, grads):
                part(dqkv_ref, n, s, j)[...] = grad.astype(BF)
        return carry

    lax.fori_loop(0, spans // 2, step, 0, unroll=2)


def attn_back(pos, dh1, qkv, lse, w, turned, name):
    rows = qkv.shape[0]
    out = [((rows, HALF_QKV), BF)]
    if turned:
        out.append(((2, NB, RB, rows), BF))
    return call(
        attn_back_kernel, out,
        [SM] + [VM] * 7, pos, *dh1, qkv, lse, w,
        vmem=16, flops=rows * 6e6, moved=rows * 10000 + 3e6, trans=rows * 800, name=name,
    )


def last_value(order, xt_ref, dqkv_ref, dat_ref, ctx_ref, t):
    rows = xt_ref.shape[3]
    if t < 3:
        return mm(xt_ref[order].reshape(D, rows), dqkv_ref[:, t * HALF_OUT : (t + 1) * HALF_OUT])
    return mm(dat_ref[order].reshape(D, rows), ctx_ref[...])


def norm_columns(sums):
    total = sums[0][0:4, :]
    for ref in sums[1:]:
        total = total + ref[0:4, :]
    return jnp.concatenate([total, jnp.zeros((124, D), F32)], axis=0).T


def last_other_kernel(pos, xt_ref, dqkv_ref, dat_ref, ctx_ref, s0, s1, s2, s3, out_ref):
    for t in range(4):
        grad = last_value(1, xt_ref, dqkv_ref, dat_ref, ctx_ref, t)
        lo = t * HALF_OUT
        out_ref[:, :, lo : lo + HALF_OUT] = grad.astype(BF).reshape(NB, RB, HALF_OUT)
    norm = norm_columns((s0, s1, s2, s3)).astype(BF)
    for j in range(NB):
        out_ref[pos[POS_EARLY + NB + j], :, HALF_QKV + HALF_OUT :] = norm[j * RB : (j + 1) * RB]


def last_other(pos, xt, dqkv, dat, ctx, sums):
    rows = xt.shape[3]
    return call(
        last_other_kernel,
        [((NB, RB, ONE), BF)],
        [SM] + [VM] * 8, pos, xt, dqkv, dat, ctx, *sums,
        vmem=12, flops=2 * rows * D * HALF_FF, moved=rows * 8000 + 2.4e6, name="last_other",
    )[0]


def last_own_kernel(
    pos, xt_ref, dqkv_ref, dat_ref, ctx_ref, s0, s1, s2, s3, came_ref, keep_ref, send_ref, cols
):
    nh = NB // 2
    norm = norm_columns((s0, s1, s2, s3))
    for j in range(NB):
        cols[pos[POS_EARLY + j]] = norm[j * RB : (j + 1) * RB]
    for t in range(5):
        lo = t * HALF_OUT
        hi = min(lo + HALF_OUT, ONE)
        if t < 4:
            grad = last_value(0, xt_ref, dqkv_ref, dat_ref, ctx_ref, t).reshape(NB, RB, HALF_OUT)
        else:
            grad = cols[...]
        grad = (grad + came_ref[:, :, lo:hi].astype(F32)).astype(BF)
        keep_ref[:, :, lo:hi] = grad[:nh]
        send_ref[:, :, lo:hi] = grad[nh:]


def last_own(pos, xt, dqkv, dat, ctx, sums, came):
    rows = xt.shape[3]
    return call(
        last_own_kernel,
        [((NB // 2, RB, ONE), BF)] * 2,
        [SM] + [VM] * 9, pos, xt, dqkv, dat, ctx, *sums, came,
        vmem=12, flops=2 * rows * D * HALF_FF, moved=rows * 8000 + 4.8e6,
        scratch=[pltpu.VMEM((NB, RB, 128), F32)], name="last_own",
    )


def input_grad_kernel(r0_ref, r1_ref, r2_ref, r3_ref, own_ref, other_ref, w0_ref, w1_ref, out_ref):
    spans = r0_ref.shape[0]

    def step(i, carry):
        rs = pl.ds(pl.multiple_of(i * BLK, BLK), BLK)
        total = natural((r0_ref, r1_ref, r2_ref, r3_ref), i)
        total = total + mm(own_ref[rs, :], weight(w0_ref, 0, HALF_QKV), NT)
        total = total + mm(other_ref[rs, :], weight(w1_ref, 0, HALF_QKV), NT)
        out_ref[rs, :] = total
        return carry

    lax.fori_loop(0, spans // 2, step, 0, unroll=2)


def input_grads(dh1, own, other, w_own, w_other):
    rows = own.shape[0]
    return call(
        input_grad_kernel,
        [((rows, D), F32)],
        [VM] * 8, *dh1, own, other, w_own, w_other,
        vmem=12, flops=rows * 3.6e6, moved=rows * 12000 + 5e6, name="input_grads",
    )[0]


def place_kernel(half, *refs):
    own, other, g_own, g_other = refs[0:4], refs[4:8], refs[8], refs[9]
    mixed_ref, grad_ref, sems = refs[10:]
    spans = g_own.shape[0]
    copies = []
    for n, (pieces, g) in enumerate(((own, g_own), (other, g_other))):
        at = pl.ds(half[HALF_AT + n] * spans, spans)
        for q in range(4):
            to = mixed_ref.at[at, 32 * q : 32 * q + 32, :]
            copies.append(pltpu.make_async_copy(pieces[q], to, sems.at[5 * n + q]))
        copies.append(pltpu.make_async_copy(g, grad_ref.at[at], sems.at[5 * n + 4]))
    for c in copies:
        c.start()
    for c in copies:
        c.wait()


def place(half, own, other, g_own, g_other):
    spans = own[0].shape[0]
    g_own, g_other = (g.reshape(spans, SPAN, D) for g in (g_own, g_other))
    return pl.pallas_call(
        place_kernel,
        out_shape=[
            jax.ShapeDtypeStruct((2 * spans, SPAN, D), BF),
            jax.ShapeDtypeStruct((2 * spans, SPAN, D), F32),
        ],
        in_specs=[SM] + [VM] * 10,
        out_specs=[HBM] * 2,
        scratch_shapes=[pltpu.SemaphoreType.DMA((10,))],
        compiler_params=params(16),
        cost_estimate=cost(0, spans * SPAN * D * 24),
        name="place",
    )(half, *own, *other, g_own, g_other)


def squares_kernel(k0, c0, k1, c1, k2, c2, g0, g1, g2, sq_ref):
    main = HALF_QKV + HALF_OUT
    total = jnp.zeros((1, 1), F32)
    for keep, came, out in ((k0, c0, g0), (k1, c1, g1), (k2, c2, g2)):
        grad = keep[0].astype(F32) + came[0].astype(F32)
        out[...] = grad
        sq = jnp.sum(grad[:, :main] * grad[:, :main], axis=1, keepdims=True)
        if grad.shape[1] > main:
            cols = grad[:, main:]
            sq = sq + 0.5 * jnp.sum(cols * cols, axis=1, keepdims=True)
        total = total + jnp.sum(sq, axis=0, keepdims=True)
    sq_ref[...] = jnp.broadcast_to(total, sq_ref.shape)


def squares_of(pairs):
    shard = pairs[0][0].shape[1]
    out = [((shard, k.shape[2]), F32) for k, _ in pairs] + [((8, 128), F32)]
    flat = [a for pair in pairs for a in pair]
    return call(squares_kernel, out, [VM] * 6, *flat, vmem=8, moved=shard * 40000, name="squares")


def adam_parts(weight, gradient, moment_one, moment_two, step_rate, decay_rate):
    first_new = 0.9 * moment_one + 0.1 * gradient
    second_new = 0.999 * moment_two + 0.001 * gradient * gradient
    corr_first = first_new * (1.0 / (1.0 - 0.9**STEP))
    corr_second = second_new * (1.0 / (1.0 - 0.999**STEP))
    weight_new = weight - step_rate * (
        corr_first / (jnp.sqrt(corr_second) + 1e-08) + decay_rate * weight
    )
    return first_new, second_new, weight_new


def adam_kernel(sq_ref, last_ref, up_ref, down_ref, cols_ref, *refs):
    ins, outs, wide = refs[:15], refs[15:-1], refs[-1]
    norm = jnp.sqrt(sq_ref[0:1, 0:1])
    outs[15][...] = jnp.broadcast_to(norm, outs[15].shape)
    scale = 1.0 / jnp.maximum(norm, 1.0)

    def update(n, at, grad, rate, decay):
        new = adam_parts(ins[n][at], grad * scale, ins[5 + 2 * n][at], ins[6 + 2 * n][at], rate, decay)
        for m in range(3):
            outs[3 * n + m][at] = new[m]

    for part in range(3):
        update(0, part, last_ref[:, part * HALF_OUT : (part + 1) * HALF_OUT], 0.02, 0.01)
    update(1, Ellipsis, last_ref[:, HALF_QKV : HALF_QKV + HALF_OUT], 0.02, 0.01)
    update(2, Ellipsis, up_ref[...], 0.02, 0.01)
    update(3, Ellipsis, down_ref[...], 0.02, 0.01)
    shard = last_ref.shape[0]
    wide[...] = jnp.zeros_like(wide)
    wide[0:shard, :] = 0.5 * (last_ref[:, HALF_QKV + HALF_OUT :] + cols_ref[...])
    update(4, Ellipsis, wide[...].T[0:4, 0:shard], 0.5, 0.0)


def adam(squares, last, up, down, cols, weights, moments):
    shapes = [w.shape for w in weights]
    out = [(s, F32) for s in shapes for _ in range(3)] + [((8, 128), F32)]
    args = (squares, last, up, down, cols, *weights, *moments)
    return call(
        adam_kernel, out, [VM] * len(args), *args, vmem=16, moved=7 * 4 * last.shape[0] * 4608,
        scratch=[pltpu.VMEM((128, 128), F32)], name="adam",
    )


def after(value, *others):
    return lax.optimization_barrier((value, others))[0]


def body(
    tokens,
    cotangent,
    span_doc,
    qkv_weight,
    out_weight,
    ffn_in_weight,
    ffn_out_weight,
    norm_params,
    qkv_first,
    qkv_second,
    out_first,
    out_second,
    ffn_in_first,
    ffn_in_second,
    ffn_out_first,
    ffn_out_second,
    norm_first,
    norm_second,
):
    n_dp = lax.axis_size("dp")
    dp = lax.axis_index("dp")
    core = lax.axis_index("tensor")
    shard = D // n_dp
    rows = tokens.shape[0] // 2
    spans = rows // SPAN
    direct = n_dp == NB
    early, late = bit_orders(n_dp)
    steps = len(early[0])
    last = steps - 1

    tab = lax.dynamic_index_in_dim(device_tables(n_dp), dp * 2 + core, 0, keepdims=False)
    x = lax.dynamic_slice_in_dim(tokens, core * rows, rows, 0)
    cot = lax.dynamic_slice_in_dim(cotangent, core * rows, rows, 0).reshape(spans, SPAN, D)

    def places(orders, other=0):
        return dp ^ jnp.array([rel_of(order) for order in orders], jnp.int32)[core ^ other]

    def send_on(block, orders, k):
        return lax.ppermute(block, AXES, pairs_of(n_dp, orders, k))

    def join(held, came):
        return jnp.concatenate([held, came], axis=0)

    def pieces(at, low, high):
        if direct:
            return at, tab, low, high
        which = {AT_EARLY: places(early), AT_LATE: places(late), AT_OTHER: places(early, 1)}[at]
        full = join(low, high)[jnp.argsort(which)].reshape(NB, RB, -1)
        return at, tab, full[: NB // 2], full[NB // 2 :]

    def halves(orders, keep, send):
        if direct:
            return keep, send
        full = join(keep, send).reshape(n_dp, shard, -1)[places(orders)]
        return full[: n_dp // 2], full[n_dp // 2 :]

    def add(keep, came):
        total = keep.astype(F32) + came.astype(F32)
        size = total.shape[0] // 2
        return total[:size].astype(BF), total[size:].astype(BF)

    turned = ((1, 0, 2), (1, 0), (0, 1), (1, 0), (0, 1))
    weights = (qkv_weight, out_weight, ffn_in_weight, ffn_out_weight, norm_params)
    weights = tuple(w.transpose(t) for w, t in zip(weights, turned))
    one, up, down = pack(*weights)
    one_came = send_on(one, early, 0)
    up_came = send_on(up, late, 0)
    one, tab, x, cot = after((join(one, one_came), tab, x, cot), up_came)
    for k in range(1, last):
        one_came = send_on(one, early, k)
        if k == 1:
            tokt = turn(tab, x)
            one_came = after(one_came, tokt)
        else:
            up = after(join(up, up_came), one)
            up_came = send_on(up, late, k - 1)
        one = join(one, one_came)
        if k > 1:
            one = after(one, up_came)
    one_came = send_on(one, early, last)
    for k in range(max(last - 1, 1), last):
        up = join(up, up_came)
        up_came = send_on(up, late, k)
    down_came = send_on(after(down, one), early, 0)
    one, one_came = after((one, one_came), up_came, down_came)
    up = after(join(up, up_came), one_came)
    up_came = send_on(up, late, last)
    down = after(join(down, down_came), one_came)
    down_came = send_on(down, early, 1)

    one_other = (core_swap(one), core_swap(one_came))
    qkv0, ctx0, lse0, w10 = attn_one(*pieces(AT_EARLY, one, one_came), x)
    ctx0 = after(ctx0, down_came)
    for k in range(2, last):
        down = join(down, after(down_came, ctx0))
        down_came = send_on(down, early, k)
    qkv1, ctx1, lse1, xh1, rstd1, prow, w11 = attn_two(*pieces(AT_OTHER, *one_other), x, w10, ctx0)
    w1 = (w10, w11)
    xh1 = xh1.reshape(rows, D)
    rstd1 = rstd1.reshape(rows, 128)
    up_came, down_came = after((up_came, down_came), xh1)
    wu = assemble(*pieces(AT_LATE, up, up_came), "up_own")
    wu = (wu, core_swap(wu))
    down = join(down, down_came)
    down_came = send_on(down, early, last)
    act0, gp0, yt = ffn_up(tab, after(xh1, down), prow, wu[0], True, "ffn_up_own")
    wd = assemble(*pieces(AT_EARLY, down, after(down_came, act0)), "down_own")
    wd = (wd, core_swap(wd))
    act1, gp1 = ffn_up(tab, after(xh1, wd[0]), prow, wu[1], False, "ffn_up_other")
    acts, gps = (act0, act1), (gp0, gp1)
    mixed0, cls_own, xh2, rstd2 = first_rows(xh1, prow, acts, wd)

    held = cls_own.astype(BF)[None]
    back = []
    for k in reversed(range(steps)):
        came = lax.ppermute(held, "dp", [(d, d ^ (1 << k)) for d in range(n_dp)])
        if len(back) < 3:
            at = len(back) + 1
            back.append(rest_rows(at, tab, after(xh1, held), rstd1, prow, acts, gps, cot, wu, wd))
            came = after(came, back[-1][4])
        held = join(held, came)
    held = join(held, core_swap(held))
    loss, grad_cls = contrast(tab, span_doc.reshape(1, -1), held)
    back.insert(0, (*class_rows(tab, grad_cls, cot, xh2, rstd2, xh1, rstd1, prow, gps, wu, wd), mixed0))
    dft, du0, du1, dh1, sums, mixed_own = zip(*back)

    d_other = grad_other(dft, (act1,), "grad_down_other")
    d_came = core_swap(d_other)
    u_other = grad_other((after(yt, d_other),), du1, "grad_up_other")
    u_came = core_swap(u_other)
    d_keep, d_send = halves(
        late, *grad_own((after(dft[0], u_other),) + dft[1:], (act0,), d_came, "grad_down_own")
    )
    d_came = send_on(d_send, late, last)
    u_keep, u_send = halves(early, *grad_own((after(yt, d_keep),), du0, u_came, "grad_up_own"))
    dh1 = (after(dh1[0], u_keep),) + dh1[1:]
    dqkv1, dat = attn_back(tab, dh1, qkv1, lse1, w1[1], True, "attn_back_other")
    l_other = last_other(tab, tokt, dqkv1, dat, ctx1, sums)

    d_came, l_other = after((d_came, l_other))
    d_keep, d_send = add(d_keep, d_came)
    u_came = send_on(after(u_send, l_other), early, last)
    d_came = send_on(d_send, late, last - 1)
    l_came = core_swap(l_other)
    (dqkv0,) = attn_back(
        tab, (after(dh1[0], l_other),) + dh1[1:], qkv0, lse0, w1[0], False, "attn_back_own"
    )
    l_keep, l_send = halves(early, *last_own(tab, tokt, dqkv0, dat, ctx0, sums, l_came))
    l_came = send_on(l_send, early, last)
    grad_in = input_grads((after(dh1[0], l_send),) + dh1[1:], dqkv0, dqkv1, w1[0], w1[1])
    u_came, d_came = after((u_came, d_came), l_send)
    u_keep, u_send = add(u_keep, u_came)
    d_keep, d_send = add(d_keep, d_came)
    u_came = send_on(u_send, early, last - 1)
    d_came = send_on(d_send, late, last - 2)
    for k in reversed(range(last)):
        l_came, u_came, d_came = after((l_came, u_came, d_came))
        l_keep, l_send = add(l_keep, l_came)
        l_came = send_on(l_send, early, k)
        if k > 0:
            u_keep, u_send = add(u_keep, u_came)
            u_came = send_on(u_send, early, k - 1)
        if k > 1:
            d_keep, d_send = add(d_keep, d_came)
            d_came = send_on(d_send, late, k - 2)
        if k == last - 1:
            grad_came = core_swap(after(grad_in, l_send))
            mixed_other = tuple(core_swap(m) for m in after(mixed_own, l_send))
            l_came = after(l_came, grad_came, mixed_other)
        if k == last - 2:
            mixed, input_grad = place(tab, mixed_own, mixed_other, after(grad_in, l_send), grad_came)
            l_came = after(l_came, input_grad)

    last_grad, down_grad, up_grad, squares = squares_of(((l_keep, l_came), (d_keep, d_came), (u_keep, u_came)))
    cols = core_swap(last_grad[:, HALF_QKV + HALF_OUT :])
    squares = squares + core_swap(squares)
    bits = [1 << k for k in reversed(range(steps))]
    for one_bit, two_bit in zip(bits[::2], bits[1::2]):
        near, far, both = (
            lax.ppermute(squares, "dp", [(d, d ^ b) for d in range(n_dp)])
            for b in (one_bit, two_bit, one_bit ^ two_bit)
        )
        squares = (squares + near) + (far + both)
    moments = (
        qkv_first, qkv_second, out_first, out_second, ffn_in_first, ffn_in_second,
        ffn_out_first, ffn_out_second, norm_first, norm_second,
    )
    new = adam(
        squares, last_grad, up_grad, down_grad, cols,
        weights,
        [m.transpose(turned[n // 2]) for n, m in enumerate(moments)],
    )
    updated = [value.transpose(turned[n // 3]) for n, value in enumerate(new[:15])]
    return (
        mixed.reshape(2 * rows, D),
        input_grad.reshape(2 * rows, D),
        loss[0, 0],
        new[15][0, 0],
        *updated,
    )


def solution(mesh):
    rows = P("dp", None)
    qkv = P("dp", None, "tensor")
    turned = P("tensor", "dp")
    up = P("dp", "tensor")
    norm = P(None, "dp")
    weights = (qkv, turned, up, turned, norm)
    moments = tuple(spec for spec in weights for _ in range(2))
    updated = tuple(spec for spec in weights for _ in range(3))
    return jax.shard_map(
        body,
        mesh=mesh,
        in_specs=(rows, rows, P()) + weights + moments,
        out_specs=(rows, rows, P(), P()) + updated,
        check_vma=False,
    )
```

```python
from functools import partial

import jax
import jax.numpy as jnp
import numpy as np
from jax import lax
from jax.experimental import pallas as pl
from jax.experimental.pallas import tpu as pltpu
from jax.sharding import PartitionSpec as P

HEAD = 64
SPAN = 128
STEP = 10
D = 768
FF = 3072
NB = 16
RB = D // NB
HALF_QKV = 1152
HALF_OUT = 384
HALF_FF = 1536
ONE = HALF_QKV + HALF_OUT + 128
CONTRAST = 4.0
EPS = 1e-06
BF = jnp.bfloat16
F32 = jnp.float32
AXES = ("dp", "tensor")
SHRINK = 100

NN = (((1,), (0,)), ((), ()))
NT = (((1,), (1,)), ((), ()))
TN = (((0,), (0,)), ((), ()))


def mm(left, right, dims=NN):
    return lax.dot_general(left, right, dims, preferred_element_type=F32)


def params(vmem=56):
    vmem = vmem if vmem > 24 else min(vmem, 8)
    return pltpu.CompilerParams(vmem_limit_bytes=vmem * 2**20)


def cost(flops, bytes_accessed, trans=0):
    flops, bytes_accessed, trans = (n // SHRINK + 1 for n in (flops, bytes_accessed, trans))
    return pl.CostEstimate(flops=int(flops), bytes_accessed=int(bytes_accessed), transcendentals=int(trans))


HBM = pl.BlockSpec(memory_space=pl.ANY)


def bit_orders(n_dp):
    bits = n_dp.bit_length() - 1
    if bits == 4:
        return ((4, 8, 2, 1), (8, 4, 1, 2)), ((1, 4, 8, 2), (2, 8, 4, 1))
    up = tuple(1 << b for b in range(bits))[::-1]
    both = (up, up[: bits // 2] + up[bits // 2 :][::-1])
    return both, both


def pairs_of(n_dp, orders, step):
    out = []
    for d in range(n_dp):
        for c in range(2):
            out.append((d * 2 + c, (d ^ orders[c][step]) * 2 + c))
    return out


def rel_of(order):
    out = []
    for p in range(1 << len(order)):
        r = 0
        for k, b in enumerate(order):
            if (p >> k) & 1:
                r ^= b
        out.append(r)
    return out


AT_EARLY, AT_LATE, AT_OTHER, POS_EARLY, POS_LATE = 0, NB, 2 * NB, 3 * NB, 5 * NB
HALF_AT, CLASS_AT = 7 * NB, 7 * NB + 2


class At:
    def __init__(self, ref, first):
        self.ref, self.first = ref, first

    def __getitem__(self, n):
        return self.ref[self.first + n]


def device_tables(n_dp):
    kinds = [[rel_of(order) for order in orders] for orders in bit_orders(n_dp)]
    classes = rel_of([1 << k for k in reversed(range(n_dp.bit_length() - 1))])
    plain = list(range(NB))
    table = []
    for d in range(n_dp):
        for c in range(2):
            direct = n_dp == NB
            row = []
            for rel in kinds:
                row += [d ^ r for r in rel[c]] if direct else plain
            row += [d ^ r for r in kinds[0][1 - c]] if direct else plain
            for rel in kinds:
                for half in (c, 1 - c):
                    row += [rel[half].index(d ^ j) for j in range(NB)] if direct else plain
            me = d * 2 + c
            row += [c, 1 - c, me] + [me ^ (r << 1 | b) for b in range(2) for r in classes]
            table.append(row)
    return np.array(table, np.int32)


def core_swap(block):
    return lax.ppermute(block, "tensor", [(0, 1), (1, 0)])


VM = pl.BlockSpec(memory_space=pltpu.VMEM)
SM = pl.BlockSpec(memory_space=pltpu.SMEM)
BLK = 256


def call(kernel, out, in_specs, *args, vmem=16, flops=0, moved=0, trans=0, scratch=(), name=None):
    return pl.pallas_call(
        kernel,
        out_shape=[jax.ShapeDtypeStruct(s, t) for s, t in out],
        in_specs=in_specs,
        out_specs=[VM] * len(out),
        scratch_shapes=list(scratch),
        compiler_params=params(vmem),
        cost_estimate=cost(flops, moved, trans),
        name=name,
    )(*args)


def pack_kernel(qkv, out, up, down, norm, one_ref, two_ref, three_ref, wide, a0, a1, a2, a3, sems):
    rows = up.shape[0]
    wide[...] = jnp.zeros_like(wide)
    copies = [
        pltpu.make_async_copy(src, dst, sems.at[n])
        for n, (src, dst) in enumerate(
            ((qkv, a0), (out, a1), (down, a3), (up, a2))
        )
    ]
    for c in copies:
        c.start()
    copies[0].wait()
    for part in range(3):
        one_ref[0, :, part * HALF_OUT : (part + 1) * HALF_OUT] = a0[part].astype(BF)
    copies[1].wait()
    one_ref[0, :, HALF_QKV : HALF_QKV + HALF_OUT] = a1[...].astype(BF)
    wide[0:4, 0:rows] = norm[...]
    one_ref[0, :, HALF_QKV + HALF_OUT :] = wide[...].T[0:rows].astype(BF)
    copies[2].wait()
    three_ref[0] = a3[...].astype(BF)
    copies[3].wait()
    two_ref[0] = a2[...].astype(BF)


def pack(*shards):
    rows = shards[2].shape[0]
    return call(
        pack_kernel,
        [((1, rows, ONE), BF), ((1, rows, HALF_FF), BF), ((1, rows, HALF_FF), BF)],
        [pl.BlockSpec(memory_space=pltpu.HBM)] * 4 + [VM], *shards,
        vmem=60, moved=rows * 28000,
        scratch=[pltpu.VMEM((128, 128), F32)]
        + [pltpu.VMEM(w.shape, F32) for w in shards[:4]]
        + [pltpu.SemaphoreType.DMA((4,))],
        name="pack",
    )


def assemble_kernel(first, tab, low, high, out_ref):
    for n, ref in enumerate((low, high)):
        for p in range(NB // 2):
            out_ref[tab[first + n * (NB // 2) + p]] = ref[p]


def assemble(first, tab, low, high, name):
    width = low.shape[-1]
    return call(
        partial(assemble_kernel, first),
        [((NB, RB, width), BF)],
        [SM, VM, VM], tab, low, high,
        moved=4 * D * width, name=name,
    )[0]


def weight(w_ref, first, last):
    return w_ref[:, :, first:last].reshape(D, last - first)


def norm_fwd(hidden):
    center = hidden - jnp.mean(hidden, axis=-1, keepdims=True)
    spread = jnp.mean(center * center, axis=-1, keepdims=True)
    rstd = lax.rsqrt(spread + EPS)
    return center * rstd, rstd


def norm_bwd(grad, xh, rstd, gain):
    e = grad * gain
    m1 = jnp.mean(e, axis=-1, keepdims=True)
    m2 = jnp.mean(e * xh, axis=-1, keepdims=True)
    return rstd * (e - m1 - xh * m2)


def store_turned(ref, tab, value, col, width):
    turned = value.T
    for j in range(NB):
        block = turned[j * RB : (j + 1) * RB]
        for n in range(2):
            ref[n, tab[n * NB + j], :, pl.ds(col, width)] = block


def head_masks(rows, scale):
    lane = lax.broadcasted_iota(jnp.int32, (rows, 128), 1)
    return (
        jnp.where(lane < HEAD, scale, 0.0).astype(BF),
        jnp.where(lane < HEAD, 0.0, scale).astype(BF),
    )


def stack_heads(pair, masks):
    return jnp.concatenate([pair * masks[0], pair * masks[1]], axis=0)


def merge_heads(both):
    lane = lax.broadcasted_iota(jnp.int32, (SPAN, 128), 1)
    return jnp.where(lane < HEAD, both[:SPAN], both[SPAN:])


def turn_kernel(pos, x_ref, out_ref):
    rows = x_ref.shape[0]
    for i in range(rows // BLK):
        store_turned(out_ref, At(pos, POS_EARLY), x_ref[i * BLK : (i + 1) * BLK, :], i * BLK, BLK)


def turn(pos, x):
    rows = x.shape[0]
    return call(
        turn_kernel, [((2, NB, RB, rows), BF)], [SM, VM], pos, x, moved=rows * D * 6, name="turn"
    )[0]


def attn_rows(i, x, w_ref, masks, qkv_ref, ctx_ref, lse_ref):
    r0 = pl.multiple_of(i * BLK, BLK)
    qkv = mm(x, weight(w_ref, 0, HALF_QKV)).astype(BF)
    qkv_ref[pl.ds(r0, BLK), :] = qkv
    pairs = [(s, j) for s in range(2) for j in range(3)]

    def part(n, s, j):
        return qkv[s * SPAN : (s + 1) * SPAN, n * HALF_OUT + j * 128 : n * HALF_OUT + (j + 1) * 128]

    sts = [mm(part(1, s, j), stack_heads(part(0, s, j), masks), NT) for s, j in pairs]
    tops = [jnp.max(st, axis=0, keepdims=True) for st in sts]
    exs = [jnp.exp(st - top) for st, top in zip(sts, tops)]
    totals = [jnp.sum(ex, axis=0, keepdims=True) for ex in exs]
    pts = [(ex * (1.0 / total)).astype(BF) for ex, total in zip(exs, totals)]
    parts = [merge_heads(mm(pt, part(2, s, j), TN)).astype(BF) for pt, (s, j) in zip(pts, pairs)]
    for (s, j), top, total in zip(pairs, tops, totals):
        lse_ref[i * 2 + s, j : j + 1, :] = top + jnp.log(total)
    ctx = jnp.concatenate([jnp.concatenate(parts[s * 3 : s * 3 + 3], axis=1) for s in range(2)], axis=0)
    ctx_ref[pl.ds(r0, BLK), :] = ctx
    return ctx


def attn_one_kernel(first, tab, low, high, x_ref, qkv_ref, ctx_ref, lse_ref, w_ref):
    assemble_kernel(first, tab, low, high, w_ref)
    masks = head_masks(SPAN, HEAD ** (-0.5))

    def step(i, carry):
        x = x_ref[pl.ds(pl.multiple_of(i * BLK, BLK), BLK), :]
        attn_rows(i, x, w_ref, masks, qkv_ref, ctx_ref, lse_ref)
        return carry

    lax.fori_loop(0, x_ref.shape[0] // BLK, step, 0, unroll=2)


def attn_two_kernel(
    first, tab, low, high, x_ref, wo_ref, ctxo_ref,
    qkv_ref, ctx_ref, lse_ref, xh_ref, rstd_ref, p_ref, w_ref,
):
    assemble_kernel(first, tab, low, high, w_ref)
    cols = weight(w_ref, HALF_QKV + HALF_OUT, ONE).astype(F32)
    p_ref[...] = cols.T[:8]
    masks = head_masks(SPAN, HEAD ** (-0.5))

    def step(i, carry):
        rs = pl.ds(pl.multiple_of(i * BLK, BLK), BLK)
        x = x_ref[rs, :]
        ctx = attn_rows(i, x, w_ref, masks, qkv_ref, ctx_ref, lse_ref)
        attn = x.astype(F32) + mm(ctxo_ref[rs, :], weight(wo_ref, HALF_QKV, HALF_QKV + HALF_OUT), NT)
        attn = attn + mm(ctx, weight(w_ref, HALF_QKV, HALF_QKV + HALF_OUT), NT)
        xh, rstd = norm_fwd(attn)
        rstd = jnp.broadcast_to(rstd, (BLK, 128))
        for s in range(2):
            for q in range(4):
                r = s * SPAN + q * 32
                xh_ref[q, i * 2 + s] = xh[r : r + 32]
                rstd_ref[q, i * 2 + s] = rstd[r : r + 32]
        return carry

    lax.fori_loop(0, x_ref.shape[0] // BLK, step, 0, unroll=2)


def attn_shapes(rows):
    return [((rows, HALF_QKV), BF), ((rows, HALF_OUT), BF), ((rows // SPAN, 8, 2 * SPAN), F32)]


def attn_one(first, tab, low, high, x):
    rows = x.shape[0]
    return call(
        partial(attn_one_kernel, first), attn_shapes(rows) + [((NB, RB, ONE), BF)],
        [SM, VM, VM, VM], tab, low, high, x,
        vmem=16, flops=rows * 4e6, moved=rows * 8000 + 2e6, trans=rows * 800, name="attn_one",
    )


def attn_two(first, tab, low, high, x, w_own, ctx_own):
    rows = x.shape[0]
    spans = rows // SPAN
    out = attn_shapes(rows) + [
        ((4, spans, 32, D), F32),
        ((4, spans, 32, 128), F32),
        ((8, D), F32),
        ((NB, RB, ONE), BF),
    ]
    return call(
        partial(attn_two_kernel, first), out, [SM] + [VM] * 5, tab, low, high, x, w_own, ctx_own,
        vmem=16, flops=rows * 5e6, moved=rows * 12000 + 4e6, trans=rows * 800, name="attn_two",
    )


def gelu_pair(u):
    a = jnp.abs(u)
    d = 1.0 + (0.3275911 * 0.5**0.5) * a
    t = pl.reciprocal(d, approx=True)
    t = t * (2.0 - d * t)
    e = jnp.exp(-0.5 * u * u)
    poly = 0.5307027145 * t - 0.7265760135
    poly = poly * t + 0.7107068705
    poly = poly * t - 0.142248368
    poly = poly * t + 0.127414796
    tail = (poly * t) * e
    phi = jnp.where(u >= 0.0, 1.0 - tail, tail)
    return u * phi, phi + (0.3989422804014327 * u) * e


TILE = 512


def ffn_up_kernel(pos, xh_ref, p_ref, w_ref, g_ref, gp_ref, *yt_ref):
    def step(i, carry):
        rs = pl.ds(pl.multiple_of(i * BLK, BLK), BLK)
        y = xh_ref[rs, :] * p_ref[0:1, :] + p_ref[1:2, :]
        yb = y.astype(BF)
        if yt_ref:
            store_turned(yt_ref[0], At(pos, POS_EARLY), yb, pl.multiple_of(i * BLK, BLK), BLK)
        for t in range(HALF_FF // TILE):
            u = mm(yb, weight(w_ref, t * TILE, (t + 1) * TILE))
            g, gp = gelu_pair(u)
            g_ref[rs, t * TILE : (t + 1) * TILE] = g.astype(BF)
            gp_ref[rs, t * TILE : (t + 1) * TILE] = gp.astype(BF)
        return carry

    lax.fori_loop(0, xh_ref.shape[0] // BLK, step, 0, unroll=2)


def ffn_up(pos, xh, prow, w, turned, name):
    rows = xh.shape[0]
    out = [((rows, HALF_FF), BF), ((rows, HALF_FF), BF)]
    if turned:
        out.append(((2, NB, RB, rows), BF))
    return call(
        ffn_up_kernel, out, [SM, VM, VM, VM], pos, xh, prow, w,
        vmem=16, flops=rows * 2.4e6, moved=rows * 9000 + 2e6, trans=rows * 6000, name=name,
    )


def down_block(r0, xh1_ref, p_ref, acts, downs):
    rs = pl.ds(r0, BLK)
    total = xh1_ref[rs, :] * p_ref[0:1, :] + p_ref[1:2, :]
    for g_ref, w_ref in zip(acts, downs):
        total = total + mm(g_ref[rs, :], weight(w_ref, 0, HALF_FF), NT)
    return norm_fwd(total)


def first_kernel(xh1_ref, p_ref, g0, g1, d0, d1, mixed_ref, cls_ref, xh_ref, rstd_ref):
    xh, rstd = down_block(0, xh1_ref, p_ref, (g0, g1), (d0, d1))
    xh_ref[...] = xh
    rstd_ref[...] = jnp.broadcast_to(rstd, rstd_ref.shape)
    out = (xh * p_ref[2:3, :] + p_ref[3:4, :]).reshape(mixed_ref.shape)
    mixed_ref[...] = out.astype(BF)
    cls_ref[...] = out[:, 0, :]


def first_rows(xh1, prow, acts, downs):
    spans = BLK // 32
    return call(
        first_kernel,
        [((spans, 32, D), BF), ((spans, D), F32), ((BLK, D), F32), ((BLK, 128), F32)],
        [VM] * 6, xh1, prow, *acts, *downs,
        vmem=8, flops=BLK * 4.8e6, moved=BLK * 16000 + 5e6, name="first_rows",
    )


def back_block(r0, grad, xh2, rstd2, gps, xh1_ref, rstd1_ref, p_ref, ups, downs, dus):
    rs = pl.ds(r0, BLK)
    sum_g2 = jnp.sum(grad * xh2, axis=0, keepdims=True)
    sum_b2 = jnp.sum(grad, axis=0, keepdims=True)
    dh = norm_bwd(grad, xh2, rstd2, p_ref[2:3, :])
    df = dh.astype(BF)
    total = dh
    for gp_ref, up_ref, down_ref, du_ref in zip(gps, ups, downs, dus):
        for t in range(HALF_FF // TILE):
            lo, hi = t * TILE, (t + 1) * TILE
            dg = mm(df, weight(down_ref, lo, hi))
            du_ref[:, lo:hi] = (dg * gp_ref[rs, lo:hi].astype(F32)).astype(BF)
        total = total + mm(du_ref[...], weight(up_ref, 0, HALF_FF), NT)
    xh1 = xh1_ref[rs, :]
    sum_g1 = jnp.sum(total * xh1, axis=0, keepdims=True)
    sum_b1 = jnp.sum(total, axis=0, keepdims=True)
    dh1 = norm_bwd(total, xh1, rstd1_ref[rs, 0:1], p_ref[0:1, :])
    return df, dh1, (sum_g1, sum_b1, sum_g2, sum_b2)


def back_shapes():
    return [
        ((2, NB, RB, BLK), BF),
        ((BLK, HALF_FF), BF),
        ((BLK, HALF_FF), BF),
        ((BLK // 32, 32, D), F32),
        ((8, D), F32),
    ]


def rest_kernel(
    at, pos, xh1_ref, rstd1_ref, p_ref, g0, g1, gp0, gp1, cot_ref, u0, u1, d0, d1,
    dft_ref, du0_ref, du1_ref, dh1_ref, sums_ref, mixed_ref,
):
    r0, c0 = at * BLK, at * 32
    xh, rstd = down_block(r0, xh1_ref, p_ref, (g0, g1), (d0, d1))
    out = xh * p_ref[2:3, :] + p_ref[3:4, :]
    mixed_ref[...] = out.reshape(mixed_ref.shape).astype(BF)
    grad = cot_ref[:, c0 : c0 + 32, :].astype(F32).reshape(BLK, D)
    df, dh1, sums = back_block(
        r0, grad, xh, rstd, (gp0, gp1), xh1_ref, rstd1_ref, p_ref, (u0, u1), (d0, d1), (du0_ref, du1_ref)
    )
    store_turned(dft_ref, At(pos, POS_LATE), df, 0, BLK)
    dh1_ref[...] = dh1.reshape(dh1_ref.shape)
    for n in range(4):
        sums_ref[n : n + 1, :] = sums[n]


def rest_rows(at, pos, xh1, rstd1, prow, acts, gps, cot, ups, downs):
    return call(
        partial(rest_kernel, at),
        back_shapes() + [((BLK // 32, 32, D), BF)],
        [SM] + [VM] * 12, pos, xh1, rstd1, prow, *acts, *gps, cot, *ups, *downs,
        vmem=16, flops=BLK * 14.5e6, moved=BLK * 40000 + 1e7, name=f"rest_rows_{at}",
    )


def class_kernel(
    pos, cls_ref, cot_ref, xh2_ref, rstd2_ref, xh1_ref, rstd1_ref, p_ref, gp0, gp1, u0, u1, d0, d1,
    dft_ref, du0_ref, du1_ref, dh1_ref, sums_ref,
):
    spans = cls_ref.shape[0]
    grad = cot_ref[:, 0:32, :].astype(F32)
    first = lax.broadcasted_iota(jnp.int32, grad.shape, 1) == 0
    grad = grad + jnp.where(first, cls_ref[...].reshape(spans, 1, D), 0.0)
    grad = grad.reshape(BLK, D)
    df, dh1, sums = back_block(
        0, grad, xh2_ref[...], rstd2_ref[:, 0:1], (gp0, gp1), xh1_ref, rstd1_ref, p_ref,
        (u0, u1), (d0, d1), (du0_ref, du1_ref),
    )
    store_turned(dft_ref, At(pos, POS_LATE), df, 0, BLK)
    dh1_ref[...] = dh1.reshape(dh1_ref.shape)
    for n in range(4):
        sums_ref[n : n + 1, :] = sums[n]


def class_rows(pos, grad_cls, cot, xh2, rstd2, xh1, rstd1, prow, gps, ups, downs):
    return call(
        class_kernel,
        back_shapes(),
        [SM] + [VM] * 13, pos, grad_cls, cot, xh2, rstd2, xh1, rstd1, prow, *gps, *ups, *downs,
        vmem=16, flops=BLK * 9.7e6, moved=BLK * 30000 + 1e7, name="class_rows",
    )


def contrast_kernel(where, doc_ref, cls_ref, loss_ref, grad_ref, rows, own_doc):
    spans = doc_ref.shape[1]
    doc_row = doc_ref[...].astype(F32)
    doc_col = jnp.broadcast_to(doc_row, (128, spans)).T[:, 0:1]
    blocks, per = cls_ref.shape[0], cls_ref.shape[1]
    where = At(where, CLASS_AT)
    me = where[0]
    for n in range(blocks):
        rows[where[1 + n]] = cls_ref[n].astype(F32)
    a = rows[...].reshape(spans, D).astype(BF)
    own = rows[me].astype(BF)
    scale = D ** (-0.5)
    col = lax.broadcasted_iota(jnp.int32, (spans, spans), 1)
    row = lax.broadcasted_iota(jnp.int32, (spans, spans), 0)
    logits = mm(a, a, NT) * scale
    partner = (doc_col == doc_row) & (row != col)
    masked = jnp.where(row == col, -1000000000.0, logits)
    top = jnp.max(masked, axis=0, keepdims=True)
    lse = jnp.log(jnp.sum(jnp.exp(masked - top), axis=0, keepdims=True)) + top
    positive = jnp.sum(jnp.where(partner, logits, 0.0), axis=0, keepdims=True)
    flagged = jnp.max(jnp.where(partner, 1.0, 0.0), axis=0, keepdims=True)
    count = jnp.sum(flagged, axis=1, keepdims=True)
    loss = jnp.sum(flagged * (lse - positive), axis=1, keepdims=True) / count
    loss_ref[...] = jnp.broadcast_to(loss, loss_ref.shape)

    weight_row = flagged * (CONTRAST * spans) / count
    own_doc[...] = doc_col.reshape(blocks, per, 1)
    docs = own_doc[me]
    col = lax.broadcasted_iota(jnp.int32, (per, spans), 1)
    row = lax.broadcasted_iota(jnp.int32, (per, spans), 0) + me * per
    logits = mm(own, a, NT) * scale
    same = jnp.where((docs == doc_row) & (row != col), 1.0, 0.0)
    masked = jnp.where(row == col, -1000000000.0, logits)
    top = jnp.max(masked, axis=1, keepdims=True)
    ex = jnp.exp(masked - top)
    soft = ex / jnp.sum(ex, axis=1, keepdims=True)
    own_weight = jnp.max(same, axis=1, keepdims=True) * (CONTRAST * spans) / count
    sym = own_weight * (soft - same) + weight_row * (jnp.exp(masked - lse) - same)
    high = sym.astype(BF)
    low = (sym - high.astype(F32)).astype(BF)
    grad_ref[...] = (mm(high, a) + mm(low, a)) * scale


def contrast(where, doc_row, cls_all):
    blocks, per, _ = cls_all.shape
    spans = blocks * per
    return call(
        contrast_kernel,
        [((1, 128), F32), ((per, D), F32)],
        [SM, VM, VM],
        where, doc_row, cls_all,
        vmem=8 if spans <= 256 else 40, flops=2 * spans * spans * D, moved=spans * D * 2,
        scratch=[pltpu.VMEM((blocks, per, D), F32), pltpu.VMEM((blocks, per, 1), F32)],
        name="contrast",
    )


def turned_of(refs, n):
    return jnp.concatenate([ref[n].reshape(D, ref.shape[3]) for ref in refs], axis=1)


def grad_other_kernel(count, *refs):
    xts, ys, out_ref = refs[:count], refs[count:-1], refs[-1]
    xt = turned_of(xts, 1)
    for t in range(HALF_FF // TILE):
        lo, hi = t * TILE, (t + 1) * TILE
        grad = mm(xt, jnp.concatenate([y[:, lo:hi] for y in ys], axis=0))
        out_ref[:, :, lo:hi] = grad.astype(BF).reshape(NB, RB, TILE)


def grad_other(xts, ys, name):
    rows = sum(y.shape[0] for y in ys)
    return call(
        partial(grad_other_kernel, len(xts)),
        [((NB, RB, HALF_FF), BF)],
        [VM] * (len(xts) + len(ys)), *xts, *ys,
        vmem=12, flops=2 * rows * D * HALF_FF, moved=rows * 8000 + 2.4e6, name=name,
    )[0]


def grad_own_kernel(count, came_ref, *refs):
    xts, ys, keep_ref, send_ref = refs[:count], refs[count:-2], refs[-2], refs[-1]
    nh = NB // 2
    xt = turned_of(xts, 0)
    for t in range(HALF_FF // TILE):
        lo, hi = t * TILE, (t + 1) * TILE
        grad = mm(xt, jnp.concatenate([y[:, lo:hi] for y in ys], axis=0))
        grad = (grad.reshape(NB, RB, TILE) + came_ref[:, :, lo:hi].astype(F32)).astype(BF)
        keep_ref[:, :, lo:hi] = grad[:nh]
        send_ref[:, :, lo:hi] = grad[nh:]


def grad_own(xts, ys, came, name):
    rows = sum(y.shape[0] for y in ys)
    return call(
        partial(grad_own_kernel, len(xts)),
        [((NB // 2, RB, HALF_FF), BF)] * 2,
        [VM] * (1 + len(xts) + len(ys)), came, *xts, *ys,
        vmem=12, flops=2 * rows * D * HALF_FF, moved=rows * 8000 + 4.8e6, name=name,
    )


def natural(refs, i):
    return jnp.concatenate([ref[i * 2 + s] for s in range(2) for ref in refs], axis=0)


def attn_back_kernel(pos, r0_ref, r1_ref, r2_ref, r3_ref, qkv_ref, lse_ref, w_ref, dqkv_ref, *dat_ref):
    masks = head_masks(SPAN, HEAD ** (-0.5))
    plain = head_masks(SPAN, 1.0)
    spans = r0_ref.shape[0]

    def step(i, carry):
        r0 = pl.multiple_of(i * BLK, BLK)
        da = natural((r0_ref, r1_ref, r2_ref, r3_ref), i).astype(BF)
        if dat_ref:
            store_turned(dat_ref[0], At(pos, POS_EARLY), da, r0, BLK)
        dctx = mm(da, weight(w_ref, HALF_QKV, HALF_QKV + HALF_OUT)).astype(BF)
        pairs = [(s, j) for s in range(2) for j in range(3)]

        def part(ref, n, s, j):
            rs = pl.ds(pl.multiple_of(r0 + s * SPAN, SPAN), SPAN)
            return ref.at[rs, n * HALF_OUT + j * 128 : n * HALF_OUT + (j + 1) * 128]

        qs = [stack_heads(part(qkv_ref, 0, s, j)[...], masks) for s, j in pairs]
        ks = [part(qkv_ref, 1, s, j)[...] for s, j in pairs]
        sts = [mm(k, q, NT) for k, q in zip(ks, qs)]
        dcs = [stack_heads(dctx[s * SPAN : (s + 1) * SPAN, j * 128 : (j + 1) * 128], plain) for s, j in pairs]
        dpts = [mm(part(qkv_ref, 2, s, j)[...], dc, NT) for (s, j), dc in zip(pairs, dcs)]
        pts = [jnp.exp(st - lse_ref[i * 2 + s, j : j + 1, :]) for (s, j), st in zip(pairs, sts)]
        dvs = [mm(pt.astype(BF), dc) for pt, dc in zip(pts, dcs)]
        dsts = [
            (pt * (dpt - jnp.sum(pt * dpt, axis=0, keepdims=True))).astype(BF) for pt, dpt in zip(pts, dpts)
        ]
        dks = [mm(dst, q) for dst, q in zip(dsts, qs)]
        dqs = [merge_heads(mm(dst, k, TN)) * HEAD ** (-0.5) for dst, k in zip(dsts, ks)]
        for n, grads in enumerate((dqs, dks, dvs)):
            for (s, j), grad in zip(pairs, grads):
                part(dqkv_ref, n, s, j)[...] = grad.astype(BF)
        return carry

    lax.fori_loop(0, spans // 2, step, 0, unroll=2)


def attn_back(pos, dh1, qkv, lse, w, turned, name):
    rows = qkv.shape[0]
    out = [((rows, HALF_QKV), BF)]
    if turned:
        out.append(((2, NB, RB, rows), BF))
    return call(
        attn_back_kernel, out,
        [SM] + [VM] * 7, pos, *dh1, qkv, lse, w,
        vmem=16, flops=rows * 6e6, moved=rows * 10000 + 3e6, trans=rows * 800, name=name,
    )


def last_value(order, xt_ref, dqkv_ref, dat_ref, ctx_ref, t):
    rows = xt_ref.shape[3]
    if t < 3:
        return mm(xt_ref[order].reshape(D, rows), dqkv_ref[:, t * HALF_OUT : (t + 1) * HALF_OUT])
    return mm(dat_ref[order].reshape(D, rows), ctx_ref[...])


def norm_columns(sums):
    total = sums[0][0:4, :]
    for ref in sums[1:]:
        total = total + ref[0:4, :]
    return jnp.concatenate([total, jnp.zeros((124, D), F32)], axis=0).T


def last_other_kernel(pos, xt_ref, dqkv_ref, dat_ref, ctx_ref, s0, s1, s2, s3, out_ref):
    for t in range(4):
        grad = last_value(1, xt_ref, dqkv_ref, dat_ref, ctx_ref, t)
        lo = t * HALF_OUT
        out_ref[:, :, lo : lo + HALF_OUT] = grad.astype(BF).reshape(NB, RB, HALF_OUT)
    norm = norm_columns((s0, s1, s2, s3)).astype(BF)
    for j in range(NB):
        out_ref[pos[POS_EARLY + NB + j], :, HALF_QKV + HALF_OUT :] = norm[j * RB : (j + 1) * RB]


def last_other(pos, xt, dqkv, dat, ctx, sums):
    rows = xt.shape[3]
    return call(
        last_other_kernel,
        [((NB, RB, ONE), BF)],
        [SM] + [VM] * 8, pos, xt, dqkv, dat, ctx, *sums,
        vmem=12, flops=2 * rows * D * HALF_FF, moved=rows * 8000 + 2.4e6, name="last_other",
    )[0]


def last_own_kernel(
    pos, xt_ref, dqkv_ref, dat_ref, ctx_ref, s0, s1, s2, s3, came_ref, keep_ref, send_ref, cols
):
    nh = NB // 2
    norm = norm_columns((s0, s1, s2, s3))
    for j in range(NB):
        cols[pos[POS_EARLY + j]] = norm[j * RB : (j + 1) * RB]
    for t in range(5):
        lo = t * HALF_OUT
        hi = min(lo + HALF_OUT, ONE)
        if t < 4:
            grad = last_value(0, xt_ref, dqkv_ref, dat_ref, ctx_ref, t).reshape(NB, RB, HALF_OUT)
        else:
            grad = cols[...]
        grad = (grad + came_ref[:, :, lo:hi].astype(F32)).astype(BF)
        keep_ref[:, :, lo:hi] = grad[:nh]
        send_ref[:, :, lo:hi] = grad[nh:]


def last_own(pos, xt, dqkv, dat, ctx, sums, came):
    rows = xt.shape[3]
    return call(
        last_own_kernel,
        [((NB // 2, RB, ONE), BF)] * 2,
        [SM] + [VM] * 9, pos, xt, dqkv, dat, ctx, *sums, came,
        vmem=12, flops=2 * rows * D * HALF_FF, moved=rows * 8000 + 4.8e6,
        scratch=[pltpu.VMEM((NB, RB, 128), F32)], name="last_own",
    )


def input_grad_kernel(r0_ref, r1_ref, r2_ref, r3_ref, own_ref, other_ref, w0_ref, w1_ref, out_ref):
    spans = r0_ref.shape[0]

    def step(i, carry):
        rs = pl.ds(pl.multiple_of(i * BLK, BLK), BLK)
        total = natural((r0_ref, r1_ref, r2_ref, r3_ref), i)
        total = total + mm(own_ref[rs, :], weight(w0_ref, 0, HALF_QKV), NT)
        total = total + mm(other_ref[rs, :], weight(w1_ref, 0, HALF_QKV), NT)
        out_ref[rs, :] = total
        return carry

    lax.fori_loop(0, spans // 2, step, 0, unroll=2)


def input_grads(dh1, own, other, w_own, w_other):
    rows = own.shape[0]
    return call(
        input_grad_kernel,
        [((rows, D), F32)],
        [VM] * 8, *dh1, own, other, w_own, w_other,
        vmem=12, flops=rows * 3.6e6, moved=rows * 12000 + 5e6, name="input_grads",
    )[0]


def place_kernel(half, *refs):
    own, other, g_own, g_other = refs[0:4], refs[4:8], refs[8], refs[9]
    mixed_ref, grad_ref, sems = refs[10:]
    spans = g_own.shape[0]
    copies = []
    for n, (pieces, g) in enumerate(((own, g_own), (other, g_other))):
        at = pl.ds(half[HALF_AT + n] * spans, spans)
        for q in range(4):
            to = mixed_ref.at[at, 32 * q : 32 * q + 32, :]
            copies.append(pltpu.make_async_copy(pieces[q], to, sems.at[5 * n + q]))
        copies.append(pltpu.make_async_copy(g, grad_ref.at[at], sems.at[5 * n + 4]))
    for c in copies:
        c.start()
    for c in copies:
        c.wait()


def place(half, own, other, g_own, g_other):
    spans = own[0].shape[0]
    g_own, g_other = (g.reshape(spans, SPAN, D) for g in (g_own, g_other))
    return pl.pallas_call(
        place_kernel,
        out_shape=[
            jax.ShapeDtypeStruct((2 * spans, SPAN, D), BF),
            jax.ShapeDtypeStruct((2 * spans, SPAN, D), F32),
        ],
        in_specs=[SM] + [VM] * 10,
        out_specs=[HBM] * 2,
        scratch_shapes=[pltpu.SemaphoreType.DMA((10,))],
        compiler_params=params(16),
        cost_estimate=cost(0, spans * SPAN * D * 24),
        name="place",
    )(half, *own, *other, g_own, g_other)


def squares_kernel(k0, c0, k1, c1, k2, c2, g0, g1, g2, sq_ref):
    main = HALF_QKV + HALF_OUT
    total = jnp.zeros((1, 1), F32)
    for keep, came, out in ((k0, c0, g0), (k1, c1, g1), (k2, c2, g2)):
        grad = keep[0].astype(F32) + came[0].astype(F32)
        out[...] = grad
        sq = jnp.sum(grad[:, :main] * grad[:, :main], axis=1, keepdims=True)
        if grad.shape[1] > main:
            cols = grad[:, main:]
            sq = sq + 0.5 * jnp.sum(cols * cols, axis=1, keepdims=True)
        total = total + jnp.sum(sq, axis=0, keepdims=True)
    sq_ref[...] = jnp.broadcast_to(total, sq_ref.shape)


def squares_of(pairs):
    shard = pairs[0][0].shape[1]
    out = [((shard, k.shape[2]), F32) for k, _ in pairs] + [((8, 128), F32)]
    flat = [a for pair in pairs for a in pair]
    return call(squares_kernel, out, [VM] * 6, *flat, vmem=8, moved=shard * 40000, name="squares")


def adam_parts(weight, gradient, moment_one, moment_two, step_rate, decay_rate):
    first_new = 0.9 * moment_one + 0.1 * gradient
    second_new = 0.999 * moment_two + 0.001 * gradient * gradient
    corr_first = first_new * (1.0 / (1.0 - 0.9**STEP))
    corr_second = second_new * (1.0 / (1.0 - 0.999**STEP))
    weight_new = weight - step_rate * (
        corr_first / (jnp.sqrt(corr_second) + 1e-08) + decay_rate * weight
    )
    return first_new, second_new, weight_new


def adam_kernel(sq_ref, last_ref, up_ref, down_ref, cols_ref, *refs):
    ins, outs, wide = refs[:15], refs[15:-1], refs[-1]
    norm = jnp.sqrt(sq_ref[0:1, 0:1])
    outs[15][...] = jnp.broadcast_to(norm, outs[15].shape)
    scale = 1.0 / jnp.maximum(norm, 1.0)

    def update(n, at, grad, rate, decay):
        new = adam_parts(ins[n][at], grad * scale, ins[5 + 2 * n][at], ins[6 + 2 * n][at], rate, decay)
        for m in range(3):
            outs[3 * n + m][at] = new[m]

    for part in range(3):
        update(0, part, last_ref[:, part * HALF_OUT : (part + 1) * HALF_OUT], 0.02, 0.01)
    update(1, Ellipsis, last_ref[:, HALF_QKV : HALF_QKV + HALF_OUT], 0.02, 0.01)
    update(2, Ellipsis, up_ref[...], 0.02, 0.01)
    update(3, Ellipsis, down_ref[...], 0.02, 0.01)
    shard = last_ref.shape[0]
    wide[...] = jnp.zeros_like(wide)
    wide[0:shard, :] = 0.5 * (last_ref[:, HALF_QKV + HALF_OUT :] + cols_ref[...])
    update(4, Ellipsis, wide[...].T[0:4, 0:shard], 0.5, 0.0)


def adam(squares, last, up, down, cols, weights, moments):
    shapes = [w.shape for w in weights]
    out = [(s, F32) for s in shapes for _ in range(3)] + [((8, 128), F32)]
    args = (squares, last, up, down, cols, *weights, *moments)
    return call(
        adam_kernel, out, [VM] * len(args), *args, vmem=16, moved=7 * 4 * last.shape[0] * 4608,
        scratch=[pltpu.VMEM((128, 128), F32)], name="adam",
    )


def after(value, *others):
    return lax.optimization_barrier((value, others))[0]


def body(
    tokens,
    cotangent,
    span_doc,
    qkv_weight,
    out_weight,
    ffn_in_weight,
    ffn_out_weight,
    norm_params,
    qkv_first,
    qkv_second,
    out_first,
    out_second,
    ffn_in_first,
    ffn_in_second,
    ffn_out_first,
    ffn_out_second,
    norm_first,
    norm_second,
):
    n_dp = lax.axis_size("dp")
    dp = lax.axis_index("dp")
    core = lax.axis_index("tensor")
    shard = D // n_dp
    rows = tokens.shape[0] // 2
    spans = rows // SPAN
    direct = n_dp == NB
    early, late = bit_orders(n_dp)
    steps = len(early[0])
    last = steps - 1

    tab = lax.dynamic_index_in_dim(device_tables(n_dp), dp * 2 + core, 0, keepdims=False)
    x = lax.dynamic_slice_in_dim(tokens, core * rows, rows, 0)
    cot = lax.dynamic_slice_in_dim(cotangent, core * rows, rows, 0).reshape(spans, SPAN, D)

    def places(orders, other=0):
        return dp ^ jnp.array([rel_of(order) for order in orders], jnp.int32)[core ^ other]

    def send_on(block, orders, k):
        return lax.ppermute(block, AXES, pairs_of(n_dp, orders, k))

    def join(held, came):
        return jnp.concatenate([held, came], axis=0)

    def pieces(at, low, high):
        if direct:
            return at, tab, low, high
        which = {AT_EARLY: places(early), AT_LATE: places(late), AT_OTHER: places(early, 1)}[at]
        full = join(low, high)[jnp.argsort(which)].reshape(NB, RB, -1)
        return at, tab, full[: NB // 2], full[NB // 2 :]

    def halves(orders, keep, send):
        if direct:
            return keep, send
        full = join(keep, send).reshape(n_dp, shard, -1)[places(orders)]
        return full[: n_dp // 2], full[n_dp // 2 :]

    def add(keep, came):
        total = keep.astype(F32) + came.astype(F32)
        size = total.shape[0] // 2
        return total[:size].astype(BF), total[size:].astype(BF)

    turned = ((1, 0, 2), (1, 0), (0, 1), (1, 0), (0, 1))
    weights = (qkv_weight, out_weight, ffn_in_weight, ffn_out_weight, norm_params)
    weights = tuple(w.transpose(t) for w, t in zip(weights, turned))
    one, up, down = pack(*weights)
    one_came = send_on(one, early, 0)
    up_came = send_on(up, late, 0)
    down_came = send_on(down, early, 0)
    one, tab, x, cot, down_came = after((join(one, one_came), tab, x, cot, down_came), up_came)
    for k in range(1, last):
        one_came = send_on(one, early, k)
        if k == 1:
            tokt = turn(tab, x)
            one_came = after(one_came, tokt)
        else:
            up = after(join(up, up_came), one)
            up_came = send_on(up, late, k - 1)
        one = join(one, one_came)
        if k > 1:
            one = after(one, up_came)
    one_came = send_on(one, early, last)
    for k in range(max(last - 1, 1), last):
        up = join(up, up_came)
        up_came = send_on(up, late, k)
    one, one_came = after((one, one_came), up_came)
    up = after(join(up, up_came), one_came)
    up_came = send_on(up, late, last)
    down = after(join(down, down_came), one_came)
    down_came = send_on(down, early, 1)

    one_other = (core_swap(one), core_swap(one_came))
    qkv0, ctx0, lse0, w10 = attn_one(*pieces(AT_EARLY, one, one_came), x)
    ctx0 = after(ctx0, down_came)
    for k in range(2, last):
        down = join(down, after(down_came, ctx0))
        down_came = send_on(down, early, k)
    qkv1, ctx1, lse1, xh1, rstd1, prow, w11 = attn_two(*pieces(AT_OTHER, *one_other), x, w10, ctx0)
    w1 = (w10, w11)
    xh1 = xh1.reshape(rows, D)
    rstd1 = rstd1.reshape(rows, 128)
    up_came, down_came = after((up_came, down_came), xh1)
    wu = assemble(*pieces(AT_LATE, up, up_came), "up_own")
    wu = (wu, core_swap(wu))
    down = join(down, down_came)
    down_came = send_on(down, early, last)
    act0, gp0, yt = ffn_up(tab, after(xh1, down), prow, wu[0], True, "ffn_up_own")
    wd = assemble(*pieces(AT_EARLY, down, after(down_came, act0)), "down_own")
    wd = (wd, core_swap(wd))
    act1, gp1 = ffn_up(tab, after(xh1, wd[0]), prow, wu[1], False, "ffn_up_other")
    acts, gps = (act0, act1), (gp0, gp1)
    mixed0, cls_own, xh2, rstd2 = first_rows(xh1, prow, acts, wd)

    held = cls_own.astype(BF)[None]
    back = []
    for k in reversed(range(steps)):
        came = lax.ppermute(held, "dp", [(d, d ^ (1 << k)) for d in range(n_dp)])
        if len(back) < 3:
            at = len(back) + 1
            back.append(rest_rows(at, tab, after(xh1, held), rstd1, prow, acts, gps, cot, wu, wd))
            came = after(came, back[-1][4])
        held = join(held, came)
    held = join(held, core_swap(held))
    loss, grad_cls = contrast(tab, span_doc.reshape(1, -1), held)
    back.insert(0, (*class_rows(tab, grad_cls, cot, xh2, rstd2, xh1, rstd1, prow, gps, wu, wd), mixed0))
    dft, du0, du1, dh1, sums, mixed_own = zip(*back)

    d_other = grad_other(dft, (act1,), "grad_down_other")
    d_came = core_swap(d_other)
    u_other = grad_other((after(yt, d_other),), du1, "grad_up_other")
    u_came = core_swap(u_other)
    d_keep, d_send = halves(
        late, *grad_own((after(dft[0], u_other),) + dft[1:], (act0,), d_came, "grad_down_own")
    )
    d_came = send_on(d_send, late, last)
    u_keep, u_send = halves(early, *grad_own((after(yt, d_keep),), du0, u_came, "grad_up_own"))
    dh1 = (after(dh1[0], u_keep),) + dh1[1:]
    dqkv1, dat = attn_back(tab, dh1, qkv1, lse1, w1[1], True, "attn_back_other")
    l_other = last_other(tab, tokt, dqkv1, dat, ctx1, sums)

    d_came, l_other = after((d_came, l_other))
    d_keep, d_send = add(d_keep, d_came)
    u_came = send_on(after(u_send, l_other), early, last)
    d_came = send_on(d_send, late, last - 1)
    l_came = core_swap(l_other)
    (dqkv0,) = attn_back(
        tab, (after(dh1[0], l_other),) + dh1[1:], qkv0, lse0, w1[0], False, "attn_back_own"
    )
    l_keep, l_send = halves(early, *last_own(tab, tokt, dqkv0, dat, ctx0, sums, l_came))
    l_came = send_on(l_send, early, last)
    grad_in = input_grads((after(dh1[0], l_send),) + dh1[1:], dqkv0, dqkv1, w1[0], w1[1])
    u_came, d_came = after((u_came, d_came), l_send)
    u_keep, u_send = add(u_keep, u_came)
    d_keep, d_send = add(d_keep, d_came)
    u_came = send_on(u_send, early, last - 1)
    d_came = send_on(d_send, late, last - 2)
    for k in reversed(range(last)):
        l_came, u_came, d_came = after((l_came, u_came, d_came))
        l_keep, l_send = add(l_keep, l_came)
        l_came = send_on(l_send, early, k)
        if k > 0:
            u_keep, u_send = add(u_keep, u_came)
            u_came = send_on(u_send, early, k - 1)
        if k > 1:
            d_keep, d_send = add(d_keep, d_came)
            d_came = send_on(d_send, late, k - 2)
        if k == last - 1:
            grad_came = core_swap(after(grad_in, l_send))
            mixed_other = tuple(core_swap(m) for m in after(mixed_own, l_send))
            l_came = after(l_came, grad_came, mixed_other)
        if k == last - 2:
            mixed, input_grad = place(tab, mixed_own, mixed_other, after(grad_in, l_send), grad_came)
            l_came = after(l_came, input_grad)

    last_grad, down_grad, up_grad, squares = squares_of(((l_keep, l_came), (d_keep, d_came), (u_keep, u_came)))
    cols = core_swap(last_grad[:, HALF_QKV + HALF_OUT :])
    squares = squares + core_swap(squares)
    bits = [1 << k for k in reversed(range(steps))]
    for one_bit, two_bit in zip(bits[::2], bits[1::2]):
        near, far, both = (
            lax.ppermute(squares, "dp", [(d, d ^ b) for d in range(n_dp)])
            for b in (one_bit, two_bit, one_bit ^ two_bit)
        )
        squares = (squares + near) + (far + both)
    moments = (
        qkv_first, qkv_second, out_first, out_second, ffn_in_first, ffn_in_second,
        ffn_out_first, ffn_out_second, norm_first, norm_second,
    )
    new = adam(
        squares, last_grad, up_grad, down_grad, cols,
        weights,
        [m.transpose(turned[n // 2]) for n, m in enumerate(moments)],
    )
    updated = [value.transpose(turned[n // 3]) for n, value in enumerate(new[:15])]
    return (
        mixed.reshape(2 * rows, D),
        input_grad.reshape(2 * rows, D),
        loss[0, 0],
        new[15][0, 0],
        *updated,
    )


def solution(mesh):
    rows = P("dp", None)
    qkv = P("dp", None, "tensor")
    turned = P("tensor", "dp")
    up = P("dp", "tensor")
    norm = P(None, "dp")
    weights = (qkv, turned, up, turned, norm)
    moments = tuple(spec for spec in weights for _ in range(2))
    updated = tuple(spec for spec in weights for _ in range(3))
    return jax.shard_map(
        body,
        mesh=mesh,
        in_specs=(rows, rows, P()) + weights + moments,
        out_specs=(rows, rows, P(), P()) + updated,
        check_vma=False,
    )
```

```python
from functools import partial

import jax
import jax.numpy as jnp
import numpy as np
from jax import lax
from jax.experimental import pallas as pl
from jax.experimental.pallas import tpu as pltpu
from jax.sharding import PartitionSpec as P

HEAD = 64
SPAN = 128
STEP = 10
D = 768
FF = 3072
NB = 16
RB = D // NB
HALF_QKV = 1152
HALF_OUT = 384
HALF_FF = 1536
ONE = HALF_QKV + HALF_OUT + 128
CONTRAST = 4.0
EPS = 1e-06
BF = jnp.bfloat16
F32 = jnp.float32
AXES = ("dp", "tensor")
SHRINK = 100

NN = (((1,), (0,)), ((), ()))
NT = (((1,), (1,)), ((), ()))
TN = (((0,), (0,)), ((), ()))


def mm(left, right, dims=NN):
    return lax.dot_general(left, right, dims, preferred_element_type=F32)


def params(vmem=56):
    vmem = vmem if vmem > 24 else min(vmem, 8)
    return pltpu.CompilerParams(vmem_limit_bytes=vmem * 2**20)


def cost(flops, bytes_accessed, trans=0):
    flops, bytes_accessed, trans = (n // SHRINK + 1 for n in (flops, bytes_accessed, trans))
    return pl.CostEstimate(flops=int(flops), bytes_accessed=int(bytes_accessed), transcendentals=int(trans))


HBM = pl.BlockSpec(memory_space=pl.ANY)


def bit_orders(n_dp):
    bits = n_dp.bit_length() - 1
    if bits == 4:
        return ((4, 8, 2, 1), (8, 4, 1, 2)), ((1, 4, 8, 2), (2, 8, 4, 1)), ((4, 2, 8, 1), (8, 1, 4, 2))
    up = tuple(1 << b for b in range(bits))[::-1]
    both = (up, up[: bits // 2] + up[bits // 2 :][::-1])
    return both, both, both


def pairs_of(n_dp, orders, step):
    out = []
    for d in range(n_dp):
        for c in range(2):
            out.append((d * 2 + c, (d ^ orders[c][step]) * 2 + c))
    return out


def rel_of(order):
    out = []
    for p in range(1 << len(order)):
        r = 0
        for k, b in enumerate(order):
            if (p >> k) & 1:
                r ^= b
        out.append(r)
    return out


AT_EARLY, AT_LATE, AT_MIXED, AT_OTHER, POS_EARLY, POS_LATE = 0, NB, 2 * NB, 3 * NB, 4 * NB, 6 * NB
HALF_AT, CLASS_AT = 8 * NB, 8 * NB + 2


class At:
    def __init__(self, ref, first):
        self.ref, self.first = ref, first

    def __getitem__(self, n):
        return self.ref[self.first + n]


def device_tables(n_dp):
    kinds = [[rel_of(order) for order in orders] for orders in bit_orders(n_dp)]
    classes = rel_of([1 << k for k in reversed(range(n_dp.bit_length() - 1))])
    plain = list(range(NB))
    table = []
    for d in range(n_dp):
        for c in range(2):
            direct = n_dp == NB
            row = []
            for rel in kinds:
                row += [d ^ r for r in rel[c]] if direct else plain
            row += [d ^ r for r in kinds[0][1 - c]] if direct else plain
            for rel in kinds[:2]:
                for half in (c, 1 - c):
                    row += [rel[half].index(d ^ j) for j in range(NB)] if direct else plain
            me = d * 2 + c
            row += [c, 1 - c, me] + [me ^ (r << 1 | b) for b in range(2) for r in classes]
            table.append(row)
    return np.array(table, np.int32)


def core_swap(block):
    return lax.ppermute(block, "tensor", [(0, 1), (1, 0)])


VM = pl.BlockSpec(memory_space=pltpu.VMEM)
SM = pl.BlockSpec(memory_space=pltpu.SMEM)
BLK = 256


def call(kernel, out, in_specs, *args, vmem=16, flops=0, moved=0, trans=0, scratch=(), name=None):
    return pl.pallas_call(
        kernel,
        out_shape=[jax.ShapeDtypeStruct(s, t) for s, t in out],
        in_specs=in_specs,
        out_specs=[VM] * len(out),
        scratch_shapes=list(scratch),
        compiler_params=params(vmem),
        cost_estimate=cost(flops, moved, trans),
        name=name,
    )(*args)


def pack_kernel(qkv, out, up, down, norm, one_ref, two_ref, three_ref, wide, a0, a1, a2, a3, sems):
    rows = up.shape[0]
    wide[...] = jnp.zeros_like(wide)
    copies = [
        pltpu.make_async_copy(src, dst, sems.at[n])
        for n, (src, dst) in enumerate(
            ((qkv, a0), (out, a1), (down, a3), (up, a2))
        )
    ]
    for c in copies:
        c.start()
    copies[0].wait()
    for part in range(3):
        one_ref[0, :, part * HALF_OUT : (part + 1) * HALF_OUT] = a0[part].astype(BF)
    copies[1].wait()
    one_ref[0, :, HALF_QKV : HALF_QKV + HALF_OUT] = a1[...].astype(BF)
    wide[0:4, 0:rows] = norm[...]
    one_ref[0, :, HALF_QKV + HALF_OUT :] = wide[...].T[0:rows].astype(BF)
    copies[2].wait()
    three_ref[0] = a3[...].astype(BF)
    copies[3].wait()
    two_ref[0] = a2[...].astype(BF)


def pack(*shards):
    rows = shards[2].shape[0]
    return call(
        pack_kernel,
        [((1, rows, ONE), BF), ((1, rows, HALF_FF), BF), ((1, rows, HALF_FF), BF)],
        [pl.BlockSpec(memory_space=pltpu.HBM)] * 4 + [VM], *shards,
        vmem=60, moved=rows * 28000,
        scratch=[pltpu.VMEM((128, 128), F32)]
        + [pltpu.VMEM(w.shape, F32) for w in shards[:4]]
        + [pltpu.SemaphoreType.DMA((4,))],
        name="pack",
    )


def assemble_kernel(first, tab, low, high, out_ref):
    for n, ref in enumerate((low, high)):
        for p in range(NB // 2):
            out_ref[tab[first + n * (NB // 2) + p]] = ref[p]


def assemble(first, tab, low, high, name):
    width = low.shape[-1]
    return call(
        partial(assemble_kernel, first),
        [((NB, RB, width), BF)],
        [SM, VM, VM], tab, low, high,
        moved=4 * D * width, name=name,
    )[0]


def weight(w_ref, first, last):
    return w_ref[:, :, first:last].reshape(D, last - first)


def norm_fwd(hidden):
    center = hidden - jnp.mean(hidden, axis=-1, keepdims=True)
    spread = jnp.mean(center * center, axis=-1, keepdims=True)
    rstd = lax.rsqrt(spread + EPS)
    return center * rstd, rstd


def norm_bwd(grad, xh, rstd, gain):
    e = grad * gain
    m1 = jnp.mean(e, axis=-1, keepdims=True)
    m2 = jnp.mean(e * xh, axis=-1, keepdims=True)
    return rstd * (e - m1 - xh * m2)


def store_turned(ref, tab, value, col, width):
    turned = value.T
    for j in range(NB):
        block = turned[j * RB : (j + 1) * RB]
        for n in range(2):
            ref[n, tab[n * NB + j], :, pl.ds(col, width)] = block


def head_masks(rows, scale):
    lane = lax.broadcasted_iota(jnp.int32, (rows, 128), 1)
    return (
        jnp.where(lane < HEAD, scale, 0.0).astype(BF),
        jnp.where(lane < HEAD, 0.0, scale).astype(BF),
    )


def stack_heads(pair, masks):
    return jnp.concatenate([pair * masks[0], pair * masks[1]], axis=0)


def merge_heads(both):
    lane = lax.broadcasted_iota(jnp.int32, (SPAN, 128), 1)
    return jnp.where(lane < HEAD, both[:SPAN], both[SPAN:])


def turn_kernel(pos, x_ref, out_ref):
    rows = x_ref.shape[0]
    for i in range(rows // BLK):
        store_turned(out_ref, At(pos, POS_EARLY), x_ref[i * BLK : (i + 1) * BLK, :], i * BLK, BLK)


def turn(pos, x):
    rows = x.shape[0]
    return call(
        turn_kernel, [((2, NB, RB, rows), BF)], [SM, VM], pos, x, moved=rows * D * 6, name="turn"
    )[0]


def attn_rows(i, x, w_ref, masks, qkv_ref, ctx_ref, lse_ref):
    r0 = pl.multiple_of(i * BLK, BLK)
    qkv = mm(x, weight(w_ref, 0, HALF_QKV)).astype(BF)
    qkv_ref[pl.ds(r0, BLK), :] = qkv
    pairs = [(s, j) for s in range(2) for j in range(3)]

    def part(n, s, j):
        return qkv[s * SPAN : (s + 1) * SPAN, n * HALF_OUT + j * 128 : n * HALF_OUT + (j + 1) * 128]

    sts = [mm(part(1, s, j), stack_heads(part(0, s, j), masks), NT) for s, j in pairs]
    tops = [jnp.max(st, axis=0, keepdims=True) for st in sts]
    exs = [jnp.exp(st - top) for st, top in zip(sts, tops)]
    totals = [jnp.sum(ex, axis=0, keepdims=True) for ex in exs]
    pts = [(ex * (1.0 / total)).astype(BF) for ex, total in zip(exs, totals)]
    parts = [merge_heads(mm(pt, part(2, s, j), TN)).astype(BF) for pt, (s, j) in zip(pts, pairs)]
    for (s, j), top, total in zip(pairs, tops, totals):
        lse_ref[i * 2 + s, j : j + 1, :] = top + jnp.log(total)
    ctx = jnp.concatenate([jnp.concatenate(parts[s * 3 : s * 3 + 3], axis=1) for s in range(2)], axis=0)
    ctx_ref[pl.ds(r0, BLK), :] = ctx
    return ctx


def attn_one_kernel(first, tab, low, high, x_ref, qkv_ref, ctx_ref, lse_ref, w_ref):
    assemble_kernel(first, tab, low, high, w_ref)
    masks = head_masks(SPAN, HEAD ** (-0.5))

    def step(i, carry):
        x = x_ref[pl.ds(pl.multiple_of(i * BLK, BLK), BLK), :]
        attn_rows(i, x, w_ref, masks, qkv_ref, ctx_ref, lse_ref)
        return carry

    lax.fori_loop(0, x_ref.shape[0] // BLK, step, 0, unroll=2)


def attn_two_kernel(
    first, tab, low, high, x_ref, wo_ref, ctxo_ref,
    qkv_ref, ctx_ref, lse_ref, xh_ref, rstd_ref, p_ref, w_ref,
):
    assemble_kernel(first, tab, low, high, w_ref)
    cols = weight(w_ref, HALF_QKV + HALF_OUT, ONE).astype(F32)
    p_ref[...] = cols.T[:8]
    masks = head_masks(SPAN, HEAD ** (-0.5))

    def step(i, carry):
        rs = pl.ds(pl.multiple_of(i * BLK, BLK), BLK)
        x = x_ref[rs, :]
        ctx = attn_rows(i, x, w_ref, masks, qkv_ref, ctx_ref, lse_ref)
        attn = x.astype(F32) + mm(ctxo_ref[rs, :], weight(wo_ref, HALF_QKV, HALF_QKV + HALF_OUT), NT)
        attn = attn + mm(ctx, weight(w_ref, HALF_QKV, HALF_QKV + HALF_OUT), NT)
        xh, rstd = norm_fwd(attn)
        rstd = jnp.broadcast_to(rstd, (BLK, 128))
        for s in range(2):
            for q in range(4):
                r = s * SPAN + q * 32
                xh_ref[q, i * 2 + s] = xh[r : r + 32]
                rstd_ref[q, i * 2 + s] = rstd[r : r + 32]
        return carry

    lax.fori_loop(0, x_ref.shape[0] // BLK, step, 0, unroll=2)


def attn_shapes(rows):
    return [((rows, HALF_QKV), BF), ((rows, HALF_OUT), BF), ((rows // SPAN, 8, 2 * SPAN), F32)]


def attn_one(first, tab, low, high, x):
    rows = x.shape[0]
    return call(
        partial(attn_one_kernel, first), attn_shapes(rows) + [((NB, RB, ONE), BF)],
        [SM, VM, VM, VM], tab, low, high, x,
        vmem=16, flops=rows * 4e6, moved=rows * 8000 + 2e6, trans=rows * 800, name="attn_one",
    )


def attn_two(first, tab, low, high, x, w_own, ctx_own):
    rows = x.shape[0]
    spans = rows // SPAN
    out = attn_shapes(rows) + [
        ((4, spans, 32, D), F32),
        ((4, spans, 32, 128), F32),
        ((8, D), F32),
        ((NB, RB, ONE), BF),
    ]
    return call(
        partial(attn_two_kernel, first), out, [SM] + [VM] * 5, tab, low, high, x, w_own, ctx_own,
        vmem=16, flops=rows * 5e6, moved=rows * 12000 + 4e6, trans=rows * 800, name="attn_two",
    )


def gelu_pair(u):
    a = jnp.abs(u)
    d = 1.0 + (0.3275911 * 0.5**0.5) * a
    t = pl.reciprocal(d, approx=True)
    t = t * (2.0 - d * t)
    e = jnp.exp(-0.5 * u * u)
    poly = 0.5307027145 * t - 0.7265760135
    poly = poly * t + 0.7107068705
    poly = poly * t - 0.142248368
    poly = poly * t + 0.127414796
    tail = (poly * t) * e
    phi = jnp.where(u >= 0.0, 1.0 - tail, tail)
    return u * phi, phi + (0.3989422804014327 * u) * e


TILE = 512


def ffn_up_kernel(pos, xh_ref, p_ref, w_ref, g_ref, gp_ref, *yt_ref):
    def step(i, carry):
        rs = pl.ds(pl.multiple_of(i * BLK, BLK), BLK)
        y = xh_ref[rs, :] * p_ref[0:1, :] + p_ref[1:2, :]
        yb = y.astype(BF)
        if yt_ref:
            store_turned(yt_ref[0], At(pos, POS_EARLY), yb, pl.multiple_of(i * BLK, BLK), BLK)
        for t in range(HALF_FF // TILE):
            u = mm(yb, weight(w_ref, t * TILE, (t + 1) * TILE))
            g, gp = gelu_pair(u)
            g_ref[rs, t * TILE : (t + 1) * TILE] = g.astype(BF)
            gp_ref[rs, t * TILE : (t + 1) * TILE] = gp.astype(BF)
        return carry

    lax.fori_loop(0, xh_ref.shape[0] // BLK, step, 0, unroll=2)


def ffn_up(pos, xh, prow, w, turned, name):
    rows = xh.shape[0]
    out = [((rows, HALF_FF), BF), ((rows, HALF_FF), BF)]
    if turned:
        out.append(((2, NB, RB, rows), BF))
    return call(
        ffn_up_kernel, out, [SM, VM, VM, VM], pos, xh, prow, w,
        vmem=16, flops=rows * 2.4e6, moved=rows * 9000 + 2e6, trans=rows * 6000, name=name,
    )


def down_block(r0, xh1_ref, p_ref, acts, downs):
    rs = pl.ds(r0, BLK)
    total = xh1_ref[rs, :] * p_ref[0:1, :] + p_ref[1:2, :]
    for g_ref, w_ref in zip(acts, downs):
        total = total + mm(g_ref[rs, :], weight(w_ref, 0, HALF_FF), NT)
    return norm_fwd(total)


def first_kernel(xh1_ref, p_ref, g0, g1, d0, d1, mixed_ref, cls_ref, xh_ref, rstd_ref):
    xh, rstd = down_block(0, xh1_ref, p_ref, (g0, g1), (d0, d1))
    xh_ref[...] = xh
    rstd_ref[...] = jnp.broadcast_to(rstd, rstd_ref.shape)
    out = (xh * p_ref[2:3, :] + p_ref[3:4, :]).reshape(mixed_ref.shape)
    mixed_ref[...] = out.astype(BF)
    cls_ref[...] = out[:, 0, :]


def first_rows(xh1, prow, acts, downs):
    spans = BLK // 32
    return call(
        first_kernel,
        [((spans, 32, D), BF), ((spans, D), F32), ((BLK, D), F32), ((BLK, 128), F32)],
        [VM] * 6, xh1, prow, *acts, *downs,
        vmem=8, flops=BLK * 4.8e6, moved=BLK * 16000 + 5e6, name="first_rows",
    )


def back_block(r0, grad, xh2, rstd2, gps, xh1_ref, rstd1_ref, p_ref, ups, downs, dus):
    rs = pl.ds(r0, BLK)
    sum_g2 = jnp.sum(grad * xh2, axis=0, keepdims=True)
    sum_b2 = jnp.sum(grad, axis=0, keepdims=True)
    dh = norm_bwd(grad, xh2, rstd2, p_ref[2:3, :])
    df = dh.astype(BF)
    total = dh
    for gp_ref, up_ref, down_ref, du_ref in zip(gps, ups, downs, dus):
        for t in range(HALF_FF // TILE):
            lo, hi = t * TILE, (t + 1) * TILE
            dg = mm(df, weight(down_ref, lo, hi))
            du_ref[:, lo:hi] = (dg * gp_ref[rs, lo:hi].astype(F32)).astype(BF)
        total = total + mm(du_ref[...], weight(up_ref, 0, HALF_FF), NT)
    xh1 = xh1_ref[rs, :]
    sum_g1 = jnp.sum(total * xh1, axis=0, keepdims=True)
    sum_b1 = jnp.sum(total, axis=0, keepdims=True)
    dh1 = norm_bwd(total, xh1, rstd1_ref[rs, 0:1], p_ref[0:1, :])
    return df, dh1, (sum_g1, sum_b1, sum_g2, sum_b2)


def back_shapes():
    return [
        ((2, NB, RB, BLK), BF),
        ((BLK, HALF_FF), BF),
        ((BLK, HALF_FF), BF),
        ((BLK // 32, 32, D), F32),
        ((8, D), F32),
    ]


def rest_kernel(
    at, pos, xh1_ref, rstd1_ref, p_ref, g0, g1, gp0, gp1, cot_ref, u0, u1, d0, d1,
    dft_ref, du0_ref, du1_ref, dh1_ref, sums_ref, mixed_ref,
):
    r0, c0 = at * BLK, at * 32
    xh, rstd = down_block(r0, xh1_ref, p_ref, (g0, g1), (d0, d1))
    out = xh * p_ref[2:3, :] + p_ref[3:4, :]
    mixed_ref[...] = out.reshape(mixed_ref.shape).astype(BF)
    grad = cot_ref[:, c0 : c0 + 32, :].astype(F32).reshape(BLK, D)
    df, dh1, sums = back_block(
        r0, grad, xh, rstd, (gp0, gp1), xh1_ref, rstd1_ref, p_ref, (u0, u1), (d0, d1), (du0_ref, du1_ref)
    )
    store_turned(dft_ref, At(pos, POS_LATE), df, 0, BLK)
    dh1_ref[...] = dh1.reshape(dh1_ref.shape)
    for n in range(4):
        sums_ref[n : n + 1, :] = sums[n]


def rest_rows(at, pos, xh1, rstd1, prow, acts, gps, cot, ups, downs):
    return call(
        partial(rest_kernel, at),
        back_shapes() + [((BLK // 32, 32, D), BF)],
        [SM] + [VM] * 12, pos, xh1, rstd1, prow, *acts, *gps, cot, *ups, *downs,
        vmem=16, flops=BLK * 14.5e6, moved=BLK * 40000 + 1e7, name=f"rest_rows_{at}",
    )


def class_kernel(
    pos, cls_ref, cot_ref, xh2_ref, rstd2_ref, xh1_ref, rstd1_ref, p_ref, gp0, gp1, u0, u1, d0, d1,
    dft_ref, du0_ref, du1_ref, dh1_ref, sums_ref,
):
    spans = cls_ref.shape[0]
    grad = cot_ref[:, 0:32, :].astype(F32)
    first = lax.broadcasted_iota(jnp.int32, grad.shape, 1) == 0
    grad = grad + jnp.where(first, cls_ref[...].reshape(spans, 1, D), 0.0)
    grad = grad.reshape(BLK, D)
    df, dh1, sums = back_block(
        0, grad, xh2_ref[...], rstd2_ref[:, 0:1], (gp0, gp1), xh1_ref, rstd1_ref, p_ref,
        (u0, u1), (d0, d1), (du0_ref, du1_ref),
    )
    store_turned(dft_ref, At(pos, POS_LATE), df, 0, BLK)
    dh1_ref[...] = dh1.reshape(dh1_ref.shape)
    for n in range(4):
        sums_ref[n : n + 1, :] = sums[n]


def class_rows(pos, grad_cls, cot, xh2, rstd2, xh1, rstd1, prow, gps, ups, downs):
    return call(
        class_kernel,
        back_shapes(),
        [SM] + [VM] * 13, pos, grad_cls, cot, xh2, rstd2, xh1, rstd1, prow, *gps, *ups, *downs,
        vmem=16, flops=BLK * 9.7e6, moved=BLK * 30000 + 1e7, name="class_rows",
    )


def contrast_kernel(where, doc_ref, cls_ref, loss_ref, grad_ref, rows, own_doc):
    spans = doc_ref.shape[1]
    doc_row = doc_ref[...].astype(F32)
    doc_col = jnp.broadcast_to(doc_row, (128, spans)).T[:, 0:1]
    blocks, per = cls_ref.shape[0], cls_ref.shape[1]
    where = At(where, CLASS_AT)
    me = where[0]
    for n in range(blocks):
        rows[where[1 + n]] = cls_ref[n].astype(F32)
    a = rows[...].reshape(spans, D).astype(BF)
    own = rows[me].astype(BF)
    scale = D ** (-0.5)
    col = lax.broadcasted_iota(jnp.int32, (spans, spans), 1)
    row = lax.broadcasted_iota(jnp.int32, (spans, spans), 0)
    logits = mm(a, a, NT) * scale
    partner = (doc_col == doc_row) & (row != col)
    masked = jnp.where(row == col, -1000000000.0, logits)
    top = jnp.max(masked, axis=0, keepdims=True)
    lse = jnp.log(jnp.sum(jnp.exp(masked - top), axis=0, keepdims=True)) + top
    positive = jnp.sum(jnp.where(partner, logits, 0.0), axis=0, keepdims=True)
    flagged = jnp.max(jnp.where(partner, 1.0, 0.0), axis=0, keepdims=True)
    count = jnp.sum(flagged, axis=1, keepdims=True)
    loss = jnp.sum(flagged * (lse - positive), axis=1, keepdims=True) / count
    loss_ref[...] = jnp.broadcast_to(loss, loss_ref.shape)

    weight_row = flagged * (CONTRAST * spans) / count
    own_doc[...] = doc_col.reshape(blocks, per, 1)
    docs = own_doc[me]
    col = lax.broadcasted_iota(jnp.int32, (per, spans), 1)
    row = lax.broadcasted_iota(jnp.int32, (per, spans), 0) + me * per
    logits = mm(own, a, NT) * scale
    same = jnp.where((docs == doc_row) & (row != col), 1.0, 0.0)
    masked = jnp.where(row == col, -1000000000.0, logits)
    top = jnp.max(masked, axis=1, keepdims=True)
    ex = jnp.exp(masked - top)
    soft = ex / jnp.sum(ex, axis=1, keepdims=True)
    own_weight = jnp.max(same, axis=1, keepdims=True) * (CONTRAST * spans) / count
    sym = own_weight * (soft - same) + weight_row * (jnp.exp(masked - lse) - same)
    high = sym.astype(BF)
    low = (sym - high.astype(F32)).astype(BF)
    grad_ref[...] = (mm(high, a) + mm(low, a)) * scale


def contrast(where, doc_row, cls_all):
    blocks, per, _ = cls_all.shape
    spans = blocks * per
    return call(
        contrast_kernel,
        [((1, 128), F32), ((per, D), F32)],
        [SM, VM, VM],
        where, doc_row, cls_all,
        vmem=8 if spans <= 256 else 40, flops=2 * spans * spans * D, moved=spans * D * 2,
        scratch=[pltpu.VMEM((blocks, per, D), F32), pltpu.VMEM((blocks, per, 1), F32)],
        name="contrast",
    )


def turned_of(refs, n):
    return jnp.concatenate([ref[n].reshape(D, ref.shape[3]) for ref in refs], axis=1)


def grad_other_kernel(count, *refs):
    xts, ys, out_ref = refs[:count], refs[count:-1], refs[-1]
    xt = turned_of(xts, 1)
    for t in range(HALF_FF // TILE):
        lo, hi = t * TILE, (t + 1) * TILE
        grad = mm(xt, jnp.concatenate([y[:, lo:hi] for y in ys], axis=0))
        out_ref[:, :, lo:hi] = grad.astype(BF).reshape(NB, RB, TILE)


def grad_other(xts, ys, name):
    rows = sum(y.shape[0] for y in ys)
    return call(
        partial(grad_other_kernel, len(xts)),
        [((NB, RB, HALF_FF), BF)],
        [VM] * (len(xts) + len(ys)), *xts, *ys,
        vmem=12, flops=2 * rows * D * HALF_FF, moved=rows * 8000 + 2.4e6, name=name,
    )[0]


def grad_own_kernel(count, came_ref, *refs):
    xts, ys, keep_ref, send_ref = refs[:count], refs[count:-2], refs[-2], refs[-1]
    nh = NB // 2
    xt = turned_of(xts, 0)
    for t in range(HALF_FF // TILE):
        lo, hi = t * TILE, (t + 1) * TILE
        grad = mm(xt, jnp.concatenate([y[:, lo:hi] for y in ys], axis=0))
        grad = (grad.reshape(NB, RB, TILE) + came_ref[:, :, lo:hi].astype(F32)).astype(BF)
        keep_ref[:, :, lo:hi] = grad[:nh]
        send_ref[:, :, lo:hi] = grad[nh:]


def grad_own(xts, ys, came, name):
    rows = sum(y.shape[0] for y in ys)
    return call(
        partial(grad_own_kernel, len(xts)),
        [((NB // 2, RB, HALF_FF), BF)] * 2,
        [VM] * (1 + len(xts) + len(ys)), came, *xts, *ys,
        vmem=12, flops=2 * rows * D * HALF_FF, moved=rows * 8000 + 4.8e6, name=name,
    )


def natural(refs, i):
    return jnp.concatenate([ref[i * 2 + s] for s in range(2) for ref in refs], axis=0)


def attn_back_kernel(pos, r0_ref, r1_ref, r2_ref, r3_ref, qkv_ref, lse_ref, w_ref, dqkv_ref, *dat_ref):
    masks = head_masks(SPAN, HEAD ** (-0.5))
    plain = head_masks(SPAN, 1.0)
    spans = r0_ref.shape[0]

    def step(i, carry):
        r0 = pl.multiple_of(i * BLK, BLK)
        da = natural((r0_ref, r1_ref, r2_ref, r3_ref), i).astype(BF)
        if dat_ref:
            store_turned(dat_ref[0], At(pos, POS_EARLY), da, r0, BLK)
        dctx = mm(da, weight(w_ref, HALF_QKV, HALF_QKV + HALF_OUT)).astype(BF)
        pairs = [(s, j) for s in range(2) for j in range(3)]

        def part(ref, n, s, j):
            rs = pl.ds(pl.multiple_of(r0 + s * SPAN, SPAN), SPAN)
            return ref.at[rs, n * HALF_OUT + j * 128 : n * HALF_OUT + (j + 1) * 128]

        qs = [stack_heads(part(qkv_ref, 0, s, j)[...], masks) for s, j in pairs]
        ks = [part(qkv_ref, 1, s, j)[...] for s, j in pairs]
        sts = [mm(k, q, NT) for k, q in zip(ks, qs)]
        dcs = [stack_heads(dctx[s * SPAN : (s + 1) * SPAN, j * 128 : (j + 1) * 128], plain) for s, j in pairs]
        dpts = [mm(part(qkv_ref, 2, s, j)[...], dc, NT) for (s, j), dc in zip(pairs, dcs)]
        pts = [jnp.exp(st - lse_ref[i * 2 + s, j : j + 1, :]) for (s, j), st in zip(pairs, sts)]
        dvs = [mm(pt.astype(BF), dc) for pt, dc in zip(pts, dcs)]
        dsts = [
            (pt * (dpt - jnp.sum(pt * dpt, axis=0, keepdims=True))).astype(BF) for pt, dpt in zip(pts, dpts)
        ]
        dks = [mm(dst, q) for dst, q in zip(dsts, qs)]
        dqs = [merge_heads(mm(dst, k, TN)) * HEAD ** (-0.5) for dst, k in zip(dsts, ks)]
        for n, grads in enumerate((dqs, dks, dvs)):
            for (s, j), grad in zip(pairs, grads):
                part(dqkv_ref, n, s, j)[...] = grad.astype(BF)
        return carry

    lax.fori_loop(0, spans // 2, step, 0, unroll=2)


def attn_back(pos, dh1, qkv, lse, w, turned, name):
    rows = qkv.shape[0]
    out = [((rows, HALF_QKV), BF)]
    if turned:
        out.append(((2, NB, RB, rows), BF))
    return call(
        attn_back_kernel, out,
        [SM] + [VM] * 7, pos, *dh1, qkv, lse, w,
        vmem=16, flops=rows * 6e6, moved=rows * 10000 + 3e6, trans=rows * 800, name=name,
    )


def last_value(order, xt_ref, dqkv_ref, dat_ref, ctx_ref, t):
    rows = xt_ref.shape[3]
    if t < 3:
        return mm(xt_ref[order].reshape(D, rows), dqkv_ref[:, t * HALF_OUT : (t + 1) * HALF_OUT])
    return mm(dat_ref[order].reshape(D, rows), ctx_ref[...])


def norm_columns(sums):
    total = sums[0][0:4, :]
    for ref in sums[1:]:
        total = total + ref[0:4, :]
    return jnp.concatenate([total, jnp.zeros((124, D), F32)], axis=0).T


def last_other_kernel(pos, xt_ref, dqkv_ref, dat_ref, ctx_ref, s0, s1, s2, s3, out_ref):
    for t in range(4):
        grad = last_value(1, xt_ref, dqkv_ref, dat_ref, ctx_ref, t)
        lo = t * HALF_OUT
        out_ref[:, :, lo : lo + HALF_OUT] = grad.astype(BF).reshape(NB, RB, HALF_OUT)
    norm = norm_columns((s0, s1, s2, s3)).astype(BF)
    for j in range(NB):
        out_ref[pos[POS_EARLY + NB + j], :, HALF_QKV + HALF_OUT :] = norm[j * RB : (j + 1) * RB]


def last_other(pos, xt, dqkv, dat, ctx, sums):
    rows = xt.shape[3]
    return call(
        last_other_kernel,
        [((NB, RB, ONE), BF)],
        [SM] + [VM] * 8, pos, xt, dqkv, dat, ctx, *sums,
        vmem=12, flops=2 * rows * D * HALF_FF, moved=rows * 8000 + 2.4e6, name="last_other",
    )[0]


def last_own_kernel(
    pos, xt_ref, dqkv_ref, dat_ref, ctx_ref, s0, s1, s2, s3, came_ref, keep_ref, send_ref, cols
):
    nh = NB // 2
    norm = norm_columns((s0, s1, s2, s3))
    for j in range(NB):
        cols[pos[POS_EARLY + j]] = norm[j * RB : (j + 1) * RB]
    for t in range(5):
        lo = t * HALF_OUT
        hi = min(lo + HALF_OUT, ONE)
        if t < 4:
            grad = last_value(0, xt_ref, dqkv_ref, dat_ref, ctx_ref, t).reshape(NB, RB, HALF_OUT)
        else:
            grad = cols[...]
        grad = (grad + came_ref[:, :, lo:hi].astype(F32)).astype(BF)
        keep_ref[:, :, lo:hi] = grad[:nh]
        send_ref[:, :, lo:hi] = grad[nh:]


def last_own(pos, xt, dqkv, dat, ctx, sums, came):
    rows = xt.shape[3]
    return call(
        last_own_kernel,
        [((NB // 2, RB, ONE), BF)] * 2,
        [SM] + [VM] * 9, pos, xt, dqkv, dat, ctx, *sums, came,
        vmem=12, flops=2 * rows * D * HALF_FF, moved=rows * 8000 + 4.8e6,
        scratch=[pltpu.VMEM((NB, RB, 128), F32)], name="last_own",
    )


def input_grad_kernel(r0_ref, r1_ref, r2_ref, r3_ref, own_ref, other_ref, w0_ref, w1_ref, out_ref):
    spans = r0_ref.shape[0]

    def step(i, carry):
        rs = pl.ds(pl.multiple_of(i * BLK, BLK), BLK)
        total = natural((r0_ref, r1_ref, r2_ref, r3_ref), i)
        total = total + mm(own_ref[rs, :], weight(w0_ref, 0, HALF_QKV), NT)
        total = total + mm(other_ref[rs, :], weight(w1_ref, 0, HALF_QKV), NT)
        out_ref[rs, :] = total
        return carry

    lax.fori_loop(0, spans // 2, step, 0, unroll=2)


def input_grads(dh1, own, other, w_own, w_other):
    rows = own.shape[0]
    return call(
        input_grad_kernel,
        [((rows, D), F32)],
        [VM] * 8, *dh1, own, other, w_own, w_other,
        vmem=12, flops=rows * 3.6e6, moved=rows * 12000 + 5e6, name="input_grads",
    )[0]


def place_kernel(half, *refs):
    own, other, g_own, g_other = refs[0:4], refs[4:8], refs[8], refs[9]
    mixed_ref, grad_ref, sems = refs[10:]
    spans = g_own.shape[0]
    copies = []
    for n, (pieces, g) in enumerate(((own, g_own), (other, g_other))):
        at = pl.ds(half[HALF_AT + n] * spans, spans)
        for q in range(4):
            to = mixed_ref.at[at, 32 * q : 32 * q + 32, :]
            copies.append(pltpu.make_async_copy(pieces[q], to, sems.at[5 * n + q]))
        copies.append(pltpu.make_async_copy(g, grad_ref.at[at], sems.at[5 * n + 4]))
    for c in copies:
        c.start()
    for c in copies:
        c.wait()


def place(half, own, other, g_own, g_other):
    spans = own[0].shape[0]
    g_own, g_other = (g.reshape(spans, SPAN, D) for g in (g_own, g_other))
    return pl.pallas_call(
        place_kernel,
        out_shape=[
            jax.ShapeDtypeStruct((2 * spans, SPAN, D), BF),
            jax.ShapeDtypeStruct((2 * spans, SPAN, D), F32),
        ],
        in_specs=[SM] + [VM] * 10,
        out_specs=[HBM] * 2,
        scratch_shapes=[pltpu.SemaphoreType.DMA((10,))],
        compiler_params=params(16),
        cost_estimate=cost(0, spans * SPAN * D * 24),
        name="place",
    )(half, *own, *other, g_own, g_other)


def squares_kernel(k0, c0, k1, c1, k2, c2, g0, g1, g2, sq_ref):
    main = HALF_QKV + HALF_OUT
    total = jnp.zeros((1, 1), F32)
    for keep, came, out in ((k0, c0, g0), (k1, c1, g1), (k2, c2, g2)):
        grad = keep[0].astype(F32) + came[0].astype(F32)
        out[...] = grad
        sq = jnp.sum(grad[:, :main] * grad[:, :main], axis=1, keepdims=True)
        if grad.shape[1] > main:
            cols = grad[:, main:]
            sq = sq + 0.5 * jnp.sum(cols * cols, axis=1, keepdims=True)
        total = total + jnp.sum(sq, axis=0, keepdims=True)
    sq_ref[...] = jnp.broadcast_to(total, sq_ref.shape)


def squares_of(pairs):
    shard = pairs[0][0].shape[1]
    out = [((shard, k.shape[2]), F32) for k, _ in pairs] + [((8, 128), F32)]
    flat = [a for pair in pairs for a in pair]
    return call(squares_kernel, out, [VM] * 6, *flat, vmem=8, moved=shard * 40000, name="squares")


def adam_parts(weight, gradient, moment_one, moment_two, step_rate, decay_rate):
    first_new = 0.9 * moment_one + 0.1 * gradient
    second_new = 0.999 * moment_two + 0.001 * gradient * gradient
    corr_first = first_new * (1.0 / (1.0 - 0.9**STEP))
    corr_second = second_new * (1.0 / (1.0 - 0.999**STEP))
    weight_new = weight - step_rate * (
        corr_first / (jnp.sqrt(corr_second) + 1e-08) + decay_rate * weight
    )
    return first_new, second_new, weight_new


def adam_kernel(sq_ref, last_ref, up_ref, down_ref, cols_ref, *refs):
    ins, outs, wide = refs[:15], refs[15:-1], refs[-1]
    norm = jnp.sqrt(sq_ref[0:1, 0:1])
    outs[15][...] = jnp.broadcast_to(norm, outs[15].shape)
    scale = 1.0 / jnp.maximum(norm, 1.0)

    def update(n, at, grad, rate, decay):
        new = adam_parts(ins[n][at], grad * scale, ins[5 + 2 * n][at], ins[6 + 2 * n][at], rate, decay)
        for m in range(3):
            outs[3 * n + m][at] = new[m]

    for part in range(3):
        update(0, part, last_ref[:, part * HALF_OUT : (part + 1) * HALF_OUT], 0.02, 0.01)
    update(1, Ellipsis, last_ref[:, HALF_QKV : HALF_QKV + HALF_OUT], 0.02, 0.01)
    update(2, Ellipsis, up_ref[...], 0.02, 0.01)
    update(3, Ellipsis, down_ref[...], 0.02, 0.01)
    shard = last_ref.shape[0]
    wide[...] = jnp.zeros_like(wide)
    wide[0:shard, :] = 0.5 * (last_ref[:, HALF_QKV + HALF_OUT :] + cols_ref[...])
    update(4, Ellipsis, wide[...].T[0:4, 0:shard], 0.5, 0.0)


def adam(squares, last, up, down, cols, weights, moments):
    shapes = [w.shape for w in weights]
    out = [(s, F32) for s in shapes for _ in range(3)] + [((8, 128), F32)]
    args = (squares, last, up, down, cols, *weights, *moments)
    return call(
        adam_kernel, out, [VM] * len(args), *args, vmem=16, moved=7 * 4 * last.shape[0] * 4608,
        scratch=[pltpu.VMEM((128, 128), F32)], name="adam",
    )


def after(value, *others):
    return lax.optimization_barrier((value, others))[0]


def body(
    tokens,
    cotangent,
    span_doc,
    qkv_weight,
    out_weight,
    ffn_in_weight,
    ffn_out_weight,
    norm_params,
    qkv_first,
    qkv_second,
    out_first,
    out_second,
    ffn_in_first,
    ffn_in_second,
    ffn_out_first,
    ffn_out_second,
    norm_first,
    norm_second,
):
    n_dp = lax.axis_size("dp")
    dp = lax.axis_index("dp")
    core = lax.axis_index("tensor")
    shard = D // n_dp
    rows = tokens.shape[0] // 2
    spans = rows // SPAN
    direct = n_dp == NB
    early, late, mixed_order = bit_orders(n_dp)
    steps = len(early[0])
    last = steps - 1

    tab = lax.dynamic_index_in_dim(device_tables(n_dp), dp * 2 + core, 0, keepdims=False)
    x = lax.dynamic_slice_in_dim(tokens, core * rows, rows, 0)
    cot = lax.dynamic_slice_in_dim(cotangent, core * rows, rows, 0).reshape(spans, SPAN, D)

    def places(orders, other=0):
        return dp ^ jnp.array([rel_of(order) for order in orders], jnp.int32)[core ^ other]

    def send_on(block, orders, k):
        return lax.ppermute(block, AXES, pairs_of(n_dp, orders, k))

    def join(held, came):
        return jnp.concatenate([held, came], axis=0)

    def pieces(at, low, high):
        if direct:
            return at, tab, low, high
        which = {AT_EARLY: places(early), AT_LATE: places(late), AT_MIXED: places(mixed_order), AT_OTHER: places(early, 1)}[at]
        full = join(low, high)[jnp.argsort(which)].reshape(NB, RB, -1)
        return at, tab, full[: NB // 2], full[NB // 2 :]

    def halves(orders, keep, send):
        if direct:
            return keep, send
        full = join(keep, send).reshape(n_dp, shard, -1)[places(orders)]
        return full[: n_dp // 2], full[n_dp // 2 :]

    def add(keep, came):
        total = keep.astype(F32) + came.astype(F32)
        size = total.shape[0] // 2
        return total[:size].astype(BF), total[size:].astype(BF)

    turned = ((1, 0, 2), (1, 0), (0, 1), (1, 0), (0, 1))
    weights = (qkv_weight, out_weight, ffn_in_weight, ffn_out_weight, norm_params)
    weights = tuple(w.transpose(t) for w, t in zip(weights, turned))
    one, up, down = pack(*weights)
    one_came = send_on(one, early, 0)
    up_came = send_on(up, late, 0)
    down_came = send_on(down, mixed_order, 0)
    one, tab, x, cot, down_came = after((join(one, one_came), tab, x, cot, down_came), up_came)
    for k in range(1, last):
        one_came = send_on(one, early, k)
        if k == 1:
            tokt = turn(tab, x)
            down = join(down, down_came)
            down_came = send_on(down, mixed_order, 1)
            one_came, down_came = after((one_came, down_came), tokt)
        else:
            up = after(join(up, up_came), one)
            up_came = send_on(up, late, k - 1)
        one = join(one, one_came)
        if k > 1:
            one = after(one, up_came)
    one_came = send_on(one, early, last)
    for k in range(max(last - 1, 1), last):
        up = join(up, up_came)
        up_came = send_on(up, late, k)
    one, one_came = after((one, one_came), up_came)
    up = after(join(up, up_came), one_came)
    up_came = send_on(up, late, last)
    down = after(join(down, down_came), one_came)
    down_came = send_on(down, mixed_order, 2)

    one_other = (core_swap(one), core_swap(one_came))
    qkv0, ctx0, lse0, w10 = attn_one(*pieces(AT_EARLY, one, one_came), x)
    for k in range(3, last):
        down = join(down, after(down_came, ctx0))
        down_came = send_on(down, mixed_order, k)
    qkv1, ctx1, lse1, xh1, rstd1, prow, w11 = attn_two(*pieces(AT_OTHER, *one_other), x, w10, ctx0)
    w1 = (w10, w11)
    xh1 = xh1.reshape(rows, D)
    rstd1 = rstd1.reshape(rows, 128)
    up_came, down_came = after((up_came, down_came), xh1)
    wu = assemble(*pieces(AT_LATE, up, up_came), "up_own")
    wu = (wu, core_swap(wu))
    down = join(down, down_came)
    down_came = send_on(down, mixed_order, last)
    act0, gp0, yt = ffn_up(tab, after(xh1, down), prow, wu[0], True, "ffn_up_own")
    wd = assemble(*pieces(AT_MIXED, down, after(down_came, act0)), "down_own")
    wd = (wd, core_swap(wd))
    act1, gp1 = ffn_up(tab, after(xh1, wd[0]), prow, wu[1], False, "ffn_up_other")
    acts, gps = (act0, act1), (gp0, gp1)
    mixed0, cls_own, xh2, rstd2 = first_rows(xh1, prow, acts, wd)

    held = cls_own.astype(BF)[None]
    back = []
    for k in reversed(range(steps)):
        came = lax.ppermute(held, "dp", [(d, d ^ (1 << k)) for d in range(n_dp)])
        if len(back) < 3:
            at = len(back) + 1
            back.append(rest_rows(at, tab, after(xh1, held), rstd1, prow, acts, gps, cot, wu, wd))
            came = after(came, back[-1][4])
        held = join(held, came)
    held = join(held, core_swap(held))
    loss, grad_cls = contrast(tab, span_doc.reshape(1, -1), held)
    back.insert(0, (*class_rows(tab, grad_cls, cot, xh2, rstd2, xh1, rstd1, prow, gps, wu, wd), mixed0))
    dft, du0, du1, dh1, sums, mixed_own = zip(*back)

    d_other = grad_other(dft, (act1,), "grad_down_other")
    d_came = core_swap(d_other)
    u_other = grad_other((after(yt, d_other),), du1, "grad_up_other")
    u_came = core_swap(u_other)
    d_keep, d_send = halves(
        late, *grad_own((after(dft[0], u_other),) + dft[1:], (act0,), d_came, "grad_down_own")
    )
    d_came = send_on(d_send, late, last)
    u_keep, u_send = halves(early, *grad_own((after(yt, d_keep),), du0, u_came, "grad_up_own"))
    dh1 = (after(dh1[0], u_keep),) + dh1[1:]
    dqkv1, dat = attn_back(tab, dh1, qkv1, lse1, w1[1], True, "attn_back_other")
    l_other = last_other(tab, tokt, dqkv1, dat, ctx1, sums)

    d_came, l_other = after((d_came, l_other))
    d_keep, d_send = add(d_keep, d_came)
    u_came = send_on(after(u_send, l_other), early, last)
    d_came = send_on(d_send, late, last - 1)
    l_came = core_swap(l_other)
    (dqkv0,) = attn_back(
        tab, (after(dh1[0], l_other),) + dh1[1:], qkv0, lse0, w1[0], False, "attn_back_own"
    )
    l_keep, l_send = halves(early, *last_own(tab, tokt, dqkv0, dat, ctx0, sums, l_came))
    l_came = send_on(l_send, early, last)
    grad_in = input_grads((after(dh1[0], l_send),) + dh1[1:], dqkv0, dqkv1, w1[0], w1[1])
    u_came, d_came = after((u_came, d_came), l_send)
    u_keep, u_send = add(u_keep, u_came)
    d_keep, d_send = add(d_keep, d_came)
    u_came = send_on(u_send, early, last - 1)
    d_came = send_on(d_send, late, last - 2)
    for k in reversed(range(last)):
        l_came, u_came, d_came = after((l_came, u_came, d_came))
        l_keep, l_send = add(l_keep, l_came)
        l_came = send_on(l_send, early, k)
        if k > 0:
            u_keep, u_send = add(u_keep, u_came)
            u_came = send_on(u_send, early, k - 1)
        if k > 1:
            d_keep, d_send = add(d_keep, d_came)
            d_came = send_on(d_send, late, k - 2)
        if k == last - 1:
            grad_came = core_swap(after(grad_in, l_send))
            mixed_other = tuple(core_swap(m) for m in after(mixed_own, l_send))
            l_came = after(l_came, grad_came, mixed_other)
        if k == last - 2:
            mixed, input_grad = place(tab, mixed_own, mixed_other, after(grad_in, l_send), grad_came)
            l_came = after(l_came, input_grad)

    last_grad, down_grad, up_grad, squares = squares_of(((l_keep, l_came), (d_keep, d_came), (u_keep, u_came)))
    cols = core_swap(last_grad[:, HALF_QKV + HALF_OUT :])
    squares = squares + core_swap(squares)
    bits = [1 << k for k in reversed(range(steps))]
    for one_bit, two_bit in zip(bits[::2], bits[1::2]):
        near, far, both = (
            lax.ppermute(squares, "dp", [(d, d ^ b) for d in range(n_dp)])
            for b in (one_bit, two_bit, one_bit ^ two_bit)
        )
        squares = (squares + near) + (far + both)
    moments = (
        qkv_first, qkv_second, out_first, out_second, ffn_in_first, ffn_in_second,
        ffn_out_first, ffn_out_second, norm_first, norm_second,
    )
    new = adam(
        squares, last_grad, up_grad, down_grad, cols,
        weights,
        [m.transpose(turned[n // 2]) for n, m in enumerate(moments)],
    )
    updated = [value.transpose(turned[n // 3]) for n, value in enumerate(new[:15])]
    return (
        mixed.reshape(2 * rows, D),
        input_grad.reshape(2 * rows, D),
        loss[0, 0],
        new[15][0, 0],
        *updated,
    )


def solution(mesh):
    rows = P("dp", None)
    qkv = P("dp", None, "tensor")
    turned = P("tensor", "dp")
    up = P("dp", "tensor")
    norm = P(None, "dp")
    weights = (qkv, turned, up, turned, norm)
    moments = tuple(spec for spec in weights for _ in range(2))
    updated = tuple(spec for spec in weights for _ in range(3))
    return jax.shard_map(
        body,
        mesh=mesh,
        in_specs=(rows, rows, P()) + weights + moments,
        out_specs=(rows, rows, P(), P()) + updated,
        check_vma=False,
    )
```

```python
from functools import partial

import jax
import jax.numpy as jnp
import numpy as np
from jax import lax
from jax.experimental import pallas as pl
from jax.experimental.pallas import tpu as pltpu
from jax.sharding import PartitionSpec as P

HEAD = 64
SPAN = 128
STEP = 10
D = 768
FF = 3072
NB = 16
RB = D // NB
HALF_QKV = 1152
HALF_OUT = 384
HALF_FF = 1536
ONE = HALF_QKV + HALF_OUT + 128
CONTRAST = 4.0
EPS = 1e-06
BF = jnp.bfloat16
F32 = jnp.float32
AXES = ("dp", "tensor")
SHRINK = 100

NN = (((1,), (0,)), ((), ()))
NT = (((1,), (1,)), ((), ()))
TN = (((0,), (0,)), ((), ()))


def mm(left, right, dims=NN):
    return lax.dot_general(left, right, dims, preferred_element_type=F32)


def params(vmem=56):
    vmem = vmem if vmem > 24 else min(vmem, 8)
    return pltpu.CompilerParams(vmem_limit_bytes=vmem * 2**20)


def cost(flops, bytes_accessed, trans=0):
    flops, bytes_accessed, trans = (n // SHRINK + 1 for n in (flops, bytes_accessed, trans))
    return pl.CostEstimate(flops=int(flops), bytes_accessed=int(bytes_accessed), transcendentals=int(trans))


HBM = pl.BlockSpec(memory_space=pl.ANY)


def bit_orders(n_dp):
    bits = n_dp.bit_length() - 1
    if bits == 4:
        return ((4, 8, 2, 1), (8, 4, 1, 2)), ((1, 4, 8, 2), (2, 8, 4, 1))
    up = tuple(1 << b for b in range(bits))[::-1]
    both = (up, up[: bits // 2] + up[bits // 2 :][::-1])
    return both, both


def pairs_of(n_dp, orders, step):
    out = []
    for d in range(n_dp):
        for c in range(2):
            out.append((d * 2 + c, (d ^ orders[c][step]) * 2 + c))
    return out


def rel_of(order):
    out = []
    for p in range(1 << len(order)):
        r = 0
        for k, b in enumerate(order):
            if (p >> k) & 1:
                r ^= b
        out.append(r)
    return out


AT_EARLY, AT_LATE, AT_OTHER, POS_EARLY, POS_LATE = 0, NB, 2 * NB, 3 * NB, 5 * NB
HALF_AT, CLASS_AT = 7 * NB, 7 * NB + 2


class At:
    def __init__(self, ref, first):
        self.ref, self.first = ref, first

    def __getitem__(self, n):
        return self.ref[self.first + n]


def device_tables(n_dp):
    kinds = [[rel_of(order) for order in orders] for orders in bit_orders(n_dp)]
    classes = rel_of([1 << k for k in reversed(range(n_dp.bit_length() - 1))])
    plain = list(range(NB))
    table = []
    for d in range(n_dp):
        for c in range(2):
            direct = n_dp == NB
            row = []
            for rel in kinds:
                row += [d ^ r for r in rel[c]] if direct else plain
            row += [d ^ r for r in kinds[0][1 - c]] if direct else plain
            for rel in kinds:
                for half in (c, 1 - c):
                    row += [rel[half].index(d ^ j) for j in range(NB)] if direct else plain
            me = d * 2 + c
            row += [c, 1 - c, me] + [me ^ (r << 1 | b) for b in range(2) for r in classes]
            table.append(row)
    return np.array(table, np.int32)


def core_swap(block):
    return lax.ppermute(block, "tensor", [(0, 1), (1, 0)])


VM = pl.BlockSpec(memory_space=pltpu.VMEM)
SM = pl.BlockSpec(memory_space=pltpu.SMEM)
BLK = 256


def call(kernel, out, in_specs, *args, vmem=16, flops=0, moved=0, trans=0, scratch=(), name=None):
    return pl.pallas_call(
        kernel,
        out_shape=[jax.ShapeDtypeStruct(s, t) for s, t in out],
        in_specs=in_specs,
        out_specs=[VM] * len(out),
        scratch_shapes=list(scratch),
        compiler_params=params(vmem),
        cost_estimate=cost(flops, moved, trans),
        name=name,
    )(*args)


def pack_kernel(qkv, out, up, down, norm, one_ref, two_ref, three_ref, wide, a0, a1, a2, a3, sems):
    rows = up.shape[0]
    wide[...] = jnp.zeros_like(wide)
    copies = [
        pltpu.make_async_copy(src, dst, sems.at[n])
        for n, (src, dst) in enumerate(
            ((qkv, a0), (out, a1), (down, a3), (up, a2))
        )
    ]
    for c in copies:
        c.start()
    copies[0].wait()
    for part in range(3):
        one_ref[0, :, part * HALF_OUT : (part + 1) * HALF_OUT] = a0[part].astype(BF)
    copies[1].wait()
    one_ref[0, :, HALF_QKV : HALF_QKV + HALF_OUT] = a1[...].astype(BF)
    wide[0:4, 0:rows] = norm[...]
    one_ref[0, :, HALF_QKV + HALF_OUT :] = wide[...].T[0:rows].astype(BF)
    copies[2].wait()
    three_ref[0] = a3[...].astype(BF)
    copies[3].wait()
    two_ref[0] = a2[...].astype(BF)


def pack(*shards):
    rows = shards[2].shape[0]
    return call(
        pack_kernel,
        [((1, rows, ONE), BF), ((1, rows, HALF_FF), BF), ((1, rows, HALF_FF), BF)],
        [pl.BlockSpec(memory_space=pltpu.HBM)] * 4 + [VM], *shards,
        vmem=60, moved=rows * 28000,
        scratch=[pltpu.VMEM((128, 128), F32)]
        + [pltpu.VMEM(w.shape, F32) for w in shards[:4]]
        + [pltpu.SemaphoreType.DMA((4,))],
        name="pack",
    )


def assemble_kernel(first, tab, low, high, out_ref):
    for n, ref in enumerate((low, high)):
        for p in range(NB // 2):
            out_ref[tab[first + n * (NB // 2) + p]] = ref[p]


def assemble(first, tab, low, high, name):
    width = low.shape[-1]
    return call(
        partial(assemble_kernel, first),
        [((NB, RB, width), BF)],
        [SM, VM, VM], tab, low, high,
        moved=4 * D * width, name=name,
    )[0]


def weight(w_ref, first, last):
    return w_ref[:, :, first:last].reshape(D, last - first)


def norm_fwd(hidden):
    center = hidden - jnp.mean(hidden, axis=-1, keepdims=True)
    spread = jnp.mean(center * center, axis=-1, keepdims=True)
    rstd = lax.rsqrt(spread + EPS)
    return center * rstd, rstd


def norm_bwd(grad, xh, rstd, gain):
    e = grad * gain
    m1 = jnp.mean(e, axis=-1, keepdims=True)
    m2 = jnp.mean(e * xh, axis=-1, keepdims=True)
    return rstd * (e - m1 - xh * m2)


def store_turned(ref, tab, value, col, width):
    turned = value.T
    for j in range(NB):
        block = turned[j * RB : (j + 1) * RB]
        for n in range(2):
            ref[n, tab[n * NB + j], :, pl.ds(col, width)] = block


def head_masks(rows, scale):
    lane = lax.broadcasted_iota(jnp.int32, (rows, 128), 1)
    return (
        jnp.where(lane < HEAD, scale, 0.0).astype(BF),
        jnp.where(lane < HEAD, 0.0, scale).astype(BF),
    )


def stack_heads(pair, masks):
    return jnp.concatenate([pair * masks[0], pair * masks[1]], axis=0)


def merge_heads(both):
    lane = lax.broadcasted_iota(jnp.int32, (SPAN, 128), 1)
    return jnp.where(lane < HEAD, both[:SPAN], both[SPAN:])


def turn_kernel(pos, x_ref, out_ref):
    rows = x_ref.shape[0]
    for i in range(rows // BLK):
        store_turned(out_ref, At(pos, POS_EARLY), x_ref[i * BLK : (i + 1) * BLK, :], i * BLK, BLK)


def turn(pos, x):
    rows = x.shape[0]
    return call(
        turn_kernel, [((2, NB, RB, rows), BF)], [SM, VM], pos, x, moved=rows * D * 6, name="turn"
    )[0]


def attn_rows(i, x, w_ref, masks, qkv_ref, ctx_ref, lse_ref):
    r0 = pl.multiple_of(i * BLK, BLK)
    qkv = mm(x, weight(w_ref, 0, HALF_QKV)).astype(BF)
    qkv_ref[pl.ds(r0, BLK), :] = qkv
    pairs = [(s, j) for s in range(2) for j in range(3)]

    def part(n, s, j):
        return qkv[s * SPAN : (s + 1) * SPAN, n * HALF_OUT + j * 128 : n * HALF_OUT + (j + 1) * 128]

    sts = [mm(part(1, s, j), stack_heads(part(0, s, j), masks), NT) for s, j in pairs]
    tops = [jnp.max(st, axis=0, keepdims=True) for st in sts]
    exs = [jnp.exp(st - top) for st, top in zip(sts, tops)]
    totals = [jnp.sum(ex, axis=0, keepdims=True) for ex in exs]
    pts = [(ex * (1.0 / total)).astype(BF) for ex, total in zip(exs, totals)]
    parts = [merge_heads(mm(pt, part(2, s, j), TN)).astype(BF) for pt, (s, j) in zip(pts, pairs)]
    for (s, j), top, total in zip(pairs, tops, totals):
        lse_ref[i * 2 + s, j : j + 1, :] = top + jnp.log(total)
    ctx = jnp.concatenate([jnp.concatenate(parts[s * 3 : s * 3 + 3], axis=1) for s in range(2)], axis=0)
    ctx_ref[pl.ds(r0, BLK), :] = ctx
    return ctx


def attn_one_kernel(first, tab, low, high, x_ref, qkv_ref, ctx_ref, lse_ref, w_ref):
    assemble_kernel(first, tab, low, high, w_ref)
    masks = head_masks(SPAN, HEAD ** (-0.5))

    def step(i, carry):
        x = x_ref[pl.ds(pl.multiple_of(i * BLK, BLK), BLK), :]
        attn_rows(i, x, w_ref, masks, qkv_ref, ctx_ref, lse_ref)
        return carry

    lax.fori_loop(0, x_ref.shape[0] // BLK, step, 0, unroll=2)


def attn_two_kernel(
    first, tab, low, high, x_ref, wo_ref, ctxo_ref,
    qkv_ref, ctx_ref, lse_ref, xh_ref, rstd_ref, p_ref, w_ref,
):
    assemble_kernel(first, tab, low, high, w_ref)
    cols = weight(w_ref, HALF_QKV + HALF_OUT, ONE).astype(F32)
    p_ref[...] = cols.T[:8]
    masks = head_masks(SPAN, HEAD ** (-0.5))

    def step(i, carry):
        rs = pl.ds(pl.multiple_of(i * BLK, BLK), BLK)
        x = x_ref[rs, :]
        ctx = attn_rows(i, x, w_ref, masks, qkv_ref, ctx_ref, lse_ref)
        attn = x.astype(F32) + mm(ctxo_ref[rs, :], weight(wo_ref, HALF_QKV, HALF_QKV + HALF_OUT), NT)
        attn = attn + mm(ctx, weight(w_ref, HALF_QKV, HALF_QKV + HALF_OUT), NT)
        xh, rstd = norm_fwd(attn)
        rstd = jnp.broadcast_to(rstd, (BLK, 128))
        for s in range(2):
            for q in range(4):
                r = s * SPAN + q * 32
                xh_ref[q, i * 2 + s] = xh[r : r + 32]
                rstd_ref[q, i * 2 + s] = rstd[r : r + 32]
        return carry

    lax.fori_loop(0, x_ref.shape[0] // BLK, step, 0, unroll=2)


def attn_shapes(rows):
    return [((rows, HALF_QKV), BF), ((rows, HALF_OUT), BF), ((rows // SPAN, 8, 2 * SPAN), F32)]


def attn_one(first, tab, low, high, x):
    rows = x.shape[0]
    return call(
        partial(attn_one_kernel, first), attn_shapes(rows) + [((NB, RB, ONE), BF)],
        [SM, VM, VM, VM], tab, low, high, x,
        vmem=16, flops=rows * 4e6, moved=rows * 8000 + 2e6, trans=rows * 800, name="attn_one",
    )


def attn_two(first, tab, low, high, x, w_own, ctx_own):
    rows = x.shape[0]
    spans = rows // SPAN
    out = attn_shapes(rows) + [
        ((4, spans, 32, D), F32),
        ((4, spans, 32, 128), F32),
        ((8, D), F32),
        ((NB, RB, ONE), BF),
    ]
    return call(
        partial(attn_two_kernel, first), out, [SM] + [VM] * 5, tab, low, high, x, w_own, ctx_own,
        vmem=16, flops=rows * 5e6, moved=rows * 12000 + 4e6, trans=rows * 800, name="attn_two",
    )


def gelu_pair(u):
    a = jnp.abs(u)
    d = 1.0 + (0.3275911 * 0.5**0.5) * a
    t = pl.reciprocal(d, approx=True)
    t = t * (2.0 - d * t)
    e = jnp.exp(-0.5 * u * u)
    poly = 0.5307027145 * t - 0.7265760135
    poly = poly * t + 0.7107068705
    poly = poly * t - 0.142248368
    poly = poly * t + 0.127414796
    tail = (poly * t) * e
    phi = jnp.where(u >= 0.0, 1.0 - tail, tail)
    return u * phi, phi + (0.3989422804014327 * u) * e


TILE = 512


def ffn_up_kernel(pos, xh_ref, p_ref, w_ref, g_ref, gp_ref, *yt_ref):
    def step(i, carry):
        rs = pl.ds(pl.multiple_of(i * BLK, BLK), BLK)
        y = xh_ref[rs, :] * p_ref[0:1, :] + p_ref[1:2, :]
        yb = y.astype(BF)
        if yt_ref:
            store_turned(yt_ref[0], At(pos, POS_EARLY), yb, pl.multiple_of(i * BLK, BLK), BLK)
        for t in range(HALF_FF // TILE):
            u = mm(yb, weight(w_ref, t * TILE, (t + 1) * TILE))
            g, gp = gelu_pair(u)
            g_ref[rs, t * TILE : (t + 1) * TILE] = g.astype(BF)
            gp_ref[rs, t * TILE : (t + 1) * TILE] = gp.astype(BF)
        return carry

    lax.fori_loop(0, xh_ref.shape[0] // BLK, step, 0, unroll=2)


def ffn_up(pos, xh, prow, w, turned, name):
    rows = xh.shape[0]
    out = [((rows, HALF_FF), BF), ((rows, HALF_FF), BF)]
    if turned:
        out.append(((2, NB, RB, rows), BF))
    return call(
        ffn_up_kernel, out, [SM, VM, VM, VM], pos, xh, prow, w,
        vmem=16, flops=rows * 2.4e6, moved=rows * 9000 + 2e6, trans=rows * 6000, name=name,
    )


def down_block(r0, xh1_ref, p_ref, acts, downs):
    rs = pl.ds(r0, BLK)
    total = xh1_ref[rs, :] * p_ref[0:1, :] + p_ref[1:2, :]
    for g_ref, w_ref in zip(acts, downs):
        total = total + mm(g_ref[rs, :], weight(w_ref, 0, HALF_FF), NT)
    return norm_fwd(total)


def first_kernel(xh1_ref, p_ref, g0, g1, d0, d1, mixed_ref, cls_ref, xh_ref, rstd_ref):
    xh, rstd = down_block(0, xh1_ref, p_ref, (g0, g1), (d0, d1))
    xh_ref[...] = xh
    rstd_ref[...] = jnp.broadcast_to(rstd, rstd_ref.shape)
    out = (xh * p_ref[2:3, :] + p_ref[3:4, :]).reshape(mixed_ref.shape)
    mixed_ref[...] = out.astype(BF)
    cls_ref[...] = out[:, 0, :]


def first_rows(xh1, prow, acts, downs):
    spans = BLK // 32
    return call(
        first_kernel,
        [((spans, 32, D), BF), ((spans, D), F32), ((BLK, D), F32), ((BLK, 128), F32)],
        [VM] * 6, xh1, prow, *acts, *downs,
        vmem=8, flops=BLK * 4.8e6, moved=BLK * 16000 + 5e6, name="first_rows",
    )


def back_block(r0, grad, xh2, rstd2, gps, xh1_ref, rstd1_ref, p_ref, ups, downs, dus):
    rs = pl.ds(r0, BLK)
    sum_g2 = jnp.sum(grad * xh2, axis=0, keepdims=True)
    sum_b2 = jnp.sum(grad, axis=0, keepdims=True)
    dh = norm_bwd(grad, xh2, rstd2, p_ref[2:3, :])
    df = dh.astype(BF)
    total = dh
    for gp_ref, up_ref, down_ref, du_ref in zip(gps, ups, downs, dus):
        for t in range(HALF_FF // TILE):
            lo, hi = t * TILE, (t + 1) * TILE
            dg = mm(df, weight(down_ref, lo, hi))
            du_ref[:, lo:hi] = (dg * gp_ref[rs, lo:hi].astype(F32)).astype(BF)
        total = total + mm(du_ref[...], weight(up_ref, 0, HALF_FF), NT)
    xh1 = xh1_ref[rs, :]
    sum_g1 = jnp.sum(total * xh1, axis=0, keepdims=True)
    sum_b1 = jnp.sum(total, axis=0, keepdims=True)
    dh1 = norm_bwd(total, xh1, rstd1_ref[rs, 0:1], p_ref[0:1, :])
    return df, dh1, (sum_g1, sum_b1, sum_g2, sum_b2)


def back_shapes():
    return [
        ((2, NB, RB, BLK), BF),
        ((BLK, HALF_FF), BF),
        ((BLK, HALF_FF), BF),
        ((BLK // 32, 32, D), F32),
        ((8, D), F32),
    ]


def rest_kernel(
    at, pos, xh1_ref, rstd1_ref, p_ref, g0, g1, gp0, gp1, cot_ref, u0, u1, d0, d1,
    dft_ref, du0_ref, du1_ref, dh1_ref, sums_ref, mixed_ref,
):
    r0, c0 = at * BLK, at * 32
    xh, rstd = down_block(r0, xh1_ref, p_ref, (g0, g1), (d0, d1))
    out = xh * p_ref[2:3, :] + p_ref[3:4, :]
    mixed_ref[...] = out.reshape(mixed_ref.shape).astype(BF)
    grad = cot_ref[:, c0 : c0 + 32, :].astype(F32).reshape(BLK, D)
    df, dh1, sums = back_block(
        r0, grad, xh, rstd, (gp0, gp1), xh1_ref, rstd1_ref, p_ref, (u0, u1), (d0, d1), (du0_ref, du1_ref)
    )
    store_turned(dft_ref, At(pos, POS_LATE), df, 0, BLK)
    dh1_ref[...] = dh1.reshape(dh1_ref.shape)
    for n in range(4):
        sums_ref[n : n + 1, :] = sums[n]


def rest_rows(at, pos, xh1, rstd1, prow, acts, gps, cot, ups, downs):
    return call(
        partial(rest_kernel, at),
        back_shapes() + [((BLK // 32, 32, D), BF)],
        [SM] + [VM] * 12, pos, xh1, rstd1, prow, *acts, *gps, cot, *ups, *downs,
        vmem=16, flops=BLK * 14.5e6, moved=BLK * 40000 + 1e7, name=f"rest_rows_{at}",
    )


def class_kernel(
    pos, cls_ref, cot_ref, xh2_ref, rstd2_ref, xh1_ref, rstd1_ref, p_ref, gp0, gp1, u0, u1, d0, d1,
    dft_ref, du0_ref, du1_ref, dh1_ref, sums_ref,
):
    spans = cls_ref.shape[0]
    grad = cot_ref[:, 0:32, :].astype(F32)
    first = lax.broadcasted_iota(jnp.int32, grad.shape, 1) == 0
    grad = grad + jnp.where(first, cls_ref[...].reshape(spans, 1, D), 0.0)
    grad = grad.reshape(BLK, D)
    df, dh1, sums = back_block(
        0, grad, xh2_ref[...], rstd2_ref[:, 0:1], (gp0, gp1), xh1_ref, rstd1_ref, p_ref,
        (u0, u1), (d0, d1), (du0_ref, du1_ref),
    )
    store_turned(dft_ref, At(pos, POS_LATE), df, 0, BLK)
    dh1_ref[...] = dh1.reshape(dh1_ref.shape)
    for n in range(4):
        sums_ref[n : n + 1, :] = sums[n]


def class_rows(pos, grad_cls, cot, xh2, rstd2, xh1, rstd1, prow, gps, ups, downs):
    return call(
        class_kernel,
        back_shapes(),
        [SM] + [VM] * 13, pos, grad_cls, cot, xh2, rstd2, xh1, rstd1, prow, *gps, *ups, *downs,
        vmem=16, flops=BLK * 9.7e6, moved=BLK * 30000 + 1e7, name="class_rows",
    )


def contrast_kernel(where, doc_ref, cls_ref, loss_ref, grad_ref, rows, own_doc):
    spans = doc_ref.shape[1]
    doc_row = doc_ref[...].astype(F32)
    doc_col = jnp.broadcast_to(doc_row, (128, spans)).T[:, 0:1]
    blocks, per = cls_ref.shape[0], cls_ref.shape[1]
    where = At(where, CLASS_AT)
    me = where[0]
    for n in range(blocks):
        rows[where[1 + n]] = cls_ref[n].astype(F32)
    a = rows[...].reshape(spans, D).astype(BF)
    own = rows[me].astype(BF)
    scale = D ** (-0.5)
    col = lax.broadcasted_iota(jnp.int32, (spans, spans), 1)
    row = lax.broadcasted_iota(jnp.int32, (spans, spans), 0)
    logits = mm(a, a, NT) * scale
    partner = (doc_col == doc_row) & (row != col)
    masked = jnp.where(row == col, -1000000000.0, logits)
    top = jnp.max(masked, axis=0, keepdims=True)
    lse = jnp.log(jnp.sum(jnp.exp(masked - top), axis=0, keepdims=True)) + top
    positive = jnp.sum(jnp.where(partner, logits, 0.0), axis=0, keepdims=True)
    flagged = jnp.max(jnp.where(partner, 1.0, 0.0), axis=0, keepdims=True)
    count = jnp.sum(flagged, axis=1, keepdims=True)
    loss = jnp.sum(flagged * (lse - positive), axis=1, keepdims=True) / count
    loss_ref[...] = jnp.broadcast_to(loss, loss_ref.shape)

    weight_row = flagged * (CONTRAST * spans) / count
    own_doc[...] = doc_col.reshape(blocks, per, 1)
    docs = own_doc[me]
    col = lax.broadcasted_iota(jnp.int32, (per, spans), 1)
    row = lax.broadcasted_iota(jnp.int32, (per, spans), 0) + me * per
    logits = mm(own, a, NT) * scale
    same = jnp.where((docs == doc_row) & (row != col), 1.0, 0.0)
    masked = jnp.where(row == col, -1000000000.0, logits)
    top = jnp.max(masked, axis=1, keepdims=True)
    ex = jnp.exp(masked - top)
    soft = ex / jnp.sum(ex, axis=1, keepdims=True)
    own_weight = jnp.max(same, axis=1, keepdims=True) * (CONTRAST * spans) / count
    sym = own_weight * (soft - same) + weight_row * (jnp.exp(masked - lse) - same)
    high = sym.astype(BF)
    low = (sym - high.astype(F32)).astype(BF)
    grad_ref[...] = (mm(high, a) + mm(low, a)) * scale


def contrast(where, doc_row, cls_all):
    blocks, per, _ = cls_all.shape
    spans = blocks * per
    return call(
        contrast_kernel,
        [((1, 128), F32), ((per, D), F32)],
        [SM, VM, VM],
        where, doc_row, cls_all,
        vmem=8 if spans <= 256 else 40, flops=2 * spans * spans * D, moved=spans * D * 2,
        scratch=[pltpu.VMEM((blocks, per, D), F32), pltpu.VMEM((blocks, per, 1), F32)],
        name="contrast",
    )


def turned_of(refs, n):
    return jnp.concatenate([ref[n].reshape(D, ref.shape[3]) for ref in refs], axis=1)


def grad_other_kernel(count, *refs):
    xts, ys, out_ref = refs[:count], refs[count:-1], refs[-1]
    xt = turned_of(xts, 1)
    for t in range(HALF_FF // TILE):
        lo, hi = t * TILE, (t + 1) * TILE
        grad = mm(xt, jnp.concatenate([y[:, lo:hi] for y in ys], axis=0))
        out_ref[:, :, lo:hi] = grad.astype(BF).reshape(NB, RB, TILE)


def grad_other(xts, ys, name):
    rows = sum(y.shape[0] for y in ys)
    return call(
        partial(grad_other_kernel, len(xts)),
        [((NB, RB, HALF_FF), BF)],
        [VM] * (len(xts) + len(ys)), *xts, *ys,
        vmem=12, flops=2 * rows * D * HALF_FF, moved=rows * 8000 + 2.4e6, name=name,
    )[0]


def grad_own_kernel(count, came_ref, *refs):
    xts, ys, keep_ref, send_ref = refs[:count], refs[count:-2], refs[-2], refs[-1]
    nh = NB // 2
    xt = turned_of(xts, 0)
    for t in range(HALF_FF // TILE):
        lo, hi = t * TILE, (t + 1) * TILE
        grad = mm(xt, jnp.concatenate([y[:, lo:hi] for y in ys], axis=0))
        grad = (grad.reshape(NB, RB, TILE) + came_ref[:, :, lo:hi].astype(F32)).astype(BF)
        keep_ref[:, :, lo:hi] = grad[:nh]
        send_ref[:, :, lo:hi] = grad[nh:]


def grad_own(xts, ys, came, name):
    rows = sum(y.shape[0] for y in ys)
    return call(
        partial(grad_own_kernel, len(xts)),
        [((NB // 2, RB, HALF_FF), BF)] * 2,
        [VM] * (1 + len(xts) + len(ys)), came, *xts, *ys,
        vmem=12, flops=2 * rows * D * HALF_FF, moved=rows * 8000 + 4.8e6, name=name,
    )


def natural(refs, i):
    return jnp.concatenate([ref[i * 2 + s] for s in range(2) for ref in refs], axis=0)


def attn_back_kernel(pos, r0_ref, r1_ref, r2_ref, r3_ref, qkv_ref, lse_ref, w_ref, dqkv_ref, *dat_ref):
    masks = head_masks(SPAN, HEAD ** (-0.5))
    plain = head_masks(SPAN, 1.0)
    spans = r0_ref.shape[0]

    def step(i, carry):
        r0 = pl.multiple_of(i * BLK, BLK)
        da = natural((r0_ref, r1_ref, r2_ref, r3_ref), i).astype(BF)
        if dat_ref:
            store_turned(dat_ref[0], At(pos, POS_EARLY), da, r0, BLK)
        dctx = mm(da, weight(w_ref, HALF_QKV, HALF_QKV + HALF_OUT)).astype(BF)
        pairs = [(s, j) for s in range(2) for j in range(3)]

        def part(ref, n, s, j):
            rs = pl.ds(pl.multiple_of(r0 + s * SPAN, SPAN), SPAN)
            return ref.at[rs, n * HALF_OUT + j * 128 : n * HALF_OUT + (j + 1) * 128]

        qs = [stack_heads(part(qkv_ref, 0, s, j)[...], masks) for s, j in pairs]
        ks = [part(qkv_ref, 1, s, j)[...] for s, j in pairs]
        sts = [mm(k, q, NT) for k, q in zip(ks, qs)]
        dcs = [stack_heads(dctx[s * SPAN : (s + 1) * SPAN, j * 128 : (j + 1) * 128], plain) for s, j in pairs]
        dpts = [mm(part(qkv_ref, 2, s, j)[...], dc, NT) for (s, j), dc in zip(pairs, dcs)]
        pts = [jnp.exp(st - lse_ref[i * 2 + s, j : j + 1, :]) for (s, j), st in zip(pairs, sts)]
        dvs = [mm(pt.astype(BF), dc) for pt, dc in zip(pts, dcs)]
        dsts = [
            (pt * (dpt - jnp.sum(pt * dpt, axis=0, keepdims=True))).astype(BF) for pt, dpt in zip(pts, dpts)
        ]
        dks = [mm(dst, q) for dst, q in zip(dsts, qs)]
        dqs = [merge_heads(mm(dst, k, TN)) * HEAD ** (-0.5) for dst, k in zip(dsts, ks)]
        for n, grads in enumerate((dqs, dks, dvs)):
            for (s, j), grad in zip(pairs, grads):
                part(dqkv_ref, n, s, j)[...] = grad.astype(BF)
        return carry

    lax.fori_loop(0, spans // 2, step, 0, unroll=2)


def attn_back(pos, dh1, qkv, lse, w, turned, name):
    rows = qkv.shape[0]
    out = [((rows, HALF_QKV), BF)]
    if turned:
        out.append(((2, NB, RB, rows), BF))
    return call(
        attn_back_kernel, out,
        [SM] + [VM] * 7, pos, *dh1, qkv, lse, w,
        vmem=16, flops=rows * 6e6, moved=rows * 10000 + 3e6, trans=rows * 800, name=name,
    )


def last_value(order, xt_ref, dqkv_ref, dat_ref, ctx_ref, t):
    rows = xt_ref.shape[3]
    if t < 3:
        return mm(xt_ref[order].reshape(D, rows), dqkv_ref[:, t * HALF_OUT : (t + 1) * HALF_OUT])
    return mm(dat_ref[order].reshape(D, rows), ctx_ref[...])


def norm_columns(sums):
    total = sums[0][0:4, :]
    for ref in sums[1:]:
        total = total + ref[0:4, :]
    return jnp.concatenate([total, jnp.zeros((124, D), F32)], axis=0).T


def last_other_kernel(pos, xt_ref, dqkv_ref, dat_ref, ctx_ref, s0, s1, s2, s3, out_ref):
    for t in range(4):
        grad = last_value(1, xt_ref, dqkv_ref, dat_ref, ctx_ref, t)
        lo = t * HALF_OUT
        out_ref[:, :, lo : lo + HALF_OUT] = grad.astype(BF).reshape(NB, RB, HALF_OUT)
    norm = norm_columns((s0, s1, s2, s3)).astype(BF)
    for j in range(NB):
        out_ref[pos[POS_EARLY + NB + j], :, HALF_QKV + HALF_OUT :] = norm[j * RB : (j + 1) * RB]


def last_other(pos, xt, dqkv, dat, ctx, sums):
    rows = xt.shape[3]
    return call(
        last_other_kernel,
        [((NB, RB, ONE), BF)],
        [SM] + [VM] * 8, pos, xt, dqkv, dat, ctx, *sums,
        vmem=12, flops=2 * rows * D * HALF_FF, moved=rows * 8000 + 2.4e6, name="last_other",
    )[0]


def last_own_kernel(
    pos, xt_ref, dqkv_ref, dat_ref, ctx_ref, s0, s1, s2, s3, came_ref, keep_ref, send_ref, cols
):
    nh = NB // 2
    norm = norm_columns((s0, s1, s2, s3))
    for j in range(NB):
        cols[pos[POS_EARLY + j]] = norm[j * RB : (j + 1) * RB]
    for t in range(5):
        lo = t * HALF_OUT
        hi = min(lo + HALF_OUT, ONE)
        if t < 4:
            grad = last_value(0, xt_ref, dqkv_ref, dat_ref, ctx_ref, t).reshape(NB, RB, HALF_OUT)
        else:
            grad = cols[...]
        grad = (grad + came_ref[:, :, lo:hi].astype(F32)).astype(BF)
        keep_ref[:, :, lo:hi] = grad[:nh]
        send_ref[:, :, lo:hi] = grad[nh:]


def last_own(pos, xt, dqkv, dat, ctx, sums, came):
    rows = xt.shape[3]
    return call(
        last_own_kernel,
        [((NB // 2, RB, ONE), BF)] * 2,
        [SM] + [VM] * 9, pos, xt, dqkv, dat, ctx, *sums, came,
        vmem=12, flops=2 * rows * D * HALF_FF, moved=rows * 8000 + 4.8e6,
        scratch=[pltpu.VMEM((NB, RB, 128), F32)], name="last_own",
    )


def input_grad_kernel(r0_ref, r1_ref, r2_ref, r3_ref, own_ref, other_ref, w0_ref, w1_ref, out_ref):
    spans = r0_ref.shape[0]

    def step(i, carry):
        rs = pl.ds(pl.multiple_of(i * BLK, BLK), BLK)
        total = natural((r0_ref, r1_ref, r2_ref, r3_ref), i)
        total = total + mm(own_ref[rs, :], weight(w0_ref, 0, HALF_QKV), NT)
        total = total + mm(other_ref[rs, :], weight(w1_ref, 0, HALF_QKV), NT)
        out_ref[rs, :] = total
        return carry

    lax.fori_loop(0, spans // 2, step, 0, unroll=2)


def input_grads(dh1, own, other, w_own, w_other):
    rows = own.shape[0]
    return call(
        input_grad_kernel,
        [((rows, D), F32)],
        [VM] * 8, *dh1, own, other, w_own, w_other,
        vmem=12, flops=rows * 3.6e6, moved=rows * 12000 + 5e6, name="input_grads",
    )[0]


def place_kernel(half, *refs):
    own, other, g_own, g_other = refs[0:4], refs[4:8], refs[8], refs[9]
    mixed_ref, grad_ref, sems = refs[10:]
    spans = g_own.shape[0]
    copies = []
    for n, (pieces, g) in enumerate(((own, g_own), (other, g_other))):
        at = pl.ds(half[HALF_AT + n] * spans, spans)
        for q in range(4):
            to = mixed_ref.at[at, 32 * q : 32 * q + 32, :]
            copies.append(pltpu.make_async_copy(pieces[q], to, sems.at[5 * n + q]))
        copies.append(pltpu.make_async_copy(g, grad_ref.at[at], sems.at[5 * n + 4]))
    for c in copies:
        c.start()
    for c in copies:
        c.wait()


def place(half, own, other, g_own, g_other):
    spans = own[0].shape[0]
    g_own, g_other = (g.reshape(spans, SPAN, D) for g in (g_own, g_other))
    return pl.pallas_call(
        place_kernel,
        out_shape=[
            jax.ShapeDtypeStruct((2 * spans, SPAN, D), BF),
            jax.ShapeDtypeStruct((2 * spans, SPAN, D), F32),
        ],
        in_specs=[SM] + [VM] * 10,
        out_specs=[HBM] * 2,
        scratch_shapes=[pltpu.SemaphoreType.DMA((10,))],
        compiler_params=params(16),
        cost_estimate=cost(0, spans * SPAN * D * 24),
        name="place",
    )(half, *own, *other, g_own, g_other)


def squares_kernel(k0, c0, k1, c1, k2, c2, g0, g1, g2, sq_ref):
    main = HALF_QKV + HALF_OUT
    total = jnp.zeros((1, 1), F32)
    for keep, came, out in ((k0, c0, g0), (k1, c1, g1), (k2, c2, g2)):
        grad = keep[0].astype(F32) + came[0].astype(F32)
        out[...] = grad
        sq = jnp.sum(grad[:, :main] * grad[:, :main], axis=1, keepdims=True)
        if grad.shape[1] > main:
            cols = grad[:, main:]
            sq = sq + 0.5 * jnp.sum(cols * cols, axis=1, keepdims=True)
        total = total + jnp.sum(sq, axis=0, keepdims=True)
    sq_ref[...] = jnp.broadcast_to(total, sq_ref.shape)


def squares_of(pairs):
    shard = pairs[0][0].shape[1]
    out = [((shard, k.shape[2]), F32) for k, _ in pairs] + [((8, 128), F32)]
    flat = [a for pair in pairs for a in pair]
    return call(squares_kernel, out, [VM] * 6, *flat, vmem=8, moved=shard * 40000, name="squares")


def adam_parts(weight, gradient, moment_one, moment_two, step_rate, decay_rate):
    first_new = 0.9 * moment_one + 0.1 * gradient
    second_new = 0.999 * moment_two + 0.001 * gradient * gradient
    corr_first = first_new * (1.0 / (1.0 - 0.9**STEP))
    corr_second = second_new * (1.0 / (1.0 - 0.999**STEP))
    weight_new = weight - step_rate * (
        corr_first / (jnp.sqrt(corr_second) + 1e-08) + decay_rate * weight
    )
    return first_new, second_new, weight_new


def adam_kernel(sq_ref, last_ref, up_ref, down_ref, cols_ref, *refs):
    ins, outs, wide = refs[:15], refs[15:-1], refs[-1]
    norm = jnp.sqrt(sq_ref[0:1, 0:1])
    outs[15][...] = jnp.broadcast_to(norm, outs[15].shape)
    scale = 1.0 / jnp.maximum(norm, 1.0)

    def update(n, at, grad, rate, decay):
        new = adam_parts(ins[n][at], grad * scale, ins[5 + 2 * n][at], ins[6 + 2 * n][at], rate, decay)
        for m in range(3):
            outs[3 * n + m][at] = new[m]

    for part in range(3):
        update(0, part, last_ref[:, part * HALF_OUT : (part + 1) * HALF_OUT], 0.02, 0.01)
    update(1, Ellipsis, last_ref[:, HALF_QKV : HALF_QKV + HALF_OUT], 0.02, 0.01)
    update(2, Ellipsis, up_ref[...], 0.02, 0.01)
    update(3, Ellipsis, down_ref[...], 0.02, 0.01)
    shard = last_ref.shape[0]
    wide[...] = jnp.zeros_like(wide)
    wide[0:shard, :] = 0.5 * (last_ref[:, HALF_QKV + HALF_OUT :] + cols_ref[...])
    update(4, Ellipsis, wide[...].T[0:4, 0:shard], 0.5, 0.0)


def adam(squares, last, up, down, cols, weights, moments):
    shapes = [w.shape for w in weights]
    out = [(s, F32) for s in shapes for _ in range(3)] + [((8, 128), F32)]
    args = (squares, last, up, down, cols, *weights, *moments)
    return call(
        adam_kernel, out, [VM] * len(args), *args, vmem=16, moved=7 * 4 * last.shape[0] * 4608,
        scratch=[pltpu.VMEM((128, 128), F32)], name="adam",
    )


def after(value, *others):
    return lax.optimization_barrier((value, others))[0]


def body(
    tokens,
    cotangent,
    span_doc,
    qkv_weight,
    out_weight,
    ffn_in_weight,
    ffn_out_weight,
    norm_params,
    qkv_first,
    qkv_second,
    out_first,
    out_second,
    ffn_in_first,
    ffn_in_second,
    ffn_out_first,
    ffn_out_second,
    norm_first,
    norm_second,
):
    n_dp = lax.axis_size("dp")
    dp = lax.axis_index("dp")
    core = lax.axis_index("tensor")
    shard = D // n_dp
    rows = tokens.shape[0] // 2
    spans = rows // SPAN
    direct = n_dp == NB
    early, late = bit_orders(n_dp)
    steps = len(early[0])
    last = steps - 1

    tab = lax.dynamic_index_in_dim(device_tables(n_dp), dp * 2 + core, 0, keepdims=False)
    x = lax.dynamic_slice_in_dim(tokens, core * rows, rows, 0)
    cot = lax.dynamic_slice_in_dim(cotangent, core * rows, rows, 0).reshape(spans, SPAN, D)

    def places(orders, other=0):
        return dp ^ jnp.array([rel_of(order) for order in orders], jnp.int32)[core ^ other]

    def send_on(block, orders, k):
        return lax.ppermute(block, AXES, pairs_of(n_dp, orders, k))

    def join(held, came):
        return jnp.concatenate([held, came], axis=0)

    def pieces(at, low, high):
        if direct:
            return at, tab, low, high
        which = {AT_EARLY: places(early), AT_LATE: places(late), AT_OTHER: places(early, 1)}[at]
        full = join(low, high)[jnp.argsort(which)].reshape(NB, RB, -1)
        return at, tab, full[: NB // 2], full[NB // 2 :]

    def halves(orders, keep, send):
        if direct:
            return keep, send
        full = join(keep, send).reshape(n_dp, shard, -1)[places(orders)]
        return full[: n_dp // 2], full[n_dp // 2 :]

    def add(keep, came):
        total = keep.astype(F32) + came.astype(F32)
        size = total.shape[0] // 2
        return total[:size].astype(BF), total[size:].astype(BF)

    turned = ((1, 0, 2), (1, 0), (0, 1), (1, 0), (0, 1))
    weights = (qkv_weight, out_weight, ffn_in_weight, ffn_out_weight, norm_params)
    weights = tuple(w.transpose(t) for w, t in zip(weights, turned))
    one, up, down = pack(*weights)
    one_came = send_on(one, early, 0)
    up_came = send_on(up, late, 0)
    down_came = send_on(down, early, 0)
    one, tab, x, cot, down_came = after((join(one, one_came), tab, x, cot, down_came), up_came)
    for k in range(1, last):
        one_came = send_on(one, early, k)
        if k > 1:
            up = after(join(up, up_came), one)
            up_came = send_on(up, late, k - 1)
        one = join(one, one_came)
        if k > 1:
            one = after(one, up_came)
    one_came = send_on(one, early, last)
    for k in range(max(last - 1, 1), last):
        up = join(up, up_came)
        up_came = send_on(up, late, k)
    one, one_came = after((one, one_came), up_came)
    up = after(join(up, up_came), one_came)
    up_came = send_on(up, late, last)
    down = after(join(down, down_came), one_came)
    down_came = send_on(down, early, 1)

    one_other = (core_swap(one), core_swap(one_came))
    qkv0, ctx0, lse0, w10 = attn_one(*pieces(AT_EARLY, one, one_came), x)
    ctx0 = after(ctx0, down_came)
    for k in range(2, last):
        down = join(down, after(down_came, ctx0))
        down_came = send_on(down, early, k)
    qkv1, ctx1, lse1, xh1, rstd1, prow, w11 = attn_two(*pieces(AT_OTHER, *one_other), x, w10, ctx0)
    w1 = (w10, w11)
    xh1 = xh1.reshape(rows, D)
    rstd1 = rstd1.reshape(rows, 128)
    up_came, down_came = after((up_came, down_came), xh1)
    wu = assemble(*pieces(AT_LATE, up, up_came), "up_own")
    wu = (wu, core_swap(wu))
    down = join(down, down_came)
    down_came = send_on(down, early, last)
    act0, gp0, yt = ffn_up(tab, after(xh1, down), prow, wu[0], True, "ffn_up_own")
    wd = assemble(*pieces(AT_EARLY, down, after(down_came, act0)), "down_own")
    wd = (wd, core_swap(wd))
    act1, gp1 = ffn_up(tab, after(xh1, wd[0]), prow, wu[1], False, "ffn_up_other")
    acts, gps = (act0, act1), (gp0, gp1)
    mixed0, cls_own, xh2, rstd2 = first_rows(xh1, prow, acts, wd)

    held = cls_own.astype(BF)[None]
    back = []
    for k in reversed(range(steps)):
        came = lax.ppermute(held, "dp", [(d, d ^ (1 << k)) for d in range(n_dp)])
        if len(back) < 3:
            at = len(back) + 1
            back.append(rest_rows(at, tab, after(xh1, held), rstd1, prow, acts, gps, cot, wu, wd))
            came = after(came, back[-1][4])
        held = join(held, came)
    held = join(held, core_swap(held))
    loss, grad_cls = contrast(tab, span_doc.reshape(1, -1), held)
    back.insert(0, (*class_rows(tab, grad_cls, cot, xh2, rstd2, xh1, rstd1, prow, gps, wu, wd), mixed0))
    dft, du0, du1, dh1, sums, mixed_own = zip(*back)

    d_other = grad_other(dft, (act1,), "grad_down_other")
    d_came = core_swap(d_other)
    u_other = grad_other((after(yt, d_other),), du1, "grad_up_other")
    u_came = core_swap(u_other)
    d_keep, d_send = halves(
        late, *grad_own((after(dft[0], u_other),) + dft[1:], (act0,), d_came, "grad_down_own")
    )
    d_came = send_on(d_send, late, last)
    u_keep, u_send = halves(early, *grad_own((after(yt, d_keep),), du0, u_came, "grad_up_own"))
    dh1 = (after(dh1[0], u_keep),) + dh1[1:]
    tokt = turn(tab, after(x, u_keep))
    dqkv1, dat = attn_back(tab, dh1, qkv1, lse1, w1[1], True, "attn_back_other")
    l_other = last_other(tab, tokt, dqkv1, dat, ctx1, sums)

    d_came, l_other = after((d_came, l_other))
    d_keep, d_send = add(d_keep, d_came)
    u_came = send_on(after(u_send, l_other), early, last)
    d_came = send_on(d_send, late, last - 1)
    l_came = core_swap(l_other)
    (dqkv0,) = attn_back(
        tab, (after(dh1[0], l_other),) + dh1[1:], qkv0, lse0, w1[0], False, "attn_back_own"
    )
    l_keep, l_send = halves(early, *last_own(tab, tokt, dqkv0, dat, ctx0, sums, l_came))
    l_came = send_on(l_send, early, last)
    grad_in = input_grads((after(dh1[0], l_send),) + dh1[1:], dqkv0, dqkv1, w1[0], w1[1])
    u_came, d_came = after((u_came, d_came), l_send)
    u_keep, u_send = add(u_keep, u_came)
    d_keep, d_send = add(d_keep, d_came)
    u_came = send_on(u_send, early, last - 1)
    d_came = send_on(d_send, late, last - 2)
    for k in reversed(range(last)):
        l_came, u_came, d_came = after((l_came, u_came, d_came))
        l_keep, l_send = add(l_keep, l_came)
        l_came = send_on(l_send, early, k)
        if k > 0:
            u_keep, u_send = add(u_keep, u_came)
            u_came = send_on(u_send, early, k - 1)
        if k > 1:
            d_keep, d_send = add(d_keep, d_came)
            d_came = send_on(d_send, late, k - 2)
        if k == last - 1:
            grad_came = core_swap(after(grad_in, l_send))
            mixed_other = tuple(core_swap(m) for m in after(mixed_own, l_send))
            l_came = after(l_came, grad_came, mixed_other)
        if k == last - 2:
            mixed, input_grad = place(tab, mixed_own, mixed_other, after(grad_in, l_send), grad_came)
            l_came = after(l_came, input_grad)

    last_grad, down_grad, up_grad, squares = squares_of(((l_keep, l_came), (d_keep, d_came), (u_keep, u_came)))
    cols = core_swap(last_grad[:, HALF_QKV + HALF_OUT :])
    squares = squares + core_swap(squares)
    bits = [1 << k for k in reversed(range(steps))]
    for one_bit, two_bit in zip(bits[::2], bits[1::2]):
        near, far, both = (
            lax.ppermute(squares, "dp", [(d, d ^ b) for d in range(n_dp)])
            for b in (one_bit, two_bit, one_bit ^ two_bit)
        )
        squares = (squares + near) + (far + both)
    moments = (
        qkv_first, qkv_second, out_first, out_second, ffn_in_first, ffn_in_second,
        ffn_out_first, ffn_out_second, norm_first, norm_second,
    )
    new = adam(
        squares, last_grad, up_grad, down_grad, cols,
        weights,
        [m.transpose(turned[n // 2]) for n, m in enumerate(moments)],
    )
    updated = [value.transpose(turned[n // 3]) for n, value in enumerate(new[:15])]
    return (
        mixed.reshape(2 * rows, D),
        input_grad.reshape(2 * rows, D),
        loss[0, 0],
        new[15][0, 0],
        *updated,
    )


def solution(mesh):
    rows = P("dp", None)
    qkv = P("dp", None, "tensor")
    turned = P("tensor", "dp")
    up = P("dp", "tensor")
    norm = P(None, "dp")
    weights = (qkv, turned, up, turned, norm)
    moments = tuple(spec for spec in weights for _ in range(2))
    updated = tuple(spec for spec in weights for _ in range(3))
    return jax.shard_map(
        body,
        mesh=mesh,
        in_specs=(rows, rows, P()) + weights + moments,
        out_specs=(rows, rows, P(), P()) + updated,
        check_vma=False,
    )
```

```python
from functools import partial

import jax
import jax.numpy as jnp
import numpy as np
from jax import lax
from jax.experimental import pallas as pl
from jax.experimental.pallas import tpu as pltpu
from jax.sharding import PartitionSpec as P

HEAD = 64
SPAN = 128
STEP = 10
D = 768
FF = 3072
NB = 16
RB = D // NB
HALF_QKV = 1152
HALF_OUT = 384
HALF_FF = 1536
ONE = HALF_QKV + HALF_OUT + 128
CONTRAST = 4.0
EPS = 1e-06
BF = jnp.bfloat16
F32 = jnp.float32
AXES = ("dp", "tensor")
SHRINK = 100

NN = (((1,), (0,)), ((), ()))
NT = (((1,), (1,)), ((), ()))
TN = (((0,), (0,)), ((), ()))


def mm(left, right, dims=NN):
    return lax.dot_general(left, right, dims, preferred_element_type=F32)


def params(vmem=56):
    vmem = vmem if vmem > 24 else min(vmem, 8)
    return pltpu.CompilerParams(vmem_limit_bytes=vmem * 2**20)


def cost(flops, bytes_accessed, trans=0):
    flops, bytes_accessed, trans = (n // SHRINK + 1 for n in (flops, bytes_accessed, trans))
    return pl.CostEstimate(flops=int(flops), bytes_accessed=int(bytes_accessed), transcendentals=int(trans))


HBM = pl.BlockSpec(memory_space=pl.ANY)


def bit_orders(n_dp):
    bits = n_dp.bit_length() - 1
    if bits == 4:
        return ((4, 8, 2, 1), (8, 4, 1, 2)), ((1, 4, 8, 2), (2, 8, 4, 1))
    up = tuple(1 << b for b in range(bits))[::-1]
    both = (up, up[: bits // 2] + up[bits // 2 :][::-1])
    return both, both


def pairs_of(n_dp, orders, step):
    out = []
    for d in range(n_dp):
        for c in range(2):
            out.append((d * 2 + c, (d ^ orders[c][step]) * 2 + c))
    return out


def rel_of(order):
    out = []
    for p in range(1 << len(order)):
        r = 0
        for k, b in enumerate(order):
            if (p >> k) & 1:
                r ^= b
        out.append(r)
    return out


AT_EARLY, AT_LATE, AT_OTHER, POS_EARLY, POS_LATE = 0, NB, 2 * NB, 3 * NB, 5 * NB
HALF_AT, CLASS_AT = 7 * NB, 7 * NB + 2


class At:
    def __init__(self, ref, first):
        self.ref, self.first = ref, first

    def __getitem__(self, n):
        return self.ref[self.first + n]


def device_tables(n_dp):
    kinds = [[rel_of(order) for order in orders] for orders in bit_orders(n_dp)]
    classes = rel_of([1 << k for k in reversed(range(n_dp.bit_length() - 1))])
    plain = list(range(NB))
    table = []
    for d in range(n_dp):
        for c in range(2):
            direct = n_dp == NB
            row = []
            for rel in kinds:
                row += [d ^ r for r in rel[c]] if direct else plain
            row += [d ^ r for r in kinds[0][1 - c]] if direct else plain
            for rel in kinds:
                for half in (c, 1 - c):
                    row += [rel[half].index(d ^ j) for j in range(NB)] if direct else plain
            me = d * 2 + c
            row += [c, 1 - c, me] + [me ^ (r << 1 | b) for b in range(2) for r in classes]
            table.append(row)
    return np.array(table, np.int32)


def core_swap(block):
    return lax.ppermute(block, "tensor", [(0, 1), (1, 0)])


VM = pl.BlockSpec(memory_space=pltpu.VMEM)
SM = pl.BlockSpec(memory_space=pltpu.SMEM)
BLK = 256


def call(kernel, out, in_specs, *args, vmem=16, flops=0, moved=0, trans=0, scratch=(), name=None):
    return pl.pallas_call(
        kernel,
        out_shape=[jax.ShapeDtypeStruct(s, t) for s, t in out],
        in_specs=in_specs,
        out_specs=[VM] * len(out),
        scratch_shapes=list(scratch),
        compiler_params=params(vmem),
        cost_estimate=cost(flops, moved, trans),
        name=name,
    )(*args)


def pack_kernel(qkv, out, up, down, norm, one_ref, two_ref, three_ref, wide, a0, a1, a2, a3, sems):
    rows = up.shape[0]
    wide[...] = jnp.zeros_like(wide)
    copies = [
        pltpu.make_async_copy(src, dst, sems.at[n])
        for n, (src, dst) in enumerate(
            ((qkv, a0), (out, a1), (down, a3), (up, a2))
        )
    ]
    for c in copies:
        c.start()
    copies[0].wait()
    for part in range(3):
        one_ref[0, :, part * HALF_OUT : (part + 1) * HALF_OUT] = a0[part].astype(BF)
    copies[1].wait()
    one_ref[0, :, HALF_QKV : HALF_QKV + HALF_OUT] = a1[...].astype(BF)
    wide[0:4, 0:rows] = norm[...]
    one_ref[0, :, HALF_QKV + HALF_OUT :] = wide[...].T[0:rows].astype(BF)
    copies[2].wait()
    three_ref[0] = a3[...].astype(BF)
    copies[3].wait()
    two_ref[0] = a2[...].astype(BF)


def pack(*shards):
    rows = shards[2].shape[0]
    return call(
        pack_kernel,
        [((1, rows, ONE), BF), ((1, rows, HALF_FF), BF), ((1, rows, HALF_FF), BF)],
        [pl.BlockSpec(memory_space=pltpu.HBM)] * 4 + [VM], *shards,
        vmem=60, moved=rows * 28000,
        scratch=[pltpu.VMEM((128, 128), F32)]
        + [pltpu.VMEM(w.shape, F32) for w in shards[:4]]
        + [pltpu.SemaphoreType.DMA((4,))],
        name="pack",
    )


def assemble_kernel(first, tab, low, high, out_ref):
    for n, ref in enumerate((low, high)):
        for p in range(NB // 2):
            out_ref[tab[first + n * (NB // 2) + p]] = ref[p]


def assemble(first, tab, low, high, name):
    width = low.shape[-1]
    return call(
        partial(assemble_kernel, first),
        [((NB, RB, width), BF)],
        [SM, VM, VM], tab, low, high,
        moved=4 * D * width, name=name,
    )[0]


def weight(w_ref, first, last):
    return w_ref[:, :, first:last].reshape(D, last - first)


def norm_fwd(hidden):
    center = hidden - jnp.mean(hidden, axis=-1, keepdims=True)
    spread = jnp.mean(center * center, axis=-1, keepdims=True)
    rstd = lax.rsqrt(spread + EPS)
    return center * rstd, rstd


def norm_bwd(grad, xh, rstd, gain):
    e = grad * gain
    m1 = jnp.mean(e, axis=-1, keepdims=True)
    m2 = jnp.mean(e * xh, axis=-1, keepdims=True)
    return rstd * (e - m1 - xh * m2)


def store_turned(ref, tab, value, col, width):
    turned = value.T
    for j in range(NB):
        block = turned[j * RB : (j + 1) * RB]
        for n in range(2):
            ref[n, tab[n * NB + j], :, pl.ds(col, width)] = block


def head_masks(rows, scale):
    lane = lax.broadcasted_iota(jnp.int32, (rows, 128), 1)
    return (
        jnp.where(lane < HEAD, scale, 0.0).astype(BF),
        jnp.where(lane < HEAD, 0.0, scale).astype(BF),
    )


def stack_heads(pair, masks):
    return jnp.concatenate([pair * masks[0], pair * masks[1]], axis=0)


def merge_heads(both):
    lane = lax.broadcasted_iota(jnp.int32, (SPAN, 128), 1)
    return jnp.where(lane < HEAD, both[:SPAN], both[SPAN:])


def turn_kernel(pos, x_ref, out_ref):
    rows = x_ref.shape[0]
    for i in range(rows // BLK):
        store_turned(out_ref, At(pos, POS_EARLY), x_ref[i * BLK : (i + 1) * BLK, :], i * BLK, BLK)


def turn(pos, x):
    rows = x.shape[0]
    return call(
        turn_kernel, [((2, NB, RB, rows), BF)], [SM, VM], pos, x, moved=rows * D * 6, name="turn"
    )[0]


def attn_rows(i, x, w_ref, masks, qkv_ref, ctx_ref, lse_ref):
    r0 = pl.multiple_of(i * BLK, BLK)
    qkv = mm(x, weight(w_ref, 0, HALF_QKV)).astype(BF)
    qkv_ref[pl.ds(r0, BLK), :] = qkv
    pairs = [(s, j) for s in range(2) for j in range(3)]

    def part(n, s, j):
        return qkv[s * SPAN : (s + 1) * SPAN, n * HALF_OUT + j * 128 : n * HALF_OUT + (j + 1) * 128]

    sts = [mm(part(1, s, j), stack_heads(part(0, s, j), masks), NT) for s, j in pairs]
    tops = [jnp.max(st, axis=0, keepdims=True) for st in sts]
    exs = [jnp.exp(st - top) for st, top in zip(sts, tops)]
    totals = [jnp.sum(ex, axis=0, keepdims=True) for ex in exs]
    pts = [(ex * (1.0 / total)).astype(BF) for ex, total in zip(exs, totals)]
    parts = [merge_heads(mm(pt, part(2, s, j), TN)).astype(BF) for pt, (s, j) in zip(pts, pairs)]
    for (s, j), top, total in zip(pairs, tops, totals):
        lse_ref[i * 2 + s, j : j + 1, :] = top + jnp.log(total)
    ctx = jnp.concatenate([jnp.concatenate(parts[s * 3 : s * 3 + 3], axis=1) for s in range(2)], axis=0)
    ctx_ref[pl.ds(r0, BLK), :] = ctx
    return ctx


def attn_one_kernel(first, tab, low, high, x_ref, qkv_ref, ctx_ref, lse_ref, w_ref):
    assemble_kernel(first, tab, low, high, w_ref)
    masks = head_masks(SPAN, HEAD ** (-0.5))

    def step(i, carry):
        x = x_ref[pl.ds(pl.multiple_of(i * BLK, BLK), BLK), :]
        attn_rows(i, x, w_ref, masks, qkv_ref, ctx_ref, lse_ref)
        return carry

    lax.fori_loop(0, x_ref.shape[0] // BLK, step, 0, unroll=2)


def attn_two_kernel(
    first, tab, low, high, x_ref, wo_ref, ctxo_ref,
    qkv_ref, ctx_ref, lse_ref, xh_ref, rstd_ref, p_ref, w_ref,
):
    assemble_kernel(first, tab, low, high, w_ref)
    cols = weight(w_ref, HALF_QKV + HALF_OUT, ONE).astype(F32)
    p_ref[...] = cols.T[:8]
    masks = head_masks(SPAN, HEAD ** (-0.5))

    def step(i, carry):
        rs = pl.ds(pl.multiple_of(i * BLK, BLK), BLK)
        x = x_ref[rs, :]
        ctx = attn_rows(i, x, w_ref, masks, qkv_ref, ctx_ref, lse_ref)
        attn = x.astype(F32) + mm(ctxo_ref[rs, :], weight(wo_ref, HALF_QKV, HALF_QKV + HALF_OUT), NT)
        attn = attn + mm(ctx, weight(w_ref, HALF_QKV, HALF_QKV + HALF_OUT), NT)
        xh, rstd = norm_fwd(attn)
        rstd = jnp.broadcast_to(rstd, (BLK, 128))
        for s in range(2):
            for q in range(4):
                r = s * SPAN + q * 32
                xh_ref[q, i * 2 + s] = xh[r : r + 32]
                rstd_ref[q, i * 2 + s] = rstd[r : r + 32]
        return carry

    lax.fori_loop(0, x_ref.shape[0] // BLK, step, 0, unroll=2)


def attn_shapes(rows):
    return [((rows, HALF_QKV), BF), ((rows, HALF_OUT), BF), ((rows // SPAN, 8, 2 * SPAN), F32)]


def attn_one(first, tab, low, high, x):
    rows = x.shape[0]
    return call(
        partial(attn_one_kernel, first), attn_shapes(rows) + [((NB, RB, ONE), BF)],
        [SM, VM, VM, VM], tab, low, high, x,
        vmem=16, flops=rows * 4e6, moved=rows * 8000 + 2e6, trans=rows * 800, name="attn_one",
    )


def attn_two(first, tab, low, high, x, w_own, ctx_own):
    rows = x.shape[0]
    spans = rows // SPAN
    out = attn_shapes(rows) + [
        ((4, spans, 32, D), F32),
        ((4, spans, 32, 128), F32),
        ((8, D), F32),
        ((NB, RB, ONE), BF),
    ]
    return call(
        partial(attn_two_kernel, first), out, [SM] + [VM] * 5, tab, low, high, x, w_own, ctx_own,
        vmem=16, flops=rows * 5e6, moved=rows * 12000 + 4e6, trans=rows * 800, name="attn_two",
    )


def gelu_pair(u):
    a = jnp.abs(u)
    d = 1.0 + (0.3275911 * 0.5**0.5) * a
    t = pl.reciprocal(d, approx=True)
    t = t * (2.0 - d * t)
    e = jnp.exp(-0.5 * u * u)
    poly = 0.5307027145 * t - 0.7265760135
    poly = poly * t + 0.7107068705
    poly = poly * t - 0.142248368
    poly = poly * t + 0.127414796
    tail = (poly * t) * e
    phi = jnp.where(u >= 0.0, 1.0 - tail, tail)
    return u * phi, phi + (0.3989422804014327 * u) * e


TILE = 512


def ffn_up_kernel(pos, xh_ref, p_ref, w_ref, g_ref, gp_ref, *yt_ref):
    def step(i, carry):
        rs = pl.ds(pl.multiple_of(i * BLK, BLK), BLK)
        y = xh_ref[rs, :] * p_ref[0:1, :] + p_ref[1:2, :]
        yb = y.astype(BF)
        if yt_ref:
            store_turned(yt_ref[0], At(pos, POS_EARLY), yb, pl.multiple_of(i * BLK, BLK), BLK)
        for t in range(HALF_FF // TILE):
            u = mm(yb, weight(w_ref, t * TILE, (t + 1) * TILE))
            g, gp = gelu_pair(u)
            g_ref[rs, t * TILE : (t + 1) * TILE] = g.astype(BF)
            gp_ref[rs, t * TILE : (t + 1) * TILE] = gp.astype(BF)
        return carry

    lax.fori_loop(0, xh_ref.shape[0] // BLK, step, 0, unroll=2)


def ffn_up(pos, xh, prow, w, turned, name):
    rows = xh.shape[0]
    out = [((rows, HALF_FF), BF), ((rows, HALF_FF), BF)]
    if turned:
        out.append(((2, NB, RB, rows), BF))
    return call(
        ffn_up_kernel, out, [SM, VM, VM, VM], pos, xh, prow, w,
        vmem=16, flops=rows * 2.4e6, moved=rows * 9000 + 2e6, trans=rows * 6000, name=name,
    )


def down_block(r0, xh1_ref, p_ref, acts, downs):
    rs = pl.ds(r0, BLK)
    total = xh1_ref[rs, :] * p_ref[0:1, :] + p_ref[1:2, :]
    for g_ref, w_ref in zip(acts, downs):
        total = total + mm(g_ref[rs, :], weight(w_ref, 0, HALF_FF), NT)
    return norm_fwd(total)


def first_kernel(xh1_ref, p_ref, g0, g1, d0, d1, mixed_ref, cls_ref, xh_ref, rstd_ref):
    xh, rstd = down_block(0, xh1_ref, p_ref, (g0, g1), (d0, d1))
    xh_ref[...] = xh
    rstd_ref[...] = jnp.broadcast_to(rstd, rstd_ref.shape)
    out = (xh * p_ref[2:3, :] + p_ref[3:4, :]).reshape(mixed_ref.shape)
    mixed_ref[...] = out.astype(BF)
    cls_ref[...] = out[:, 0, :]


def first_rows(xh1, prow, acts, downs):
    spans = BLK // 32
    return call(
        first_kernel,
        [((spans, 32, D), BF), ((spans, D), F32), ((BLK, D), F32), ((BLK, 128), F32)],
        [VM] * 6, xh1, prow, *acts, *downs,
        vmem=8, flops=BLK * 4.8e6, moved=BLK * 16000 + 5e6, name="first_rows",
    )


def back_block(r0, grad, xh2, rstd2, gps, xh1_ref, rstd1_ref, p_ref, ups, downs, dus):
    rs = pl.ds(r0, BLK)
    sum_g2 = jnp.sum(grad * xh2, axis=0, keepdims=True)
    sum_b2 = jnp.sum(grad, axis=0, keepdims=True)
    dh = norm_bwd(grad, xh2, rstd2, p_ref[2:3, :])
    df = dh.astype(BF)
    total = dh
    for gp_ref, up_ref, down_ref, du_ref in zip(gps, ups, downs, dus):
        for t in range(HALF_FF // TILE):
            lo, hi = t * TILE, (t + 1) * TILE
            dg = mm(df, weight(down_ref, lo, hi))
            du_ref[:, lo:hi] = (dg * gp_ref[rs, lo:hi].astype(F32)).astype(BF)
        total = total + mm(du_ref[...], weight(up_ref, 0, HALF_FF), NT)
    xh1 = xh1_ref[rs, :]
    sum_g1 = jnp.sum(total * xh1, axis=0, keepdims=True)
    sum_b1 = jnp.sum(total, axis=0, keepdims=True)
    dh1 = norm_bwd(total, xh1, rstd1_ref[rs, 0:1], p_ref[0:1, :])
    return df, dh1, (sum_g1, sum_b1, sum_g2, sum_b2)


def back_shapes():
    return [
        ((2, NB, RB, BLK), BF),
        ((BLK, HALF_FF), BF),
        ((BLK, HALF_FF), BF),
        ((BLK // 32, 32, D), F32),
        ((8, D), F32),
    ]


def rest_kernel(
    at, pos, xh1_ref, rstd1_ref, p_ref, g0, g1, gp0, gp1, cot_ref, u0, u1, d0, d1,
    dft_ref, du0_ref, du1_ref, dh1_ref, sums_ref, mixed_ref,
):
    r0, c0 = at * BLK, at * 32
    xh, rstd = down_block(r0, xh1_ref, p_ref, (g0, g1), (d0, d1))
    out = xh * p_ref[2:3, :] + p_ref[3:4, :]
    mixed_ref[...] = out.reshape(mixed_ref.shape).astype(BF)
    grad = cot_ref[:, c0 : c0 + 32, :].astype(F32).reshape(BLK, D)
    df, dh1, sums = back_block(
        r0, grad, xh, rstd, (gp0, gp1), xh1_ref, rstd1_ref, p_ref, (u0, u1), (d0, d1), (du0_ref, du1_ref)
    )
    store_turned(dft_ref, At(pos, POS_LATE), df, 0, BLK)
    dh1_ref[...] = dh1.reshape(dh1_ref.shape)
    for n in range(4):
        sums_ref[n : n + 1, :] = sums[n]


def rest_rows(at, pos, xh1, rstd1, prow, acts, gps, cot, ups, downs):
    return call(
        partial(rest_kernel, at),
        back_shapes() + [((BLK // 32, 32, D), BF)],
        [SM] + [VM] * 12, pos, xh1, rstd1, prow, *acts, *gps, cot, *ups, *downs,
        vmem=16, flops=BLK * 14.5e6, moved=BLK * 40000 + 1e7, name=f"rest_rows_{at}",
    )


def class_kernel(
    pos, cls_ref, cot_ref, xh2_ref, rstd2_ref, xh1_ref, rstd1_ref, p_ref, gp0, gp1, u0, u1, d0, d1,
    dft_ref, du0_ref, du1_ref, dh1_ref, sums_ref,
):
    spans = cls_ref.shape[0]
    grad = cot_ref[:, 0:32, :].astype(F32)
    first = lax.broadcasted_iota(jnp.int32, grad.shape, 1) == 0
    grad = grad + jnp.where(first, cls_ref[...].reshape(spans, 1, D), 0.0)
    grad = grad.reshape(BLK, D)
    df, dh1, sums = back_block(
        0, grad, xh2_ref[...], rstd2_ref[:, 0:1], (gp0, gp1), xh1_ref, rstd1_ref, p_ref,
        (u0, u1), (d0, d1), (du0_ref, du1_ref),
    )
    store_turned(dft_ref, At(pos, POS_LATE), df, 0, BLK)
    dh1_ref[...] = dh1.reshape(dh1_ref.shape)
    for n in range(4):
        sums_ref[n : n + 1, :] = sums[n]


def class_rows(pos, grad_cls, cot, xh2, rstd2, xh1, rstd1, prow, gps, ups, downs):
    return call(
        class_kernel,
        back_shapes(),
        [SM] + [VM] * 13, pos, grad_cls, cot, xh2, rstd2, xh1, rstd1, prow, *gps, *ups, *downs,
        vmem=16, flops=BLK * 9.7e6, moved=BLK * 30000 + 1e7, name="class_rows",
    )


def contrast_kernel(where, doc_ref, cls_ref, loss_ref, grad_ref, rows, own_doc):
    spans = doc_ref.shape[1]
    doc_row = doc_ref[...].astype(F32)
    doc_col = jnp.broadcast_to(doc_row, (128, spans)).T[:, 0:1]
    blocks, per = cls_ref.shape[0], cls_ref.shape[1]
    where = At(where, CLASS_AT)
    me = where[0]
    for n in range(blocks):
        rows[where[1 + n]] = cls_ref[n].astype(F32)
    a = rows[...].reshape(spans, D).astype(BF)
    own = rows[me].astype(BF)
    scale = D ** (-0.5)
    col = lax.broadcasted_iota(jnp.int32, (spans, spans), 1)
    row = lax.broadcasted_iota(jnp.int32, (spans, spans), 0)
    logits = mm(a, a, NT) * scale
    partner = (doc_col == doc_row) & (row != col)
    masked = jnp.where(row == col, -1000000000.0, logits)
    top = jnp.max(masked, axis=0, keepdims=True)
    lse = jnp.log(jnp.sum(jnp.exp(masked - top), axis=0, keepdims=True)) + top
    positive = jnp.sum(jnp.where(partner, logits, 0.0), axis=0, keepdims=True)
    flagged = jnp.max(jnp.where(partner, 1.0, 0.0), axis=0, keepdims=True)
    count = jnp.sum(flagged, axis=1, keepdims=True)
    loss = jnp.sum(flagged * (lse - positive), axis=1, keepdims=True) / count
    loss_ref[...] = jnp.broadcast_to(loss, loss_ref.shape)

    weight_row = flagged * (CONTRAST * spans) / count
    own_doc[...] = doc_col.reshape(blocks, per, 1)
    docs = own_doc[me]
    col = lax.broadcasted_iota(jnp.int32, (per, spans), 1)
    row = lax.broadcasted_iota(jnp.int32, (per, spans), 0) + me * per
    logits = mm(own, a, NT) * scale
    same = jnp.where((docs == doc_row) & (row != col), 1.0, 0.0)
    masked = jnp.where(row == col, -1000000000.0, logits)
    top = jnp.max(masked, axis=1, keepdims=True)
    ex = jnp.exp(masked - top)
    soft = ex / jnp.sum(ex, axis=1, keepdims=True)
    own_weight = jnp.max(same, axis=1, keepdims=True) * (CONTRAST * spans) / count
    sym = own_weight * (soft - same) + weight_row * (jnp.exp(masked - lse) - same)
    high = sym.astype(BF)
    low = (sym - high.astype(F32)).astype(BF)
    grad_ref[...] = (mm(high, a) + mm(low, a)) * scale


def contrast(where, doc_row, cls_all):
    blocks, per, _ = cls_all.shape
    spans = blocks * per
    return call(
        contrast_kernel,
        [((1, 128), F32), ((per, D), F32)],
        [SM, VM, VM],
        where, doc_row, cls_all,
        vmem=8 if spans <= 256 else 40, flops=2 * spans * spans * D, moved=spans * D * 2,
        scratch=[pltpu.VMEM((blocks, per, D), F32), pltpu.VMEM((blocks, per, 1), F32)],
        name="contrast",
    )


def turned_of(refs, n):
    return jnp.concatenate([ref[n].reshape(D, ref.shape[3]) for ref in refs], axis=1)


def grad_other_kernel(count, *refs):
    xts, ys, out_ref = refs[:count], refs[count:-1], refs[-1]
    xt = turned_of(xts, 1)
    for t in range(HALF_FF // TILE):
        lo, hi = t * TILE, (t + 1) * TILE
        grad = mm(xt, jnp.concatenate([y[:, lo:hi] for y in ys], axis=0))
        out_ref[:, :, lo:hi] = grad.astype(BF).reshape(NB, RB, TILE)


def grad_other(xts, ys, name):
    rows = sum(y.shape[0] for y in ys)
    return call(
        partial(grad_other_kernel, len(xts)),
        [((NB, RB, HALF_FF), BF)],
        [VM] * (len(xts) + len(ys)), *xts, *ys,
        vmem=12, flops=2 * rows * D * HALF_FF, moved=rows * 8000 + 2.4e6, name=name,
    )[0]


def grad_own_kernel(count, came_ref, *refs):
    xts, ys, keep_ref, send_ref = refs[:count], refs[count:-2], refs[-2], refs[-1]
    nh = NB // 2
    xt = turned_of(xts, 0)
    for t in range(HALF_FF // TILE):
        lo, hi = t * TILE, (t + 1) * TILE
        grad = mm(xt, jnp.concatenate([y[:, lo:hi] for y in ys], axis=0))
        grad = (grad.reshape(NB, RB, TILE) + came_ref[:, :, lo:hi].astype(F32)).astype(BF)
        keep_ref[:, :, lo:hi] = grad[:nh]
        send_ref[:, :, lo:hi] = grad[nh:]


def grad_own(xts, ys, came, name):
    rows = sum(y.shape[0] for y in ys)
    return call(
        partial(grad_own_kernel, len(xts)),
        [((NB // 2, RB, HALF_FF), BF)] * 2,
        [VM] * (1 + len(xts) + len(ys)), came, *xts, *ys,
        vmem=12, flops=2 * rows * D * HALF_FF, moved=rows * 8000 + 4.8e6, name=name,
    )


def natural(refs, i):
    return jnp.concatenate([ref[i * 2 + s] for s in range(2) for ref in refs], axis=0)


def attn_back_kernel(pos, r0_ref, r1_ref, r2_ref, r3_ref, qkv_ref, lse_ref, w_ref, dqkv_ref, *dat_ref):
    masks = head_masks(SPAN, HEAD ** (-0.5))
    plain = head_masks(SPAN, 1.0)
    spans = r0_ref.shape[0]

    def step(i, carry):
        r0 = pl.multiple_of(i * BLK, BLK)
        da = natural((r0_ref, r1_ref, r2_ref, r3_ref), i).astype(BF)
        if dat_ref:
            store_turned(dat_ref[0], At(pos, POS_EARLY), da, r0, BLK)
        dctx = mm(da, weight(w_ref, HALF_QKV, HALF_QKV + HALF_OUT)).astype(BF)
        pairs = [(s, j) for s in range(2) for j in range(3)]

        def part(ref, n, s, j):
            rs = pl.ds(pl.multiple_of(r0 + s * SPAN, SPAN), SPAN)
            return ref.at[rs, n * HALF_OUT + j * 128 : n * HALF_OUT + (j + 1) * 128]

        qs = [stack_heads(part(qkv_ref, 0, s, j)[...], masks) for s, j in pairs]
        ks = [part(qkv_ref, 1, s, j)[...] for s, j in pairs]
        sts = [mm(k, q, NT) for k, q in zip(ks, qs)]
        dcs = [stack_heads(dctx[s * SPAN : (s + 1) * SPAN, j * 128 : (j + 1) * 128], plain) for s, j in pairs]
        dpts = [mm(part(qkv_ref, 2, s, j)[...], dc, NT) for (s, j), dc in zip(pairs, dcs)]
        pts = [jnp.exp(st - lse_ref[i * 2 + s, j : j + 1, :]) for (s, j), st in zip(pairs, sts)]
        dvs = [mm(pt.astype(BF), dc) for pt, dc in zip(pts, dcs)]
        dsts = [
            (pt * (dpt - jnp.sum(pt * dpt, axis=0, keepdims=True))).astype(BF) for pt, dpt in zip(pts, dpts)
        ]
        dks = [mm(dst, q) for dst, q in zip(dsts, qs)]
        dqs = [merge_heads(mm(dst, k, TN)) * HEAD ** (-0.5) for dst, k in zip(dsts, ks)]
        for n, grads in enumerate((dqs, dks, dvs)):
            for (s, j), grad in zip(pairs, grads):
                part(dqkv_ref, n, s, j)[...] = grad.astype(BF)
        return carry

    lax.fori_loop(0, spans // 2, step, 0, unroll=2)


def attn_back(pos, dh1, qkv, lse, w, turned, name):
    rows = qkv.shape[0]
    out = [((rows, HALF_QKV), BF)]
    if turned:
        out.append(((2, NB, RB, rows), BF))
    return call(
        attn_back_kernel, out,
        [SM] + [VM] * 7, pos, *dh1, qkv, lse, w,
        vmem=16, flops=rows * 6e6, moved=rows * 10000 + 3e6, trans=rows * 800, name=name,
    )


def last_value(order, xt_ref, dqkv_ref, dat_ref, ctx_ref, t):
    rows = xt_ref.shape[3]
    if t < 3:
        return mm(xt_ref[order].reshape(D, rows), dqkv_ref[:, t * HALF_OUT : (t + 1) * HALF_OUT])
    return mm(dat_ref[order].reshape(D, rows), ctx_ref[...])


def norm_columns(sums):
    total = sums[0][0:4, :]
    for ref in sums[1:]:
        total = total + ref[0:4, :]
    return jnp.concatenate([total, jnp.zeros((124, D), F32)], axis=0).T


def last_other_kernel(pos, xt_ref, dqkv_ref, dat_ref, ctx_ref, s0, s1, s2, s3, out_ref):
    for t in range(4):
        grad = last_value(1, xt_ref, dqkv_ref, dat_ref, ctx_ref, t)
        lo = t * HALF_OUT
        out_ref[:, :, lo : lo + HALF_OUT] = grad.astype(BF).reshape(NB, RB, HALF_OUT)
    norm = norm_columns((s0, s1, s2, s3)).astype(BF)
    for j in range(NB):
        out_ref[pos[POS_EARLY + NB + j], :, HALF_QKV + HALF_OUT :] = norm[j * RB : (j + 1) * RB]


def last_other(pos, xt, dqkv, dat, ctx, sums):
    rows = xt.shape[3]
    return call(
        last_other_kernel,
        [((NB, RB, ONE), BF)],
        [SM] + [VM] * 8, pos, xt, dqkv, dat, ctx, *sums,
        vmem=12, flops=2 * rows * D * HALF_FF, moved=rows * 8000 + 2.4e6, name="last_other",
    )[0]


def last_own_kernel(
    pos, xt_ref, dqkv_ref, dat_ref, ctx_ref, s0, s1, s2, s3, came_ref, keep_ref, send_ref, cols
):
    nh = NB // 2
    norm = norm_columns((s0, s1, s2, s3))
    for j in range(NB):
        cols[pos[POS_EARLY + j]] = norm[j * RB : (j + 1) * RB]
    for t in range(5):
        lo = t * HALF_OUT
        hi = min(lo + HALF_OUT, ONE)
        if t < 4:
            grad = last_value(0, xt_ref, dqkv_ref, dat_ref, ctx_ref, t).reshape(NB, RB, HALF_OUT)
        else:
            grad = cols[...]
        grad = (grad + came_ref[:, :, lo:hi].astype(F32)).astype(BF)
        keep_ref[:, :, lo:hi] = grad[:nh]
        send_ref[:, :, lo:hi] = grad[nh:]


def last_own(pos, xt, dqkv, dat, ctx, sums, came):
    rows = xt.shape[3]
    return call(
        last_own_kernel,
        [((NB // 2, RB, ONE), BF)] * 2,
        [SM] + [VM] * 9, pos, xt, dqkv, dat, ctx, *sums, came,
        vmem=12, flops=2 * rows * D * HALF_FF, moved=rows * 8000 + 4.8e6,
        scratch=[pltpu.VMEM((NB, RB, 128), F32)], name="last_own",
    )


def input_grad_kernel(r0_ref, r1_ref, r2_ref, r3_ref, own_ref, other_ref, w0_ref, w1_ref, out_ref):
    spans = r0_ref.shape[0]

    def step(i, carry):
        rs = pl.ds(pl.multiple_of(i * BLK, BLK), BLK)
        total = natural((r0_ref, r1_ref, r2_ref, r3_ref), i)
        total = total + mm(own_ref[rs, :], weight(w0_ref, 0, HALF_QKV), NT)
        total = total + mm(other_ref[rs, :], weight(w1_ref, 0, HALF_QKV), NT)
        out_ref[rs, :] = total
        return carry

    lax.fori_loop(0, spans // 2, step, 0, unroll=2)


def input_grads(dh1, own, other, w_own, w_other):
    rows = own.shape[0]
    return call(
        input_grad_kernel,
        [((rows, D), F32)],
        [VM] * 8, *dh1, own, other, w_own, w_other,
        vmem=12, flops=rows * 3.6e6, moved=rows * 12000 + 5e6, name="input_grads",
    )[0]


def place_kernel(half, *refs):
    own, other, g_own, g_other = refs[0:4], refs[4:8], refs[8], refs[9]
    mixed_ref, grad_ref, sems = refs[10:]
    spans = g_own.shape[0]
    copies = []
    for n, (pieces, g) in enumerate(((own, g_own), (other, g_other))):
        at = pl.ds(half[HALF_AT + n] * spans, spans)
        for q in range(4):
            to = mixed_ref.at[at, 32 * q : 32 * q + 32, :]
            copies.append(pltpu.make_async_copy(pieces[q], to, sems.at[5 * n + q]))
        copies.append(pltpu.make_async_copy(g, grad_ref.at[at], sems.at[5 * n + 4]))
    for c in copies:
        c.start()
    for c in copies:
        c.wait()


def place(half, own, other, g_own, g_other):
    spans = own[0].shape[0]
    g_own, g_other = (g.reshape(spans, SPAN, D) for g in (g_own, g_other))
    return pl.pallas_call(
        place_kernel,
        out_shape=[
            jax.ShapeDtypeStruct((2 * spans, SPAN, D), BF),
            jax.ShapeDtypeStruct((2 * spans, SPAN, D), F32),
        ],
        in_specs=[SM] + [VM] * 10,
        out_specs=[HBM] * 2,
        scratch_shapes=[pltpu.SemaphoreType.DMA((10,))],
        compiler_params=params(16),
        cost_estimate=cost(0, spans * SPAN * D * 24),
        name="place",
    )(half, *own, *other, g_own, g_other)


def squares_kernel(k0, c0, k1, c1, k2, c2, g0, g1, g2, sq_ref):
    main = HALF_QKV + HALF_OUT
    total = jnp.zeros((1, 1), F32)
    for keep, came, out in ((k0, c0, g0), (k1, c1, g1), (k2, c2, g2)):
        grad = keep[0].astype(F32) + came[0].astype(F32)
        out[...] = grad
        sq = jnp.sum(grad[:, :main] * grad[:, :main], axis=1, keepdims=True)
        if grad.shape[1] > main:
            cols = grad[:, main:]
            sq = sq + 0.5 * jnp.sum(cols * cols, axis=1, keepdims=True)
        total = total + jnp.sum(sq, axis=0, keepdims=True)
    sq_ref[...] = jnp.broadcast_to(total, sq_ref.shape)


def squares_of(pairs):
    shard = pairs[0][0].shape[1]
    out = [((shard, k.shape[2]), F32) for k, _ in pairs] + [((8, 128), F32)]
    flat = [a for pair in pairs for a in pair]
    return call(squares_kernel, out, [VM] * 6, *flat, vmem=8, moved=shard * 40000, name="squares")


def adam_parts(weight, gradient, moment_one, moment_two, step_rate, decay_rate):
    first_new = 0.9 * moment_one + 0.1 * gradient
    second_new = 0.999 * moment_two + 0.001 * gradient * gradient
    corr_first = first_new * (1.0 / (1.0 - 0.9**STEP))
    corr_second = second_new * (1.0 / (1.0 - 0.999**STEP))
    weight_new = weight - step_rate * (
        corr_first / (jnp.sqrt(corr_second) + 1e-08) + decay_rate * weight
    )
    return first_new, second_new, weight_new


def adam_kernel(sq_ref, last_ref, up_ref, down_ref, cols_ref, *refs):
    ins, outs, wide = refs[:15], refs[15:-1], refs[-1]
    norm = jnp.sqrt(sq_ref[0:1, 0:1])
    outs[15][...] = jnp.broadcast_to(norm, outs[15].shape)
    scale = 1.0 / jnp.maximum(norm, 1.0)

    def update(n, at, grad, rate, decay):
        new = adam_parts(ins[n][at], grad * scale, ins[5 + 2 * n][at], ins[6 + 2 * n][at], rate, decay)
        for m in range(3):
            outs[3 * n + m][at] = new[m]

    for part in range(3):
        update(0, part, last_ref[:, part * HALF_OUT : (part + 1) * HALF_OUT], 0.02, 0.01)
    update(1, Ellipsis, last_ref[:, HALF_QKV : HALF_QKV + HALF_OUT], 0.02, 0.01)
    update(2, Ellipsis, up_ref[...], 0.02, 0.01)
    update(3, Ellipsis, down_ref[...], 0.02, 0.01)
    shard = last_ref.shape[0]
    wide[...] = jnp.zeros_like(wide)
    wide[0:shard, :] = 0.5 * (last_ref[:, HALF_QKV + HALF_OUT :] + cols_ref[...])
    update(4, Ellipsis, wide[...].T[0:4, 0:shard], 0.5, 0.0)


def adam(squares, last, up, down, cols, weights, moments):
    shapes = [w.shape for w in weights]
    out = [(s, F32) for s in shapes for _ in range(3)] + [((8, 128), F32)]
    args = (squares, last, up, down, cols, *weights, *moments)
    return call(
        adam_kernel, out, [VM] * len(args), *args, vmem=16, moved=7 * 4 * last.shape[0] * 4608,
        scratch=[pltpu.VMEM((128, 128), F32)], name="adam",
    )


def after(value, *others):
    return lax.optimization_barrier((value, others))[0]


def body(
    tokens,
    cotangent,
    span_doc,
    qkv_weight,
    out_weight,
    ffn_in_weight,
    ffn_out_weight,
    norm_params,
    qkv_first,
    qkv_second,
    out_first,
    out_second,
    ffn_in_first,
    ffn_in_second,
    ffn_out_first,
    ffn_out_second,
    norm_first,
    norm_second,
):
    n_dp = lax.axis_size("dp")
    dp = lax.axis_index("dp")
    core = lax.axis_index("tensor")
    shard = D // n_dp
    rows = tokens.shape[0] // 2
    spans = rows // SPAN
    direct = n_dp == NB
    early, late = bit_orders(n_dp)
    steps = len(early[0])
    last = steps - 1

    tab = lax.dynamic_index_in_dim(device_tables(n_dp), dp * 2 + core, 0, keepdims=False)
    x = lax.dynamic_slice_in_dim(tokens, core * rows, rows, 0)
    cot = lax.dynamic_slice_in_dim(cotangent, core * rows, rows, 0).reshape(spans, SPAN, D)

    def places(orders, other=0):
        return dp ^ jnp.array([rel_of(order) for order in orders], jnp.int32)[core ^ other]

    def send_on(block, orders, k):
        return lax.ppermute(block, AXES, pairs_of(n_dp, orders, k))

    def join(held, came):
        return jnp.concatenate([held, came], axis=0)

    def pieces(at, low, high):
        if direct:
            return at, tab, low, high
        which = {AT_EARLY: places(early), AT_LATE: places(late), AT_OTHER: places(early, 1)}[at]
        full = join(low, high)[jnp.argsort(which)].reshape(NB, RB, -1)
        return at, tab, full[: NB // 2], full[NB // 2 :]

    def halves(orders, keep, send):
        if direct:
            return keep, send
        full = join(keep, send).reshape(n_dp, shard, -1)[places(orders)]
        return full[: n_dp // 2], full[n_dp // 2 :]

    def add(keep, came):
        total = keep.astype(F32) + came.astype(F32)
        size = total.shape[0] // 2
        return total[:size].astype(BF), total[size:].astype(BF)

    turned = ((1, 0, 2), (1, 0), (0, 1), (1, 0), (0, 1))
    weights = (qkv_weight, out_weight, ffn_in_weight, ffn_out_weight, norm_params)
    weights = tuple(w.transpose(t) for w, t in zip(weights, turned))
    one, up, down = pack(*weights)
    one_came = send_on(one, early, 0)
    up_came = send_on(up, late, 0)
    down_came = send_on(down, early, 0)
    one, tab, x, cot, down_came = after((join(one, one_came), tab, x, cot, down_came), up_came)
    for k in range(1, last):
        one_came = send_on(one, early, k)
        if k > 1:
            up = after(join(up, up_came), one)
            up_came = send_on(up, late, k - 1)
        one = join(one, one_came)
        if k > 1:
            one = after(one, up_came)
    one_came = send_on(one, early, last)
    for k in range(max(last - 1, 1), last):
        up = join(up, up_came)
        up_came = send_on(up, late, k)
    one, one_came = after((one, one_came), up_came)
    up = after(join(up, up_came), one_came)
    up_came = send_on(up, late, last)
    down = after(join(down, down_came), one_came)
    down_came = send_on(down, early, 1)

    one_other = (core_swap(one), core_swap(one_came))
    qkv0, ctx0, lse0, w10 = attn_one(*pieces(AT_EARLY, one, one_came), x)
    ctx0 = after(ctx0, down_came)
    for k in range(2, last):
        down = join(down, after(down_came, ctx0))
        down_came = send_on(down, early, k)
    qkv1, ctx1, lse1, xh1, rstd1, prow, w11 = attn_two(*pieces(AT_OTHER, *one_other), x, w10, ctx0)
    w1 = (w10, w11)
    xh1 = xh1.reshape(rows, D)
    rstd1 = rstd1.reshape(rows, 128)
    up_came, down_came = after((up_came, down_came), xh1)
    wu = assemble(*pieces(AT_LATE, up, up_came), "up_own")
    wu = (wu, core_swap(wu))
    down = join(down, down_came)
    down_came = send_on(down, early, last)
    act0, gp0, yt = ffn_up(tab, after(xh1, down), prow, wu[0], True, "ffn_up_own")
    wd = assemble(*pieces(AT_EARLY, down, after(down_came, act0)), "down_own")
    wd = (wd, core_swap(wd))
    act1, gp1 = ffn_up(tab, after(xh1, wd[0]), prow, wu[1], False, "ffn_up_other")
    acts, gps = (act0, act1), (gp0, gp1)
    mixed0, cls_own, xh2, rstd2 = first_rows(xh1, prow, acts, wd)

    held = cls_own.astype(BF)[None]
    back = []
    one_bit, two_bit = 1 << last, 1 << (last - 1)
    for bits in [(one_bit, two_bit, one_bit ^ two_bit)] + [(1 << k,) for k in reversed(range(last - 1))]:
        came = tuple(lax.ppermute(held, "dp", [(d, d ^ bit) for d in range(n_dp)]) for bit in bits)
        if len(back) < 3:
            at = len(back) + 1
            back.append(rest_rows(at, tab, after(xh1, held), rstd1, prow, acts, gps, cot, wu, wd))
            came = after(came, back[-1][4])
        held = jnp.concatenate((held,) + came, axis=0)
    held = join(held, core_swap(held))
    loss, grad_cls = contrast(tab, span_doc.reshape(1, -1), held)
    back.insert(0, (*class_rows(tab, grad_cls, cot, xh2, rstd2, xh1, rstd1, prow, gps, wu, wd), mixed0))
    dft, du0, du1, dh1, sums, mixed_own = zip(*back)

    d_other = grad_other(dft, (act1,), "grad_down_other")
    d_came = core_swap(d_other)
    u_other = grad_other((after(yt, d_other),), du1, "grad_up_other")
    u_came = core_swap(u_other)
    d_keep, d_send = halves(
        late, *grad_own((after(dft[0], u_other),) + dft[1:], (act0,), d_came, "grad_down_own")
    )
    d_came = send_on(d_send, late, last)
    u_keep, u_send = halves(early, *grad_own((after(yt, d_keep),), du0, u_came, "grad_up_own"))
    dh1 = (after(dh1[0], u_keep),) + dh1[1:]
    tokt = turn(tab, after(x, u_keep))
    dqkv1, dat = attn_back(tab, dh1, qkv1, lse1, w1[1], True, "attn_back_other")
    l_other = last_other(tab, tokt, dqkv1, dat, ctx1, sums)

    d_came, l_other = after((d_came, l_other))
    d_keep, d_send = add(d_keep, d_came)
    u_came = send_on(after(u_send, l_other), early, last)
    d_came = send_on(d_send, late, last - 1)
    l_came = core_swap(l_other)
    (dqkv0,) = attn_back(
        tab, (after(dh1[0], l_other),) + dh1[1:], qkv0, lse0, w1[0], False, "attn_back_own"
    )
    l_keep, l_send = halves(early, *last_own(tab, tokt, dqkv0, dat, ctx0, sums, l_came))
    l_came = send_on(l_send, early, last)
    grad_in = input_grads((after(dh1[0], l_send),) + dh1[1:], dqkv0, dqkv1, w1[0], w1[1])
    u_came, d_came = after((u_came, d_came), l_send)
    u_keep, u_send = add(u_keep, u_came)
    d_keep, d_send = add(d_keep, d_came)
    u_came = send_on(u_send, early, last - 1)
    d_came = send_on(d_send, late, last - 2)
    for k in reversed(range(last)):
        l_came, u_came, d_came = after((l_came, u_came, d_came))
        l_keep, l_send = add(l_keep, l_came)
        l_came = send_on(l_send, early, k)
        if k > 0:
            u_keep, u_send = add(u_keep, u_came)
            u_came = send_on(u_send, early, k - 1)
        if k > 1:
            d_keep, d_send = add(d_keep, d_came)
            d_came = send_on(d_send, late, k - 2)
        if k == last - 1:
            grad_came = core_swap(after(grad_in, l_send))
            mixed_other = tuple(core_swap(m) for m in after(mixed_own, l_send))
            l_came = after(l_came, grad_came, mixed_other)
        if k == last - 2:
            mixed, input_grad = place(tab, mixed_own, mixed_other, after(grad_in, l_send), grad_came)
            l_came = after(l_came, input_grad)

    last_grad, down_grad, up_grad, squares = squares_of(((l_keep, l_came), (d_keep, d_came), (u_keep, u_came)))
    cols = core_swap(last_grad[:, HALF_QKV + HALF_OUT :])
    squares = squares + core_swap(squares)
    bits = [1 << k for k in reversed(range(steps))]
    for one_bit, two_bit in zip(bits[::2], bits[1::2]):
        near, far, both = (
            lax.ppermute(squares, "dp", [(d, d ^ b) for d in range(n_dp)])
            for b in (one_bit, two_bit, one_bit ^ two_bit)
        )
        squares = (squares + near) + (far + both)
    moments = (
        qkv_first, qkv_second, out_first, out_second, ffn_in_first, ffn_in_second,
        ffn_out_first, ffn_out_second, norm_first, norm_second,
    )
    new = adam(
        squares, last_grad, up_grad, down_grad, cols,
        weights,
        [m.transpose(turned[n // 2]) for n, m in enumerate(moments)],
    )
    updated = [value.transpose(turned[n // 3]) for n, value in enumerate(new[:15])]
    return (
        mixed.reshape(2 * rows, D),
        input_grad.reshape(2 * rows, D),
        loss[0, 0],
        new[15][0, 0],
        *updated,
    )


def solution(mesh):
    rows = P("dp", None)
    qkv = P("dp", None, "tensor")
    turned = P("tensor", "dp")
    up = P("dp", "tensor")
    norm = P(None, "dp")
    weights = (qkv, turned, up, turned, norm)
    moments = tuple(spec for spec in weights for _ in range(2))
    updated = tuple(spec for spec in weights for _ in range(3))
    return jax.shard_map(
        body,
        mesh=mesh,
        in_specs=(rows, rows, P()) + weights + moments,
        out_specs=(rows, rows, P(), P()) + updated,
        check_vma=False,
    )
```

```python
from functools import partial

import jax
import jax.numpy as jnp
import numpy as np
from jax import lax
from jax.experimental import pallas as pl
from jax.experimental.pallas import tpu as pltpu
from jax.sharding import PartitionSpec as P

HEAD = 64
SPAN = 128
STEP = 10
D = 768
FF = 3072
NB = 16
RB = D // NB
HALF_QKV = 1152
HALF_OUT = 384
HALF_FF = 1536
ONE = HALF_QKV + HALF_OUT + 128
CONTRAST = 4.0
EPS = 1e-06
BF = jnp.bfloat16
F32 = jnp.float32
AXES = ("dp", "tensor")
SHRINK = 100

NN = (((1,), (0,)), ((), ()))
NT = (((1,), (1,)), ((), ()))
TN = (((0,), (0,)), ((), ()))


def mm(left, right, dims=NN):
    return lax.dot_general(left, right, dims, preferred_element_type=F32)


def params(vmem=56):
    vmem = vmem if vmem > 24 else min(vmem, 8)
    return pltpu.CompilerParams(vmem_limit_bytes=vmem * 2**20)


def cost(flops, bytes_accessed, trans=0):
    flops, bytes_accessed, trans = (n // SHRINK + 1 for n in (flops, bytes_accessed, trans))
    return pl.CostEstimate(flops=int(flops), bytes_accessed=int(bytes_accessed), transcendentals=int(trans))


HBM = pl.BlockSpec(memory_space=pl.ANY)


def bit_orders(n_dp):
    bits = n_dp.bit_length() - 1
    if bits == 4:
        return ((4, 8, 2, 1), (8, 4, 1, 2)), ((1, 4, 8, 2), (2, 8, 4, 1))
    up = tuple(1 << b for b in range(bits))[::-1]
    both = (up, up[: bits // 2] + up[bits // 2 :][::-1])
    return both, both


def pairs_of(n_dp, orders, step):
    out = []
    for d in range(n_dp):
        for c in range(2):
            out.append((d * 2 + c, (d ^ orders[c][step]) * 2 + c))
    return out


def rel_of(order):
    out = []
    for p in range(1 << len(order)):
        r = 0
        for k, b in enumerate(order):
            if (p >> k) & 1:
                r ^= b
        out.append(r)
    return out


AT_EARLY, AT_LATE, AT_OTHER, POS_EARLY, POS_LATE = 0, NB, 2 * NB, 3 * NB, 5 * NB
HALF_AT, CLASS_AT = 7 * NB, 7 * NB + 2


class At:
    def __init__(self, ref, first):
        self.ref, self.first = ref, first

    def __getitem__(self, n):
        return self.ref[self.first + n]


def device_tables(n_dp):
    kinds = [[rel_of(order) for order in orders] for orders in bit_orders(n_dp)]
    classes = rel_of([1 << k for k in reversed(range(n_dp.bit_length() - 1))])
    plain = list(range(NB))
    table = []
    for d in range(n_dp):
        for c in range(2):
            direct = n_dp == NB
            row = []
            for rel in kinds:
                row += [d ^ r for r in rel[c]] if direct else plain
            row += [d ^ r for r in kinds[0][1 - c]] if direct else plain
            for rel in kinds:
                for half in (c, 1 - c):
                    row += [rel[half].index(d ^ j) for j in range(NB)] if direct else plain
            me = d * 2 + c
            row += [c, 1 - c, me] + [me ^ (r << 1 | b) for b in range(2) for r in classes]
            table.append(row)
    return np.array(table, np.int32)


def core_swap(block):
    return lax.ppermute(block, "tensor", [(0, 1), (1, 0)])


VM = pl.BlockSpec(memory_space=pltpu.VMEM)
SM = pl.BlockSpec(memory_space=pltpu.SMEM)
BLK = 256


def call(kernel, out, in_specs, *args, vmem=16, flops=0, moved=0, trans=0, scratch=(), name=None):
    return pl.pallas_call(
        kernel,
        out_shape=[jax.ShapeDtypeStruct(s, t) for s, t in out],
        in_specs=in_specs,
        out_specs=[VM] * len(out),
        scratch_shapes=list(scratch),
        compiler_params=params(vmem),
        cost_estimate=cost(flops, moved, trans),
        name=name,
    )(*args)


def pack_kernel(qkv, out, up, down, norm, one_ref, two_ref, three_ref, wide, a0, a1, a2, a3, sems):
    rows = up.shape[0]
    wide[...] = jnp.zeros_like(wide)
    copies = [
        pltpu.make_async_copy(src, dst, sems.at[n])
        for n, (src, dst) in enumerate(
            ((qkv, a0), (out, a1), (down, a3), (up, a2))
        )
    ]
    for c in copies:
        c.start()
    copies[0].wait()
    for part in range(3):
        one_ref[0, :, part * HALF_OUT : (part + 1) * HALF_OUT] = a0[part].astype(BF)
    copies[1].wait()
    one_ref[0, :, HALF_QKV : HALF_QKV + HALF_OUT] = a1[...].astype(BF)
    wide[0:4, 0:rows] = norm[...]
    one_ref[0, :, HALF_QKV + HALF_OUT :] = wide[...].T[0:rows].astype(BF)
    copies[2].wait()
    three_ref[0] = a3[...].astype(BF)
    copies[3].wait()
    two_ref[0] = a2[...].astype(BF)


def pack(*shards):
    rows = shards[2].shape[0]
    return call(
        pack_kernel,
        [((1, rows, ONE), BF), ((1, rows, HALF_FF), BF), ((1, rows, HALF_FF), BF)],
        [pl.BlockSpec(memory_space=pltpu.HBM)] * 4 + [VM], *shards,
        vmem=60, moved=rows * 28000,
        scratch=[pltpu.VMEM((128, 128), F32)]
        + [pltpu.VMEM(w.shape, F32) for w in shards[:4]]
        + [pltpu.SemaphoreType.DMA((4,))],
        name="pack",
    )


def assemble_kernel(first, tab, low, high, out_ref):
    for n, ref in enumerate((low, high)):
        for p in range(NB // 2):
            out_ref[tab[first + n * (NB // 2) + p]] = ref[p]


def assemble(first, tab, low, high, name):
    width = low.shape[-1]
    return call(
        partial(assemble_kernel, first),
        [((NB, RB, width), BF)],
        [SM, VM, VM], tab, low, high,
        moved=4 * D * width, name=name,
    )[0]


def weight(w_ref, first, last):
    return w_ref[:, :, first:last].reshape(D, last - first)


def norm_fwd(hidden):
    center = hidden - jnp.mean(hidden, axis=-1, keepdims=True)
    spread = jnp.mean(center * center, axis=-1, keepdims=True)
    rstd = lax.rsqrt(spread + EPS)
    return center * rstd, rstd


def norm_bwd(grad, xh, rstd, gain):
    e = grad * gain
    m1 = jnp.mean(e, axis=-1, keepdims=True)
    m2 = jnp.mean(e * xh, axis=-1, keepdims=True)
    return rstd * (e - m1 - xh * m2)


def store_turned(ref, tab, value, col, width):
    turned = value.T
    for j in range(NB):
        block = turned[j * RB : (j + 1) * RB]
        for n in range(2):
            ref[n, tab[n * NB + j], :, pl.ds(col, width)] = block


def head_masks(rows, scale):
    lane = lax.broadcasted_iota(jnp.int32, (rows, 128), 1)
    return (
        jnp.where(lane < HEAD, scale, 0.0).astype(BF),
        jnp.where(lane < HEAD, 0.0, scale).astype(BF),
    )


def stack_heads(pair, masks):
    return jnp.concatenate([pair * masks[0], pair * masks[1]], axis=0)


def merge_heads(both):
    lane = lax.broadcasted_iota(jnp.int32, (SPAN, 128), 1)
    return jnp.where(lane < HEAD, both[:SPAN], both[SPAN:])


def turn_kernel(pos, x_ref, out_ref):
    rows = x_ref.shape[0]
    for i in range(rows // BLK):
        store_turned(out_ref, At(pos, POS_EARLY), x_ref[i * BLK : (i + 1) * BLK, :], i * BLK, BLK)


def turn(pos, x):
    rows = x.shape[0]
    return call(
        turn_kernel, [((2, NB, RB, rows), BF)], [SM, VM], pos, x, moved=rows * D * 6, name="turn"
    )[0]


def attn_rows(i, x, w_ref, masks, qkv_ref, ctx_ref, lse_ref):
    r0 = pl.multiple_of(i * BLK, BLK)
    qkv = mm(x, weight(w_ref, 0, HALF_QKV)).astype(BF)
    qkv_ref[pl.ds(r0, BLK), :] = qkv
    pairs = [(s, j) for s in range(2) for j in range(3)]

    def part(n, s, j):
        return qkv[s * SPAN : (s + 1) * SPAN, n * HALF_OUT + j * 128 : n * HALF_OUT + (j + 1) * 128]

    sts = [mm(part(1, s, j), stack_heads(part(0, s, j), masks), NT) for s, j in pairs]
    tops = [jnp.max(st, axis=0, keepdims=True) for st in sts]
    exs = [jnp.exp(st - top) for st, top in zip(sts, tops)]
    totals = [jnp.sum(ex, axis=0, keepdims=True) for ex in exs]
    pts = [(ex * (1.0 / total)).astype(BF) for ex, total in zip(exs, totals)]
    parts = [merge_heads(mm(pt, part(2, s, j), TN)).astype(BF) for pt, (s, j) in zip(pts, pairs)]
    for (s, j), top, total in zip(pairs, tops, totals):
        lse_ref[i * 2 + s, j : j + 1, :] = top + jnp.log(total)
    ctx = jnp.concatenate([jnp.concatenate(parts[s * 3 : s * 3 + 3], axis=1) for s in range(2)], axis=0)
    ctx_ref[pl.ds(r0, BLK), :] = ctx
    return ctx


def attn_one_kernel(first, tab, low, high, x_ref, qkv_ref, ctx_ref, lse_ref, w_ref):
    assemble_kernel(first, tab, low, high, w_ref)
    masks = head_masks(SPAN, HEAD ** (-0.5))

    def step(i, carry):
        x = x_ref[pl.ds(pl.multiple_of(i * BLK, BLK), BLK), :]
        attn_rows(i, x, w_ref, masks, qkv_ref, ctx_ref, lse_ref)
        return carry

    lax.fori_loop(0, x_ref.shape[0] // BLK, step, 0, unroll=2)


def attn_two_kernel(
    first, tab, low, high, x_ref, wo_ref, ctxo_ref,
    qkv_ref, ctx_ref, lse_ref, xh_ref, rstd_ref, p_ref, w_ref,
):
    assemble_kernel(first, tab, low, high, w_ref)
    cols = weight(w_ref, HALF_QKV + HALF_OUT, ONE).astype(F32)
    p_ref[...] = cols.T[:8]
    masks = head_masks(SPAN, HEAD ** (-0.5))

    def step(i, carry):
        rs = pl.ds(pl.multiple_of(i * BLK, BLK), BLK)
        x = x_ref[rs, :]
        ctx = attn_rows(i, x, w_ref, masks, qkv_ref, ctx_ref, lse_ref)
        attn = x.astype(F32) + mm(ctxo_ref[rs, :], weight(wo_ref, HALF_QKV, HALF_QKV + HALF_OUT), NT)
        attn = attn + mm(ctx, weight(w_ref, HALF_QKV, HALF_QKV + HALF_OUT), NT)
        xh, rstd = norm_fwd(attn)
        rstd = jnp.broadcast_to(rstd, (BLK, 128))
        for s in range(2):
            for q in range(4):
                r = s * SPAN + q * 32
                xh_ref[q, i * 2 + s] = xh[r : r + 32]
                rstd_ref[q, i * 2 + s] = rstd[r : r + 32]
        return carry

    lax.fori_loop(0, x_ref.shape[0] // BLK, step, 0, unroll=2)


def attn_shapes(rows):
    return [((rows, HALF_QKV), BF), ((rows, HALF_OUT), BF), ((rows // SPAN, 8, 2 * SPAN), F32)]


def attn_one(first, tab, low, high, x):
    rows = x.shape[0]
    return call(
        partial(attn_one_kernel, first), attn_shapes(rows) + [((NB, RB, ONE), BF)],
        [SM, VM, VM, VM], tab, low, high, x,
        vmem=16, flops=rows * 4e6, moved=rows * 8000 + 2e6, trans=rows * 800, name="attn_one",
    )


def attn_two(first, tab, low, high, x, w_own, ctx_own):
    rows = x.shape[0]
    spans = rows // SPAN
    out = attn_shapes(rows) + [
        ((4, spans, 32, D), F32),
        ((4, spans, 32, 128), F32),
        ((8, D), F32),
        ((NB, RB, ONE), BF),
    ]
    return call(
        partial(attn_two_kernel, first), out, [SM] + [VM] * 5, tab, low, high, x, w_own, ctx_own,
        vmem=16, flops=rows * 5e6, moved=rows * 12000 + 4e6, trans=rows * 800, name="attn_two",
    )


def gelu_pair(u):
    a = jnp.abs(u)
    d = 1.0 + (0.3275911 * 0.5**0.5) * a
    t = pl.reciprocal(d, approx=True)
    t = t * (2.0 - d * t)
    e = jnp.exp(-0.5 * u * u)
    poly = 0.5307027145 * t - 0.7265760135
    poly = poly * t + 0.7107068705
    poly = poly * t - 0.142248368
    poly = poly * t + 0.127414796
    tail = (poly * t) * e
    phi = jnp.where(u >= 0.0, 1.0 - tail, tail)
    return u * phi, phi + (0.3989422804014327 * u) * e


TILE = 512


def ffn_up_kernel(pos, xh_ref, p_ref, w_ref, g_ref, gp_ref, *yt_ref):
    def step(i, carry):
        rs = pl.ds(pl.multiple_of(i * BLK, BLK), BLK)
        y = xh_ref[rs, :] * p_ref[0:1, :] + p_ref[1:2, :]
        yb = y.astype(BF)
        if yt_ref:
            store_turned(yt_ref[0], At(pos, POS_EARLY), yb, pl.multiple_of(i * BLK, BLK), BLK)
        for t in range(HALF_FF // TILE):
            u = mm(yb, weight(w_ref, t * TILE, (t + 1) * TILE))
            g, gp = gelu_pair(u)
            g_ref[rs, t * TILE : (t + 1) * TILE] = g.astype(BF)
            gp_ref[rs, t * TILE : (t + 1) * TILE] = gp.astype(BF)
        return carry

    lax.fori_loop(0, xh_ref.shape[0] // BLK, step, 0, unroll=2)


def ffn_up(pos, xh, prow, w, turned, name):
    rows = xh.shape[0]
    out = [((rows, HALF_FF), BF), ((rows, HALF_FF), BF)]
    if turned:
        out.append(((2, NB, RB, rows), BF))
    return call(
        ffn_up_kernel, out, [SM, VM, VM, VM], pos, xh, prow, w,
        vmem=16, flops=rows * 2.4e6, moved=rows * 9000 + 2e6, trans=rows * 6000, name=name,
    )


def down_block(r0, xh1_ref, p_ref, acts, downs):
    rs = pl.ds(r0, BLK)
    total = xh1_ref[rs, :] * p_ref[0:1, :] + p_ref[1:2, :]
    for g_ref, w_ref in zip(acts, downs):
        total = total + mm(g_ref[rs, :], weight(w_ref, 0, HALF_FF), NT)
    return norm_fwd(total)


def first_kernel(xh1_ref, p_ref, g0, g1, d0, d1, mixed_ref, cls_ref, xh_ref, rstd_ref):
    xh, rstd = down_block(0, xh1_ref, p_ref, (g0, g1), (d0, d1))
    xh_ref[...] = xh
    rstd_ref[...] = jnp.broadcast_to(rstd, rstd_ref.shape)
    out = (xh * p_ref[2:3, :] + p_ref[3:4, :]).reshape(mixed_ref.shape)
    mixed_ref[...] = out.astype(BF)
    cls_ref[...] = out[:, 0, :]


def first_rows(xh1, prow, acts, downs):
    spans = BLK // 32
    return call(
        first_kernel,
        [((spans, 32, D), BF), ((spans, D), F32), ((BLK, D), F32), ((BLK, 128), F32)],
        [VM] * 6, xh1, prow, *acts, *downs,
        vmem=8, flops=BLK * 4.8e6, moved=BLK * 16000 + 5e6, name="first_rows",
    )


def back_block(r0, grad, xh2, rstd2, gps, xh1_ref, rstd1_ref, p_ref, ups, downs, dus):
    rs = pl.ds(r0, BLK)
    sum_g2 = jnp.sum(grad * xh2, axis=0, keepdims=True)
    sum_b2 = jnp.sum(grad, axis=0, keepdims=True)
    dh = norm_bwd(grad, xh2, rstd2, p_ref[2:3, :])
    df = dh.astype(BF)
    total = dh
    for gp_ref, up_ref, down_ref, du_ref in zip(gps, ups, downs, dus):
        for t in range(HALF_FF // TILE):
            lo, hi = t * TILE, (t + 1) * TILE
            dg = mm(df, weight(down_ref, lo, hi))
            du_ref[:, lo:hi] = (dg * gp_ref[rs, lo:hi].astype(F32)).astype(BF)
        total = total + mm(du_ref[...], weight(up_ref, 0, HALF_FF), NT)
    xh1 = xh1_ref[rs, :]
    sum_g1 = jnp.sum(total * xh1, axis=0, keepdims=True)
    sum_b1 = jnp.sum(total, axis=0, keepdims=True)
    dh1 = norm_bwd(total, xh1, rstd1_ref[rs, 0:1], p_ref[0:1, :])
    return df, dh1, (sum_g1, sum_b1, sum_g2, sum_b2)


def back_shapes():
    return [
        ((2, NB, RB, BLK), BF),
        ((BLK, HALF_FF), BF),
        ((BLK, HALF_FF), BF),
        ((BLK // 32, 32, D), F32),
        ((8, D), F32),
    ]


def rest_kernel(
    at, pos, xh1_ref, rstd1_ref, p_ref, g0, g1, gp0, gp1, cot_ref, u0, u1, d0, d1,
    dft_ref, du0_ref, du1_ref, dh1_ref, sums_ref, mixed_ref,
):
    r0, c0 = at * BLK, at * 32
    xh, rstd = down_block(r0, xh1_ref, p_ref, (g0, g1), (d0, d1))
    out = xh * p_ref[2:3, :] + p_ref[3:4, :]
    mixed_ref[...] = out.reshape(mixed_ref.shape).astype(BF)
    grad = cot_ref[:, c0 : c0 + 32, :].astype(F32).reshape(BLK, D)
    df, dh1, sums = back_block(
        r0, grad, xh, rstd, (gp0, gp1), xh1_ref, rstd1_ref, p_ref, (u0, u1), (d0, d1), (du0_ref, du1_ref)
    )
    store_turned(dft_ref, At(pos, POS_LATE), df, 0, BLK)
    dh1_ref[...] = dh1.reshape(dh1_ref.shape)
    for n in range(4):
        sums_ref[n : n + 1, :] = sums[n]


def rest_rows(at, pos, xh1, rstd1, prow, acts, gps, cot, ups, downs):
    return call(
        partial(rest_kernel, at),
        back_shapes() + [((BLK // 32, 32, D), BF)],
        [SM] + [VM] * 12, pos, xh1, rstd1, prow, *acts, *gps, cot, *ups, *downs,
        vmem=16, flops=BLK * 14.5e6, moved=BLK * 40000 + 1e7, name=f"rest_rows_{at}",
    )


def class_kernel(
    pos, cls_ref, cot_ref, xh2_ref, rstd2_ref, xh1_ref, rstd1_ref, p_ref, gp0, gp1, u0, u1, d0, d1,
    dft_ref, du0_ref, du1_ref, dh1_ref, sums_ref,
):
    spans = cls_ref.shape[0]
    grad = cot_ref[:, 0:32, :].astype(F32)
    first = lax.broadcasted_iota(jnp.int32, grad.shape, 1) == 0
    grad = grad + jnp.where(first, cls_ref[...].reshape(spans, 1, D), 0.0)
    grad = grad.reshape(BLK, D)
    df, dh1, sums = back_block(
        0, grad, xh2_ref[...], rstd2_ref[:, 0:1], (gp0, gp1), xh1_ref, rstd1_ref, p_ref,
        (u0, u1), (d0, d1), (du0_ref, du1_ref),
    )
    store_turned(dft_ref, At(pos, POS_LATE), df, 0, BLK)
    dh1_ref[...] = dh1.reshape(dh1_ref.shape)
    for n in range(4):
        sums_ref[n : n + 1, :] = sums[n]


def class_rows(pos, grad_cls, cot, xh2, rstd2, xh1, rstd1, prow, gps, ups, downs):
    return call(
        class_kernel,
        back_shapes(),
        [SM] + [VM] * 13, pos, grad_cls, cot, xh2, rstd2, xh1, rstd1, prow, *gps, *ups, *downs,
        vmem=16, flops=BLK * 9.7e6, moved=BLK * 30000 + 1e7, name="class_rows",
    )


def contrast_kernel(where, doc_ref, cls_ref, loss_ref, grad_ref, rows, own_doc):
    spans = doc_ref.shape[1]
    doc_row = doc_ref[...].astype(F32)
    doc_col = jnp.broadcast_to(doc_row, (128, spans)).T[:, 0:1]
    blocks, per = cls_ref.shape[0], cls_ref.shape[1]
    where = At(where, CLASS_AT)
    me = where[0]
    for n in range(blocks):
        rows[where[1 + n]] = cls_ref[n].astype(F32)
    a = rows[...].reshape(spans, D).astype(BF)
    own = rows[me].astype(BF)
    scale = D ** (-0.5)
    col = lax.broadcasted_iota(jnp.int32, (spans, spans), 1)
    row = lax.broadcasted_iota(jnp.int32, (spans, spans), 0)
    logits = mm(a, a, NT) * scale
    partner = (doc_col == doc_row) & (row != col)
    masked = jnp.where(row == col, -1000000000.0, logits)
    top = jnp.max(masked, axis=0, keepdims=True)
    lse = jnp.log(jnp.sum(jnp.exp(masked - top), axis=0, keepdims=True)) + top
    positive = jnp.sum(jnp.where(partner, logits, 0.0), axis=0, keepdims=True)
    flagged = jnp.max(jnp.where(partner, 1.0, 0.0), axis=0, keepdims=True)
    count = jnp.sum(flagged, axis=1, keepdims=True)
    loss = jnp.sum(flagged * (lse - positive), axis=1, keepdims=True) / count
    loss_ref[...] = jnp.broadcast_to(loss, loss_ref.shape)

    weight_row = flagged * (CONTRAST * spans) / count
    own_doc[...] = doc_col.reshape(blocks, per, 1)
    docs = own_doc[me]
    col = lax.broadcasted_iota(jnp.int32, (per, spans), 1)
    row = lax.broadcasted_iota(jnp.int32, (per, spans), 0) + me * per
    logits = mm(own, a, NT) * scale
    same = jnp.where((docs == doc_row) & (row != col), 1.0, 0.0)
    masked = jnp.where(row == col, -1000000000.0, logits)
    top = jnp.max(masked, axis=1, keepdims=True)
    ex = jnp.exp(masked - top)
    soft = ex / jnp.sum(ex, axis=1, keepdims=True)
    own_weight = jnp.max(same, axis=1, keepdims=True) * (CONTRAST * spans) / count
    sym = own_weight * (soft - same) + weight_row * (jnp.exp(masked - lse) - same)
    high = sym.astype(BF)
    low = (sym - high.astype(F32)).astype(BF)
    grad_ref[...] = (mm(high, a) + mm(low, a)) * scale


def contrast(where, doc_row, cls_all):
    blocks, per, _ = cls_all.shape
    spans = blocks * per
    return call(
        contrast_kernel,
        [((1, 128), F32), ((per, D), F32)],
        [SM, VM, VM],
        where, doc_row, cls_all,
        vmem=8 if spans <= 256 else 40, flops=2 * spans * spans * D, moved=spans * D * 2,
        scratch=[pltpu.VMEM((blocks, per, D), F32), pltpu.VMEM((blocks, per, 1), F32)],
        name="contrast",
    )


def turned_of(refs, n):
    return jnp.concatenate([ref[n].reshape(D, ref.shape[3]) for ref in refs], axis=1)


def grad_other_kernel(count, *refs):
    xts, ys, out_ref = refs[:count], refs[count:-1], refs[-1]
    xt = turned_of(xts, 1)
    for t in range(HALF_FF // TILE):
        lo, hi = t * TILE, (t + 1) * TILE
        grad = mm(xt, jnp.concatenate([y[:, lo:hi] for y in ys], axis=0))
        out_ref[:, :, lo:hi] = grad.astype(BF).reshape(NB, RB, TILE)


def grad_other(xts, ys, name):
    rows = sum(y.shape[0] for y in ys)
    return call(
        partial(grad_other_kernel, len(xts)),
        [((NB, RB, HALF_FF), BF)],
        [VM] * (len(xts) + len(ys)), *xts, *ys,
        vmem=12, flops=2 * rows * D * HALF_FF, moved=rows * 8000 + 2.4e6, name=name,
    )[0]


def grad_own_kernel(count, came_ref, *refs):
    xts, ys, keep_ref, send_ref = refs[:count], refs[count:-2], refs[-2], refs[-1]
    nh = NB // 2
    xt = turned_of(xts, 0)
    for t in range(HALF_FF // TILE):
        lo, hi = t * TILE, (t + 1) * TILE
        grad = mm(xt, jnp.concatenate([y[:, lo:hi] for y in ys], axis=0))
        grad = (grad.reshape(NB, RB, TILE) + came_ref[:, :, lo:hi].astype(F32)).astype(BF)
        keep_ref[:, :, lo:hi] = grad[:nh]
        send_ref[:, :, lo:hi] = grad[nh:]


def grad_own(xts, ys, came, name):
    rows = sum(y.shape[0] for y in ys)
    return call(
        partial(grad_own_kernel, len(xts)),
        [((NB // 2, RB, HALF_FF), BF)] * 2,
        [VM] * (1 + len(xts) + len(ys)), came, *xts, *ys,
        vmem=12, flops=2 * rows * D * HALF_FF, moved=rows * 8000 + 4.8e6, name=name,
    )


def natural(refs, i):
    return jnp.concatenate([ref[i * 2 + s] for s in range(2) for ref in refs], axis=0)


def attn_back_kernel(pos, r0_ref, r1_ref, r2_ref, r3_ref, qkv_ref, lse_ref, w_ref, dqkv_ref, *dat_ref):
    masks = head_masks(SPAN, HEAD ** (-0.5))
    plain = head_masks(SPAN, 1.0)
    spans = r0_ref.shape[0]

    def step(i, carry):
        r0 = pl.multiple_of(i * BLK, BLK)
        da = natural((r0_ref, r1_ref, r2_ref, r3_ref), i).astype(BF)
        if dat_ref:
            store_turned(dat_ref[0], At(pos, POS_EARLY), da, r0, BLK)
        dctx = mm(da, weight(w_ref, HALF_QKV, HALF_QKV + HALF_OUT)).astype(BF)
        pairs = [(s, j) for s in range(2) for j in range(3)]

        def part(ref, n, s, j):
            rs = pl.ds(pl.multiple_of(r0 + s * SPAN, SPAN), SPAN)
            return ref.at[rs, n * HALF_OUT + j * 128 : n * HALF_OUT + (j + 1) * 128]

        qs = [stack_heads(part(qkv_ref, 0, s, j)[...], masks) for s, j in pairs]
        ks = [part(qkv_ref, 1, s, j)[...] for s, j in pairs]
        sts = [mm(k, q, NT) for k, q in zip(ks, qs)]
        dcs = [stack_heads(dctx[s * SPAN : (s + 1) * SPAN, j * 128 : (j + 1) * 128], plain) for s, j in pairs]
        dpts = [mm(part(qkv_ref, 2, s, j)[...], dc, NT) for (s, j), dc in zip(pairs, dcs)]
        pts = [jnp.exp(st - lse_ref[i * 2 + s, j : j + 1, :]) for (s, j), st in zip(pairs, sts)]
        dvs = [mm(pt.astype(BF), dc) for pt, dc in zip(pts, dcs)]
        dsts = [
            (pt * (dpt - jnp.sum(pt * dpt, axis=0, keepdims=True))).astype(BF) for pt, dpt in zip(pts, dpts)
        ]
        dks = [mm(dst, q) for dst, q in zip(dsts, qs)]
        dqs = [merge_heads(mm(dst, k, TN)) * HEAD ** (-0.5) for dst, k in zip(dsts, ks)]
        for n, grads in enumerate((dqs, dks, dvs)):
            for (s, j), grad in zip(pairs, grads):
                part(dqkv_ref, n, s, j)[...] = grad.astype(BF)
        return carry

    lax.fori_loop(0, spans // 2, step, 0, unroll=2)


def attn_back(pos, dh1, qkv, lse, w, turned, name):
    rows = qkv.shape[0]
    out = [((rows, HALF_QKV), BF)]
    if turned:
        out.append(((2, NB, RB, rows), BF))
    return call(
        attn_back_kernel, out,
        [SM] + [VM] * 7, pos, *dh1, qkv, lse, w,
        vmem=16, flops=rows * 6e6, moved=rows * 10000 + 3e6, trans=rows * 800, name=name,
    )


def last_value(order, xt_ref, dqkv_ref, dat_ref, ctx_ref, t):
    rows = xt_ref.shape[3]
    if t < 3:
        return mm(xt_ref[order].reshape(D, rows), dqkv_ref[:, t * HALF_OUT : (t + 1) * HALF_OUT])
    return mm(dat_ref[order].reshape(D, rows), ctx_ref[...])


def norm_columns(sums):
    total = sums[0][0:4, :]
    for ref in sums[1:]:
        total = total + ref[0:4, :]
    return jnp.concatenate([total, jnp.zeros((124, D), F32)], axis=0).T


def last_other_kernel(pos, xt_ref, dqkv_ref, dat_ref, ctx_ref, s0, s1, s2, s3, out_ref):
    for t in range(4):
        grad = last_value(1, xt_ref, dqkv_ref, dat_ref, ctx_ref, t)
        lo = t * HALF_OUT
        out_ref[:, :, lo : lo + HALF_OUT] = grad.astype(BF).reshape(NB, RB, HALF_OUT)
    norm = norm_columns((s0, s1, s2, s3)).astype(BF)
    for j in range(NB):
        out_ref[pos[POS_EARLY + NB + j], :, HALF_QKV + HALF_OUT :] = norm[j * RB : (j + 1) * RB]


def last_other(pos, xt, dqkv, dat, ctx, sums):
    rows = xt.shape[3]
    return call(
        last_other_kernel,
        [((NB, RB, ONE), BF)],
        [SM] + [VM] * 8, pos, xt, dqkv, dat, ctx, *sums,
        vmem=12, flops=2 * rows * D * HALF_FF, moved=rows * 8000 + 2.4e6, name="last_other",
    )[0]


def last_own_kernel(
    pos, xt_ref, dqkv_ref, dat_ref, ctx_ref, s0, s1, s2, s3, came_ref, keep_ref, send_ref, cols
):
    nh = NB // 2
    norm = norm_columns((s0, s1, s2, s3))
    for j in range(NB):
        cols[pos[POS_EARLY + j]] = norm[j * RB : (j + 1) * RB]
    for t in range(5):
        lo = t * HALF_OUT
        hi = min(lo + HALF_OUT, ONE)
        if t < 4:
            grad = last_value(0, xt_ref, dqkv_ref, dat_ref, ctx_ref, t).reshape(NB, RB, HALF_OUT)
        else:
            grad = cols[...]
        grad = (grad + came_ref[:, :, lo:hi].astype(F32)).astype(BF)
        keep_ref[:, :, lo:hi] = grad[:nh]
        send_ref[:, :, lo:hi] = grad[nh:]


def last_own(pos, xt, dqkv, dat, ctx, sums, came):
    rows = xt.shape[3]
    return call(
        last_own_kernel,
        [((NB // 2, RB, ONE), BF)] * 2,
        [SM] + [VM] * 9, pos, xt, dqkv, dat, ctx, *sums, came,
        vmem=12, flops=2 * rows * D * HALF_FF, moved=rows * 8000 + 4.8e6,
        scratch=[pltpu.VMEM((NB, RB, 128), F32)], name="last_own",
    )


def input_grad_kernel(r0_ref, r1_ref, r2_ref, r3_ref, own_ref, other_ref, w0_ref, w1_ref, out_ref):
    spans = r0_ref.shape[0]

    def step(i, carry):
        rs = pl.ds(pl.multiple_of(i * BLK, BLK), BLK)
        total = natural((r0_ref, r1_ref, r2_ref, r3_ref), i)
        total = total + mm(own_ref[rs, :], weight(w0_ref, 0, HALF_QKV), NT)
        total = total + mm(other_ref[rs, :], weight(w1_ref, 0, HALF_QKV), NT)
        out_ref[rs, :] = total
        return carry

    lax.fori_loop(0, spans // 2, step, 0, unroll=2)


def input_grads(dh1, own, other, w_own, w_other):
    rows = own.shape[0]
    return call(
        input_grad_kernel,
        [((rows, D), F32)],
        [VM] * 8, *dh1, own, other, w_own, w_other,
        vmem=12, flops=rows * 3.6e6, moved=rows * 12000 + 5e6, name="input_grads",
    )[0]


def place_kernel(half, *refs):
    own, other, g_own, g_other = refs[0:4], refs[4:8], refs[8], refs[9]
    mixed_ref, grad_ref, sems = refs[10:]
    spans = g_own.shape[0]
    copies = []
    for n, (pieces, g) in enumerate(((own, g_own), (other, g_other))):
        at = pl.ds(half[HALF_AT + n] * spans, spans)
        for q in range(4):
            to = mixed_ref.at[at, 32 * q : 32 * q + 32, :]
            copies.append(pltpu.make_async_copy(pieces[q], to, sems.at[5 * n + q]))
        copies.append(pltpu.make_async_copy(g, grad_ref.at[at], sems.at[5 * n + 4]))
    for c in copies:
        c.start()
    for c in copies:
        c.wait()


def place(half, own, other, g_own, g_other):
    spans = own[0].shape[0]
    g_own, g_other = (g.reshape(spans, SPAN, D) for g in (g_own, g_other))
    return pl.pallas_call(
        place_kernel,
        out_shape=[
            jax.ShapeDtypeStruct((2 * spans, SPAN, D), BF),
            jax.ShapeDtypeStruct((2 * spans, SPAN, D), F32),
        ],
        in_specs=[SM] + [VM] * 10,
        out_specs=[HBM] * 2,
        scratch_shapes=[pltpu.SemaphoreType.DMA((10,))],
        compiler_params=params(16),
        cost_estimate=cost(0, spans * SPAN * D * 24),
        name="place",
    )(half, *own, *other, g_own, g_other)


def squares_kernel(k0, c0, k1, c1, k2, c2, g0, g1, g2, sq_ref):
    main = HALF_QKV + HALF_OUT
    total = jnp.zeros((1, 1), F32)
    for keep, came, out in ((k0, c0, g0), (k1, c1, g1), (k2, c2, g2)):
        grad = keep[0].astype(F32) + came[0].astype(F32)
        out[...] = grad
        sq = jnp.sum(grad[:, :main] * grad[:, :main], axis=1, keepdims=True)
        if grad.shape[1] > main:
            cols = grad[:, main:]
            sq = sq + 0.5 * jnp.sum(cols * cols, axis=1, keepdims=True)
        total = total + jnp.sum(sq, axis=0, keepdims=True)
    sq_ref[...] = jnp.broadcast_to(total, sq_ref.shape)


def squares_of(pairs):
    shard = pairs[0][0].shape[1]
    out = [((shard, k.shape[2]), F32) for k, _ in pairs] + [((8, 128), F32)]
    flat = [a for pair in pairs for a in pair]
    return call(squares_kernel, out, [VM] * 6, *flat, vmem=8, moved=shard * 40000, name="squares")


def adam_parts(weight, gradient, moment_one, moment_two, step_rate, decay_rate):
    first_new = 0.9 * moment_one + 0.1 * gradient
    second_new = 0.999 * moment_two + 0.001 * gradient * gradient
    corr_first = first_new * (1.0 / (1.0 - 0.9**STEP))
    corr_second = second_new * (1.0 / (1.0 - 0.999**STEP))
    weight_new = weight - step_rate * (
        corr_first / (jnp.sqrt(corr_second) + 1e-08) + decay_rate * weight
    )
    return first_new, second_new, weight_new


def adam_kernel(sq_ref, last_ref, up_ref, down_ref, cols_ref, *refs):
    ins, outs, wide = refs[:15], refs[15:-1], refs[-1]
    norm = jnp.sqrt(sq_ref[0:1, 0:1])
    outs[15][...] = jnp.broadcast_to(norm, outs[15].shape)
    scale = 1.0 / jnp.maximum(norm, 1.0)

    def update(n, at, grad, rate, decay):
        new = adam_parts(ins[n][at], grad * scale, ins[5 + 2 * n][at], ins[6 + 2 * n][at], rate, decay)
        for m in range(3):
            outs[3 * n + m][at] = new[m]

    for part in range(3):
        update(0, part, last_ref[:, part * HALF_OUT : (part + 1) * HALF_OUT], 0.02, 0.01)
    update(1, Ellipsis, last_ref[:, HALF_QKV : HALF_QKV + HALF_OUT], 0.02, 0.01)
    update(2, Ellipsis, up_ref[...], 0.02, 0.01)
    update(3, Ellipsis, down_ref[...], 0.02, 0.01)
    shard = last_ref.shape[0]
    wide[...] = jnp.zeros_like(wide)
    wide[0:shard, :] = 0.5 * (last_ref[:, HALF_QKV + HALF_OUT :] + cols_ref[...])
    update(4, Ellipsis, wide[...].T[0:4, 0:shard], 0.5, 0.0)


def adam(squares, last, up, down, cols, weights, moments):
    shapes = [w.shape for w in weights]
    out = [(s, F32) for s in shapes for _ in range(3)] + [((8, 128), F32)]
    args = (squares, last, up, down, cols, *weights, *moments)
    return call(
        adam_kernel, out, [VM] * len(args), *args, vmem=16, moved=7 * 4 * last.shape[0] * 4608,
        scratch=[pltpu.VMEM((128, 128), F32)], name="adam",
    )


def after(value, *others):
    return lax.optimization_barrier((value, others))[0]


def body(
    tokens,
    cotangent,
    span_doc,
    qkv_weight,
    out_weight,
    ffn_in_weight,
    ffn_out_weight,
    norm_params,
    qkv_first,
    qkv_second,
    out_first,
    out_second,
    ffn_in_first,
    ffn_in_second,
    ffn_out_first,
    ffn_out_second,
    norm_first,
    norm_second,
):
    n_dp = lax.axis_size("dp")
    dp = lax.axis_index("dp")
    core = lax.axis_index("tensor")
    shard = D // n_dp
    rows = tokens.shape[0] // 2
    spans = rows // SPAN
    direct = n_dp == NB
    early, late = bit_orders(n_dp)
    steps = len(early[0])
    last = steps - 1

    tab = lax.dynamic_index_in_dim(device_tables(n_dp), dp * 2 + core, 0, keepdims=False)
    x = lax.dynamic_slice_in_dim(tokens, core * rows, rows, 0)
    cot = lax.dynamic_slice_in_dim(cotangent, core * rows, rows, 0).reshape(spans, SPAN, D)

    def places(orders, other=0):
        return dp ^ jnp.array([rel_of(order) for order in orders], jnp.int32)[core ^ other]

    def send_on(block, orders, k):
        return lax.ppermute(block, AXES, pairs_of(n_dp, orders, k))

    def join(held, came):
        return jnp.concatenate([held, came], axis=0)

    def pieces(at, low, high):
        if direct:
            return at, tab, low, high
        which = {AT_EARLY: places(early), AT_LATE: places(late), AT_OTHER: places(early, 1)}[at]
        full = join(low, high)[jnp.argsort(which)].reshape(NB, RB, -1)
        return at, tab, full[: NB // 2], full[NB // 2 :]

    def halves(orders, keep, send):
        if direct:
            return keep, send
        full = join(keep, send).reshape(n_dp, shard, -1)[places(orders)]
        return full[: n_dp // 2], full[n_dp // 2 :]

    def add(keep, came):
        total = keep.astype(F32) + came.astype(F32)
        size = total.shape[0] // 2
        return total[:size].astype(BF), total[size:].astype(BF)

    turned = ((1, 0, 2), (1, 0), (0, 1), (1, 0), (0, 1))
    weights = (qkv_weight, out_weight, ffn_in_weight, ffn_out_weight, norm_params)
    weights = tuple(w.transpose(t) for w, t in zip(weights, turned))
    one, up, down = pack(*weights)
    one_came = send_on(one, early, 0)
    up_came = send_on(up, late, 0)
    down_came = send_on(down, early, 0)
    one, tab, x, cot, down_came = after((join(one, one_came), tab, x, cot, down_came), up_came)
    for k in range(1, last):
        one_came = send_on(one, early, k)
        if k > 1:
            up = after(join(up, up_came), one)
            up_came = send_on(up, late, k - 1)
        one = join(one, one_came)
        if k > 1:
            one = after(one, up_came)
    one_came = send_on(one, early, last)
    for k in range(max(last - 1, 1), last):
        up = join(up, up_came)
        up_came = send_on(up, late, k)
    one, one_came = after((one, one_came), up_came)
    up = after(join(up, up_came), one_came)
    up_came = send_on(up, late, last)
    down = after(join(down, down_came), one_came)
    down_came = send_on(down, early, 1)

    one_other = (core_swap(one), core_swap(one_came))
    qkv0, ctx0, lse0, w10 = attn_one(*pieces(AT_EARLY, one, one_came), x)
    ctx0 = after(ctx0, down_came)
    for k in range(2, last):
        down = join(down, after(down_came, ctx0))
        down_came = send_on(down, early, k)
    qkv1, ctx1, lse1, xh1, rstd1, prow, w11 = attn_two(*pieces(AT_OTHER, *one_other), x, w10, ctx0)
    w1 = (w10, w11)
    xh1 = xh1.reshape(rows, D)
    rstd1 = rstd1.reshape(rows, 128)
    up_came, down_came = after((up_came, down_came), xh1)
    wu = assemble(*pieces(AT_LATE, up, up_came), "up_own")
    wu = (wu, core_swap(wu))
    down = join(down, down_came)
    down_came = send_on(down, early, last)
    act0, gp0, yt = ffn_up(tab, after(xh1, down), prow, wu[0], True, "ffn_up_own")
    wd = assemble(*pieces(AT_EARLY, down, after(down_came, act0)), "down_own")
    wd = (wd, core_swap(wd))
    act1, gp1 = ffn_up(tab, after(xh1, wd[0]), prow, wu[1], False, "ffn_up_other")
    acts, gps = (act0, act1), (gp0, gp1)
    mixed0, cls_own, xh2, rstd2 = first_rows(xh1, prow, acts, wd)

    held = cls_own.astype(BF)[None]
    back = []
    one_bit, two_bit = 1 << last, 1 << (last - 1)
    for bits in [(one_bit, two_bit, one_bit ^ two_bit)] + [(1 << k,) for k in reversed(range(last - 1))]:
        came = tuple(lax.ppermute(held, "dp", [(d, d ^ bit) for d in range(n_dp)]) for bit in bits)
        if len(back) < 3:
            at = len(back) + 1
            back.append(rest_rows(at, tab, after(xh1, held), rstd1, prow, acts, gps, cot, wu, wd))
            came = after(came, back[-1][4])
        held = jnp.concatenate((held,) + came, axis=0)
    held = join(held, core_swap(held))
    loss, grad_cls = contrast(tab, span_doc.reshape(1, -1), held)
    back.insert(0, (*class_rows(tab, grad_cls, cot, xh2, rstd2, xh1, rstd1, prow, gps, wu, wd), mixed0))
    dft, du0, du1, dh1, sums, mixed_own = zip(*back)

    d_other = grad_other(dft, (act1,), "grad_down_other")
    d_came = core_swap(d_other)
    u_other = grad_other((after(yt, d_other),), du1, "grad_up_other")
    u_came = core_swap(u_other)
    d_keep, d_send = halves(
        late, *grad_own((after(dft[0], u_other),) + dft[1:], (act0,), d_came, "grad_down_own")
    )
    d_came = send_on(d_send, late, last)
    u_keep, u_send = halves(early, *grad_own((after(yt, d_keep),), du0, u_came, "grad_up_own"))
    dh1 = (after(dh1[0], u_keep),) + dh1[1:]
    tokt = turn(tab, after(x, u_keep))
    dqkv1, dat = attn_back(tab, dh1, qkv1, lse1, w1[1], True, "attn_back_other")
    l_other = last_other(tab, tokt, dqkv1, dat, ctx1, sums)

    d_came, l_other = after((d_came, l_other))
    d_keep, d_send = add(d_keep, d_came)
    u_came = send_on(after(u_send, l_other), early, last)
    d_came = send_on(d_send, late, last - 1)
    l_came = core_swap(l_other)
    (dqkv0,) = attn_back(
        tab, (after(dh1[0], l_other),) + dh1[1:], qkv0, lse0, w1[0], False, "attn_back_own"
    )
    l_keep, l_send = halves(early, *last_own(tab, tokt, dqkv0, dat, ctx0, sums, l_came))
    l_came = send_on(l_send, early, last)
    grad_in = input_grads((after(dh1[0], l_send),) + dh1[1:], dqkv0, dqkv1, w1[0], w1[1])
    u_came, d_came = after((u_came, d_came), l_send)
    u_keep, u_send = add(u_keep, u_came)
    d_keep, d_send = add(d_keep, d_came)
    u_came = send_on(u_send, early, last - 1)
    d_came = send_on(d_send, late, last - 2)
    for k in reversed(range(last)):
        l_came, *others = after((l_came, u_came, d_came)[: min(k, 2) + 1])
        u_came, d_came = (tuple(others) + (u_came, d_came)[len(others) :])
        l_keep, l_send = add(l_keep, l_came)
        l_came = send_on(l_send, early, k)
        if k > 0:
            u_keep, u_send = add(u_keep, u_came)
            u_came = send_on(u_send, early, k - 1)
        if k > 1:
            d_keep, d_send = add(d_keep, d_came)
            d_came = send_on(d_send, late, k - 2)
        if k == last - 1:
            grad_came = core_swap(after(grad_in, l_send))
            mixed_other = tuple(core_swap(m) for m in after(mixed_own, l_send))
            l_came = after(l_came, grad_came, mixed_other)
        if k == last - 2:
            mixed, input_grad = place(tab, mixed_own, mixed_other, after(grad_in, l_send), grad_came)
            l_came = after(l_came, input_grad)

    last_grad, down_grad, up_grad, squares = squares_of(((l_keep, l_came), (d_keep, d_came), (u_keep, u_came)))
    cols = core_swap(last_grad[:, HALF_QKV + HALF_OUT :])
    squares = squares + core_swap(squares)
    bits = [1 << k for k in reversed(range(steps))]
    for one_bit, two_bit in zip(bits[::2], bits[1::2]):
        near, far, both = (
            lax.ppermute(squares, "dp", [(d, d ^ b) for d in range(n_dp)])
            for b in (one_bit, two_bit, one_bit ^ two_bit)
        )
        squares = (squares + near) + (far + both)
    moments = (
        qkv_first, qkv_second, out_first, out_second, ffn_in_first, ffn_in_second,
        ffn_out_first, ffn_out_second, norm_first, norm_second,
    )
    new = adam(
        squares, last_grad, up_grad, down_grad, cols,
        weights,
        [m.transpose(turned[n // 2]) for n, m in enumerate(moments)],
    )
    updated = [value.transpose(turned[n // 3]) for n, value in enumerate(new[:15])]
    return (
        mixed.reshape(2 * rows, D),
        input_grad.reshape(2 * rows, D),
        loss[0, 0],
        new[15][0, 0],
        *updated,
    )


def solution(mesh):
    rows = P("dp", None)
    qkv = P("dp", None, "tensor")
    turned = P("tensor", "dp")
    up = P("dp", "tensor")
    norm = P(None, "dp")
    weights = (qkv, turned, up, turned, norm)
    moments = tuple(spec for spec in weights for _ in range(2))
    updated = tuple(spec for spec in weights for _ in range(3))
    return jax.shard_map(
        body,
        mesh=mesh,
        in_specs=(rows, rows, P()) + weights + moments,
        out_specs=(rows, rows, P(), P()) + updated,
        check_vma=False,
    )
```
